32 devices in a mesh: gx: 4 (over z), gy: 8 (over y, x, core).
Axes of the slice: x: 2, y: 2, z: 4, core: 2. Of those that a mesh axis runs over, the one named last changes fastest.
Arguments:
- connectivity: int32 [8, 32768], P(None, ('gx', 'gy')), may hold values from 0 to 1407, as said below
- face_nodes: int32 [4, 4896], P(None, ('gx', 'gy')), may hold values from 0 to 1407, as said below
- coords: float32 [3, 45056], P(None, ('gx', 'gy')), may hold values from -0.1 to 80.1, as said below
- displacement: float32 [3, 45056], P(None, ('gx', 'gy')), may hold values from -0.2 to 0.2, as said below
- velocity: float32 [3, 45056], P(None, ('gx', 'gy')), may hold values from -0.4 to 0.4, as said below
- node_mass: float32 [45056], P(('gx', 'gy')), may hold values from 0.5 to 2, as said below
- modulus: float32 [32768], P(('gx', 'gy')), may hold values from 1 to 10
- surf_nodes: int32 [8192, 128], P(('gx', 'gy')), may hold values from 0 to 1376
- surf_ref: float32 [8192, 3, 128], P(('gx', 'gy')), may hold values from -4 to 4
- surf_angles: float32 [8192, 2, 128], P(('gx', 'gy')), may hold values from -3.140625 to 3.140625
- owner_map: int32 [8192], replicated, may hold values from 0 to 31, as said below
- pair_blocks: int32 [2, 2048], P(None, ('gx', 'gy')), may hold values from 0 to 511, as said below
- pair_masks: int32 [2, 2048, 128], P(None, ('gx', 'gy')), may hold values 0 or 1
- pair_count: int32 [32], P(('gx', 'gy')), may hold values from 8 to 64, as said below
Outputs:
- velocity_next: float32 [3, 45056], P(None, ('gx', 'gy'))
The draws below stay inside these ranges and needn't reach their ends.
Inputs may be any that keep to these rules, and one draw needn't show every extreme that they name: `connectivity`: each device's elements are hexahedra over that device's node numbers, corners in the order of the steps; elements of one device share nodes among themselves. `face_nodes`: rows 0 and 1 list a device's nodes on its faces toward ix - 1 and ix + 1, rows 2 and 3 toward iy - 1 and iy + 1. Entry e of row 1 of a device and entry e of row 0 of the next device along gx are copies of one mesh node, likewise rows 3 and 2 along gy. Nodes on edges stand in a gx row and a gy row. Within a row the numbers are distinct, and rows 0 and 1 (2 and 3) share none. `coords`: copies of one mesh node on different devices carry equal values. The corners of every element are near the corners of a unit cube. `displacement`: copies of one mesh node on different devices carry equal values. `velocity`: copies of one mesh node on different devices carry equal values. `node_mass`: copies of one mesh node on different devices carry equal values. `owner_map`: block k belongs to the mesh partition of device k // 256. No partition has more than 16 blocks with one owner, and every owner has two blocks or more. `pair_blocks`: the two ranks of a pair differ and are smaller than the number of blocks that owner_map gives to the device that holds the pair. Only the first pair_count pairs of an owner are live.
All inputs are finite; a program needn't handle non-finite values. No bound on the sum of `pair_masks` on one device may be relied on, other than what follows from the above.
Results may differ from the reference program's by a relative error of at most 0.0003.
Values sent between devices are 32-bit elements; how exact they have to be, the bound alone decides.
No kernel may reach another device: no remote copies, remote signals or barrier semaphores. Data moves between devices by JAX's collectives and lax.ppermute only.
A program may use at most 128 MiB of HBM per device.

```python
import math
import jax
import jax.numpy as jnp
import numpy as np
from jax import lax

AX = 8
AZ = 16
SB_DEV = 256
SEG = 128
PAIRS_DEV = 64
E_DEV = 1024
NREAL = 1377
NODES_DEV = 1408
FACE = 153
CAP = 16
ELEMS = 32768
BLOCKS = 8192
PAIRS = 2048
N_GX = 4
N_GY = 8
DEVICES = 32


def grid_parts():
    side = AX + 1
    depth = AZ + 1
    index = np.arange(NREAL)
    return (index // (side * depth), index // depth % side, index % depth)


def local_ids(key):
    base = jax.random.fold_in(key, 11)

    def one(device):
        return jax.random.permutation(jax.random.fold_in(base, device), NODES_DEV)[:NREAL]
    return jax.vmap(one)(jnp.arange(DEVICES)).astype(jnp.int32)


def draw_connectivity(key, part):
    ids = local_ids(key)
    side = AX + 1
    depth = AZ + 1
    cell = np.arange(E_DEV)
    cell_a = cell // (AX * AZ)
    cell_b = cell // AZ % AX
    cell_c = cell % AZ
    offsets = [(0, 0, 0), (1, 0, 0), (1, 1, 0), (0, 1, 0), (0, 0, 1), (1, 0, 1), (1, 1, 1), (0, 1, 1)]
    corner_index = np.stack([((cell_a + offset[0]) * side + cell_b + offset[1]) * depth + cell_c + offset[2] for offset in offsets])
    table = ids[:, corner_index]
    return jnp.transpose(table, (1, 0, 2)).reshape(8, DEVICES * E_DEV)


def draw_face_nodes(key, part):
    ids = local_ids(key)
    side = AX + 1
    depth = AZ + 1
    across, height = np.meshgrid(np.arange(side), np.arange(depth), indexing='ij')
    across = across.reshape(-1)
    height = height.reshape(-1)
    rows = np.stack([(0 * side + across) * depth + height, (AX * side + across) * depth + height, (across * side + 0) * depth + height, (across * side + AX) * depth + height])
    table = ids[:, rows]
    return jnp.transpose(table, (1, 0, 2)).reshape(4, DEVICES * FACE)


def spread(key, glob, filler):
    ids = local_ids(key)
    part_a, part_b, part_c = grid_parts()

    def one(device, ident, padding):
        row_x = device // N_GY
        row_y = device % N_GY
        values = glob[:, row_x * AX + part_a, row_y * AX + part_b, part_c]
        return padding.at[:, ident].set(values)
    result = jax.vmap(one)(jnp.arange(DEVICES), ids, filler)
    return jnp.transpose(result, (1, 0, 2)).reshape(glob.shape[0], DEVICES * NODES_DEV)


def global_shape(comps):
    return (comps, N_GX * AX + 1, N_GY * AX + 1, AZ + 1)


def draw_coords(key, part):
    shape = global_shape(3)
    base = jnp.stack(jnp.meshgrid(jnp.arange(shape[1]), jnp.arange(shape[2]), jnp.arange(shape[3]), indexing='ij')).astype(jnp.float32)
    glob = base + jax.random.uniform(jax.random.fold_in(key, 31), shape, jnp.float32, -0.1, 0.1)
    filler = jax.random.uniform(jax.random.fold_in(key, 32), (DEVICES, 3, NODES_DEV), jnp.float32)
    return spread(key, glob, filler)


def draw_displacement(key, part):
    shape = global_shape(3)
    glob = jnp.clip(0.05 * jax.random.normal(jax.random.fold_in(key, 41), shape, jnp.float32), -0.2, 0.2)
    filler = jnp.clip(0.05 * jax.random.normal(jax.random.fold_in(key, 42), (DEVICES, 3, NODES_DEV), jnp.float32), -0.2, 0.2)
    return spread(key, glob, filler)


def draw_velocity(key, part):
    shape = global_shape(3)
    glob = jnp.clip(0.1 * jax.random.normal(jax.random.fold_in(key, 51), shape, jnp.float32), -0.4, 0.4)
    filler = jnp.clip(0.1 * jax.random.normal(jax.random.fold_in(key, 52), (DEVICES, 3, NODES_DEV), jnp.float32), -0.4, 0.4)
    return spread(key, glob, filler)


def draw_node_mass(key, part):
    shape = global_shape(1)
    low = float(np.log(0.5))
    high = float(np.log(2.0))
    glob = jnp.exp(jax.random.uniform(jax.random.fold_in(key, 61), shape, jnp.float32, low, high))
    filler = jnp.exp(jax.random.uniform(jax.random.fold_in(key, 62), (DEVICES, 1, NODES_DEV), jnp.float32, low, high))
    return spread(key, glob, filler).reshape(-1)


def owners(key):
    base = jax.random.fold_in(key, 21)
    hot = jax.random.randint(jax.random.fold_in(base, 1), (), 0, DEVICES)
    slot_total = DEVICES * CAP
    slot_owner = jnp.arange(slot_total, dtype=jnp.int32) // CAP
    index = jnp.arange(slot_total, dtype=jnp.int32)

    def one(source):
        score = jax.random.permutation(jax.random.fold_in(jax.random.fold_in(base, 2), source), slot_total).astype(jnp.int32)
        first = (source + 1) % DEVICES * CAP
        second = (source + 2) % DEVICES * CAP
        score = jnp.where((index == first) | (index == second), -2, score)
        score = jnp.where(slot_owner == hot, -3, score)
        order = jnp.argsort(score, stable=True)[:SB_DEV]
        chosen = slot_owner[order]
        shuffle = jax.random.permutation(jax.random.fold_in(jax.random.fold_in(base, 3), source), SB_DEV)
        return chosen[shuffle]
    table = jax.vmap(one)(jnp.arange(DEVICES, dtype=jnp.int32))
    return (table.reshape(-1).astype(jnp.int32), hot)


def draw_owner_map(key, part):
    table, hot = owners(key)
    return table


def draw_pair_count(key, part):
    table, hot = owners(key)
    counts = jax.random.randint(jax.random.fold_in(key, 71), (DEVICES,), PAIRS_DEV // 8, PAIRS_DEV // 2 + 1)
    return jnp.where(jnp.arange(DEVICES) == hot, PAIRS_DEV, counts).astype(jnp.int32)


def draw_pair_blocks(key, part):
    table, hot = owners(key)
    counts = jax.ops.segment_sum(jnp.ones_like(table), table, DEVICES)
    owner_of = jnp.arange(DEVICES * PAIRS_DEV, dtype=jnp.int32) // PAIRS_DEV
    owned = jnp.maximum(counts[owner_of], 2)
    first = jax.random.randint(jax.random.fold_in(key, 81), owner_of.shape, 0, owned)
    step_on = jax.random.randint(jax.random.fold_in(key, 82), owner_of.shape, 0, owned - 1)
    second = (first + 1 + step_on) % owned
    lead = jnp.arange(DEVICES * PAIRS_DEV, dtype=jnp.int32) % PAIRS_DEV == 0
    first = jnp.where(lead, 0, first)
    second = jnp.where(lead, owned - 1, second)
    return jnp.stack([first, second]).astype(jnp.int32)


def set_ends(values, rng, smallest, largest):
    dims = values.shape
    index_at = [jax.random.randint(jax.random.fold_in(rng, axis), (), 0, dims[axis]) for axis in range(len(dims))]
    values = values.at[tuple(index_at)].set(smallest)
    longest = dims.index(max(dims))
    index_at[longest] = (index_at[longest] + 1) % dims[longest]
    return values.at[tuple(index_at)].set(largest)


def block_levels(rng, dims, cuts, least, high):
    def one(axis_at, shards_of):
        steps = jax.random.uniform(jax.random.fold_in(jax.random.fold_in(rng, 6), axis_at), (shards_of,), jnp.float32, least / len(cuts), high / len(cuts))
        return jnp.repeat(jnp.exp(steps), dims[axis_at] // shards_of).reshape((-1,) + (1,) * (len(dims) - axis_at - 1))

    gain = one(*cuts[0])
    for cut in cuts[1:]:
        gain = gain * one(*cut)
    return gain


def centred(own_key, dims, scale, bound, shards=(), held_as=jnp.bfloat16):
    values = scale * jax.random.normal(own_key, dims, jnp.float32)
    if shards:
        values = values * block_levels(own_key, dims, shards, -0.22, 0.18)
    return jnp.clip(values, -bound, bound).astype(held_as)


def setup_inputs(seed: int = 0) -> dict:
    key_of = jax.random.split(jax.random.key(seed), 15)
    return {
        "connectivity": draw_connectivity(jax.random.fold_in(key_of[14], 71), 0),
        "face_nodes": draw_face_nodes(jax.random.fold_in(key_of[14], 71), 0),
        "coords": draw_coords(jax.random.fold_in(key_of[14], 71), 0),
        "displacement": draw_displacement(jax.random.fold_in(key_of[14], 71), 0),
        "velocity": draw_velocity(jax.random.fold_in(key_of[14], 71), 0),
        "node_mass": draw_node_mass(jax.random.fold_in(key_of[14], 71), 0),
        "modulus": jnp.clip(jnp.exp(math.log(10.0) - 2.3025851 * jax.random.uniform(key_of[6], (ELEMS,), jnp.float32) ** block_levels(key_of[6], (ELEMS,), ((0, 32),), -0.2, 0.2)), 1.0, 10.0),
        "surf_nodes": set_ends(jax.random.randint(key_of[7], (BLOCKS, SEG), 0, NREAL), jax.random.fold_in(key_of[7], 1), 0, NREAL - 1).astype(jnp.int32),
        "surf_ref": centred(key_of[8], (BLOCKS, 3, SEG), 1.0, 4.0, ((0, 32),), jnp.float32),
        "surf_angles": jnp.clip(jax.random.uniform(key_of[9], (BLOCKS, 2, SEG), jnp.float32, -3.140625, 3.140625), -3.140625, 3.140625),
        "owner_map": draw_owner_map(jax.random.fold_in(key_of[14], 71), 0),
        "pair_blocks": draw_pair_blocks(jax.random.fold_in(key_of[14], 71), 0),
        "pair_masks": set_ends((jax.random.randint(key_of[12], (2, PAIRS, SEG), 0, 4) < 3).astype(jnp.int32), jax.random.fold_in(key_of[12], 1), 0, 1),
        "pair_count": draw_pair_count(jax.random.fold_in(key_of[14], 71), 0),
    }


XI_SIGNS = [[-1, -1, -1], [1, -1, -1], [1, 1, -1], [-1, 1, -1], [-1, -1, 1], [1, -1, 1], [1, 1, 1], [-1, 1, 1]]
HOUR_VEC = [[1, 1, -1, -1, -1, -1, 1, 1], [1, -1, -1, 1, -1, 1, 1, -1], [1, -1, 1, -1, 1, -1, 1, -1], [-1, 1, -1, 1, 1, -1, 1, -1]]
HG_COEF = 0.05
PEN_STIFF = 0.05
PEN_DEPTH = 0.5
TIME_STEP = 0.2


def cofactor_matrix(jacobian):
    rows = [
        [jacobian[1, 1] * jacobian[2, 2] - jacobian[1, 2] * jacobian[2, 1],
         jacobian[1, 2] * jacobian[2, 0] - jacobian[1, 0] * jacobian[2, 2],
         jacobian[1, 0] * jacobian[2, 1] - jacobian[1, 1] * jacobian[2, 0]],
        [jacobian[0, 2] * jacobian[2, 1] - jacobian[0, 1] * jacobian[2, 2],
         jacobian[0, 0] * jacobian[2, 2] - jacobian[0, 2] * jacobian[2, 0],
         jacobian[0, 1] * jacobian[2, 0] - jacobian[0, 0] * jacobian[2, 1]],
        [jacobian[0, 1] * jacobian[1, 2] - jacobian[0, 2] * jacobian[1, 1],
         jacobian[0, 2] * jacobian[1, 0] - jacobian[0, 0] * jacobian[1, 2],
         jacobian[0, 0] * jacobian[1, 1] - jacobian[0, 1] * jacobian[1, 0]],
    ]
    return jnp.stack([jnp.stack(line) for line in rows])


def element_forces(coords, displacement, connectivity, modulus):
    highest = lax.Precision.HIGHEST
    real_type = coords.dtype
    signs = jnp.asarray(XI_SIGNS, real_type)
    hour = jnp.asarray(HOUR_VEC, real_type)
    corner_pos = coords[:, connectivity]
    corner_pos = corner_pos - corner_pos[:, 0:1]
    corner_disp = displacement[:, connectivity]
    jacobian = jnp.einsum("jie,ik->jke", corner_pos, signs, precision=highest) / 8.0
    cofactors = cofactor_matrix(jacobian)
    determinant = jnp.sum(jacobian[0] * cofactors[0], axis=0)
    volume = 8.0 * determinant
    gradient = jnp.einsum("jke,ik->ije", cofactors, signs, precision=highest) / (8.0 * determinant)
    disp_grad = jnp.einsum("iIe,Ije->ije", corner_disp, gradient, precision=highest)
    strain = 0.5 * (disp_grad + jnp.swapaxes(disp_grad, 0, 1))
    dilation = strain[0, 0] + strain[1, 1] + strain[2, 2]
    stress = modulus * (dilation * jnp.eye(3, dtype=real_type)[:, :, None] + 2.0 * strain)
    hour_pos = jnp.einsum("aI,jIe->aje", hour, corner_pos, precision=highest)
    hour_shape = hour[:, :, None] - jnp.einsum("aje,Ije->aIe", hour_pos, gradient, precision=highest)
    hour_mode = jnp.einsum("iIe,aIe->aie", corner_disp, hour_shape, precision=highest)
    hour_coef = HG_COEF * modulus * volume * jnp.sum(gradient * gradient, axis=(0, 1))
    corner_force = -volume * jnp.einsum("ije,Ije->iIe", stress, gradient, precision=highest)
    corner_force = corner_force - hour_coef * jnp.einsum("aie,aIe->iIe", hour_mode, hour_shape, precision=highest)
    return jnp.zeros_like(coords).at[:, connectivity.reshape(-1)].add(corner_force.reshape(3, -1))


def segment_blocks(displacement, surf_nodes, surf_ref, surf_angles):
    position = surf_ref + jnp.moveaxis(displacement[:, surf_nodes], 0, 1)
    azimuth = surf_angles[:, 0]
    polar = surf_angles[:, 1]
    normal = jnp.stack([jnp.cos(azimuth) * jnp.cos(polar), jnp.sin(azimuth) * jnp.cos(polar), jnp.sin(polar)], axis=1)
    return jnp.concatenate([position, normal], axis=1)


def tile_forces(slave, master, mask_slave, mask_master, live):
    highest = lax.Precision.HIGHEST
    distance = slave[:, 0:3, :, None] - master[:, 0:3, None, :]
    normal = master[:, 3:6]
    gap = jnp.sum(normal[:, :, None, :] * distance, axis=1)
    tangent = jnp.sum(distance * distance, axis=1) - gap * gap
    weight = jnp.exp(-0.5 * tangent) * mask_slave[:, :, None] * mask_master[:, None, :]
    press = PEN_STIFF * PEN_DEPTH * jax.nn.softplus(-gap / PEN_DEPTH) * weight * live[:, None, None]
    on_slave = jnp.einsum("bij,bkj->bki", press, normal, precision=highest)
    on_master = -normal * jnp.sum(press, axis=1)[:, None, :]
    return on_slave, on_master


def shared_section(total, faces, low_row, high_row, grid_axis):
    def pick(field, index):
        return field[:, index]

    def place(field, index, values):
        return field.at[:, index].add(values)

    lower = jax.vmap(pick)(total, faces[:, low_row])
    upper = jax.vmap(pick)(total, faces[:, high_row])
    shape = lower.shape
    lower = lower.reshape((N_GX, N_GY) + shape[1:])
    upper = upper.reshape((N_GX, N_GY) + shape[1:])
    if grid_axis == 0:
        from_prev = jnp.concatenate([jnp.zeros_like(upper[:1]), upper[:-1]], axis=0)
        from_next = jnp.concatenate([lower[1:], jnp.zeros_like(lower[:1])], axis=0)
    else:
        from_prev = jnp.concatenate([jnp.zeros_like(upper[:, :1]), upper[:, :-1]], axis=1)
        from_next = jnp.concatenate([lower[:, 1:], jnp.zeros_like(lower[:, :1])], axis=1)
    total = jax.vmap(place)(total, faces[:, low_row], from_prev.reshape(shape))
    return jax.vmap(place)(total, faces[:, high_row], from_next.reshape(shape))


def reference(connectivity, face_nodes, coords, displacement, velocity, node_mass, modulus, surf_nodes, surf_ref, surf_angles, owner_map, pair_blocks, pair_masks, pair_count):
    devices = N_GX * N_GY
    conn_dev = jnp.transpose(connectivity.reshape(8, devices, E_DEV), (1, 0, 2))
    faces_dev = jnp.transpose(face_nodes.reshape(4, devices, FACE), (1, 0, 2))
    coords_dev = jnp.transpose(coords.reshape(3, devices, NODES_DEV), (1, 0, 2))
    disp_dev = jnp.transpose(displacement.reshape(3, devices, NODES_DEV), (1, 0, 2))
    vel_dev = jnp.transpose(velocity.reshape(3, devices, NODES_DEV), (1, 0, 2))
    mass_dev = node_mass.reshape(devices, NODES_DEV)
    mod_dev = modulus.reshape(devices, E_DEV)
    internal = lax.map(lambda items: element_forces(items[0], items[1], items[2], items[3]), (coords_dev, disp_dev, conn_dev, mod_dev))
    nodes_dev = surf_nodes.reshape(devices, SB_DEV, SEG)
    segments = jax.vmap(segment_blocks)(disp_dev, nodes_dev, surf_ref.reshape(devices, SB_DEV, 3, SEG), surf_angles.reshape(devices, SB_DEV, 2, SEG))
    segments = segments.reshape(devices * SB_DEV, 6, SEG)
    block_order = jnp.argsort(owner_map, stable=True).astype(jnp.int32)
    owner_counts = jnp.sum((owner_map[None, :] == jnp.arange(devices, dtype=jnp.int32)[:, None]).astype(jnp.int32), axis=1)
    owner_starts = (jnp.cumsum(owner_counts) - owner_counts).astype(jnp.int32)
    pair_ids = jnp.transpose(pair_blocks.reshape(2, devices, PAIRS_DEV), (1, 0, 2))
    masks = jnp.transpose(pair_masks.reshape(2, devices, PAIRS_DEV, SEG), (1, 0, 2, 3)).astype(jnp.float32)

    def owner_step(totals, items):
        ranks, mask_pair, count, owner = items
        ids = block_order[jnp.clip(owner_starts[owner] + ranks, 0, devices * SB_DEV - 1).astype(jnp.int32)]
        live = (jnp.arange(PAIRS_DEV, dtype=jnp.int32) < count).astype(jnp.float32)
        on_slave, on_master = tile_forces(segments[ids[0]], segments[ids[1]], mask_pair[0], mask_pair[1], live)
        totals = totals.at[ids[0]].add(on_slave)
        return totals.at[ids[1]].add(on_master), None

    start = jnp.zeros((devices * SB_DEV, 3, SEG), jnp.float32)
    seg_force, unused = lax.scan(owner_step, start, (pair_ids, masks, pair_count, jnp.arange(devices, dtype=jnp.int32)))
    seg_force = seg_force.reshape(devices, SB_DEV, 3, SEG)

    def contact_nodes(nodes, forces):
        flat = jnp.moveaxis(forces, 1, 0).reshape(3, -1)
        return jnp.zeros((3, NODES_DEV), jnp.float32).at[:, nodes.reshape(-1)].add(flat)

    total = internal + jax.vmap(contact_nodes)(nodes_dev, seg_force)
    total = shared_section(total, faces_dev, 0, 1, 0)
    total = shared_section(total, faces_dev, 2, 3, 1)
    result = vel_dev + TIME_STEP * total / mass_dev[:, None, :]
    return jnp.transpose(result, (1, 0, 2)).reshape(3, devices * NODES_DEV)
```

```python
import functools

import jax
import jax.numpy as jnp
from jax import lax
from jax.experimental import pallas as pl
from jax.experimental.pallas import tpu as pltpu
from jax.sharding import PartitionSpec as P

XI_SIGNS = [
    [-1, -1, -1],
    [1, -1, -1],
    [1, 1, -1],
    [-1, 1, -1],
    [-1, -1, 1],
    [1, -1, 1],
    [1, 1, 1],
    [-1, 1, 1],
]
HOUR_VEC = [
    [1, 1, -1, -1, -1, -1, 1, 1],
    [1, -1, -1, 1, -1, 1, 1, -1],
    [1, -1, 1, -1, 1, -1, 1, -1],
    [-1, 1, -1, 1, 1, -1, 1, -1],
]
HG_COEF = 0.05
PEN_STIFF = 0.05
PEN_DEPTH = 0.5
TIME_STEP = 0.2
LANES = 128
GROUP = 16
F32 = jnp.float32
BF16 = jnp.bfloat16
VMEM_LIMIT = 48 * 1024 * 1024


def iota(shape, dim):
    return lax.broadcasted_iota(jnp.int32, shape, dim)


def dot_nn(a, b):
    return lax.dot_general(a, b, (((1,), (0,)), ((), ())), preferred_element_type=F32)


def dot_nt(a, b):
    return lax.dot_general(a, b, (((1,), (1,)), ((), ())), preferred_element_type=F32)


def dot_tn(a, b):
    return lax.dot_general(a, b, (((0,), (0,)), ((), ())), preferred_element_type=F32)


def as_bf16(mask):
    return jnp.where(mask, 1.0, 0.0).astype(BF16)


def split2(x):
    high = x.astype(BF16)
    return high, (x - high.astype(F32)).astype(BF16)


def split3(x):
    high = x.astype(BF16)
    rest = x - high.astype(F32)
    mid = rest.astype(BF16)
    return high, mid, (rest - mid.astype(F32)).astype(BF16)


def strict_upper(size):
    return as_bf16(iota((size, size), 0) < iota((size, size), 1))


def take_lanes(row, index):
    table = jnp.broadcast_to(row, index.shape)
    return jnp.take_along_axis(table, index, axis=1, mode="promise_in_bounds")


def gather_chunks(rows_of, fields, chunks, ids):
    high = ids >> 7
    low = ids & (LANES - 1)
    found = [jnp.zeros(ids.shape, F32) for _ in range(fields)]
    for chunk in range(chunks):
        here = high == chunk
        for field in range(fields):
            found[field] = jnp.where(here, take_lanes(rows_of(field, chunk), low), found[field])
    return found


def scatter_terms(id_rows, force_rows):
    wide = []
    table = []
    for ids, forces in zip(id_rows, force_rows):
        here = jnp.broadcast_to(ids >> 7, (GROUP, LANES)) == iota((GROUP, LANES), 0)
        wide.append(
            jnp.concatenate(
                [jnp.where(here, jnp.broadcast_to(f, (GROUP, LANES)), 0.0) for f in forces], axis=0
            )
        )
        low = jnp.broadcast_to(ids & (LANES - 1), (LANES, LANES))
        table.append(as_bf16(low == iota((LANES, LANES), 0)))
    high, rest = split2(jnp.concatenate(wide, axis=1))
    both = jnp.concatenate([high, rest], axis=0)
    return dot_nt(both, jnp.concatenate(table, axis=1))


def fold_terms(acc):
    half = acc.shape[0] // 2
    return acc[:half] + acc[half:]


def routing_kernel(rows_per, own_ref, count_ref, map_ref, pairs_ref, index_ref):
    own = own_ref[0]
    rows = map_ref.shape[0]
    devices = rows // rows_per
    pairs = pairs_ref.shape[1]
    hit = as_bf16(map_ref[...] == own)
    source_of = iota((devices, rows), 1) // rows_per
    upto = as_bf16(source_of <= iota((devices, rows), 0))
    within = as_bf16(source_of == iota((devices, rows), 0))
    ends = jnp.sum(dot_nn(upto, hit), axis=1, keepdims=True)
    counts = jnp.sum(dot_nn(within, hit), axis=1, keepdims=True)
    ranks = pairs_ref[...].astype(F32)
    for side in range(2):
        rank = ranks[side : side + 1]
        below = jnp.broadcast_to(ends, (devices, pairs)) <= rank
        source = jnp.sum(jnp.where(below, 1.0, 0.0), axis=0, keepdims=True)
        source = jnp.minimum(source, devices - 1.0)
        start = jnp.sum(jnp.where(below, counts, 0.0), axis=0, keepdims=True)
        index_ref[2 * side : 2 * side + 1, :] = source.astype(jnp.int32)
        index_ref[2 * side + 1 : 2 * side + 2, :] = (rank - start).astype(jnp.int32)


def segment_kernel(disp_ref, nodes_ref, ref_ref, pos_ref):
    chunks = disp_ref.shape[1] // LANES

    def step(turn, carry):
        base = pl.multiple_of(turn * 8, 8)
        ids = nodes_ref[pl.ds(base, 8), :]
        found = gather_chunks(
            lambda field, chunk: disp_ref[field : field + 1, chunk * LANES : (chunk + 1) * LANES],
            3,
            chunks,
            ids,
        )
        for field in range(3):
            pos_ref[field, pl.ds(base, 8), :] = found[field] + ref_ref[pl.ds(base, 8), field, :]
        return carry

    lax.fori_loop(0, nodes_ref.shape[0] // 8, step, 0, unroll=2)


def pack_kernel(slots, rows_per, own_ref, map_ref, pos_ref, angles_ref, nodes_ref, out_ref, ids_ref):
    own = own_ref[0]
    devices = map_ref.shape[0] // rows_per
    owner = jnp.concatenate(
        [map_ref[pl.ds(own * rows_per + i, 1), :] for i in range(rows_per)], axis=1
    )
    blocks = owner.shape[1]
    mine = iota((devices, blocks), 0) == owner
    before = dot_nn(as_bf16(mine), strict_upper(blocks))
    rank = jnp.sum(jnp.where(mine, before, 0.0), axis=0, keepdims=True).astype(jnp.int32)
    place = owner * slots + rank
    move = as_bf16(iota((devices * slots, blocks), 0) == place)
    for field in range(5):
        values = pos_ref[field] if field < 3 else angles_ref[:, field - 3, :]
        moved = dot_nn(move, jnp.concatenate(split3(values), axis=1))
        moved = moved[:, :LANES] + moved[:, LANES : 2 * LANES] + moved[:, 2 * LANES :]
        out_ref[:, field * slots : (field + 1) * slots, :] = moved.reshape(devices, slots, LANES)
    nodes = nodes_ref[...]
    halves = jnp.concatenate(
        [(nodes >> 7).astype(F32).astype(BF16), (nodes & (LANES - 1)).astype(F32).astype(BF16)],
        axis=1,
    )
    moved = dot_nn(move, halves)
    ids_ref[...] = (moved[:, :LANES] * LANES + moved[:, LANES:]).astype(jnp.int32)


def sine_cosine(angle):
    half = 0.5 * angle
    sq = half * half
    sine = sq * (-1.0 / 39916800.0) + 1.0 / 362880.0
    for coef in (-1.0 / 5040.0, 1.0 / 120.0, -1.0 / 6.0, 1.0):
        sine = sine * sq + coef
    sine = sine * half
    cosine = sq * (1.0 / 479001600.0) - 1.0 / 3628800.0
    for coef in (1.0 / 40320.0, -1.0 / 720.0, 1.0 / 24.0, -0.5, 1.0):
        cosine = cosine * sq + coef
    return 2.0 * sine * cosine, 1.0 - 2.0 * sine * sine


def pair_kernel(
    slots, index_ref, count_ref, in_ref, masks_ref, out_ref, slave_ref, master_ref, sin_ref, cos_ref
):
    pairs = masks_ref.shape[1]
    count = jnp.minimum(count_ref[0], pairs)
    out_ref[...] = jnp.zeros_like(out_ref)

    def stage(pair, carry):
        source = index_ref[0, pair]
        slot = index_ref[1, pair]
        for field in range(3):
            slave_ref[pl.ds(pair * 8 + field, 1), :] = in_ref[source, pl.ds(field * slots + slot, 1), :]
        slave_ref[pl.ds(pair * 8 + 3, 1), :] = masks_ref[0, pl.ds(pair, 1), :].astype(F32)
        source = index_ref[2, pair]
        slot = index_ref[3, pair]
        for field in range(5):
            master_ref[pl.ds(pair * 8 + field, 1), :] = in_ref[source, pl.ds(field * slots + slot, 1), :]
        master_ref[pl.ds(pair * 8 + 5, 1), :] = masks_ref[1, pl.ds(pair, 1), :].astype(F32)
        return carry

    lax.fori_loop(0, count, stage, 0)
    sines, cosines = sine_cosine(master_ref[...])
    sin_ref[...] = sines
    cos_ref[...] = cosines

    def tile(pair, carry):
        base = pl.multiple_of(pair * 8, 8)
        slave = slave_ref[pl.ds(base, 8), :]
        columns = jnp.transpose(slave)
        master = master_ref[pl.ds(base, 8), :]
        sin_az = sin_ref[pl.ds(base + 3, 1), :]
        sin_pol = sin_ref[pl.ds(base + 4, 1), :]
        cos_az = cos_ref[pl.ds(base + 3, 1), :]
        cos_pol = cos_ref[pl.ds(base + 4, 1), :]
        normal = [cos_az * cos_pol, sin_az * cos_pol, sin_pol]
        shape = (LANES, LANES)
        dist = [
            jnp.broadcast_to(columns[:, k : k + 1], shape) - jnp.broadcast_to(master[k : k + 1], shape)
            for k in range(3)
        ]
        gap = dist[0] * normal[0] + dist[1] * normal[1] + dist[2] * normal[2]
        tang = dist[0] * dist[0] + dist[1] * dist[1] + dist[2] * dist[2] - gap * gap
        bend = gap * (-1.0 / PEN_DEPTH)
        soft = jnp.maximum(bend, 0.0) + jnp.log(1.0 + jnp.exp(-jnp.abs(bend)))
        press = soft * jnp.exp(-0.5 * tang)
        press = press * jnp.broadcast_to(columns[:, 3:4], shape)
        total = jnp.sum(press, axis=0, keepdims=True)
        scale = PEN_STIFF * PEN_DEPTH * master[5:6]
        push = [n * scale for n in normal]
        rows = jnp.concatenate(push + [jnp.zeros((5, LANES), F32)], axis=0)
        push_high, push_rest = split2(rows)
        both = jnp.concatenate([push_high, push_rest], axis=0)
        high, rest = split2(press)
        got = dot_nt(both, high) + dot_nt(both, rest)
        on_slave = got[0:8] + got[8:16]
        source = index_ref[0, pair]
        slot = index_ref[1, pair]
        for k in range(3):
            at = pl.ds(k * slots + slot, 1)
            out_ref[source, at, :] = out_ref[source, at, :] + on_slave[k : k + 1]
        source = index_ref[2, pair]
        slot = index_ref[3, pair]
        for k in range(3):
            at = pl.ds(k * slots + slot, 1)
            out_ref[source, at, :] = out_ref[source, at, :] - push[k] * total
        return carry

    lax.fori_loop(0, count, tile, 0)


def element_kernel(conn_ref, coords_ref, disp_ref, modulus_ref, out_ref, order_ref):
    chunks = coords_ref.shape[1] // LANES
    groups = conn_ref.shape[1] // LANES
    for group in range(groups):
        order_ref[pl.ds(group * 8, 8), :] = conn_ref[:, group * LANES : (group + 1) * LANES]
    pos = []
    disp = []
    for corner in range(8):
        ids = order_ref[pl.ds(corner, groups, stride=8), :]
        found = gather_chunks(
            lambda field, chunk: (coords_ref if field < 3 else disp_ref)[
                field % 3 : field % 3 + 1, chunk * LANES : (chunk + 1) * LANES
            ],
            6,
            chunks,
            ids,
        )
        pos.append(found[:3])
        disp.append(found[3:])
    first = list(pos[0])
    pos = [[pos[corner][j] - first[j] for j in range(3)] for corner in range(8)]

    def signed(values, signs):
        total = None
        for value, sign in zip(values, signs):
            if total is None:
                total = value if sign > 0 else -value
            else:
                total = total + value if sign > 0 else total - value
        return total

    corner_signs = [[XI_SIGNS[corner][k] for corner in range(8)] for k in range(3)]
    jac = [
        [signed([pos[c][j] for c in range(8)], corner_signs[k]) * 0.125 for k in range(3)]
        for j in range(3)
    ]
    cof = [
        [
            jac[(j + 1) % 3][(k + 1) % 3] * jac[(j + 2) % 3][(k + 2) % 3]
            - jac[(j + 1) % 3][(k + 2) % 3] * jac[(j + 2) % 3][(k + 1) % 3]
            for k in range(3)
        ]
        for j in range(3)
    ]
    det = jac[0][0] * cof[0][0] + jac[0][1] * cof[0][1] + jac[0][2] * cof[0][2]
    volume = 8.0 * det
    inverse = 1.0 / volume
    scaled = [[cof[j][k] * inverse for k in range(3)] for j in range(3)]
    grad = [[signed(scaled[j], XI_SIGNS[c]) for j in range(3)] for c in range(8)]

    def summed(terms):
        total = terms[0]
        for term in terms[1:]:
            total = total + term
        return total

    ugrad = [
        [summed([disp[c][i] * grad[c][j] for c in range(8)]) for j in range(3)] for i in range(3)
    ]
    modulus = modulus_ref[...]
    dilation = ugrad[0][0] + ugrad[1][1] + ugrad[2][2]
    stress = [[modulus * (ugrad[i][j] + ugrad[j][i]) for j in range(3)] for i in range(3)]
    for i in range(3):
        stress[i][i] = stress[i][i] + modulus * dilation
    squares = summed([grad[c][j] * grad[c][j] for c in range(8) for j in range(3)])
    hour_coef = HG_COEF * modulus * volume * squares
    shapes = []
    modes = []
    for a in range(4):
        hour_pos = [signed([pos[c][j] for c in range(8)], HOUR_VEC[a]) for j in range(3)]
        gam = [
            float(HOUR_VEC[a][c]) - summed([hour_pos[j] * grad[c][j] for j in range(3)])
            for c in range(8)
        ]
        shapes.append(gam)
        modes.append(
            [hour_coef * summed([disp[c][i] * gam[c] for c in range(8)]) for i in range(3)]
        )
    flux = [[volume * stress[i][j] for j in range(3)] for i in range(3)]
    acc = jnp.zeros((6 * GROUP, LANES), F32)
    for corner in range(8):
        ids = order_ref[pl.ds(corner, groups, stride=8), :]
        force = []
        for i in range(3):
            value = summed([flux[i][j] * grad[corner][j] for j in range(3)])
            value = value + summed([modes[a][i] * shapes[a][corner] for a in range(4)])
            force.append(-value)
        for group in range(0, groups, 2):
            picks = range(group, min(group + 2, groups))
            acc = acc + scatter_terms(
                [ids[g : g + 1] for g in picks], [[f[g : g + 1] for f in force] for g in picks]
            )
    out_ref[...] = fold_terms(acc)


def send_faces(total_ref, chunks, faces_ref, low_row, low_ref, high_ref):
    low_ref[...] = jnp.zeros_like(low_ref)
    high_ref[...] = jnp.zeros_like(high_ref)
    parts = faces_ref.shape[1] // LANES
    for part in range(parts):
        ids = faces_ref[:, part * LANES : (part + 1) * LANES]
        found = gather_chunks(
            lambda field, chunk: total_ref[field * GROUP + chunk : field * GROUP + chunk + 1, :],
            3,
            chunks,
            ids,
        )
        for field in range(3):
            at = field * parts + part
            low_ref[at : at + 1, :] = found[field][low_row : low_row + 1]
            high_ref[at : at + 1, :] = found[field][low_row + 1 : low_row + 2]


def add_faces(faces_ref, low_row, low_ref, high_ref):
    parts = faces_ref.shape[1] // LANES
    acc = None
    for row, got_ref in ((low_row, low_ref), (low_row + 1, high_ref)):
        ids = [faces_ref[row : row + 1, p * LANES : (p + 1) * LANES] for p in range(parts)]
        forces = [
            [got_ref[f * parts + p : f * parts + p + 1, :] for f in range(3)] for p in range(parts)
        ]
        terms = scatter_terms(ids, forces)
        acc = terms if acc is None else acc + terms
    return fold_terms(acc)


def assemble_kernel(slots, chunks, back_ref, ids_ref, inner_ref, faces_ref, out_ref, low_ref, high_ref):
    devices = back_ref.shape[0]

    def step(turn, acc):
        ids = ids_ref[pl.ds(turn * slots, slots), :]
        values = back_ref[turn]
        for slot in range(0, slots, 2):
            picks = range(slot, min(slot + 2, slots))
            acc = acc + scatter_terms(
                [ids[s : s + 1] for s in picks],
                [[values[f * slots + s : f * slots + s + 1] for f in range(3)] for s in picks],
            )
        return acc

    acc = lax.fori_loop(0, devices, step, jnp.zeros((6 * GROUP, LANES), F32))
    out_ref[...] = inner_ref[...] + fold_terms(acc)
    send_faces(out_ref, chunks, faces_ref, 0, low_ref, high_ref)


def middle_kernel(chunks, total_ref, from_low, from_high, faces_ref, out_ref, low_ref, high_ref):
    out_ref[...] = total_ref[...] + add_faces(faces_ref, 0, from_low, from_high)
    send_faces(out_ref, chunks, faces_ref, 2, low_ref, high_ref)


def final_kernel(total_ref, from_low, from_high, faces_ref, velocity_ref, mass_ref, out_ref, sum_ref):
    sum_ref[...] = total_ref[...] + add_faces(faces_ref, 2, from_low, from_high)
    for chunk in range(out_ref.shape[1] // LANES):
        span = slice(chunk * LANES, (chunk + 1) * LANES)
        scale = TIME_STEP / mass_ref[chunk : chunk + 1, :]
        for field in range(3):
            row = field * GROUP + chunk
            out_ref[field : field + 1, span] = (
                velocity_ref[field : field + 1, span] + scale * sum_ref[row : row + 1, :]
            )


def call(kernel, outs, in_smem, args, scratch=()):
    specs = [
        pl.BlockSpec(memory_space=pltpu.SMEM if i in in_smem else pltpu.VMEM)
        for i in range(len(args))
    ]
    out_shape = [jax.ShapeDtypeStruct(shape, dtype) for shape, dtype in outs]
    return pl.pallas_call(
        kernel,
        out_shape=out_shape,
        in_specs=specs,
        out_specs=[pl.BlockSpec(memory_space=pltpu.VMEM) for _ in outs],
        scratch_shapes=list(scratch),
        compiler_params=pltpu.CompilerParams(vmem_limit_bytes=VMEM_LIMIT),
    )(*args)


def exchange(low, high, axis):
    count = lax.axis_size(axis)
    forward = [(i, i + 1) for i in range(count - 1)]
    backward = [(target, source) for source, target in forward]
    return lax.ppermute(high, axis, forward), lax.ppermute(low, axis, backward)


def local(
    connectivity,
    face_nodes,
    coords,
    displacement,
    velocity,
    node_mass,
    modulus,
    surf_nodes,
    surf_ref,
    surf_angles,
    owner_map,
    pair_blocks,
    pair_masks,
    pair_count,
):
    axes = ("gx", "gy")
    devices = lax.axis_size("gx") * lax.axis_size("gy")
    per_dev = surf_nodes.shape[0]
    rows_per = per_dev // LANES
    node_count = coords.shape[1]
    chunks = node_count // LANES
    slots = 2 * per_dev // devices
    pairs = pair_blocks.shape[1]
    own = lax.axis_index(axes).reshape(1).astype(jnp.int32)
    owners = owner_map.reshape(devices * rows_per, LANES)
    face_pad = -face_nodes.shape[1] % LANES
    faces = jnp.pad(face_nodes, ((0, 4), (0, face_pad)), constant_values=-1)
    parts = faces.shape[1] // LANES
    face_rows = -(-3 * parts // 8) * 8
    total_shape = ((3 * GROUP, LANES), F32)
    face_shape = ((face_rows, LANES), F32)

    [index] = call(
        functools.partial(routing_kernel, rows_per),
        [((4, pairs), jnp.int32)],
        (0, 1),
        (own, pair_count, owners, pair_blocks),
    )
    [pos] = call(
        segment_kernel, [((3, per_dev, LANES), F32)], (), (displacement, surf_nodes, surf_ref)
    )
    outbound, ids = call(
        functools.partial(pack_kernel, slots, rows_per),
        [((devices, 5 * slots, LANES), F32), ((devices * slots, LANES), jnp.int32)],
        (0,),
        (own, owners, pos, surf_angles, surf_nodes),
    )
    inbound = lax.all_to_all(outbound, axes, split_axis=0, concat_axis=0, tiled=True)
    [internal] = call(
        element_kernel,
        [total_shape],
        (),
        (connectivity, coords, displacement, modulus.reshape(-1, LANES)),
        [pltpu.VMEM((connectivity.shape[1] // LANES * 8, LANES), jnp.int32)],
    )
    [forces] = call(
        functools.partial(pair_kernel, slots),
        [((devices, 3 * slots, LANES), F32)],
        (0, 1),
        (index, pair_count, inbound, pair_masks),
        [pltpu.VMEM((pairs * 8, LANES), F32)] * 4,
    )
    returned = lax.all_to_all(forces, axes, split_axis=0, concat_axis=0, tiled=True)
    total, low, high = call(
        functools.partial(assemble_kernel, slots, chunks),
        [total_shape, face_shape, face_shape],
        (),
        (returned, ids, internal, faces),
    )
    from_low, from_high = exchange(low, high, "gx")
    total, low, high = call(
        functools.partial(middle_kernel, chunks),
        [total_shape, face_shape, face_shape],
        (),
        (total, from_low, from_high, faces),
    )
    from_low, from_high = exchange(low, high, "gy")
    [result] = call(
        final_kernel,
        [((3, node_count), F32)],
        (),
        (total, from_low, from_high, faces, velocity, node_mass.reshape(chunks, LANES)),
        [pltpu.VMEM((3 * GROUP, LANES), F32)],
    )
    return result


def solution(mesh):
    in_specs = (
        P(None, ("gx", "gy")),
        P(None, ("gx", "gy")),
        P(None, ("gx", "gy")),
        P(None, ("gx", "gy")),
        P(None, ("gx", "gy")),
        P(("gx", "gy")),
        P(("gx", "gy")),
        P(("gx", "gy"), None),
        P(("gx", "gy"), None, None),
        P(("gx", "gy"), None, None),
        P(),
        P(None, ("gx", "gy")),
        P(None, ("gx", "gy"), None),
        P(("gx", "gy")),
    )
    out_specs = P(None, ("gx", "gy"))
    return jax.shard_map(local, mesh=mesh, in_specs=in_specs, out_specs=out_specs, check_vma=False)
```

```python
import functools

import jax
import jax.numpy as jnp
from jax import lax
from jax.experimental import pallas as pl
from jax.experimental.pallas import tpu as pltpu
from jax.sharding import PartitionSpec as P

XI_SIGNS = [
    [-1, -1, -1],
    [1, -1, -1],
    [1, 1, -1],
    [-1, 1, -1],
    [-1, -1, 1],
    [1, -1, 1],
    [1, 1, 1],
    [-1, 1, 1],
]
HOUR_VEC = [
    [1, 1, -1, -1, -1, -1, 1, 1],
    [1, -1, -1, 1, -1, 1, 1, -1],
    [1, -1, 1, -1, 1, -1, 1, -1],
    [-1, 1, -1, 1, 1, -1, 1, -1],
]
HG_COEF = 0.05
PEN_STIFF = 0.05
PEN_DEPTH = 0.5
TIME_STEP = 0.2
LANES = 128
GROUP = 16
F32 = jnp.float32
BF16 = jnp.bfloat16
VMEM_LIMIT = 48 * 1024 * 1024
REQUEST_ROWS = 16
TASK_CAP = 7
TASK_LANE = 64
ENTRY_LANE = 4
ENTRY_CAP = 20
SEND_ROWS = 32
BACK_ROWS = 8
ENTRIES = 160
TASKS = 64


def iota(shape, dim):
    return lax.broadcasted_iota(jnp.int32, shape, dim)


def dot_nn(a, b):
    return lax.dot_general(a, b, (((1,), (0,)), ((), ())), preferred_element_type=F32)


def dot_nt(a, b):
    return lax.dot_general(a, b, (((1,), (1,)), ((), ())), preferred_element_type=F32)


def dot_tn(a, b):
    return lax.dot_general(a, b, (((0,), (0,)), ((), ())), preferred_element_type=F32)


def as_bf16(mask):
    return jnp.where(mask, 1.0, 0.0).astype(BF16)


def split2(x):
    high = x.astype(BF16)
    return high, (x - high.astype(F32)).astype(BF16)


def split3(x):
    high = x.astype(BF16)
    rest = x - high.astype(F32)
    mid = rest.astype(BF16)
    return high, mid, (rest - mid.astype(F32)).astype(BF16)


def strict_upper(size):
    return as_bf16(iota((size, size), 0) < iota((size, size), 1))


def take_lanes(row, index):
    table = jnp.broadcast_to(row, index.shape)
    return jnp.take_along_axis(table, index, axis=1, mode="promise_in_bounds")


def gather_chunks(rows_of, fields, chunks, ids):
    high = ids >> 7
    low = ids & (LANES - 1)
    found = [jnp.zeros(ids.shape, F32) for _ in range(fields)]
    for chunk in range(chunks):
        here = high == chunk
        for field in range(fields):
            found[field] = jnp.where(here, take_lanes(rows_of(field, chunk), low), found[field])
    return found


def scatter_terms(id_rows, force_rows):
    wide = []
    table = []
    for ids, forces in zip(id_rows, force_rows):
        here = jnp.broadcast_to(ids >> 7, (GROUP, LANES)) == iota((GROUP, LANES), 0)
        wide.append(
            jnp.concatenate(
                [jnp.where(here, jnp.broadcast_to(f, (GROUP, LANES)), 0.0) for f in forces], axis=0
            )
        )
        low = jnp.broadcast_to(ids & (LANES - 1), (LANES, LANES))
        table.append(as_bf16(low == iota((LANES, LANES), 0)))
    high, rest = split2(jnp.concatenate(wide, axis=1))
    both = jnp.concatenate([high, rest], axis=0)
    return dot_nt(both, jnp.concatenate(table, axis=1))


def fold_terms(acc):
    half = acc.shape[0] // 2
    return acc[:half] + acc[half:]


def routing_kernel(rows_per, own_ref, count_ref, map_ref, pairs_ref, index_ref):
    own = own_ref[0]
    rows = map_ref.shape[0]
    devices = rows // rows_per
    pairs = pairs_ref.shape[1]
    hit = as_bf16(map_ref[...] == own)
    source_of = iota((devices, rows), 1) // rows_per
    upto = as_bf16(source_of <= iota((devices, rows), 0))
    within = as_bf16(source_of == iota((devices, rows), 0))
    ends = jnp.sum(dot_nn(upto, hit), axis=1, keepdims=True)
    counts = jnp.sum(dot_nn(within, hit), axis=1, keepdims=True)
    ranks = pairs_ref[...].astype(F32)
    for side in range(2):
        rank = ranks[side : side + 1]
        below = jnp.broadcast_to(ends, (devices, pairs)) <= rank
        source = jnp.sum(jnp.where(below, 1.0, 0.0), axis=0, keepdims=True)
        source = jnp.minimum(source, devices - 1.0)
        start = jnp.sum(jnp.where(below, counts, 0.0), axis=0, keepdims=True)
        index_ref[2 * side : 2 * side + 1, :] = source.astype(jnp.int32)
        index_ref[2 * side + 1 : 2 * side + 2, :] = (rank - start).astype(jnp.int32)


def request_kernel(rows_per, own_ref, count_ref, map_ref, pairs_ref, masks_ref, out_ref):
    own = own_ref[0]
    rows = map_ref.shape[0]
    devices = rows // rows_per
    pairs = pairs_ref.shape[1]
    hit = as_bf16(map_ref[...] == own)
    source_of = iota((devices, rows), 1) // rows_per
    upto = as_bf16(source_of <= iota((devices, rows), 0))
    within = as_bf16(source_of == iota((devices, rows), 0))
    ends = jnp.sum(dot_nn(upto, hit), axis=1, keepdims=True)
    counts = jnp.sum(dot_nn(within, hit), axis=1, keepdims=True)
    ranks = pairs_ref[...].astype(F32)
    where_is = []
    for side in range(2):
        rank = ranks[side : side + 1]
        below = jnp.broadcast_to(ends, (devices, pairs)) <= rank
        source = jnp.sum(jnp.where(below, 1.0, 0.0), axis=0, keepdims=True)
        source = jnp.minimum(source, devices - 1.0)
        start = jnp.sum(jnp.where(below, counts, 0.0), axis=0, keepdims=True)
        where_is.append((source, rank - start))
    (slave, slave_rank), (master, master_rank) = where_is
    lane = iota((1, pairs), 1)
    live = lane < count_ref[0]
    me = own.astype(F32)
    device = iota((devices, pairs), 0).astype(F32)
    earlier = strict_upper(pairs)

    def pick(target, keep):
        return jnp.where((device == target) & keep, 1.0, 0.0)

    worker = jnp.where(lane == 0, me, slave)
    tasks = pick(worker, live)
    turn = jnp.sum(tasks * dot_nn(tasks.astype(BF16), earlier), axis=0, keepdims=True)
    worker = jnp.where(turn >= TASK_CAP, me, worker)
    tasks = pick(worker, live)
    turn = jnp.sum(tasks * dot_nn(tasks.astype(BF16), earlier), axis=0, keepdims=True)
    send_slave = live & (slave != worker)
    send_master = live & (master != worker)
    from_slave = pick(slave, send_slave)
    from_master = pick(master, send_master)
    both = from_slave + from_master
    ahead = dot_nn(both.astype(BF16), earlier)
    slave_at = jnp.sum(from_slave * ahead, axis=0, keepdims=True)
    master_at = jnp.sum(from_master * ahead, axis=0, keepdims=True)
    master_at = master_at + jnp.where(send_slave & (slave == master), 1.0, 0.0)

    column = iota((LANES, pairs), 0).astype(F32)

    def placed(first, fields, fits):
        total = jnp.zeros((LANES, pairs), F32)
        for at, field in enumerate(fields):
            total = jnp.where((column == first + at) & fits, field, total)
        return total.astype(BF16)

    zero = jnp.zeros_like(slave)
    entry = placed(ENTRY_LANE + 3 * slave_at, (zero, slave_rank, worker), slave_at < ENTRY_CAP)
    line = dot_nt(from_slave.astype(BF16), entry)
    entry = placed(
        ENTRY_LANE + 3 * master_at, (zero + 1.0, master_rank, worker), master_at < ENTRY_CAP
    )
    line = line + dot_nt(from_master.astype(BF16), entry)
    entry = placed(
        TASK_LANE + 4 * turn, (slave, slave_rank, master, master_rank), turn < TASK_CAP
    )
    line = line + dot_nt(tasks.astype(BF16), entry)
    entry_count = jnp.sum(both, axis=1, keepdims=True)
    task_count = jnp.sum(tasks, axis=1, keepdims=True)
    over = jnp.where((entry_count > ENTRY_CAP) | (task_count > TASK_CAP), 1.0, 0.0)
    over = jnp.max(over, axis=0, keepdims=True)
    spot = iota((devices, LANES), 1)
    line = jnp.where(spot == 0, entry_count, line)
    line = jnp.where(spot == 1, task_count, line)
    line = jnp.where(spot == 2, over, line)
    out_ref[:, 0, :] = line.astype(jnp.int32)
    chosen = [jnp.where(turn == t, tasks, 0.0) for t in range(TASK_CAP)]
    chosen = jnp.concatenate(chosen, axis=0).astype(BF16)
    masks = jnp.concatenate([masks_ref[0], masks_ref[1]], axis=1).astype(F32).astype(BF16)
    got = dot_nn(chosen, masks).astype(jnp.int32)
    for t in range(TASK_CAP):
        part = got[t * devices : (t + 1) * devices]
        out_ref[:, 1 + 2 * t, :] = part[:, :LANES]
        out_ref[:, 2 + 2 * t, :] = part[:, LANES:]
    for row in range(1 + 2 * TASK_CAP, REQUEST_ROWS):
        out_ref[:, row, :] = jnp.zeros((devices, LANES), jnp.int32)


def segment_kernel(
    cap, owners_ref, disp_ref, nodes_ref, ref_ref, angles_ref, pos_ref, normal_ref, block_ref, seen_ref
):
    chunks = disp_ref.shape[1] // LANES

    def clear(device, carry):
        seen_ref[device] = 0
        return carry

    lax.fori_loop(0, seen_ref.shape[0], clear, 0)

    def step(turn, carry):
        base = pl.multiple_of(turn * 8, 8)
        for k in range(8):
            owner = owners_ref[base + k]
            rank = seen_ref[owner]
            block_ref[owner * cap + rank] = base + k
            seen_ref[owner] = rank + 1
        ids = nodes_ref[pl.ds(base, 8), :]
        found = gather_chunks(
            lambda field, chunk: disp_ref[field : field + 1, chunk * LANES : (chunk + 1) * LANES],
            3,
            chunks,
            ids,
        )
        for field in range(3):
            pos_ref[field, pl.ds(base, 8), :] = found[field] + ref_ref[pl.ds(base, 8), field, :]
        sin_az, cos_az = sine_cosine(angles_ref[pl.ds(base, 8), 0, :])
        sin_pol, cos_pol = sine_cosine(angles_ref[pl.ds(base, 8), 1, :])
        normal_ref[0, pl.ds(base, 8), :] = cos_az * cos_pol
        normal_ref[1, pl.ds(base, 8), :] = sin_az * cos_pol
        normal_ref[2, pl.ds(base, 8), :] = sin_pol
        return carry

    lax.fori_loop(0, nodes_ref.shape[0] // 8, step, 0, unroll=2)


def plan_kernel(
    cap, own_ref, list_ref, block_ref, pos_ref, angles_ref, out_ref, entry_ref, task_ref, used_ref
):
    own = own_ref[0]
    devices = list_ref.shape[0]

    def clear(device, carry):
        for row in range(4):
            used_ref[row, device] = 0
        return carry

    lax.fori_loop(0, devices, clear, 0)

    def from_owner(owner, carry):
        def entry(turn, state):
            number, over = state
            at = ENTRY_LANE + 3 * turn
            role = list_ref[owner, at]
            block = block_ref[owner * cap + list_ref[owner, at + 1]]
            worker = list_ref[owner, at + 2]
            first = used_ref[0, worker]
            back = used_ref[1, worker]
            after = first + 3 + 2 * role
            back_after = back + 3 - 2 * role
            fits = (after < SEND_ROWS) & (back_after <= BACK_ROWS) & (number < ENTRIES)

            @pl.when(fits)
            def _():
                for field in range(3):
                    out_ref[worker, pl.ds(first + field, 1), :] = pos_ref[field, pl.ds(block, 1), :]
                entry_ref[0, number] = block
                entry_ref[1, number] = role
                entry_ref[2, number] = worker
                entry_ref[3, number] = back

            @pl.when(fits & (role == 1))
            def _():
                out_ref[worker, pl.ds(first + 3, 2), :] = angles_ref[block]

            used_ref[0, worker] = after
            used_ref[1, worker] = back_after
            return (number + 1, jnp.where(fits, over, 1))

        def task(turn, state):
            number, over = state
            at = TASK_LANE + 4 * turn
            fits = number < TASKS

            @pl.when(fits)
            def _():
                for side in range(2):
                    source = list_ref[owner, at + 2 * side]
                    here = source == own
                    block = block_ref[owner * cap + list_ref[owner, at + 2 * side + 1]]
                    used = used_ref[2, source]
                    back = used_ref[3, source]
                    task_ref[3 * side, number] = source
                    task_ref[3 * side + 1, number] = jnp.where(here, block, used)
                    task_ref[3 * side + 2, number] = back
                    used_ref[2, source] = jnp.where(here, used, used + 3 + 2 * side)
                    used_ref[3, source] = jnp.where(here, back, back + 3 - 2 * side)
                task_ref[6, number] = owner
                task_ref[7, number] = turn

            return (number + 1, jnp.where(fits, over, 1))

        entries, tasks, over = carry
        over = jnp.maximum(over, list_ref[owner, 2])
        entries, over = lax.fori_loop(
            0, jnp.minimum(list_ref[owner, 0], ENTRY_CAP), entry, (entries, over)
        )
        tasks, over = lax.fori_loop(
            0, jnp.minimum(list_ref[owner, 1], TASK_CAP), task, (tasks, over)
        )
        return (entries, tasks, over)

    zero = jnp.int32(0)
    entries, tasks, over = lax.fori_loop(0, devices, from_owner, (zero, zero, zero))
    entry_ref[4, 0] = jnp.minimum(entries, ENTRIES)
    task_ref[8, 0] = jnp.minimum(tasks, TASKS)
    mark = jnp.full((devices, LANES), over.astype(F32), F32)
    out_ref[:, SEND_ROWS - 1, :] = mark


def pack_kernel(slots, rows_per, own_ref, map_ref, pos_ref, angles_ref, nodes_ref, out_ref, ids_ref):
    own = own_ref[0]
    devices = map_ref.shape[0] // rows_per
    owner = jnp.concatenate(
        [map_ref[pl.ds(own * rows_per + i, 1), :] for i in range(rows_per)], axis=1
    )
    blocks = owner.shape[1]
    mine = iota((devices, blocks), 0) == owner
    before = dot_nn(as_bf16(mine), strict_upper(blocks))
    rank = jnp.sum(jnp.where(mine, before, 0.0), axis=0, keepdims=True).astype(jnp.int32)
    place = owner * slots + rank
    move = as_bf16(iota((devices * slots, blocks), 0) == place)
    for field in range(5):
        values = pos_ref[field] if field < 3 else angles_ref[:, field - 3, :]
        moved = dot_nn(move, jnp.concatenate(split3(values), axis=1))
        moved = moved[:, :LANES] + moved[:, LANES : 2 * LANES] + moved[:, 2 * LANES :]
        out_ref[:, field * slots : (field + 1) * slots, :] = moved.reshape(devices, slots, LANES)
    nodes = nodes_ref[...]
    halves = jnp.concatenate(
        [(nodes >> 7).astype(F32).astype(BF16), (nodes & (LANES - 1)).astype(F32).astype(BF16)],
        axis=1,
    )
    moved = dot_nn(move, halves)
    ids_ref[...] = (moved[:, :LANES] * LANES + moved[:, LANES:]).astype(jnp.int32)


def sine_cosine(angle):
    half = 0.5 * angle
    sq = half * half
    sine = sq * (-1.0 / 39916800.0) + 1.0 / 362880.0
    for coef in (-1.0 / 5040.0, 1.0 / 120.0, -1.0 / 6.0, 1.0):
        sine = sine * sq + coef
    sine = sine * half
    cosine = sq * (1.0 / 479001600.0) - 1.0 / 3628800.0
    for coef in (1.0 / 40320.0, -1.0 / 720.0, 1.0 / 24.0, -0.5, 1.0):
        cosine = cosine * sq + coef
    return 2.0 * sine * cosine, 1.0 - 2.0 * sine * sine


def pair_kernel(
    slots, index_ref, count_ref, in_ref, masks_ref, out_ref, slave_ref, master_ref, sin_ref, cos_ref
):
    pairs = masks_ref.shape[1]
    count = jnp.minimum(count_ref[0], pairs)
    out_ref[...] = jnp.zeros_like(out_ref)

    def stage(pair, carry):
        source = index_ref[0, pair]
        slot = index_ref[1, pair]
        for field in range(3):
            slave_ref[pl.ds(pair * 8 + field, 1), :] = in_ref[source, pl.ds(field * slots + slot, 1), :]
        slave_ref[pl.ds(pair * 8 + 3, 1), :] = masks_ref[0, pl.ds(pair, 1), :].astype(F32)
        source = index_ref[2, pair]
        slot = index_ref[3, pair]
        for field in range(5):
            master_ref[pl.ds(pair * 8 + field, 1), :] = in_ref[source, pl.ds(field * slots + slot, 1), :]
        master_ref[pl.ds(pair * 8 + 5, 1), :] = masks_ref[1, pl.ds(pair, 1), :].astype(F32)
        return carry

    lax.fori_loop(0, count, stage, 0)
    sines, cosines = sine_cosine(master_ref[...])
    sin_ref[...] = sines
    cos_ref[...] = cosines

    def tile(pair, carry):
        base = pl.multiple_of(pair * 8, 8)
        slave = slave_ref[pl.ds(base, 8), :]
        columns = jnp.transpose(slave)
        master = master_ref[pl.ds(base, 8), :]
        sin_az = sin_ref[pl.ds(base + 3, 1), :]
        sin_pol = sin_ref[pl.ds(base + 4, 1), :]
        cos_az = cos_ref[pl.ds(base + 3, 1), :]
        cos_pol = cos_ref[pl.ds(base + 4, 1), :]
        normal = [cos_az * cos_pol, sin_az * cos_pol, sin_pol]
        shape = (LANES, LANES)
        dist = [
            jnp.broadcast_to(columns[:, k : k + 1], shape) - jnp.broadcast_to(master[k : k + 1], shape)
            for k in range(3)
        ]
        gap = dist[0] * normal[0] + dist[1] * normal[1] + dist[2] * normal[2]
        tang = dist[0] * dist[0] + dist[1] * dist[1] + dist[2] * dist[2] - gap * gap
        bend = gap * (-1.0 / PEN_DEPTH)
        soft = jnp.maximum(bend, 0.0) + jnp.log(1.0 + jnp.exp(-jnp.abs(bend)))
        press = soft * jnp.exp(-0.5 * tang)
        press = press * jnp.broadcast_to(columns[:, 3:4], shape)
        total = jnp.sum(press, axis=0, keepdims=True)
        scale = PEN_STIFF * PEN_DEPTH * master[5:6]
        push = [n * scale for n in normal]
        rows = jnp.concatenate(push + [jnp.zeros((5, LANES), F32)], axis=0)
        push_high, push_rest = split2(rows)
        both = jnp.concatenate([push_high, push_rest], axis=0)
        high, rest = split2(press)
        got = dot_nt(both, high) + dot_nt(both, rest)
        on_slave = got[0:8] + got[8:16]
        source = index_ref[0, pair]
        slot = index_ref[1, pair]
        for k in range(3):
            at = pl.ds(k * slots + slot, 1)
            out_ref[source, at, :] = out_ref[source, at, :] + on_slave[k : k + 1]
        source = index_ref[2, pair]
        slot = index_ref[3, pair]
        for k in range(3):
            at = pl.ds(k * slots + slot, 1)
            out_ref[source, at, :] = out_ref[source, at, :] - push[k] * total
        return carry

    lax.fori_loop(0, count, tile, 0)


def work_kernel(
    own_ref,
    task_ref,
    in_ref,
    request_ref,
    pos_ref,
    angles_ref,
    back_ref,
    slave_out,
    master_out,
    slave_ref,
    master_ref,
    sin_ref,
    cos_ref,
):
    own = own_ref[0]
    count = task_ref[8, 0]

    def stage(task, carry):
        owner = task_ref[6, task]
        turn = task_ref[7, task]
        for side, stage_ref in ((0, slave_ref), (1, master_ref)):
            source = task_ref[3 * side, task]
            first = task_ref[3 * side + 1, task]

            @pl.when(source == own)
            def _():
                for field in range(3):
                    stage_ref[pl.ds(task * 8 + field, 1), :] = pos_ref[field, pl.ds(first, 1), :]
                if side == 1:
                    stage_ref[pl.ds(task * 8 + 3, 2), :] = angles_ref[first]

            @pl.when(source != own)
            def _():
                for field in range(3 + 2 * side):
                    stage_ref[pl.ds(task * 8 + field, 1), :] = in_ref[source, pl.ds(first + field, 1), :]

            stage_ref[pl.ds(task * 8 + 5, 1), :] = request_ref[
                owner, pl.ds(1 + 2 * turn + side, 1), :
            ].astype(F32)
        return carry

    lax.fori_loop(0, count, stage, 0)
    sines, cosines = sine_cosine(master_ref[...])
    sin_ref[...] = sines
    cos_ref[...] = cosines

    def tile(task, carry):
        base = pl.multiple_of(task * 8, 8)
        slave = slave_ref[pl.ds(base, 8), :]
        columns = jnp.transpose(slave)
        master = master_ref[pl.ds(base, 8), :]
        sin_az = sin_ref[pl.ds(base + 3, 1), :]
        sin_pol = sin_ref[pl.ds(base + 4, 1), :]
        cos_az = cos_ref[pl.ds(base + 3, 1), :]
        cos_pol = cos_ref[pl.ds(base + 4, 1), :]
        normal = [cos_az * cos_pol, sin_az * cos_pol, sin_pol]
        shape = (LANES, LANES)
        dist = [
            jnp.broadcast_to(columns[:, k : k + 1], shape) - jnp.broadcast_to(master[k : k + 1], shape)
            for k in range(3)
        ]
        gap = dist[0] * normal[0] + dist[1] * normal[1] + dist[2] * normal[2]
        tang = dist[0] * dist[0] + dist[1] * dist[1] + dist[2] * dist[2] - gap * gap
        bend = gap * (-1.0 / PEN_DEPTH)
        soft = jnp.maximum(bend, 0.0) + jnp.log(1.0 + jnp.exp(-jnp.abs(bend)))
        press = soft * jnp.exp(-0.5 * tang)
        press = press * jnp.broadcast_to(columns[:, 5:6], shape)
        scale = PEN_STIFF * PEN_DEPTH * master[5:6]
        total = jnp.sum(press, axis=0, keepdims=True) * scale
        rows = jnp.concatenate([n * scale for n in normal] + [jnp.zeros((5, LANES), F32)], axis=0)
        push_high, push_rest = split2(rows)
        both = jnp.concatenate([push_high, push_rest], axis=0)
        high, rest = split2(press)
        got = dot_nt(both, high) + dot_nt(both, rest)
        on_slave = got[0:8] + got[8:16]
        slave_out[pl.ds(base, 8), :] = on_slave
        for k in range(3):
            master_out[pl.ds(base + k, 1), :] = -normal[k] * total
        source = task_ref[0, task]

        @pl.when(source != own)
        def _():
            for k in range(3):
                back_ref[source, pl.ds(task_ref[2, task] + k, 1), :] = on_slave[k : k + 1]

        source = task_ref[3, task]

        @pl.when(source != own)
        def _():
            back_ref[source, pl.ds(task_ref[5, task], 1), :] = total

        return carry

    lax.fori_loop(0, count, tile, 0)


def near_kernel(own_ref, task_ref, nodes_ref, slave_ref, master_ref, inner_ref, out_ref):
    own = own_ref[0]

    def step(task, acc):
        ids = []
        forces = []
        for side, force_ref in ((0, slave_ref), (1, master_ref)):
            here = task_ref[3 * side, task] == own
            block = jnp.where(here, task_ref[3 * side + 1, task], 0)
            ids.append(nodes_ref[pl.ds(block, 1), :])
            rows = force_ref[pl.ds(pl.multiple_of(task * 8, 8), 8), :]
            rows = jnp.where(here, rows, 0.0)
            forces.append([rows[k : k + 1] for k in range(3)])
        return acc + scatter_terms(ids, forces)

    acc = lax.fori_loop(0, task_ref[8, 0], step, jnp.zeros((6 * GROUP, LANES), F32))
    out_ref[...] = inner_ref[...] + fold_terms(acc)


def far_kernel(
    chunks, entry_ref, back_ref, nodes_ref, normal_ref, near_ref, faces_ref, out_ref, low_ref, high_ref
):
    count = entry_ref[4, 0]

    def step(turn, acc):
        ids = []
        forces = []
        for k in range(2):
            valid = 2 * turn + k < count
            number = jnp.where(valid, 2 * turn + k, 0)
            block = entry_ref[0, number]
            role = entry_ref[1, number]
            worker = entry_ref[2, number]
            first = entry_ref[3, number]
            ids.append(nodes_ref[pl.ds(block, 1), :])
            total = back_ref[worker, pl.ds(first, 1), :]
            rows = []
            for field in range(3):
                row = back_ref[worker, pl.ds(jnp.minimum(first + field, BACK_ROWS - 1), 1), :]
                row = jnp.where(role == 1, -normal_ref[field, pl.ds(block, 1), :] * total, row)
                rows.append(jnp.where(valid, row, 0.0))
            forces.append(rows)
        return acc + scatter_terms(ids, forces)

    acc = lax.fori_loop(0, (count + 1) // 2, step, jnp.zeros((6 * GROUP, LANES), F32))
    out_ref[...] = near_ref[...] + fold_terms(acc)
    send_faces(out_ref, chunks, faces_ref, 0, low_ref, high_ref)


def element_kernel(conn_ref, coords_ref, disp_ref, modulus_ref, out_ref, order_ref):
    chunks = coords_ref.shape[1] // LANES
    groups = conn_ref.shape[1] // LANES
    for group in range(groups):
        order_ref[pl.ds(group * 8, 8), :] = conn_ref[:, group * LANES : (group + 1) * LANES]
    pos = []
    disp = []
    for corner in range(8):
        ids = order_ref[pl.ds(corner, groups, stride=8), :]
        found = gather_chunks(
            lambda field, chunk: (coords_ref if field < 3 else disp_ref)[
                field % 3 : field % 3 + 1, chunk * LANES : (chunk + 1) * LANES
            ],
            6,
            chunks,
            ids,
        )
        pos.append(found[:3])
        disp.append(found[3:])
    first = list(pos[0])
    pos = [[pos[corner][j] - first[j] for j in range(3)] for corner in range(8)]

    def signed(values, signs):
        total = None
        for value, sign in zip(values, signs):
            if total is None:
                total = value if sign > 0 else -value
            else:
                total = total + value if sign > 0 else total - value
        return total

    corner_signs = [[XI_SIGNS[corner][k] for corner in range(8)] for k in range(3)]
    jac = [
        [signed([pos[c][j] for c in range(8)], corner_signs[k]) * 0.125 for k in range(3)]
        for j in range(3)
    ]
    cof = [
        [
            jac[(j + 1) % 3][(k + 1) % 3] * jac[(j + 2) % 3][(k + 2) % 3]
            - jac[(j + 1) % 3][(k + 2) % 3] * jac[(j + 2) % 3][(k + 1) % 3]
            for k in range(3)
        ]
        for j in range(3)
    ]
    det = jac[0][0] * cof[0][0] + jac[0][1] * cof[0][1] + jac[0][2] * cof[0][2]
    volume = 8.0 * det
    inverse = 1.0 / volume
    scaled = [[cof[j][k] * inverse for k in range(3)] for j in range(3)]
    grad = [[signed(scaled[j], XI_SIGNS[c]) for j in range(3)] for c in range(8)]

    def summed(terms):
        total = terms[0]
        for term in terms[1:]:
            total = total + term
        return total

    ugrad = [
        [summed([disp[c][i] * grad[c][j] for c in range(8)]) for j in range(3)] for i in range(3)
    ]
    modulus = modulus_ref[...]
    dilation = ugrad[0][0] + ugrad[1][1] + ugrad[2][2]
    stress = [[modulus * (ugrad[i][j] + ugrad[j][i]) for j in range(3)] for i in range(3)]
    for i in range(3):
        stress[i][i] = stress[i][i] + modulus * dilation
    squares = summed([grad[c][j] * grad[c][j] for c in range(8) for j in range(3)])
    hour_coef = HG_COEF * modulus * volume * squares
    shapes = []
    modes = []
    for a in range(4):
        hour_pos = [signed([pos[c][j] for c in range(8)], HOUR_VEC[a]) for j in range(3)]
        gam = [
            float(HOUR_VEC[a][c]) - summed([hour_pos[j] * grad[c][j] for j in range(3)])
            for c in range(8)
        ]
        shapes.append(gam)
        modes.append(
            [hour_coef * summed([disp[c][i] * gam[c] for c in range(8)]) for i in range(3)]
        )
    flux = [[volume * stress[i][j] for j in range(3)] for i in range(3)]
    acc = jnp.zeros((6 * GROUP, LANES), F32)
    for corner in range(8):
        ids = order_ref[pl.ds(corner, groups, stride=8), :]
        force = []
        for i in range(3):
            value = summed([flux[i][j] * grad[corner][j] for j in range(3)])
            value = value + summed([modes[a][i] * shapes[a][corner] for a in range(4)])
            force.append(-value)
        for group in range(0, groups, 2):
            picks = range(group, min(group + 2, groups))
            acc = acc + scatter_terms(
                [ids[g : g + 1] for g in picks], [[f[g : g + 1] for f in force] for g in picks]
            )
    out_ref[...] = fold_terms(acc)


def send_faces(total_ref, chunks, faces_ref, low_row, low_ref, high_ref):
    low_ref[...] = jnp.zeros_like(low_ref)
    high_ref[...] = jnp.zeros_like(high_ref)
    parts = faces_ref.shape[1] // LANES
    for part in range(parts):
        ids = faces_ref[:, part * LANES : (part + 1) * LANES]
        found = gather_chunks(
            lambda field, chunk: total_ref[field * GROUP + chunk : field * GROUP + chunk + 1, :],
            3,
            chunks,
            ids,
        )
        for field in range(3):
            at = field * parts + part
            low_ref[at : at + 1, :] = found[field][low_row : low_row + 1]
            high_ref[at : at + 1, :] = found[field][low_row + 1 : low_row + 2]


def add_faces(faces_ref, low_row, low_ref, high_ref):
    parts = faces_ref.shape[1] // LANES
    acc = None
    for row, got_ref in ((low_row, low_ref), (low_row + 1, high_ref)):
        ids = [faces_ref[row : row + 1, p * LANES : (p + 1) * LANES] for p in range(parts)]
        forces = [
            [got_ref[f * parts + p : f * parts + p + 1, :] for f in range(3)] for p in range(parts)
        ]
        terms = scatter_terms(ids, forces)
        acc = terms if acc is None else acc + terms
    return fold_terms(acc)


def assemble_kernel(slots, chunks, back_ref, ids_ref, inner_ref, faces_ref, out_ref, low_ref, high_ref):
    devices = back_ref.shape[0]

    def step(turn, acc):
        ids = ids_ref[pl.ds(turn * slots, slots), :]
        values = back_ref[turn]
        for slot in range(0, slots, 2):
            picks = range(slot, min(slot + 2, slots))
            acc = acc + scatter_terms(
                [ids[s : s + 1] for s in picks],
                [[values[f * slots + s : f * slots + s + 1] for f in range(3)] for s in picks],
            )
        return acc

    acc = lax.fori_loop(0, devices, step, jnp.zeros((6 * GROUP, LANES), F32))
    out_ref[...] = inner_ref[...] + fold_terms(acc)
    send_faces(out_ref, chunks, faces_ref, 0, low_ref, high_ref)


def middle_kernel(chunks, total_ref, from_low, from_high, faces_ref, out_ref, low_ref, high_ref):
    out_ref[...] = total_ref[...] + add_faces(faces_ref, 0, from_low, from_high)
    send_faces(out_ref, chunks, faces_ref, 2, low_ref, high_ref)


def final_kernel(total_ref, from_low, from_high, faces_ref, velocity_ref, mass_ref, out_ref, sum_ref):
    sum_ref[...] = total_ref[...] + add_faces(faces_ref, 2, from_low, from_high)
    for chunk in range(out_ref.shape[1] // LANES):
        span = slice(chunk * LANES, (chunk + 1) * LANES)
        scale = TIME_STEP / mass_ref[chunk : chunk + 1, :]
        for field in range(3):
            row = field * GROUP + chunk
            out_ref[field : field + 1, span] = (
                velocity_ref[field : field + 1, span] + scale * sum_ref[row : row + 1, :]
            )


def call(kernel, outs, in_smem, args, scratch=(), out_smem=()):
    def spec(smem):
        return pl.BlockSpec(memory_space=pltpu.SMEM if smem else pltpu.VMEM)

    return pl.pallas_call(
        kernel,
        out_shape=[jax.ShapeDtypeStruct(shape, dtype) for shape, dtype in outs],
        in_specs=[spec(i in in_smem) for i in range(len(args))],
        out_specs=[spec(i in out_smem) for i in range(len(outs))],
        scratch_shapes=list(scratch),
        compiler_params=pltpu.CompilerParams(vmem_limit_bytes=VMEM_LIMIT),
    )(*args)


def exchange(low, high, axis):
    count = lax.axis_size(axis)
    forward = [(i, i + 1) for i in range(count - 1)]
    backward = [(target, source) for source, target in forward]
    return lax.ppermute(high, axis, forward), lax.ppermute(low, axis, backward)


def local(
    connectivity,
    face_nodes,
    coords,
    displacement,
    velocity,
    node_mass,
    modulus,
    surf_nodes,
    surf_ref,
    surf_angles,
    owner_map,
    pair_blocks,
    pair_masks,
    pair_count,
):
    axes = ("gx", "gy")
    devices = lax.axis_size("gx") * lax.axis_size("gy")
    per_dev = surf_nodes.shape[0]
    rows_per = per_dev // LANES
    node_count = coords.shape[1]
    chunks = node_count // LANES
    slots = 2 * per_dev // devices
    pairs = pair_blocks.shape[1]
    own = lax.axis_index(axes).reshape(1).astype(jnp.int32)
    owners = owner_map.reshape(devices * rows_per, LANES)
    face_pad = -face_nodes.shape[1] % LANES
    faces = jnp.pad(face_nodes, ((0, 4), (0, face_pad)), constant_values=-1)
    parts = faces.shape[1] // LANES
    face_rows = -(-3 * parts // 8) * 8
    total_shape = ((3 * GROUP, LANES), F32)
    face_shape = ((face_rows, LANES), F32)

    def to_all(values):
        return lax.all_to_all(values, axes, split_axis=0, concat_axis=0, tiled=True)

    [request] = call(
        functools.partial(request_kernel, rows_per),
        [((devices, REQUEST_ROWS, LANES), jnp.int32)],
        (0, 1),
        (own, pair_count, owners, pair_blocks, pair_masks),
    )
    asked = to_all(request)
    own_owners = lax.dynamic_slice_in_dim(owner_map, own[0] * per_dev, per_dev)
    pos, normals, block_of = call(
        functools.partial(segment_kernel, slots),
        [
            ((3, per_dev, LANES), F32),
            ((3, per_dev, LANES), F32),
            ((devices * slots,), jnp.int32),
        ],
        (0,),
        (own_owners, displacement, surf_nodes, surf_ref, surf_angles),
        [pltpu.SMEM((devices,), jnp.int32)],
        (2,),
    )
    [internal] = call(
        element_kernel,
        [total_shape],
        (),
        (connectivity, coords, displacement, modulus.reshape(-1, LANES)),
        [pltpu.VMEM((connectivity.shape[1] // LANES * 8, LANES), jnp.int32)],
    )
    outbound, entries, tasks = call(
        functools.partial(plan_kernel, slots),
        [
            ((devices, SEND_ROWS, LANES), F32),
            ((8, ENTRIES), jnp.int32),
            ((16, TASKS), jnp.int32),
        ],
        (0, 1, 2),
        (own, asked[:, 0, :], block_of, pos, surf_angles),
        [pltpu.SMEM((4, devices), jnp.int32)],
        (1, 2),
    )
    inbound = to_all(outbound)
    over = jnp.max(inbound[:, SEND_ROWS - 1, 0]) > 0.0

    def by_tasks():
        back, on_slave, on_master = call(
            work_kernel,
            [
                ((devices, BACK_ROWS, LANES), F32),
                ((TASKS * 8, LANES), F32),
                ((TASKS * 8, LANES), F32),
            ],
            (0, 1),
            (own, tasks, inbound, asked, pos, surf_angles),
            [pltpu.VMEM((TASKS * 8, LANES), F32)] * 4,
        )
        returned = to_all(back)
        [near] = call(
            near_kernel,
            [total_shape],
            (0, 1),
            (own, tasks, surf_nodes, on_slave, on_master, internal),
        )
        return call(
            functools.partial(far_kernel, chunks),
            [total_shape, face_shape, face_shape],
            (0,),
            (entries, returned, surf_nodes, normals, near, faces),
        )

    def by_owners():
        [index] = call(
            functools.partial(routing_kernel, rows_per),
            [((4, pairs), jnp.int32)],
            (0, 1),
            (own, pair_count, owners, pair_blocks),
        )
        outbound, ids = call(
            functools.partial(pack_kernel, slots, rows_per),
            [((devices, 5 * slots, LANES), F32), ((devices * slots, LANES), jnp.int32)],
            (0,),
            (own, owners, pos, surf_angles, surf_nodes),
        )
        [forces] = call(
            functools.partial(pair_kernel, slots),
            [((devices, 3 * slots, LANES), F32)],
            (0, 1),
            (index, pair_count, to_all(outbound), pair_masks),
            [pltpu.VMEM((pairs * 8, LANES), F32)] * 4,
        )
        return call(
            functools.partial(assemble_kernel, slots, chunks),
            [total_shape, face_shape, face_shape],
            (),
            (to_all(forces), ids, internal, faces),
        )

    total, low, high = lax.cond(over, by_owners, by_tasks)
    from_low, from_high = exchange(low, high, "gx")
    total, low, high = call(
        functools.partial(middle_kernel, chunks),
        [total_shape, face_shape, face_shape],
        (),
        (total, from_low, from_high, faces),
    )
    from_low, from_high = exchange(low, high, "gy")
    [result] = call(
        final_kernel,
        [((3, node_count), F32)],
        (),
        (total, from_low, from_high, faces, velocity, node_mass.reshape(chunks, LANES)),
        [pltpu.VMEM((3 * GROUP, LANES), F32)],
    )
    return result


def solution(mesh):
    in_specs = (
        P(None, ("gx", "gy")),
        P(None, ("gx", "gy")),
        P(None, ("gx", "gy")),
        P(None, ("gx", "gy")),
        P(None, ("gx", "gy")),
        P(("gx", "gy")),
        P(("gx", "gy")),
        P(("gx", "gy"), None),
        P(("gx", "gy"), None, None),
        P(("gx", "gy"), None, None),
        P(),
        P(None, ("gx", "gy")),
        P(None, ("gx", "gy"), None),
        P(("gx", "gy")),
    )
    out_specs = P(None, ("gx", "gy"))
    return jax.shard_map(local, mesh=mesh, in_specs=in_specs, out_specs=out_specs, check_vma=False)
```

```python
import functools

import jax
import jax.numpy as jnp
from jax import lax
from jax.experimental import pallas as pl
from jax.experimental.pallas import tpu as pltpu
from jax.sharding import PartitionSpec as P

XI_SIGNS = [
    [-1, -1, -1],
    [1, -1, -1],
    [1, 1, -1],
    [-1, 1, -1],
    [-1, -1, 1],
    [1, -1, 1],
    [1, 1, 1],
    [-1, 1, 1],
]
HOUR_VEC = [
    [1, 1, -1, -1, -1, -1, 1, 1],
    [1, -1, -1, 1, -1, 1, 1, -1],
    [1, -1, 1, -1, 1, -1, 1, -1],
    [-1, 1, -1, 1, 1, -1, 1, -1],
]
HG_COEF = 0.05
PEN_STIFF = 0.05
PEN_DEPTH = 0.5
TIME_STEP = 0.2
LANES = 128
GROUP = 16
F32 = jnp.float32
BF16 = jnp.bfloat16
VMEM_LIMIT = 48 * 1024 * 1024
REQUEST_ROWS = 16
TASK_CAP = 7
TASK_LANE = 64
ENTRY_LANE = 4
ENTRY_CAP = 20
SEND_ROWS = 32
BACK_ROWS = 8
ENTRIES = 160
TASKS = 64
TASK_STEP = 8


def iota(shape, dim):
    return lax.broadcasted_iota(jnp.int32, shape, dim)


def dot_nn(a, b):
    return lax.dot_general(a, b, (((1,), (0,)), ((), ())), preferred_element_type=F32)


def dot_nt(a, b):
    return lax.dot_general(a, b, (((1,), (1,)), ((), ())), preferred_element_type=F32)


def dot_tn(a, b):
    return lax.dot_general(a, b, (((0,), (0,)), ((), ())), preferred_element_type=F32)


def as_bf16(mask):
    return jnp.where(mask, 1.0, 0.0).astype(BF16)


def split2(x):
    high = x.astype(BF16)
    return high, (x - high.astype(F32)).astype(BF16)


def split3(x):
    high = x.astype(BF16)
    rest = x - high.astype(F32)
    mid = rest.astype(BF16)
    return high, mid, (rest - mid.astype(F32)).astype(BF16)


def strict_upper(size):
    return as_bf16(iota((size, size), 0) < iota((size, size), 1))


def take_lanes(row, index):
    table = jnp.broadcast_to(row, index.shape)
    return jnp.take_along_axis(table, index, axis=1, mode="promise_in_bounds")


def gather_chunks(rows_of, fields, chunks, ids):
    high = ids >> 7
    low = ids & (LANES - 1)
    found = [jnp.zeros(ids.shape, F32) for _ in range(fields)]
    for chunk in range(chunks):
        here = high == chunk
        for field in range(fields):
            found[field] = jnp.where(here, take_lanes(rows_of(field, chunk), low), found[field])
    return found


def scatter_terms(id_rows, force_rows):
    wide = []
    table = []
    for ids, forces in zip(id_rows, force_rows):
        here = jnp.broadcast_to(ids >> 7, (GROUP, LANES)) == iota((GROUP, LANES), 0)
        wide.append(
            jnp.concatenate(
                [jnp.where(here, jnp.broadcast_to(f, (GROUP, LANES)), 0.0) for f in forces], axis=0
            )
        )
        low = jnp.broadcast_to(ids & (LANES - 1), (LANES, LANES))
        table.append(as_bf16(low == iota((LANES, LANES), 0)))
    high, rest = split2(jnp.concatenate(wide, axis=1))
    both = jnp.concatenate([high, rest], axis=0)
    return dot_nt(both, jnp.concatenate(table, axis=1))


def fold_terms(acc):
    half = acc.shape[0] // 2
    return acc[:half] + acc[half:]


def routing_kernel(rows_per, own_ref, count_ref, map_ref, pairs_ref, index_ref):
    own = own_ref[0]
    rows = map_ref.shape[0]
    devices = rows // rows_per
    pairs = pairs_ref.shape[1]
    hit = as_bf16(map_ref[...] == own)
    source_of = iota((devices, rows), 1) // rows_per
    upto = as_bf16(source_of <= iota((devices, rows), 0))
    within = as_bf16(source_of == iota((devices, rows), 0))
    ends = jnp.sum(dot_nn(upto, hit), axis=1, keepdims=True)
    counts = jnp.sum(dot_nn(within, hit), axis=1, keepdims=True)
    ranks = pairs_ref[...].astype(F32)
    for side in range(2):
        rank = ranks[side : side + 1]
        below = jnp.broadcast_to(ends, (devices, pairs)) <= rank
        source = jnp.sum(jnp.where(below, 1.0, 0.0), axis=0, keepdims=True)
        source = jnp.minimum(source, devices - 1.0)
        start = jnp.sum(jnp.where(below, counts, 0.0), axis=0, keepdims=True)
        index_ref[2 * side : 2 * side + 1, :] = source.astype(jnp.int32)
        index_ref[2 * side + 1 : 2 * side + 2, :] = (rank - start).astype(jnp.int32)


def request_kernel(rows_per, own_ref, count_ref, map_ref, pairs_ref, masks_ref, out_ref):
    own = own_ref[0]
    rows = map_ref.shape[0]
    devices = rows // rows_per
    pairs = pairs_ref.shape[1]
    hit = as_bf16(map_ref[...] == own)
    source_of = iota((devices, rows), 1) // rows_per
    upto = as_bf16(source_of <= iota((devices, rows), 0))
    within = as_bf16(source_of == iota((devices, rows), 0))
    ends = jnp.sum(dot_nn(upto, hit), axis=1, keepdims=True)
    counts = jnp.sum(dot_nn(within, hit), axis=1, keepdims=True)
    ranks = pairs_ref[...].astype(F32)
    where_is = []
    for side in range(2):
        rank = ranks[side : side + 1]
        below = jnp.broadcast_to(ends, (devices, pairs)) <= rank
        source = jnp.sum(jnp.where(below, 1.0, 0.0), axis=0, keepdims=True)
        source = jnp.minimum(source, devices - 1.0)
        start = jnp.sum(jnp.where(below, counts, 0.0), axis=0, keepdims=True)
        where_is.append((source, rank - start))
    (slave, slave_rank), (master, master_rank) = where_is
    lane = iota((1, pairs), 1)
    live = lane < count_ref[0]
    me = own.astype(F32)
    device = iota((devices, pairs), 0).astype(F32)
    earlier = strict_upper(pairs)

    def pick(target, keep):
        return jnp.where((device == target) & keep, 1.0, 0.0)

    worker = jnp.where(lane == 0, me, slave)
    tasks = pick(worker, live)
    turn = jnp.sum(tasks * dot_nn(tasks.astype(BF16), earlier), axis=0, keepdims=True)
    worker = jnp.where(turn >= TASK_CAP, me, worker)
    tasks = pick(worker, live)
    turn = jnp.sum(tasks * dot_nn(tasks.astype(BF16), earlier), axis=0, keepdims=True)
    send_slave = live & (slave != worker)
    send_master = live & (master != worker)
    from_slave = pick(slave, send_slave)
    from_master = pick(master, send_master)
    both = from_slave + from_master
    ahead = dot_nn(both.astype(BF16), earlier)
    slave_at = jnp.sum(from_slave * ahead, axis=0, keepdims=True)
    master_at = jnp.sum(from_master * ahead, axis=0, keepdims=True)
    master_at = master_at + jnp.where(send_slave & (slave == master), 1.0, 0.0)

    column = iota((LANES, pairs), 0).astype(F32)

    def placed(first, fields, fits):
        total = jnp.zeros((LANES, pairs), F32)
        for at, field in enumerate(fields):
            total = jnp.where((column == first + at) & fits, field, total)
        return total.astype(BF16)

    zero = jnp.zeros_like(slave)
    entry = placed(ENTRY_LANE + 3 * slave_at, (zero, slave_rank, worker), slave_at < ENTRY_CAP)
    line = dot_nt(from_slave.astype(BF16), entry)
    entry = placed(
        ENTRY_LANE + 3 * master_at, (zero + 1.0, master_rank, worker), master_at < ENTRY_CAP
    )
    line = line + dot_nt(from_master.astype(BF16), entry)
    entry = placed(
        TASK_LANE + 4 * turn, (slave, slave_rank, master, master_rank), turn < TASK_CAP
    )
    line = line + dot_nt(tasks.astype(BF16), entry)
    entry_count = jnp.sum(both, axis=1, keepdims=True)
    task_count = jnp.sum(tasks, axis=1, keepdims=True)
    over = jnp.where((entry_count > ENTRY_CAP) | (task_count > TASK_CAP), 1.0, 0.0)
    over = jnp.max(over, axis=0, keepdims=True)
    spot = iota((devices, LANES), 1)
    line = jnp.where(spot == 0, entry_count, line)
    line = jnp.where(spot == 1, task_count, line)
    line = jnp.where(spot == 2, over, line)
    out_ref[:, 0, :] = line.astype(jnp.int32)
    chosen = [jnp.where(turn == t, tasks, 0.0) for t in range(TASK_CAP)]
    chosen = jnp.concatenate(chosen, axis=0).astype(BF16)
    masks = jnp.concatenate([masks_ref[0], masks_ref[1]], axis=1).astype(F32).astype(BF16)
    got = dot_nn(chosen, masks).astype(jnp.int32)
    for t in range(TASK_CAP):
        part = got[t * devices : (t + 1) * devices]
        out_ref[:, 1 + 2 * t, :] = part[:, :LANES]
        out_ref[:, 2 + 2 * t, :] = part[:, LANES:]
    for row in range(1 + 2 * TASK_CAP, REQUEST_ROWS):
        out_ref[:, row, :] = jnp.zeros((devices, LANES), jnp.int32)


def segment_kernel(
    cap, owners_ref, disp_ref, nodes_ref, ref_ref, angles_ref, pos_ref, normal_ref, block_ref, seen_ref
):
    chunks = disp_ref.shape[1] // LANES

    def clear(device, carry):
        seen_ref[device] = 0
        return carry

    lax.fori_loop(0, seen_ref.shape[0], clear, 0)

    def step(turn, carry):
        base = pl.multiple_of(turn * 8, 8)
        for k in range(8):
            owner = owners_ref[base + k]
            rank = seen_ref[owner]
            block_ref[owner * cap + rank] = base + k
            seen_ref[owner] = rank + 1
        ids = nodes_ref[pl.ds(base, 8), :]
        found = gather_chunks(
            lambda field, chunk: disp_ref[field : field + 1, chunk * LANES : (chunk + 1) * LANES],
            3,
            chunks,
            ids,
        )
        for field in range(3):
            pos_ref[field, pl.ds(base, 8), :] = found[field] + ref_ref[pl.ds(base, 8), field, :]
        sin_az, cos_az = sine_cosine(angles_ref[pl.ds(base, 8), 0, :])
        sin_pol, cos_pol = sine_cosine(angles_ref[pl.ds(base, 8), 1, :])
        normal_ref[0, pl.ds(base, 8), :] = cos_az * cos_pol
        normal_ref[1, pl.ds(base, 8), :] = sin_az * cos_pol
        normal_ref[2, pl.ds(base, 8), :] = sin_pol
        return carry

    lax.fori_loop(0, nodes_ref.shape[0] // 8, step, 0, unroll=2)


def plan_kernel(
    cap, own_ref, list_ref, block_ref, pos_ref, angles_ref, out_ref, entry_ref, task_ref, used_ref
):
    own = own_ref[0]
    devices = list_ref.shape[0]

    def clear(device, carry):
        for row in range(4):
            used_ref[row, device] = 0
        return carry

    lax.fori_loop(0, devices, clear, 0)

    def from_owner(owner, carry):
        def entry(turn, state):
            number, over = state
            at = ENTRY_LANE + 3 * turn
            role = list_ref[owner, at]
            block = block_ref[owner * cap + list_ref[owner, at + 1]]
            worker = list_ref[owner, at + 2]
            first = used_ref[0, worker]
            back = used_ref[1, worker]
            after = first + 3 + 2 * role
            back_after = back + 3 - 2 * role
            fits = (after < SEND_ROWS) & (back_after <= BACK_ROWS) & (number < ENTRIES)

            @pl.when(fits)
            def _():
                for field in range(3):
                    out_ref[worker, pl.ds(first + field, 1), :] = pos_ref[field, pl.ds(block, 1), :]
                entry_ref[0, number] = block
                entry_ref[1, number] = role
                entry_ref[2, number] = worker
                entry_ref[3, number] = back

            @pl.when(fits & (role == 1))
            def _():
                out_ref[worker, pl.ds(first + 3, 2), :] = angles_ref[block]

            used_ref[0, worker] = after
            used_ref[1, worker] = back_after
            return (number + 1, jnp.where(fits, over, 1))

        def task(turn, state):
            number, over = state
            at = TASK_LANE + 4 * turn
            fits = number < TASKS

            @pl.when(fits)
            def _():
                for side in range(2):
                    source = list_ref[owner, at + 2 * side]
                    here = source == own
                    block = block_ref[owner * cap + list_ref[owner, at + 2 * side + 1]]
                    used = used_ref[2, source]
                    back = used_ref[3, source]
                    task_ref[3 * side, number] = source
                    task_ref[3 * side + 1, number] = jnp.where(here, block, used)
                    task_ref[3 * side + 2, number] = back
                    used_ref[2, source] = jnp.where(here, used, used + 3 + 2 * side)
                    used_ref[3, source] = jnp.where(here, back, back + 3 - 2 * side)
                task_ref[6, number] = owner
                task_ref[7, number] = turn

            return (number + 1, jnp.where(fits, over, 1))

        entries, tasks, over = carry
        over = jnp.maximum(over, list_ref[owner, 2])
        entries, over = lax.fori_loop(
            0, jnp.minimum(list_ref[owner, 0], ENTRY_CAP), entry, (entries, over)
        )
        tasks, over = lax.fori_loop(
            0, jnp.minimum(list_ref[owner, 1], TASK_CAP), task, (tasks, over)
        )
        return (entries, tasks, over)

    zero = jnp.int32(0)
    entries, tasks, over = lax.fori_loop(0, devices, from_owner, (zero, zero, zero))
    entry_ref[4, 0] = jnp.minimum(entries, ENTRIES)
    task_ref[8, 0] = jnp.minimum(tasks, TASKS)
    mark = jnp.full((devices, LANES), over.astype(F32), F32)
    out_ref[:, SEND_ROWS - 1, :] = mark


def pack_kernel(slots, rows_per, own_ref, map_ref, pos_ref, angles_ref, nodes_ref, out_ref, ids_ref):
    own = own_ref[0]
    devices = map_ref.shape[0] // rows_per
    owner = jnp.concatenate(
        [map_ref[pl.ds(own * rows_per + i, 1), :] for i in range(rows_per)], axis=1
    )
    blocks = owner.shape[1]
    mine = iota((devices, blocks), 0) == owner
    before = dot_nn(as_bf16(mine), strict_upper(blocks))
    rank = jnp.sum(jnp.where(mine, before, 0.0), axis=0, keepdims=True).astype(jnp.int32)
    place = owner * slots + rank
    move = as_bf16(iota((devices * slots, blocks), 0) == place)
    for field in range(5):
        values = pos_ref[field] if field < 3 else angles_ref[:, field - 3, :]
        moved = dot_nn(move, jnp.concatenate(split3(values), axis=1))
        moved = moved[:, :LANES] + moved[:, LANES : 2 * LANES] + moved[:, 2 * LANES :]
        out_ref[:, field * slots : (field + 1) * slots, :] = moved.reshape(devices, slots, LANES)
    nodes = nodes_ref[...]
    halves = jnp.concatenate(
        [(nodes >> 7).astype(F32).astype(BF16), (nodes & (LANES - 1)).astype(F32).astype(BF16)],
        axis=1,
    )
    moved = dot_nn(move, halves)
    ids_ref[...] = (moved[:, :LANES] * LANES + moved[:, LANES:]).astype(jnp.int32)


def sine_cosine(angle):
    half = 0.5 * angle
    sq = half * half
    sine = sq * (-1.0 / 39916800.0) + 1.0 / 362880.0
    for coef in (-1.0 / 5040.0, 1.0 / 120.0, -1.0 / 6.0, 1.0):
        sine = sine * sq + coef
    sine = sine * half
    cosine = sq * (1.0 / 479001600.0) - 1.0 / 3628800.0
    for coef in (1.0 / 40320.0, -1.0 / 720.0, 1.0 / 24.0, -0.5, 1.0):
        cosine = cosine * sq + coef
    return 2.0 * sine * cosine, 1.0 - 2.0 * sine * sine


def pair_kernel(
    slots, index_ref, count_ref, in_ref, masks_ref, out_ref, slave_ref, master_ref, sin_ref, cos_ref
):
    pairs = masks_ref.shape[1]
    count = jnp.minimum(count_ref[0], pairs)
    out_ref[...] = jnp.zeros_like(out_ref)

    def stage(pair, carry):
        source = index_ref[0, pair]
        slot = index_ref[1, pair]
        for field in range(3):
            slave_ref[pl.ds(pair * 8 + field, 1), :] = in_ref[source, pl.ds(field * slots + slot, 1), :]
        slave_ref[pl.ds(pair * 8 + 3, 1), :] = masks_ref[0, pl.ds(pair, 1), :].astype(F32)
        source = index_ref[2, pair]
        slot = index_ref[3, pair]
        for field in range(5):
            master_ref[pl.ds(pair * 8 + field, 1), :] = in_ref[source, pl.ds(field * slots + slot, 1), :]
        master_ref[pl.ds(pair * 8 + 5, 1), :] = masks_ref[1, pl.ds(pair, 1), :].astype(F32)
        return carry

    lax.fori_loop(0, count, stage, 0)
    sines, cosines = sine_cosine(master_ref[...])
    sin_ref[...] = sines
    cos_ref[...] = cosines

    def tile(pair, carry):
        base = pl.multiple_of(pair * 8, 8)
        slave = slave_ref[pl.ds(base, 8), :]
        columns = jnp.transpose(slave)
        master = master_ref[pl.ds(base, 8), :]
        sin_az = sin_ref[pl.ds(base + 3, 1), :]
        sin_pol = sin_ref[pl.ds(base + 4, 1), :]
        cos_az = cos_ref[pl.ds(base + 3, 1), :]
        cos_pol = cos_ref[pl.ds(base + 4, 1), :]
        normal = [cos_az * cos_pol, sin_az * cos_pol, sin_pol]
        shape = (LANES, LANES)
        dist = [
            jnp.broadcast_to(columns[:, k : k + 1], shape) - jnp.broadcast_to(master[k : k + 1], shape)
            for k in range(3)
        ]
        gap = dist[0] * normal[0] + dist[1] * normal[1] + dist[2] * normal[2]
        tang = dist[0] * dist[0] + dist[1] * dist[1] + dist[2] * dist[2] - gap * gap
        bend = gap * (-1.0 / PEN_DEPTH)
        soft = jnp.maximum(bend, 0.0) + jnp.log(1.0 + jnp.exp(-jnp.abs(bend)))
        press = soft * jnp.exp(-0.5 * tang)
        press = press * jnp.broadcast_to(columns[:, 3:4], shape)
        total = jnp.sum(press, axis=0, keepdims=True)
        scale = PEN_STIFF * PEN_DEPTH * master[5:6]
        push = [n * scale for n in normal]
        rows = jnp.concatenate(push + [jnp.zeros((5, LANES), F32)], axis=0)
        push_high, push_rest = split2(rows)
        both = jnp.concatenate([push_high, push_rest], axis=0)
        high, rest = split2(press)
        got = dot_nt(both, high) + dot_nt(both, rest)
        on_slave = got[0:8] + got[8:16]
        source = index_ref[0, pair]
        slot = index_ref[1, pair]
        for k in range(3):
            at = pl.ds(k * slots + slot, 1)
            out_ref[source, at, :] = out_ref[source, at, :] + on_slave[k : k + 1]
        source = index_ref[2, pair]
        slot = index_ref[3, pair]
        for k in range(3):
            at = pl.ds(k * slots + slot, 1)
            out_ref[source, at, :] = out_ref[source, at, :] - push[k] * total
        return carry

    lax.fori_loop(0, count, tile, 0)


def work_kernel(
    own_ref,
    task_ref,
    in_ref,
    request_ref,
    pos_ref,
    angles_ref,
    back_ref,
    slave_out,
    master_out,
    field_ref,
    left_ref,
    gap_ref,
    far_ref,
    push_ref,
):
    own = own_ref[0]
    count = task_ref[8, 0]

    def stage(task, carry):
        owner = task_ref[6, task]
        turn = task_ref[7, task]
        for side in range(2):
            source = task_ref[3 * side, task]
            first = task_ref[3 * side + 1, task]
            base = 4 * side

            @pl.when(source == own)
            def _():
                for field in range(3):
                    field_ref[base + field, pl.ds(task, 1), :] = pos_ref[field, pl.ds(first, 1), :]
                if side == 1:
                    both = angles_ref[first]
                    field_ref[8, pl.ds(task, 1), :] = both[0:1]
                    field_ref[9, pl.ds(task, 1), :] = both[1:2]

            @pl.when(source != own)
            def _():
                for field in range(3):
                    field_ref[base + field, pl.ds(task, 1), :] = in_ref[
                        source, pl.ds(first + field, 1), :
                    ]
                if side == 1:
                    for field in range(2):
                        field_ref[8 + field, pl.ds(task, 1), :] = in_ref[
                            source, pl.ds(first + 3 + field, 1), :
                        ]

            field_ref[base + 3, pl.ds(task, 1), :] = request_ref[
                owner, pl.ds(1 + 2 * turn + side, 1), :
            ].astype(F32)
        return carry

    lax.fori_loop(0, count, stage, 0)
    size = field_ref.shape[1]
    slave = [field_ref[k] for k in range(3)]
    master = [field_ref[4 + k] for k in range(3)]
    sin_az, cos_az = sine_cosine(field_ref[8])
    sin_pol, cos_pol = sine_cosine(field_ref[9])
    normal = [cos_az * cos_pol, sin_az * cos_pol, sin_pol]

    def inner(a, b):
        return a[0] * b[0] + a[1] * b[1] + a[2] * b[2]

    zero = jnp.zeros_like(sin_pol)
    one = zero + 1.0
    slope = -1.0 / PEN_DEPTH
    hidden = 30000.0
    slave_bias = -0.5 * inner(slave, slave) - hidden * (1.0 - field_ref[3])
    master_bias = -0.5 * inner(master, master) - hidden * (1.0 - field_ref[7])
    stacks = (
        (left_ref, slave + [one, slave_bias]),
        (gap_ref, [slope * n for n in normal] + [-slope * inner(normal, master), zero]),
        (far_ref, master + [master_bias, one]),
        (push_ref, [PEN_STIFF * PEN_DEPTH * n for n in normal] + [zero, zero]),
    )
    for ref, rows in stacks:
        for row, value in enumerate(rows + [zero] * 3):
            parts = split3(value)
            for part in range(ref.shape[0]):
                ref[part, pl.ds(row, size, stride=8), :] = parts[part].astype(F32)

    def tile(step, carry):
        tasks = [TASK_STEP * step + k for k in range(TASK_STEP)]
        bases = [pl.multiple_of(task * 8, 8) for task in tasks]
        fields = []
        for base in bases:
            high, mid, low = [left_ref[p, pl.ds(base, 8), :] for p in range(3)]
            left = jnp.concatenate([high, high, mid, mid, high, low], axis=0).astype(BF16)
            sides = []
            for ref in (gap_ref, far_ref):
                high, mid, low = [ref[p, pl.ds(base, 8), :] for p in range(3)]
                sides.append(jnp.concatenate([high, mid, high, mid, low, high], axis=0))
            fields.append(dot_tn(left, jnp.concatenate(sides, axis=1).astype(BF16)))
        presses = []
        for field in fields:
            bend = field[:, :LANES]
            power = field[:, LANES:] + bend * bend * (0.5 * PEN_DEPTH * PEN_DEPTH)
            soft = jnp.maximum(bend, 0.0) + jnp.log(1.0 + jnp.exp(-jnp.abs(bend)))
            presses.append(soft * jnp.exp(power))
        results = []
        for base, press in zip(bases, presses):
            push = jnp.concatenate([push_ref[p, pl.ds(base, 8), :] for p in range(2)], axis=0)
            push = push.astype(BF16)
            got = dot_nt(
                jnp.concatenate([push, push], axis=1), jnp.concatenate(split2(press), axis=1)
            )
            total = jnp.sum(press, axis=0, keepdims=True)
            results.append((got[0:8] + got[8:16], total * (PEN_STIFF * PEN_DEPTH)))
        for task, base, (on_slave, total) in zip(tasks, bases, results):
            normals = gap_ref[0, pl.ds(base, 8), :] + gap_ref[1, pl.ds(base, 8), :]
            normals = normals + gap_ref[2, pl.ds(base, 8), :]
            slave_out[pl.ds(base, 8), :] = on_slave
            master_out[pl.ds(base, 8), :] = normals * (total * (-1.0 / slope))
            live = task < count
            slave_from = task_ref[0, task]
            master_from = task_ref[3, task]

            @pl.when(live & (slave_from != own))
            def _():
                for k in range(3):
                    back_ref[slave_from, pl.ds(task_ref[2, task] + k, 1), :] = on_slave[k : k + 1]

            @pl.when(live & (master_from != own))
            def _():
                back_ref[master_from, pl.ds(task_ref[5, task], 1), :] = total

        return carry

    lax.fori_loop(0, (count + TASK_STEP - 1) // TASK_STEP, tile, 0)


def near_kernel(own_ref, task_ref, nodes_ref, slave_ref, master_ref, inner_ref, out_ref):
    own = own_ref[0]

    def step(task, acc):
        ids = []
        forces = []
        for side, force_ref in ((0, slave_ref), (1, master_ref)):
            here = task_ref[3 * side, task] == own
            block = jnp.where(here, task_ref[3 * side + 1, task], 0)
            ids.append(nodes_ref[pl.ds(block, 1), :])
            rows = force_ref[pl.ds(pl.multiple_of(task * 8, 8), 8), :]
            rows = jnp.where(here, rows, 0.0)
            forces.append([rows[k : k + 1] for k in range(3)])
        return acc + scatter_terms(ids, forces)

    acc = lax.fori_loop(0, task_ref[8, 0], step, jnp.zeros((6 * GROUP, LANES), F32))
    out_ref[...] = inner_ref[...] + fold_terms(acc)


def far_kernel(
    chunks,
    grid,
    own_ref,
    entry_ref,
    back_ref,
    nodes_ref,
    normal_ref,
    near_ref,
    faces_ref,
    out_ref,
    send_ref,
    value_ref,
):
    count = entry_ref[4, 0]

    def step(turn, acc):
        ids = []
        forces = []
        for k in range(2):
            valid = 2 * turn + k < count
            number = jnp.where(valid, 2 * turn + k, 0)
            block = entry_ref[0, number]
            role = entry_ref[1, number]
            worker = entry_ref[2, number]
            first = entry_ref[3, number]
            ids.append(nodes_ref[pl.ds(block, 1), :])
            total = back_ref[worker, pl.ds(first, 1), :]
            rows = []
            for field in range(3):
                row = back_ref[worker, pl.ds(jnp.minimum(first + field, BACK_ROWS - 1), 1), :]
                row = jnp.where(role == 1, -normal_ref[field, pl.ds(block, 1), :] * total, row)
                rows.append(jnp.where(valid, row, 0.0))
            forces.append(rows)
        return acc + scatter_terms(ids, forces)

    acc = lax.fori_loop(0, (count + 1) // 2, step, jnp.zeros((6 * GROUP, LANES), F32))
    out_ref[...] = near_ref[...] + fold_terms(acc)
    send_faces(own_ref[0], grid, out_ref, chunks, faces_ref, send_ref, value_ref)


def element_kernel(conn_ref, coords_ref, disp_ref, modulus_ref, out_ref, order_ref):
    chunks = coords_ref.shape[1] // LANES
    groups = conn_ref.shape[1] // LANES
    for group in range(groups):
        order_ref[pl.ds(group * 8, 8), :] = conn_ref[:, group * LANES : (group + 1) * LANES]
    pos = []
    disp = []
    for corner in range(8):
        ids = order_ref[pl.ds(corner, groups, stride=8), :]
        found = gather_chunks(
            lambda field, chunk: (coords_ref if field < 3 else disp_ref)[
                field % 3 : field % 3 + 1, chunk * LANES : (chunk + 1) * LANES
            ],
            6,
            chunks,
            ids,
        )
        pos.append(found[:3])
        disp.append(found[3:])
    first = list(pos[0])
    pos = [[pos[corner][j] - first[j] for j in range(3)] for corner in range(8)]

    def signed(values, signs):
        total = None
        for value, sign in zip(values, signs):
            if total is None:
                total = value if sign > 0 else -value
            else:
                total = total + value if sign > 0 else total - value
        return total

    corner_signs = [[XI_SIGNS[corner][k] for corner in range(8)] for k in range(3)]
    jac = [
        [signed([pos[c][j] for c in range(8)], corner_signs[k]) * 0.125 for k in range(3)]
        for j in range(3)
    ]
    cof = [
        [
            jac[(j + 1) % 3][(k + 1) % 3] * jac[(j + 2) % 3][(k + 2) % 3]
            - jac[(j + 1) % 3][(k + 2) % 3] * jac[(j + 2) % 3][(k + 1) % 3]
            for k in range(3)
        ]
        for j in range(3)
    ]
    det = jac[0][0] * cof[0][0] + jac[0][1] * cof[0][1] + jac[0][2] * cof[0][2]
    volume = 8.0 * det
    inverse = 1.0 / volume
    scaled = [[cof[j][k] * inverse for k in range(3)] for j in range(3)]
    grad = [[signed(scaled[j], XI_SIGNS[c]) for j in range(3)] for c in range(8)]

    def summed(terms):
        total = terms[0]
        for term in terms[1:]:
            total = total + term
        return total

    ugrad = [
        [summed([disp[c][i] * grad[c][j] for c in range(8)]) for j in range(3)] for i in range(3)
    ]
    modulus = modulus_ref[...]
    dilation = ugrad[0][0] + ugrad[1][1] + ugrad[2][2]
    stress = [[modulus * (ugrad[i][j] + ugrad[j][i]) for j in range(3)] for i in range(3)]
    for i in range(3):
        stress[i][i] = stress[i][i] + modulus * dilation
    squares = summed([grad[c][j] * grad[c][j] for c in range(8) for j in range(3)])
    hour_coef = HG_COEF * modulus * volume * squares
    shapes = []
    modes = []
    for a in range(4):
        hour_pos = [signed([pos[c][j] for c in range(8)], HOUR_VEC[a]) for j in range(3)]
        gam = [
            float(HOUR_VEC[a][c]) - summed([hour_pos[j] * grad[c][j] for j in range(3)])
            for c in range(8)
        ]
        shapes.append(gam)
        modes.append(
            [hour_coef * summed([disp[c][i] * gam[c] for c in range(8)]) for i in range(3)]
        )
    flux = [[volume * stress[i][j] for j in range(3)] for i in range(3)]
    acc = jnp.zeros((6 * GROUP, LANES), F32)
    for corner in range(8):
        ids = order_ref[pl.ds(corner, groups, stride=8), :]
        force = []
        for i in range(3):
            value = summed([flux[i][j] * grad[corner][j] for j in range(3)])
            value = value + summed([modes[a][i] * shapes[a][corner] for a in range(4)])
            force.append(-value)
        for group in range(0, groups, 2):
            picks = range(group, min(group + 2, groups))
            acc = acc + scatter_terms(
                [ids[g : g + 1] for g in picks], [[f[g : g + 1] for f in force] for g in picks]
            )
    out_ref[...] = fold_terms(acc)


def around(grid):
    return [(dx, dy) for dx in (-1, 0, 1) for dy in (-1, 0, 1) if (dx, dy) != (0, 0)]


def face_toward(dx, dy):
    if dx:
        return 1 if dx > 0 else 0
    return 3 if dy > 0 else 2


def neighbour(own, grid, dx, dy):
    ix = own // grid[1] + dx
    iy = own % grid[1] + dy
    there = (ix >= 0) & (ix < grid[0]) & (iy >= 0) & (iy < grid[1])
    return there, jnp.where(there, ix * grid[1] + iy, 0)


def send_faces(own, grid, total_ref, chunks, faces_ref, send_ref, value_ref):
    value_ref[...] = jnp.zeros_like(value_ref)
    parts = faces_ref.shape[1] // LANES
    for part in range(parts):
        ids = faces_ref[:, part * LANES : (part + 1) * LANES]
        found = gather_chunks(
            lambda field, chunk: total_ref[field * GROUP + chunk : field * GROUP + chunk + 1, :],
            3,
            chunks,
            ids,
        )
        for field in range(3):
            at = field * parts + part
            for face in range(4):
                value_ref[face, at : at + 1, :] = found[field][face : face + 1]
    for dx, dy in around(grid):
        there, target = neighbour(own, grid, dx, dy)

        @pl.when(there)
        def _():
            send_ref[target] = value_ref[face_toward(dx, dy)]


def face_map_kernel(chunks, faces_ref, low_ref, high_ref, table_ref):
    parts = faces_ref.shape[1] // LANES
    acc = None
    for row in range(2):
        ids = [faces_ref[row : row + 1, p * LANES : (p + 1) * LANES] for p in range(parts)]
        zero = jnp.zeros((1, LANES), F32)
        places = [(iota((1, LANES), 1) + (p * LANES + 1)).astype(F32) for p in range(parts)]
        fields = [[place if f == row else zero for f in range(3)] for place in places]
        terms = scatter_terms(ids, fields)
        acc = terms if acc is None else acc + terms
    table_ref[...] = fold_terms(acc)
    low_ref[...] = jnp.zeros_like(low_ref)
    high_ref[...] = jnp.zeros_like(high_ref)
    for part in range(parts):
        ids = faces_ref[:, part * LANES : (part + 1) * LANES]
        found = gather_chunks(
            lambda field, chunk: table_ref[field * GROUP + chunk : field * GROUP + chunk + 1, :],
            2,
            chunks,
            ids,
        )
        for field in range(2):
            at = field * parts + part
            low_ref[at : at + 1, :] = found[field][2:3]
            high_ref[at : at + 1, :] = found[field][3:4]


def moved_faces(values, places, parts):
    results = [None] * (3 * parts)
    for part in range(parts):
        place = places[part].astype(jnp.int32) - 1
        low = jnp.broadcast_to(place & (LANES - 1), values.shape)
        got = jnp.take_along_axis(values, low, axis=1, mode="promise_in_bounds")
        for field in range(3):
            total = jnp.zeros((1, LANES), F32)
            for source in range(parts):
                at = field * parts + source
                total = jnp.where(place >> 7 == source, got[at : at + 1], total)
            results[field * parts + part] = total
    return results


def assemble_kernel(
    slots, chunks, grid, own_ref, back_ref, ids_ref, inner_ref, faces_ref, out_ref, send_ref, value_ref
):
    devices = back_ref.shape[0]

    def step(turn, acc):
        ids = ids_ref[pl.ds(turn * slots, slots), :]
        values = back_ref[turn]
        for slot in range(0, slots, 2):
            picks = range(slot, min(slot + 2, slots))
            acc = acc + scatter_terms(
                [ids[s : s + 1] for s in picks],
                [[values[f * slots + s : f * slots + s + 1] for f in range(3)] for s in picks],
            )
        return acc

    acc = lax.fori_loop(0, devices, step, jnp.zeros((6 * GROUP, LANES), F32))
    out_ref[...] = inner_ref[...] + fold_terms(acc)
    send_faces(own_ref[0], grid, out_ref, chunks, faces_ref, send_ref, value_ref)


def final_kernel(
    grid, own_ref, total_ref, got_ref, low_ref, high_ref, faces_ref, velocity_ref, mass_ref, out_ref, sum_ref
):
    own = own_ref[0]
    parts = faces_ref.shape[1] // LANES

    def block(dx, dy):
        there, source = neighbour(own, grid, dx, dy)
        return jnp.where(there, got_ref[source], 0.0)

    def rows_of(values):
        return [values[at : at + 1] for at in range(3 * parts)]

    def side(dy, map_ref):
        rows = rows_of(block(0, dy))
        for field, dx in enumerate((-1, 1)):
            places = [map_ref[field * parts + p : field * parts + p + 1, :] for p in range(parts)]
            rows = [a + b for a, b in zip(rows, moved_faces(block(dx, dy), places, parts))]
        return rows

    added = [rows_of(block(-1, 0)), rows_of(block(1, 0)), side(-1, low_ref), side(1, high_ref)]
    acc = jnp.zeros((6 * GROUP, LANES), F32)
    for face, rows in enumerate(added):
        ids = [faces_ref[face : face + 1, p * LANES : (p + 1) * LANES] for p in range(parts)]
        acc = acc + scatter_terms(
            ids, [[rows[f * parts + p] for f in range(3)] for p in range(parts)]
        )
    sum_ref[...] = total_ref[...] + fold_terms(acc)
    for chunk in range(out_ref.shape[1] // LANES):
        span = slice(chunk * LANES, (chunk + 1) * LANES)
        scale = TIME_STEP / mass_ref[chunk : chunk + 1, :]
        for field in range(3):
            row = field * GROUP + chunk
            out_ref[field : field + 1, span] = (
                velocity_ref[field : field + 1, span] + scale * sum_ref[row : row + 1, :]
            )


def call(kernel, outs, in_smem, args, scratch=(), out_smem=()):
    def spec(smem):
        return pl.BlockSpec(memory_space=pltpu.SMEM if smem else pltpu.VMEM)

    return pl.pallas_call(
        kernel,
        out_shape=[jax.ShapeDtypeStruct(shape, dtype) for shape, dtype in outs],
        in_specs=[spec(i in in_smem) for i in range(len(args))],
        out_specs=[spec(i in out_smem) for i in range(len(outs))],
        scratch_shapes=list(scratch),
        compiler_params=pltpu.CompilerParams(vmem_limit_bytes=VMEM_LIMIT),
    )(*args)


def exchange(low, high, axis):
    count = lax.axis_size(axis)
    forward = [(i, i + 1) for i in range(count - 1)]
    backward = [(target, source) for source, target in forward]
    return lax.ppermute(high, axis, forward), lax.ppermute(low, axis, backward)


def local(
    connectivity,
    face_nodes,
    coords,
    displacement,
    velocity,
    node_mass,
    modulus,
    surf_nodes,
    surf_ref,
    surf_angles,
    owner_map,
    pair_blocks,
    pair_masks,
    pair_count,
):
    axes = ("gx", "gy")
    devices = lax.axis_size("gx") * lax.axis_size("gy")
    per_dev = surf_nodes.shape[0]
    rows_per = per_dev // LANES
    node_count = coords.shape[1]
    chunks = node_count // LANES
    slots = 2 * per_dev // devices
    pairs = pair_blocks.shape[1]
    own = lax.axis_index(axes).reshape(1).astype(jnp.int32)
    owners = owner_map.reshape(devices * rows_per, LANES)
    face_pad = -face_nodes.shape[1] % LANES
    faces = jnp.pad(face_nodes, ((0, 4), (0, face_pad)), constant_values=-1)
    parts = faces.shape[1] // LANES
    face_rows = -(-3 * parts // 8) * 8
    total_shape = ((3 * GROUP, LANES), F32)
    face_shape = ((face_rows, LANES), F32)
    send_shape = ((devices, face_rows, LANES), F32)
    grid = (lax.axis_size("gx"), lax.axis_size("gy"))

    def to_all(values):
        return lax.all_to_all(values, axes, split_axis=0, concat_axis=0, tiled=True)

    [request] = call(
        functools.partial(request_kernel, rows_per),
        [((devices, REQUEST_ROWS, LANES), jnp.int32)],
        (0, 1),
        (own, pair_count, owners, pair_blocks, pair_masks),
    )
    asked = to_all(request)
    own_owners = lax.dynamic_slice_in_dim(owner_map, own[0] * per_dev, per_dev)
    pos, normals, block_of = call(
        functools.partial(segment_kernel, slots),
        [
            ((3, per_dev, LANES), F32),
            ((3, per_dev, LANES), F32),
            ((devices * slots,), jnp.int32),
        ],
        (0,),
        (own_owners, displacement, surf_nodes, surf_ref, surf_angles),
        [pltpu.SMEM((devices,), jnp.int32)],
        (2,),
    )
    [internal] = call(
        element_kernel,
        [total_shape],
        (),
        (connectivity, coords, displacement, modulus.reshape(-1, LANES)),
        [pltpu.VMEM((connectivity.shape[1] // LANES * 8, LANES), jnp.int32)],
    )
    map_low, map_high = call(
        functools.partial(face_map_kernel, chunks),
        [face_shape, face_shape],
        (),
        (faces,),
        [pltpu.VMEM((3 * GROUP, LANES), F32)],
    )
    map_low, map_high = exchange(map_low, map_high, "gy")
    outbound, entries, tasks = call(
        functools.partial(plan_kernel, slots),
        [
            ((devices, SEND_ROWS, LANES), F32),
            ((8, ENTRIES), jnp.int32),
            ((16, TASKS), jnp.int32),
        ],
        (0, 1, 2),
        (own, asked[:, 0, :], block_of, pos, surf_angles),
        [pltpu.SMEM((4, devices), jnp.int32)],
        (1, 2),
    )
    inbound = to_all(outbound)
    inbound, map_low, map_high = lax.optimization_barrier((inbound, map_low, map_high))
    over = jnp.max(inbound[:, SEND_ROWS - 1, 0]) > 0.0

    def by_tasks():
        back, on_slave, on_master = call(
            work_kernel,
            [
                ((devices, BACK_ROWS, LANES), F32),
                ((TASKS * 8, LANES), F32),
                ((TASKS * 8, LANES), F32),
            ],
            (0, 1),
            (own, tasks, inbound, asked, pos, surf_angles),
            [
                pltpu.VMEM((10, TASKS, LANES), F32),
                pltpu.VMEM((3, TASKS * 8, LANES), F32),
                pltpu.VMEM((3, TASKS * 8, LANES), F32),
                pltpu.VMEM((3, TASKS * 8, LANES), F32),
                pltpu.VMEM((2, TASKS * 8, LANES), F32),
            ],
        )
        returned = to_all(back)
        [near] = call(
            near_kernel,
            [total_shape],
            (0, 1),
            (own, tasks, surf_nodes, on_slave, on_master, internal),
        )
        return call(
            functools.partial(far_kernel, chunks, grid),
            [total_shape, send_shape],
            (0, 1),
            (own, entries, returned, surf_nodes, normals, near, faces),
            [pltpu.VMEM((4,) + face_shape[0], F32)],
        )

    def by_owners():
        [index] = call(
            functools.partial(routing_kernel, rows_per),
            [((4, pairs), jnp.int32)],
            (0, 1),
            (own, pair_count, owners, pair_blocks),
        )
        outbound, ids = call(
            functools.partial(pack_kernel, slots, rows_per),
            [((devices, 5 * slots, LANES), F32), ((devices * slots, LANES), jnp.int32)],
            (0,),
            (own, owners, pos, surf_angles, surf_nodes),
        )
        [forces] = call(
            functools.partial(pair_kernel, slots),
            [((devices, 3 * slots, LANES), F32)],
            (0, 1),
            (index, pair_count, to_all(outbound), pair_masks),
            [pltpu.VMEM((pairs * 8, LANES), F32)] * 4,
        )
        return call(
            functools.partial(assemble_kernel, slots, chunks, grid),
            [total_shape, send_shape],
            (0,),
            (own, to_all(forces), ids, internal, faces),
            [pltpu.VMEM((4,) + face_shape[0], F32)],
        )

    total, send = lax.cond(over, by_owners, by_tasks)
    [result] = call(
        functools.partial(final_kernel, grid),
        [((3, node_count), F32)],
        (0,),
        (
            own,
            total,
            to_all(send),
            map_low,
            map_high,
            faces,
            velocity,
            node_mass.reshape(chunks, LANES),
        ),
        [pltpu.VMEM((3 * GROUP, LANES), F32)],
    )
    return result


def solution(mesh):
    in_specs = (
        P(None, ("gx", "gy")),
        P(None, ("gx", "gy")),
        P(None, ("gx", "gy")),
        P(None, ("gx", "gy")),
        P(None, ("gx", "gy")),
        P(("gx", "gy")),
        P(("gx", "gy")),
        P(("gx", "gy"), None),
        P(("gx", "gy"), None, None),
        P(("gx", "gy"), None, None),
        P(),
        P(None, ("gx", "gy")),
        P(None, ("gx", "gy"), None),
        P(("gx", "gy")),
    )
    out_specs = P(None, ("gx", "gy"))
    return jax.shard_map(local, mesh=mesh, in_specs=in_specs, out_specs=out_specs, check_vma=False)
```

```python
import functools

import jax
import jax.numpy as jnp
from jax import lax
from jax.experimental import pallas as pl
from jax.experimental.pallas import tpu as pltpu
from jax.sharding import PartitionSpec as P

XI_SIGNS = [
    [-1, -1, -1],
    [1, -1, -1],
    [1, 1, -1],
    [-1, 1, -1],
    [-1, -1, 1],
    [1, -1, 1],
    [1, 1, 1],
    [-1, 1, 1],
]
HOUR_VEC = [
    [1, 1, -1, -1, -1, -1, 1, 1],
    [1, -1, -1, 1, -1, 1, 1, -1],
    [1, -1, 1, -1, 1, -1, 1, -1],
    [-1, 1, -1, 1, 1, -1, 1, -1],
]
HG_COEF = 0.05
PEN_STIFF = 0.05
PEN_DEPTH = 0.5
TIME_STEP = 0.2
LANES = 128
GROUP = 16
F32 = jnp.float32
BF16 = jnp.bfloat16
VMEM_LIMIT = 48 * 1024 * 1024
REQUEST_ROWS = 16
TASK_CAP = 7
TASK_LANE = 64
ENTRY_LANE = 4
ENTRY_CAP = 20
SEND_ROWS = 32
BACK_ROWS = 8
ENTRIES = 160
TASKS = 64
TASK_STEP = 8
BLOCK_STEP = 8


def iota(shape, dim):
    return lax.broadcasted_iota(jnp.int32, shape, dim)


def dot_nn(a, b):
    return lax.dot_general(a, b, (((1,), (0,)), ((), ())), preferred_element_type=F32)


def dot_nt(a, b):
    return lax.dot_general(a, b, (((1,), (1,)), ((), ())), preferred_element_type=F32)


def dot_tn(a, b):
    return lax.dot_general(a, b, (((0,), (0,)), ((), ())), preferred_element_type=F32)


def as_bf16(mask):
    return jnp.where(mask, 1.0, 0.0).astype(BF16)


def split2(x):
    high = x.astype(BF16)
    return high, (x - high.astype(F32)).astype(BF16)


def split3(x):
    high = x.astype(BF16)
    rest = x - high.astype(F32)
    mid = rest.astype(BF16)
    return high, mid, (rest - mid.astype(F32)).astype(BF16)


def strict_upper(size):
    return as_bf16(iota((size, size), 0) < iota((size, size), 1))


def take_lanes(row, index):
    table = jnp.broadcast_to(row, index.shape)
    return jnp.take_along_axis(table, index, axis=1, mode="promise_in_bounds")


def gather_chunks(rows_of, fields, chunks, ids):
    high = ids >> 7
    low = ids & (LANES - 1)
    found = [jnp.zeros(ids.shape, F32) for _ in range(fields)]
    for chunk in range(chunks):
        here = high == chunk
        for field in range(fields):
            found[field] = jnp.where(here, take_lanes(rows_of(field, chunk), low), found[field])
    return found


def scatter_terms(id_rows, force_rows):
    wide = []
    table = []
    for ids, forces in zip(id_rows, force_rows):
        here = jnp.broadcast_to(ids >> 7, (GROUP, LANES)) == iota((GROUP, LANES), 0)
        wide.append(
            jnp.concatenate(
                [jnp.where(here, jnp.broadcast_to(f, (GROUP, LANES)), 0.0) for f in forces], axis=0
            )
        )
        low = jnp.broadcast_to(ids & (LANES - 1), (LANES, LANES))
        table.append(as_bf16(low == iota((LANES, LANES), 0)))
    high, rest = split2(jnp.concatenate(wide, axis=1))
    both = jnp.concatenate([high, rest], axis=0)
    return dot_nt(both, jnp.concatenate(table, axis=1))


def fold_terms(acc):
    half = acc.shape[0] // 2
    return acc[:half] + acc[half:]


def routing_kernel(rows_per, own_ref, count_ref, map_ref, pairs_ref, index_ref):
    own = own_ref[0]
    rows = map_ref.shape[0]
    devices = rows // rows_per
    pairs = pairs_ref.shape[1]
    hit = as_bf16(map_ref[...] == own)
    source_of = iota((devices, rows), 1) // rows_per
    upto = as_bf16(source_of <= iota((devices, rows), 0))
    within = as_bf16(source_of == iota((devices, rows), 0))
    ends = jnp.sum(dot_nn(upto, hit), axis=1, keepdims=True)
    counts = jnp.sum(dot_nn(within, hit), axis=1, keepdims=True)
    ranks = pairs_ref[...].astype(F32)
    for side in range(2):
        rank = ranks[side : side + 1]
        below = jnp.broadcast_to(ends, (devices, pairs)) <= rank
        source = jnp.sum(jnp.where(below, 1.0, 0.0), axis=0, keepdims=True)
        source = jnp.minimum(source, devices - 1.0)
        start = jnp.sum(jnp.where(below, counts, 0.0), axis=0, keepdims=True)
        index_ref[2 * side : 2 * side + 1, :] = source.astype(jnp.int32)
        index_ref[2 * side + 1 : 2 * side + 2, :] = (rank - start).astype(jnp.int32)


def request_kernel(rows_per, own_ref, count_ref, map_ref, pairs_ref, masks_ref, out_ref):
    own = own_ref[0]
    rows = map_ref.shape[0]
    devices = rows // rows_per
    pairs = pairs_ref.shape[1]
    hit = as_bf16(map_ref[...] == own)
    source_of = iota((devices, rows), 1) // rows_per
    upto = as_bf16(source_of <= iota((devices, rows), 0))
    within = as_bf16(source_of == iota((devices, rows), 0))
    ends = jnp.sum(dot_nn(upto, hit), axis=1, keepdims=True)
    counts = jnp.sum(dot_nn(within, hit), axis=1, keepdims=True)
    ranks = pairs_ref[...].astype(F32)
    where_is = []
    for side in range(2):
        rank = ranks[side : side + 1]
        below = jnp.broadcast_to(ends, (devices, pairs)) <= rank
        source = jnp.sum(jnp.where(below, 1.0, 0.0), axis=0, keepdims=True)
        source = jnp.minimum(source, devices - 1.0)
        start = jnp.sum(jnp.where(below, counts, 0.0), axis=0, keepdims=True)
        where_is.append((source, rank - start))
    (slave, slave_rank), (master, master_rank) = where_is
    lane = iota((1, pairs), 1)
    live = lane < count_ref[0]
    me = own.astype(F32)
    device = iota((devices, pairs), 0).astype(F32)
    earlier = strict_upper(pairs)

    def pick(target, keep):
        return jnp.where((device == target) & keep, 1.0, 0.0)

    worker = jnp.where(lane == 0, me, slave)
    tasks = pick(worker, live)
    turn = jnp.sum(tasks * dot_nn(tasks.astype(BF16), earlier), axis=0, keepdims=True)
    worker = jnp.where(turn >= TASK_CAP, me, worker)
    tasks = pick(worker, live)
    turn = jnp.sum(tasks * dot_nn(tasks.astype(BF16), earlier), axis=0, keepdims=True)
    send_slave = live & (slave != worker)
    send_master = live & (master != worker)
    from_slave = pick(slave, send_slave)
    from_master = pick(master, send_master)
    both = from_slave + from_master
    ahead = dot_nn(both.astype(BF16), earlier)
    slave_at = jnp.sum(from_slave * ahead, axis=0, keepdims=True)
    master_at = jnp.sum(from_master * ahead, axis=0, keepdims=True)
    master_at = master_at + jnp.where(send_slave & (slave == master), 1.0, 0.0)

    column = iota((LANES, pairs), 0).astype(F32)

    def placed(first, fields, fits):
        total = jnp.zeros((LANES, pairs), F32)
        for at, field in enumerate(fields):
            total = jnp.where((column == first + at) & fits, field, total)
        return total.astype(BF16)

    zero = jnp.zeros_like(slave)
    entry = placed(ENTRY_LANE + 3 * slave_at, (zero, slave_rank, worker), slave_at < ENTRY_CAP)
    line = dot_nt(from_slave.astype(BF16), entry)
    entry = placed(
        ENTRY_LANE + 3 * master_at, (zero + 1.0, master_rank, worker), master_at < ENTRY_CAP
    )
    line = line + dot_nt(from_master.astype(BF16), entry)
    entry = placed(
        TASK_LANE + 4 * turn, (slave, slave_rank, master, master_rank), turn < TASK_CAP
    )
    line = line + dot_nt(tasks.astype(BF16), entry)
    entry_count = jnp.sum(both, axis=1, keepdims=True)
    task_count = jnp.sum(tasks, axis=1, keepdims=True)
    over = jnp.where((entry_count > ENTRY_CAP) | (task_count > TASK_CAP), 1.0, 0.0)
    over = jnp.max(over, axis=0, keepdims=True)
    spot = iota((devices, LANES), 1)
    line = jnp.where(spot == 0, entry_count, line)
    line = jnp.where(spot == 1, task_count, line)
    line = jnp.where(spot == 2, over, line)
    out_ref[:, 0, :] = line.astype(jnp.int32)
    chosen = [jnp.where(turn == t, tasks, 0.0) for t in range(TASK_CAP)]
    chosen = jnp.concatenate(chosen, axis=0).astype(BF16)
    masks = jnp.concatenate([masks_ref[0], masks_ref[1]], axis=1).astype(F32).astype(BF16)
    got = dot_nn(chosen, masks).astype(jnp.int32)
    for t in range(TASK_CAP):
        part = got[t * devices : (t + 1) * devices]
        out_ref[:, 1 + 2 * t, :] = part[:, :LANES]
        out_ref[:, 2 + 2 * t, :] = part[:, LANES:]
    for row in range(1 + 2 * TASK_CAP, REQUEST_ROWS):
        out_ref[:, row, :] = jnp.zeros((devices, LANES), jnp.int32)


def segment_kernel(
    cap, owners_ref, disp_ref, nodes_ref, ref_ref, angles_ref, pos_ref, normal_ref, block_ref, seen_ref
):
    chunks = disp_ref.shape[1] // LANES

    def clear(device, carry):
        seen_ref[device] = 0
        return carry

    lax.fori_loop(0, seen_ref.shape[0], clear, 0)

    def step(turn, carry):
        base = pl.multiple_of(turn * 8, 8)
        for k in range(8):
            owner = owners_ref[base + k]
            rank = seen_ref[owner]
            block_ref[owner * cap + rank] = base + k
            seen_ref[owner] = rank + 1
        ids = nodes_ref[pl.ds(base, 8), :]
        found = gather_chunks(
            lambda field, chunk: disp_ref[field : field + 1, chunk * LANES : (chunk + 1) * LANES],
            3,
            chunks,
            ids,
        )
        for field in range(3):
            pos_ref[field, pl.ds(base, 8), :] = found[field] + ref_ref[pl.ds(base, 8), field, :]
        sin_az, cos_az = sine_cosine(angles_ref[pl.ds(base, 8), 0, :])
        sin_pol, cos_pol = sine_cosine(angles_ref[pl.ds(base, 8), 1, :])
        normal_ref[0, pl.ds(base, 8), :] = cos_az * cos_pol
        normal_ref[1, pl.ds(base, 8), :] = sin_az * cos_pol
        normal_ref[2, pl.ds(base, 8), :] = sin_pol
        return carry

    lax.fori_loop(0, nodes_ref.shape[0] // 8, step, 0, unroll=2)


def plan_kernel(cap, list_ref, block_ref, pos_ref, angles_ref, out_ref, entry_ref, used_ref):
    devices = list_ref.shape[0]

    def clear(device, carry):
        used_ref[0, device] = 0
        used_ref[1, device] = 0
        return carry

    lax.fori_loop(0, devices, clear, 0)

    def from_owner(owner, carry):
        def entry(turn, state):
            number, over = state
            at = ENTRY_LANE + 3 * turn
            role = list_ref[owner, at]
            block = block_ref[owner * cap + list_ref[owner, at + 1]]
            worker = list_ref[owner, at + 2]
            first = used_ref[0, worker]
            back = used_ref[1, worker]
            after = first + 3 + 2 * role
            back_after = back + 3 - 2 * role
            used_ref[0, worker] = after
            used_ref[1, worker] = back_after
            fits = (after < SEND_ROWS) & (back_after <= BACK_ROWS) & (number < ENTRIES)

            @pl.when(fits)
            def _():
                for field in range(3):
                    out_ref[worker, pl.ds(first + field, 1), :] = pos_ref[field, pl.ds(block, 1), :]
                entry_ref[0, number] = block
                entry_ref[1, number] = role
                entry_ref[2, number] = worker
                entry_ref[3, number] = back

            @pl.when(fits & (role == 1))
            def _():
                out_ref[worker, pl.ds(first + 3, 2), :] = angles_ref[block]

            return (number + 1, jnp.where(fits, over, 1))

        entries, tasks, over = carry
        over = jnp.maximum(over, list_ref[owner, 2])
        entries, over = lax.fori_loop(
            0, jnp.minimum(list_ref[owner, 0], ENTRY_CAP), entry, (entries, over)
        )
        return (entries, tasks + list_ref[owner, 1], over)

    zero = jnp.int32(0)
    entries, tasks, over = lax.fori_loop(0, devices, from_owner, (zero, zero, zero))
    over = jnp.where(tasks > TASKS, 1, over)
    entry_ref[4, 0] = jnp.minimum(entries, ENTRIES)
    mark = jnp.full((devices, LANES), over.astype(F32), F32)
    out_ref[:, SEND_ROWS - 1, :] = mark


def table_kernel(
    cap,
    own_ref,
    list_ref,
    block_ref,
    request_ref,
    pos_ref,
    angles_ref,
    task_ref,
    near_ref,
    field_ref,
    used_ref,
):
    own = own_ref[0]
    devices = list_ref.shape[0]
    size = field_ref.shape[1]

    def clear(device, carry):
        used_ref[0, device] = 0
        used_ref[1, device] = 0
        return carry

    lax.fori_loop(0, devices, clear, 0)

    def from_owner(owner, carry):
        def task(turn, state):
            at = TASK_LANE + 4 * turn
            number, near = state
            for side in range(2):
                source = list_ref[owner, at + 2 * side]
                here = source == own
                block = block_ref[owner * cap + list_ref[owner, at + 2 * side + 1]]
                used = used_ref[0, source]
                back = used_ref[1, source]
                used_ref[0, source] = jnp.where(here, used, used + 3 + 2 * side)
                used_ref[1, source] = jnp.where(here, back, back + 3 - 2 * side)
                task_ref[3 * side, number] = source
                task_ref[3 * side + 1, number] = jnp.where(here, block, used)
                task_ref[3 * side + 2, number] = back
                base = 4 * side
                field_ref[base + 3, pl.ds(number, 1), :] = request_ref[
                    owner, pl.ds(1 + 2 * turn + side, 1), :
                ].astype(F32)
                spot = near

                @pl.when(here)
                def _():
                    near_ref[0, spot] = block
                    near_ref[1, spot] = (side * size + number) * 8
                    for field in range(3):
                        field_ref[base + field, pl.ds(number, 1), :] = pos_ref[
                            field, pl.ds(block, 1), :
                        ]
                    if side == 1:
                        both = angles_ref[block]
                        field_ref[8, pl.ds(number, 1), :] = both[0:1]
                        field_ref[9, pl.ds(number, 1), :] = both[1:2]

                near = near + jnp.where(here, 1, 0)
            return (number + 1, near)

        number, near = carry
        count = jnp.minimum(list_ref[owner, 1], TASK_CAP)
        count = jnp.minimum(count, TASKS - number)
        return lax.fori_loop(0, count, task, (number, near))

    tasks, near = lax.fori_loop(0, devices, from_owner, (jnp.int32(0), jnp.int32(0)))
    task_ref[6, 0] = tasks
    near_ref[2, 0] = near


def pack_kernel(slots, rows_per, own_ref, map_ref, pos_ref, angles_ref, nodes_ref, out_ref, ids_ref):
    own = own_ref[0]
    devices = map_ref.shape[0] // rows_per
    owner = jnp.concatenate(
        [map_ref[pl.ds(own * rows_per + i, 1), :] for i in range(rows_per)], axis=1
    )
    blocks = owner.shape[1]
    mine = iota((devices, blocks), 0) == owner
    before = dot_nn(as_bf16(mine), strict_upper(blocks))
    rank = jnp.sum(jnp.where(mine, before, 0.0), axis=0, keepdims=True).astype(jnp.int32)
    place = owner * slots + rank
    move = as_bf16(iota((devices * slots, blocks), 0) == place)
    for field in range(5):
        values = pos_ref[field] if field < 3 else angles_ref[:, field - 3, :]
        moved = dot_nn(move, jnp.concatenate(split3(values), axis=1))
        moved = moved[:, :LANES] + moved[:, LANES : 2 * LANES] + moved[:, 2 * LANES :]
        out_ref[:, field * slots : (field + 1) * slots, :] = moved.reshape(devices, slots, LANES)
    nodes = nodes_ref[...]
    halves = jnp.concatenate(
        [(nodes >> 7).astype(F32).astype(BF16), (nodes & (LANES - 1)).astype(F32).astype(BF16)],
        axis=1,
    )
    moved = dot_nn(move, halves)
    ids_ref[...] = (moved[:, :LANES] * LANES + moved[:, LANES:]).astype(jnp.int32)


def sine_cosine(angle):
    half = 0.5 * angle
    sq = half * half
    sine = sq * (-1.0 / 39916800.0) + 1.0 / 362880.0
    for coef in (-1.0 / 5040.0, 1.0 / 120.0, -1.0 / 6.0, 1.0):
        sine = sine * sq + coef
    sine = sine * half
    cosine = sq * (1.0 / 479001600.0) - 1.0 / 3628800.0
    for coef in (1.0 / 40320.0, -1.0 / 720.0, 1.0 / 24.0, -0.5, 1.0):
        cosine = cosine * sq + coef
    return 2.0 * sine * cosine, 1.0 - 2.0 * sine * sine


def pair_kernel(
    slots, index_ref, count_ref, in_ref, masks_ref, out_ref, slave_ref, master_ref, sin_ref, cos_ref
):
    pairs = masks_ref.shape[1]
    count = jnp.minimum(count_ref[0], pairs)
    out_ref[...] = jnp.zeros_like(out_ref)

    def stage(pair, carry):
        source = index_ref[0, pair]
        slot = index_ref[1, pair]
        for field in range(3):
            slave_ref[pl.ds(pair * 8 + field, 1), :] = in_ref[source, pl.ds(field * slots + slot, 1), :]
        slave_ref[pl.ds(pair * 8 + 3, 1), :] = masks_ref[0, pl.ds(pair, 1), :].astype(F32)
        source = index_ref[2, pair]
        slot = index_ref[3, pair]
        for field in range(5):
            master_ref[pl.ds(pair * 8 + field, 1), :] = in_ref[source, pl.ds(field * slots + slot, 1), :]
        master_ref[pl.ds(pair * 8 + 5, 1), :] = masks_ref[1, pl.ds(pair, 1), :].astype(F32)
        return carry

    lax.fori_loop(0, count, stage, 0)
    sines, cosines = sine_cosine(master_ref[...])
    sin_ref[...] = sines
    cos_ref[...] = cosines

    def tile(pair, carry):
        base = pl.multiple_of(pair * 8, 8)
        slave = slave_ref[pl.ds(base, 8), :]
        columns = jnp.transpose(slave)
        master = master_ref[pl.ds(base, 8), :]
        sin_az = sin_ref[pl.ds(base + 3, 1), :]
        sin_pol = sin_ref[pl.ds(base + 4, 1), :]
        cos_az = cos_ref[pl.ds(base + 3, 1), :]
        cos_pol = cos_ref[pl.ds(base + 4, 1), :]
        normal = [cos_az * cos_pol, sin_az * cos_pol, sin_pol]
        shape = (LANES, LANES)
        dist = [
            jnp.broadcast_to(columns[:, k : k + 1], shape) - jnp.broadcast_to(master[k : k + 1], shape)
            for k in range(3)
        ]
        gap = dist[0] * normal[0] + dist[1] * normal[1] + dist[2] * normal[2]
        tang = dist[0] * dist[0] + dist[1] * dist[1] + dist[2] * dist[2] - gap * gap
        bend = gap * (-1.0 / PEN_DEPTH)
        soft = jnp.maximum(bend, 0.0) + jnp.log(1.0 + jnp.exp(-jnp.abs(bend)))
        press = soft * jnp.exp(-0.5 * tang)
        press = press * jnp.broadcast_to(columns[:, 3:4], shape)
        total = jnp.sum(press, axis=0, keepdims=True)
        scale = PEN_STIFF * PEN_DEPTH * master[5:6]
        push = [n * scale for n in normal]
        rows = jnp.concatenate(push + [jnp.zeros((5, LANES), F32)], axis=0)
        push_high, push_rest = split2(rows)
        both = jnp.concatenate([push_high, push_rest], axis=0)
        high, rest = split2(press)
        got = dot_nt(both, high) + dot_nt(both, rest)
        on_slave = got[0:8] + got[8:16]
        source = index_ref[0, pair]
        slot = index_ref[1, pair]
        for k in range(3):
            at = pl.ds(k * slots + slot, 1)
            out_ref[source, at, :] = out_ref[source, at, :] + on_slave[k : k + 1]
        source = index_ref[2, pair]
        slot = index_ref[3, pair]
        for k in range(3):
            at = pl.ds(k * slots + slot, 1)
            out_ref[source, at, :] = out_ref[source, at, :] - push[k] * total
        return carry

    lax.fori_loop(0, count, tile, 0)


def work_kernel(
    own_ref,
    task_ref,
    in_ref,
    start_ref,
    back_ref,
    force_ref,
    field_ref,
    left_ref,
    gap_ref,
    far_ref,
    push_ref,
):
    own = own_ref[0]
    count = task_ref[6, 0]
    field_ref[...] = start_ref[...]

    def stage(task, carry):
        for side in range(2):
            source = task_ref[3 * side, task]
            first = task_ref[3 * side + 1, task]

            @pl.when(source != own)
            def _():
                for field in range(3):
                    field_ref[4 * side + field, pl.ds(task, 1), :] = in_ref[
                        source, pl.ds(first + field, 1), :
                    ]
                if side == 1:
                    for field in range(2):
                        field_ref[8 + field, pl.ds(task, 1), :] = in_ref[
                            source, pl.ds(first + 3 + field, 1), :
                        ]

        return carry

    lax.fori_loop(0, count, stage, 0)
    size = field_ref.shape[1]
    slave = [field_ref[k] for k in range(3)]
    master = [field_ref[4 + k] for k in range(3)]
    sin_az, cos_az = sine_cosine(field_ref[8])
    sin_pol, cos_pol = sine_cosine(field_ref[9])
    normal = [cos_az * cos_pol, sin_az * cos_pol, sin_pol]

    def inner(a, b):
        return a[0] * b[0] + a[1] * b[1] + a[2] * b[2]

    zero = jnp.zeros_like(sin_pol)
    one = zero + 1.0
    slope = -1.0 / PEN_DEPTH
    hidden = 30000.0
    slave_bias = -0.5 * inner(slave, slave) - hidden * (1.0 - field_ref[3])
    master_bias = -0.5 * inner(master, master) - hidden * (1.0 - field_ref[7])
    stacks = (
        (left_ref, slave + [one, slave_bias]),
        (gap_ref, [slope * n for n in normal] + [-slope * inner(normal, master), zero]),
        (far_ref, master + [master_bias, one]),
        (push_ref, [PEN_STIFF * PEN_DEPTH * n for n in normal] + [zero, zero]),
    )
    for ref, rows in stacks:
        for row, value in enumerate(rows + [zero] * 3):
            parts = split3(value)
            for part in range(ref.shape[0]):
                ref[part, pl.ds(row, size, stride=8), :] = parts[part].astype(F32)

    def tile(step, carry):
        tasks = [TASK_STEP * step + k for k in range(TASK_STEP)]
        bases = [pl.multiple_of(task * 8, 8) for task in tasks]
        fields = []
        for base in bases:
            high, mid, low = [left_ref[p, pl.ds(base, 8), :] for p in range(3)]
            left = jnp.concatenate([high, high, mid, mid, high, low], axis=0).astype(BF16)
            sides = []
            for ref in (gap_ref, far_ref):
                high, mid, low = [ref[p, pl.ds(base, 8), :] for p in range(3)]
                sides.append(jnp.concatenate([high, mid, high, mid, low, high], axis=0))
            fields.append(dot_tn(left, jnp.concatenate(sides, axis=1).astype(BF16)))
        presses = []
        for field in fields:
            bend = field[:, :LANES]
            power = field[:, LANES:] + bend * bend * (0.5 * PEN_DEPTH * PEN_DEPTH)
            soft = jnp.maximum(bend, 0.0) + jnp.log(1.0 + jnp.exp(-jnp.abs(bend)))
            presses.append(soft * jnp.exp(power))
        results = []
        for base, press in zip(bases, presses):
            push = jnp.concatenate([push_ref[p, pl.ds(base, 8), :] for p in range(2)], axis=0)
            push = push.astype(BF16)
            got = dot_nt(
                jnp.concatenate([push, push], axis=1), jnp.concatenate(split2(press), axis=1)
            )
            total = jnp.sum(press, axis=0, keepdims=True)
            results.append((got[0:8] + got[8:16], total * (PEN_STIFF * PEN_DEPTH)))
        for task, base, (on_slave, total) in zip(tasks, bases, results):
            normals = gap_ref[0, pl.ds(base, 8), :] + gap_ref[1, pl.ds(base, 8), :]
            normals = normals + gap_ref[2, pl.ds(base, 8), :]
            force_ref[pl.ds(base, 8), :] = on_slave
            force_ref[pl.ds(base + size * 8, 8), :] = normals * (total * (-1.0 / slope))
            live = task < count
            slave_from = task_ref[0, task]
            master_from = task_ref[3, task]

            @pl.when(live & (slave_from != own))
            def _():
                for k in range(3):
                    back_ref[slave_from, pl.ds(task_ref[2, task] + k, 1), :] = on_slave[k : k + 1]

            @pl.when(live & (master_from != own))
            def _():
                back_ref[master_from, pl.ds(task_ref[5, task], 1), :] = total

        return carry

    lax.fori_loop(0, (count + TASK_STEP - 1) // TASK_STEP, tile, 0)


def near_kernel(near_ref, nodes_ref, force_ref, inner_ref, out_ref):
    count = near_ref[2, 0]

    def step(turn, acc):
        ids = []
        forces = []
        for k in range(BLOCK_STEP):
            valid = BLOCK_STEP * turn + k < count
            number = jnp.where(valid, BLOCK_STEP * turn + k, 0)
            ids.append(nodes_ref[pl.ds(near_ref[0, number], 1), :])
            rows = force_ref[pl.ds(pl.multiple_of(near_ref[1, number], 8), 8), :]
            rows = jnp.where(valid, rows, 0.0)
            forces.append([rows[f : f + 1] for f in range(3)])
        return acc + scatter_terms(ids, forces)

    steps = (count + BLOCK_STEP - 1) // BLOCK_STEP
    acc = lax.fori_loop(0, steps, step, jnp.zeros((6 * GROUP, LANES), F32))
    out_ref[...] = inner_ref[...] + fold_terms(acc)


def far_kernel(
    chunks,
    grid,
    own_ref,
    entry_ref,
    back_ref,
    nodes_ref,
    normal_ref,
    near_ref,
    faces_ref,
    out_ref,
    send_ref,
    value_ref,
):
    count = entry_ref[4, 0]

    def step(turn, acc):
        ids = []
        forces = []
        for k in range(BLOCK_STEP):
            valid = BLOCK_STEP * turn + k < count
            number = jnp.where(valid, BLOCK_STEP * turn + k, 0)
            block = entry_ref[0, number]
            role = entry_ref[1, number]
            worker = entry_ref[2, number]
            first = entry_ref[3, number]
            ids.append(nodes_ref[pl.ds(block, 1), :])
            total = back_ref[worker, pl.ds(first, 1), :]
            rows = []
            for field in range(3):
                row = back_ref[worker, pl.ds(jnp.minimum(first + field, BACK_ROWS - 1), 1), :]
                row = jnp.where(role == 1, -normal_ref[field, pl.ds(block, 1), :] * total, row)
                rows.append(jnp.where(valid, row, 0.0))
            forces.append(rows)
        return acc + scatter_terms(ids, forces)

    steps = (count + BLOCK_STEP - 1) // BLOCK_STEP
    acc = lax.fori_loop(0, steps, step, jnp.zeros((6 * GROUP, LANES), F32))
    out_ref[...] = near_ref[...] + fold_terms(acc)
    send_faces(own_ref[0], grid, out_ref, chunks, faces_ref, send_ref, value_ref)


def element_kernel(conn_ref, coords_ref, disp_ref, modulus_ref, out_ref, order_ref):
    chunks = coords_ref.shape[1] // LANES
    groups = conn_ref.shape[1] // LANES
    for group in range(groups):
        order_ref[pl.ds(group * 8, 8), :] = conn_ref[:, group * LANES : (group + 1) * LANES]
    pos = []
    disp = []
    for corner in range(8):
        ids = order_ref[pl.ds(corner, groups, stride=8), :]
        found = gather_chunks(
            lambda field, chunk: (coords_ref if field < 3 else disp_ref)[
                field % 3 : field % 3 + 1, chunk * LANES : (chunk + 1) * LANES
            ],
            6,
            chunks,
            ids,
        )
        pos.append(found[:3])
        disp.append(found[3:])
    first = list(pos[0])
    pos = [[pos[corner][j] - first[j] for j in range(3)] for corner in range(8)]

    def signed(values, signs):
        total = None
        for value, sign in zip(values, signs):
            if total is None:
                total = value if sign > 0 else -value
            else:
                total = total + value if sign > 0 else total - value
        return total

    corner_signs = [[XI_SIGNS[corner][k] for corner in range(8)] for k in range(3)]
    jac = [
        [signed([pos[c][j] for c in range(8)], corner_signs[k]) * 0.125 for k in range(3)]
        for j in range(3)
    ]
    cof = [
        [
            jac[(j + 1) % 3][(k + 1) % 3] * jac[(j + 2) % 3][(k + 2) % 3]
            - jac[(j + 1) % 3][(k + 2) % 3] * jac[(j + 2) % 3][(k + 1) % 3]
            for k in range(3)
        ]
        for j in range(3)
    ]
    det = jac[0][0] * cof[0][0] + jac[0][1] * cof[0][1] + jac[0][2] * cof[0][2]
    volume = 8.0 * det
    inverse = 1.0 / volume
    scaled = [[cof[j][k] * inverse for k in range(3)] for j in range(3)]
    grad = [[signed(scaled[j], XI_SIGNS[c]) for j in range(3)] for c in range(8)]

    def summed(terms):
        total = terms[0]
        for term in terms[1:]:
            total = total + term
        return total

    ugrad = [
        [summed([disp[c][i] * grad[c][j] for c in range(8)]) for j in range(3)] for i in range(3)
    ]
    modulus = modulus_ref[...]
    dilation = ugrad[0][0] + ugrad[1][1] + ugrad[2][2]
    stress = [[modulus * (ugrad[i][j] + ugrad[j][i]) for j in range(3)] for i in range(3)]
    for i in range(3):
        stress[i][i] = stress[i][i] + modulus * dilation
    squares = summed([grad[c][j] * grad[c][j] for c in range(8) for j in range(3)])
    hour_coef = HG_COEF * modulus * volume * squares
    shapes = []
    modes = []
    for a in range(4):
        hour_pos = [signed([pos[c][j] for c in range(8)], HOUR_VEC[a]) for j in range(3)]
        gam = [
            float(HOUR_VEC[a][c]) - summed([hour_pos[j] * grad[c][j] for j in range(3)])
            for c in range(8)
        ]
        shapes.append(gam)
        modes.append(
            [hour_coef * summed([disp[c][i] * gam[c] for c in range(8)]) for i in range(3)]
        )
    flux = [[volume * stress[i][j] for j in range(3)] for i in range(3)]
    acc = jnp.zeros((6 * GROUP, LANES), F32)
    for corner in range(8):
        ids = order_ref[pl.ds(corner, groups, stride=8), :]
        force = []
        for i in range(3):
            value = summed([flux[i][j] * grad[corner][j] for j in range(3)])
            value = value + summed([modes[a][i] * shapes[a][corner] for a in range(4)])
            force.append(-value)
        for group in range(0, groups, 2):
            picks = range(group, min(group + 2, groups))
            acc = acc + scatter_terms(
                [ids[g : g + 1] for g in picks], [[f[g : g + 1] for f in force] for g in picks]
            )
    out_ref[...] = fold_terms(acc)


def around(grid):
    return [(dx, dy) for dx in (-1, 0, 1) for dy in (-1, 0, 1) if (dx, dy) != (0, 0)]


def face_toward(dx, dy):
    if dx:
        return 1 if dx > 0 else 0
    return 3 if dy > 0 else 2


def neighbour(own, grid, dx, dy):
    ix = own // grid[1] + dx
    iy = own % grid[1] + dy
    there = (ix >= 0) & (ix < grid[0]) & (iy >= 0) & (iy < grid[1])
    return there, jnp.where(there, ix * grid[1] + iy, 0)


def send_faces(own, grid, total_ref, chunks, faces_ref, send_ref, value_ref):
    value_ref[...] = jnp.zeros_like(value_ref)
    parts = faces_ref.shape[1] // LANES
    for part in range(parts):
        ids = faces_ref[:, part * LANES : (part + 1) * LANES]
        found = gather_chunks(
            lambda field, chunk: total_ref[field * GROUP + chunk : field * GROUP + chunk + 1, :],
            3,
            chunks,
            ids,
        )
        for field in range(3):
            at = field * parts + part
            for face in range(4):
                value_ref[face, at : at + 1, :] = found[field][face : face + 1]
    for dx, dy in around(grid):
        there, target = neighbour(own, grid, dx, dy)

        @pl.when(there)
        def _():
            send_ref[target] = value_ref[face_toward(dx, dy)]


def face_map_kernel(chunks, faces_ref, low_ref, high_ref, table_ref):
    parts = faces_ref.shape[1] // LANES
    acc = None
    for row in range(2):
        ids = [faces_ref[row : row + 1, p * LANES : (p + 1) * LANES] for p in range(parts)]
        zero = jnp.zeros((1, LANES), F32)
        places = [(iota((1, LANES), 1) + (p * LANES + 1)).astype(F32) for p in range(parts)]
        fields = [[place if f == row else zero for f in range(3)] for place in places]
        terms = scatter_terms(ids, fields)
        acc = terms if acc is None else acc + terms
    table_ref[...] = fold_terms(acc)
    low_ref[...] = jnp.zeros_like(low_ref)
    high_ref[...] = jnp.zeros_like(high_ref)
    for part in range(parts):
        ids = faces_ref[:, part * LANES : (part + 1) * LANES]
        found = gather_chunks(
            lambda field, chunk: table_ref[field * GROUP + chunk : field * GROUP + chunk + 1, :],
            2,
            chunks,
            ids,
        )
        for field in range(2):
            at = field * parts + part
            low_ref[at : at + 1, :] = found[field][2:3]
            high_ref[at : at + 1, :] = found[field][3:4]


def moved_faces(values, places, parts):
    results = [None] * (3 * parts)
    for part in range(parts):
        place = places[part].astype(jnp.int32) - 1
        low = jnp.broadcast_to(place & (LANES - 1), values.shape)
        got = jnp.take_along_axis(values, low, axis=1, mode="promise_in_bounds")
        for field in range(3):
            total = jnp.zeros((1, LANES), F32)
            for source in range(parts):
                at = field * parts + source
                total = jnp.where(place >> 7 == source, got[at : at + 1], total)
            results[field * parts + part] = total
    return results


def assemble_kernel(
    slots, chunks, grid, own_ref, back_ref, ids_ref, inner_ref, faces_ref, out_ref, send_ref, value_ref
):
    devices = back_ref.shape[0]

    def step(turn, acc):
        ids = ids_ref[pl.ds(turn * slots, slots), :]
        values = back_ref[turn]
        for slot in range(0, slots, 2):
            picks = range(slot, min(slot + 2, slots))
            acc = acc + scatter_terms(
                [ids[s : s + 1] for s in picks],
                [[values[f * slots + s : f * slots + s + 1] for f in range(3)] for s in picks],
            )
        return acc

    acc = lax.fori_loop(0, devices, step, jnp.zeros((6 * GROUP, LANES), F32))
    out_ref[...] = inner_ref[...] + fold_terms(acc)
    send_faces(own_ref[0], grid, out_ref, chunks, faces_ref, send_ref, value_ref)


def final_kernel(
    grid, own_ref, total_ref, got_ref, low_ref, high_ref, faces_ref, velocity_ref, mass_ref, out_ref, sum_ref
):
    own = own_ref[0]
    parts = faces_ref.shape[1] // LANES

    def block(dx, dy):
        there, source = neighbour(own, grid, dx, dy)
        return jnp.where(there, got_ref[source], 0.0)

    def rows_of(values):
        return [values[at : at + 1] for at in range(3 * parts)]

    def side(dy, map_ref):
        rows = rows_of(block(0, dy))
        for field, dx in enumerate((-1, 1)):
            places = [map_ref[field * parts + p : field * parts + p + 1, :] for p in range(parts)]
            rows = [a + b for a, b in zip(rows, moved_faces(block(dx, dy), places, parts))]
        return rows

    added = [rows_of(block(-1, 0)), rows_of(block(1, 0)), side(-1, low_ref), side(1, high_ref)]
    acc = jnp.zeros((6 * GROUP, LANES), F32)
    for face, rows in enumerate(added):
        ids = [faces_ref[face : face + 1, p * LANES : (p + 1) * LANES] for p in range(parts)]
        acc = acc + scatter_terms(
            ids, [[rows[f * parts + p] for f in range(3)] for p in range(parts)]
        )
    sum_ref[...] = total_ref[...] + fold_terms(acc)
    for chunk in range(out_ref.shape[1] // LANES):
        span = slice(chunk * LANES, (chunk + 1) * LANES)
        scale = TIME_STEP / mass_ref[chunk : chunk + 1, :]
        for field in range(3):
            row = field * GROUP + chunk
            out_ref[field : field + 1, span] = (
                velocity_ref[field : field + 1, span] + scale * sum_ref[row : row + 1, :]
            )


def call(kernel, outs, in_smem, args, scratch=(), out_smem=()):
    def spec(smem):
        return pl.BlockSpec(memory_space=pltpu.SMEM if smem else pltpu.VMEM)

    return pl.pallas_call(
        kernel,
        out_shape=[jax.ShapeDtypeStruct(shape, dtype) for shape, dtype in outs],
        in_specs=[spec(i in in_smem) for i in range(len(args))],
        out_specs=[spec(i in out_smem) for i in range(len(outs))],
        scratch_shapes=list(scratch),
        compiler_params=pltpu.CompilerParams(vmem_limit_bytes=VMEM_LIMIT),
    )(*args)


def exchange(low, high, axis):
    count = lax.axis_size(axis)
    forward = [(i, i + 1) for i in range(count - 1)]
    backward = [(target, source) for source, target in forward]
    return lax.ppermute(high, axis, forward), lax.ppermute(low, axis, backward)


def local(
    connectivity,
    face_nodes,
    coords,
    displacement,
    velocity,
    node_mass,
    modulus,
    surf_nodes,
    surf_ref,
    surf_angles,
    owner_map,
    pair_blocks,
    pair_masks,
    pair_count,
):
    axes = ("gx", "gy")
    devices = lax.axis_size("gx") * lax.axis_size("gy")
    per_dev = surf_nodes.shape[0]
    rows_per = per_dev // LANES
    node_count = coords.shape[1]
    chunks = node_count // LANES
    slots = 2 * per_dev // devices
    pairs = pair_blocks.shape[1]
    own = lax.axis_index(axes).reshape(1).astype(jnp.int32)
    owners = owner_map.reshape(devices * rows_per, LANES)
    face_pad = -face_nodes.shape[1] % LANES
    faces = jnp.pad(face_nodes, ((0, 4), (0, face_pad)), constant_values=-1)
    parts = faces.shape[1] // LANES
    face_rows = -(-3 * parts // 8) * 8
    total_shape = ((3 * GROUP, LANES), F32)
    face_shape = ((face_rows, LANES), F32)
    send_shape = ((devices, face_rows, LANES), F32)
    grid = (lax.axis_size("gx"), lax.axis_size("gy"))

    def to_all(values):
        return lax.all_to_all(values, axes, split_axis=0, concat_axis=0, tiled=True)

    [request] = call(
        functools.partial(request_kernel, rows_per),
        [((devices, REQUEST_ROWS, LANES), jnp.int32)],
        (0, 1),
        (own, pair_count, owners, pair_blocks, pair_masks),
    )
    asked = to_all(request)
    own_owners = lax.dynamic_slice_in_dim(owner_map, own[0] * per_dev, per_dev)
    pos, normals, block_of = call(
        functools.partial(segment_kernel, slots),
        [
            ((3, per_dev, LANES), F32),
            ((3, per_dev, LANES), F32),
            ((devices * slots,), jnp.int32),
        ],
        (0,),
        (own_owners, displacement, surf_nodes, surf_ref, surf_angles),
        [pltpu.SMEM((devices,), jnp.int32)],
        (2,),
    )
    [internal] = call(
        element_kernel,
        [total_shape],
        (),
        (connectivity, coords, displacement, modulus.reshape(-1, LANES)),
        [pltpu.VMEM((connectivity.shape[1] // LANES * 8, LANES), jnp.int32)],
    )
    map_low, map_high = call(
        functools.partial(face_map_kernel, chunks),
        [face_shape, face_shape],
        (),
        (faces,),
        [pltpu.VMEM((3 * GROUP, LANES), F32)],
    )
    map_low, map_high = exchange(map_low, map_high, "gy")
    lists = asked[:, 0, :]
    outbound, entries = call(
        functools.partial(plan_kernel, slots),
        [((devices, SEND_ROWS, LANES), F32), ((8, ENTRIES), jnp.int32)],
        (0, 1),
        (lists, block_of, pos, surf_angles),
        [pltpu.SMEM((2, devices), jnp.int32)],
        (1,),
    )
    tasks, near_list, fields = call(
        functools.partial(table_kernel, slots),
        [((8, TASKS), jnp.int32), ((8, 2 * TASKS), jnp.int32), ((10, TASKS, LANES), F32)],
        (0, 1, 2),
        (own, lists, block_of, asked, pos, surf_angles),
        [pltpu.SMEM((2, devices), jnp.int32)],
        (0, 1),
    )
    inbound = to_all(outbound)
    inbound, map_low, map_high = lax.optimization_barrier((inbound, map_low, map_high))
    over = jnp.max(inbound[:, SEND_ROWS - 1, 0]) > 0.0

    def by_tasks():
        back, forces = call(
            work_kernel,
            [((devices, BACK_ROWS, LANES), F32), ((2 * TASKS * 8, LANES), F32)],
            (0, 1),
            (own, tasks, inbound, fields),
            [
                pltpu.VMEM((10, TASKS, LANES), F32),
                pltpu.VMEM((3, TASKS * 8, LANES), F32),
                pltpu.VMEM((3, TASKS * 8, LANES), F32),
                pltpu.VMEM((3, TASKS * 8, LANES), F32),
                pltpu.VMEM((2, TASKS * 8, LANES), F32),
            ],
        )
        returned = to_all(back)
        [near] = call(
            near_kernel, [total_shape], (0,), (near_list, surf_nodes, forces, internal)
        )
        return call(
            functools.partial(far_kernel, chunks, grid),
            [total_shape, send_shape],
            (0, 1),
            (own, entries, returned, surf_nodes, normals, near, faces),
            [pltpu.VMEM((4,) + face_shape[0], F32)],
        )

    def by_owners():
        [index] = call(
            functools.partial(routing_kernel, rows_per),
            [((4, pairs), jnp.int32)],
            (0, 1),
            (own, pair_count, owners, pair_blocks),
        )
        outbound, ids = call(
            functools.partial(pack_kernel, slots, rows_per),
            [((devices, 5 * slots, LANES), F32), ((devices * slots, LANES), jnp.int32)],
            (0,),
            (own, owners, pos, surf_angles, surf_nodes),
        )
        [forces] = call(
            functools.partial(pair_kernel, slots),
            [((devices, 3 * slots, LANES), F32)],
            (0, 1),
            (index, pair_count, to_all(outbound), pair_masks),
            [pltpu.VMEM((pairs * 8, LANES), F32)] * 4,
        )
        return call(
            functools.partial(assemble_kernel, slots, chunks, grid),
            [total_shape, send_shape],
            (0,),
            (own, to_all(forces), ids, internal, faces),
            [pltpu.VMEM((4,) + face_shape[0], F32)],
        )

    total, send = lax.cond(over, by_owners, by_tasks)
    [result] = call(
        functools.partial(final_kernel, grid),
        [((3, node_count), F32)],
        (0,),
        (
            own,
            total,
            to_all(send),
            map_low,
            map_high,
            faces,
            velocity,
            node_mass.reshape(chunks, LANES),
        ),
        [pltpu.VMEM((3 * GROUP, LANES), F32)],
    )
    return result


def solution(mesh):
    in_specs = (
        P(None, ("gx", "gy")),
        P(None, ("gx", "gy")),
        P(None, ("gx", "gy")),
        P(None, ("gx", "gy")),
        P(None, ("gx", "gy")),
        P(("gx", "gy")),
        P(("gx", "gy")),
        P(("gx", "gy"), None),
        P(("gx", "gy"), None, None),
        P(("gx", "gy"), None, None),
        P(),
        P(None, ("gx", "gy")),
        P(None, ("gx", "gy"), None),
        P(("gx", "gy")),
    )
    out_specs = P(None, ("gx", "gy"))
    return jax.shard_map(local, mesh=mesh, in_specs=in_specs, out_specs=out_specs, check_vma=False)
```

```python
import functools

import jax
import jax.numpy as jnp
from jax import lax
from jax.experimental import pallas as pl
from jax.experimental.pallas import tpu as pltpu
from jax.sharding import PartitionSpec as P

XI_SIGNS = [
    [-1, -1, -1],
    [1, -1, -1],
    [1, 1, -1],
    [-1, 1, -1],
    [-1, -1, 1],
    [1, -1, 1],
    [1, 1, 1],
    [-1, 1, 1],
]
HOUR_VEC = [
    [1, 1, -1, -1, -1, -1, 1, 1],
    [1, -1, -1, 1, -1, 1, 1, -1],
    [1, -1, 1, -1, 1, -1, 1, -1],
    [-1, 1, -1, 1, 1, -1, 1, -1],
]
HG_COEF = 0.05
PEN_STIFF = 0.05
PEN_DEPTH = 0.5
TIME_STEP = 0.2
LANES = 128
GROUP = 16
F32 = jnp.float32
BF16 = jnp.bfloat16
VMEM_LIMIT = 48 * 1024 * 1024
REQUEST_ROWS = 16
TASK_CAP = 7
TASK_LANE = 64
ENTRY_LANE = 4
ENTRY_CAP = 20
SEND_ROWS = 32
BACK_ROWS = 8
ENTRIES = 160
TASKS = 48
TASK_STEP = 8
BLOCK_STEP = 8


def iota(shape, dim):
    return lax.broadcasted_iota(jnp.int32, shape, dim)


def dot_nn(a, b):
    return lax.dot_general(a, b, (((1,), (0,)), ((), ())), preferred_element_type=F32)


def dot_nt(a, b):
    return lax.dot_general(a, b, (((1,), (1,)), ((), ())), preferred_element_type=F32)


def dot_tn(a, b):
    return lax.dot_general(a, b, (((0,), (0,)), ((), ())), preferred_element_type=F32)


def as_bf16(mask):
    return jnp.where(mask, 1.0, 0.0).astype(BF16)


def split2(x):
    high = x.astype(BF16)
    return high, (x - high.astype(F32)).astype(BF16)


def split3(x):
    high = x.astype(BF16)
    rest = x - high.astype(F32)
    mid = rest.astype(BF16)
    return high, mid, (rest - mid.astype(F32)).astype(BF16)


def strict_upper(size):
    return as_bf16(iota((size, size), 0) < iota((size, size), 1))


def take_lanes(row, index):
    table = jnp.broadcast_to(row, index.shape)
    return jnp.take_along_axis(table, index, axis=1, mode="promise_in_bounds")


def gather_chunks(rows_of, fields, chunks, ids):
    high = ids >> 7
    low = ids & (LANES - 1)
    found = [jnp.zeros(ids.shape, F32) for _ in range(fields)]
    for chunk in range(chunks):
        here = high == chunk
        for field in range(fields):
            found[field] = jnp.where(here, take_lanes(rows_of(field, chunk), low), found[field])
    return found


def scatter_terms(id_rows, force_rows):
    wide = []
    table = []
    for ids, forces in zip(id_rows, force_rows):
        here = jnp.broadcast_to(ids >> 7, (GROUP, LANES)) == iota((GROUP, LANES), 0)
        wide.append(
            jnp.concatenate(
                [jnp.where(here, jnp.broadcast_to(f, (GROUP, LANES)), 0.0) for f in forces], axis=0
            )
        )
        low = jnp.broadcast_to(ids & (LANES - 1), (LANES, LANES))
        table.append(as_bf16(low == iota((LANES, LANES), 0)))
    high, rest = split2(jnp.concatenate(wide, axis=1))
    both = jnp.concatenate([high, rest], axis=0)
    return dot_nt(both, jnp.concatenate(table, axis=1))


def fold_terms(acc):
    half = acc.shape[0] // 2
    return acc[:half] + acc[half:]


def routing_kernel(rows_per, own_ref, count_ref, map_ref, pairs_ref, index_ref):
    own = own_ref[0]
    rows = map_ref.shape[0]
    devices = rows // rows_per
    pairs = pairs_ref.shape[1]
    hit = as_bf16(map_ref[...] == own)
    source_of = iota((devices, rows), 1) // rows_per
    upto = as_bf16(source_of <= iota((devices, rows), 0))
    within = as_bf16(source_of == iota((devices, rows), 0))
    ends = jnp.sum(dot_nn(upto, hit), axis=1, keepdims=True)
    counts = jnp.sum(dot_nn(within, hit), axis=1, keepdims=True)
    ranks = pairs_ref[...].astype(F32)
    for side in range(2):
        rank = ranks[side : side + 1]
        below = jnp.broadcast_to(ends, (devices, pairs)) <= rank
        source = jnp.sum(jnp.where(below, 1.0, 0.0), axis=0, keepdims=True)
        source = jnp.minimum(source, devices - 1.0)
        start = jnp.sum(jnp.where(below, counts, 0.0), axis=0, keepdims=True)
        index_ref[2 * side : 2 * side + 1, :] = source.astype(jnp.int32)
        index_ref[2 * side + 1 : 2 * side + 2, :] = (rank - start).astype(jnp.int32)


def request_kernel(rows_per, own_ref, count_ref, map_ref, pairs_ref, masks_ref, out_ref):
    own = own_ref[0]
    rows = map_ref.shape[0]
    devices = rows // rows_per
    pairs = pairs_ref.shape[1]
    hit = as_bf16(map_ref[...] == own)
    source_of = iota((devices, rows), 1) // rows_per
    upto = as_bf16(source_of <= iota((devices, rows), 0))
    within = as_bf16(source_of == iota((devices, rows), 0))
    ends = jnp.sum(dot_nn(upto, hit), axis=1, keepdims=True)
    counts = jnp.sum(dot_nn(within, hit), axis=1, keepdims=True)
    ranks = pairs_ref[...].astype(F32)
    where_is = []
    for side in range(2):
        rank = ranks[side : side + 1]
        below = jnp.broadcast_to(ends, (devices, pairs)) <= rank
        source = jnp.sum(jnp.where(below, 1.0, 0.0), axis=0, keepdims=True)
        source = jnp.minimum(source, devices - 1.0)
        start = jnp.sum(jnp.where(below, counts, 0.0), axis=0, keepdims=True)
        where_is.append((source, rank - start))
    (slave, slave_rank), (master, master_rank) = where_is
    lane = iota((1, pairs), 1)
    live = lane < count_ref[0]
    me = own.astype(F32)
    device = iota((devices, pairs), 0).astype(F32)
    earlier = strict_upper(pairs)

    def pick(target, keep):
        return jnp.where((device == target) & keep, 1.0, 0.0)

    worker = jnp.where(lane == 0, me, slave)
    tasks = pick(worker, live)
    turn = jnp.sum(tasks * dot_nn(tasks.astype(BF16), earlier), axis=0, keepdims=True)
    worker = jnp.where(turn >= TASK_CAP, me, worker)
    tasks = pick(worker, live)
    turn = jnp.sum(tasks * dot_nn(tasks.astype(BF16), earlier), axis=0, keepdims=True)
    send_slave = live & (slave != worker)
    send_master = live & (master != worker)
    from_slave = pick(slave, send_slave)
    from_master = pick(master, send_master)
    both = from_slave + from_master
    ahead = dot_nn(both.astype(BF16), earlier)
    slave_at = jnp.sum(from_slave * ahead, axis=0, keepdims=True)
    master_at = jnp.sum(from_master * ahead, axis=0, keepdims=True)
    master_at = master_at + jnp.where(send_slave & (slave == master), 1.0, 0.0)

    column = iota((LANES, pairs), 0).astype(F32)

    def placed(first, fields, fits):
        total = jnp.zeros((LANES, pairs), F32)
        for at, field in enumerate(fields):
            total = jnp.where((column == first + at) & fits, field, total)
        return total.astype(BF16)

    zero = jnp.zeros_like(slave)
    entry = placed(ENTRY_LANE + 3 * slave_at, (zero, slave_rank, worker), slave_at < ENTRY_CAP)
    line = dot_nt(from_slave.astype(BF16), entry)
    entry = placed(
        ENTRY_LANE + 3 * master_at, (zero + 1.0, master_rank, worker), master_at < ENTRY_CAP
    )
    line = line + dot_nt(from_master.astype(BF16), entry)
    entry = placed(
        TASK_LANE + 4 * turn, (slave, slave_rank, master, master_rank), turn < TASK_CAP
    )
    line = line + dot_nt(tasks.astype(BF16), entry)
    entry_count = jnp.sum(both, axis=1, keepdims=True)
    task_count = jnp.sum(tasks, axis=1, keepdims=True)
    over = jnp.where((entry_count > ENTRY_CAP) | (task_count > TASK_CAP), 1.0, 0.0)
    over = jnp.max(over, axis=0, keepdims=True)
    spot = iota((devices, LANES), 1)
    line = jnp.where(spot == 0, entry_count, line)
    line = jnp.where(spot == 1, task_count, line)
    line = jnp.where(spot == 2, over, line)
    out_ref[:, 0, :] = line.astype(jnp.int32)
    chosen = [jnp.where(turn == t, tasks, 0.0) for t in range(TASK_CAP)]
    chosen = jnp.concatenate(chosen, axis=0).astype(BF16)
    masks = jnp.concatenate([masks_ref[0], masks_ref[1]], axis=1).astype(F32).astype(BF16)
    got = dot_nn(chosen, masks).astype(jnp.int32)
    for t in range(TASK_CAP):
        part = got[t * devices : (t + 1) * devices]
        out_ref[:, 1 + 2 * t, :] = part[:, :LANES]
        out_ref[:, 2 + 2 * t, :] = part[:, LANES:]
    for row in range(1 + 2 * TASK_CAP, REQUEST_ROWS):
        out_ref[:, row, :] = jnp.zeros((devices, LANES), jnp.int32)


def segment_kernel(
    cap, owners_ref, disp_ref, nodes_ref, ref_ref, angles_ref, pos_ref, normal_ref, block_ref, seen_ref
):
    chunks = disp_ref.shape[1] // LANES

    def clear(device, carry):
        seen_ref[device] = 0
        return carry

    lax.fori_loop(0, seen_ref.shape[0], clear, 0)

    def step(turn, carry):
        base = pl.multiple_of(turn * 8, 8)
        for k in range(8):
            owner = owners_ref[base + k]
            rank = seen_ref[owner]
            block_ref[owner * cap + rank] = base + k
            seen_ref[owner] = rank + 1
        ids = nodes_ref[pl.ds(base, 8), :]
        found = gather_chunks(
            lambda field, chunk: disp_ref[field : field + 1, chunk * LANES : (chunk + 1) * LANES],
            3,
            chunks,
            ids,
        )
        for field in range(3):
            pos_ref[field, pl.ds(base, 8), :] = found[field] + ref_ref[pl.ds(base, 8), field, :]
        sin_az, cos_az = sine_cosine(angles_ref[pl.ds(base, 8), 0, :])
        sin_pol, cos_pol = sine_cosine(angles_ref[pl.ds(base, 8), 1, :])
        normal_ref[0, pl.ds(base, 8), :] = cos_az * cos_pol
        normal_ref[1, pl.ds(base, 8), :] = sin_az * cos_pol
        normal_ref[2, pl.ds(base, 8), :] = sin_pol
        return carry

    lax.fori_loop(0, nodes_ref.shape[0] // 8, step, 0, unroll=2)


def plan_kernel(cap, list_ref, block_ref, pos_ref, angles_ref, out_ref, entry_ref, used_ref):
    devices = list_ref.shape[0]

    def clear(device, carry):
        used_ref[0, device] = 0
        used_ref[1, device] = 0
        return carry

    lax.fori_loop(0, devices, clear, 0)

    def from_owner(owner, carry):
        def entry(turn, state):
            number, over = state
            at = ENTRY_LANE + 3 * turn
            role = list_ref[owner, at]
            block = block_ref[owner * cap + list_ref[owner, at + 1]]
            worker = list_ref[owner, at + 2]
            first = used_ref[0, worker]
            back = used_ref[1, worker]
            after = first + 3 + 2 * role
            back_after = back + 3 - 2 * role
            used_ref[0, worker] = after
            used_ref[1, worker] = back_after
            fits = (after < SEND_ROWS) & (back_after <= BACK_ROWS) & (number < ENTRIES)

            @pl.when(fits)
            def _():
                for field in range(3):
                    out_ref[worker, pl.ds(first + field, 1), :] = pos_ref[field, pl.ds(block, 1), :]
                entry_ref[0, number] = block
                entry_ref[1, number] = role
                entry_ref[2, number] = worker
                entry_ref[3, number] = back

            @pl.when(fits & (role == 1))
            def _():
                out_ref[worker, pl.ds(first + 3, 2), :] = angles_ref[block]

            return (number + 1, jnp.where(fits, over, 1))

        entries, tasks, over = carry
        over = jnp.maximum(over, list_ref[owner, 2])
        entries, over = lax.fori_loop(
            0, jnp.minimum(list_ref[owner, 0], ENTRY_CAP), entry, (entries, over)
        )
        return (entries, tasks + list_ref[owner, 1], over)

    zero = jnp.int32(0)
    entries, tasks, over = lax.fori_loop(0, devices, from_owner, (zero, zero, zero))
    over = jnp.where(tasks > TASKS, 1, over)
    entry_ref[4, 0] = jnp.minimum(entries, ENTRIES)
    mark = jnp.full((devices, LANES), over.astype(F32), F32)
    out_ref[:, SEND_ROWS - 1, :] = mark


def table_kernel(
    cap,
    own_ref,
    list_ref,
    block_ref,
    request_ref,
    pos_ref,
    angles_ref,
    task_ref,
    near_ref,
    field_ref,
    used_ref,
):
    own = own_ref[0]
    devices = list_ref.shape[0]
    size = field_ref.shape[1]

    def clear(device, carry):
        used_ref[0, device] = 0
        used_ref[1, device] = 0
        return carry

    lax.fori_loop(0, devices, clear, 0)

    def from_owner(owner, carry):
        def task(turn, state):
            at = TASK_LANE + 4 * turn
            number, near = state
            for side in range(2):
                source = list_ref[owner, at + 2 * side]
                here = source == own
                block = block_ref[owner * cap + list_ref[owner, at + 2 * side + 1]]
                used = used_ref[0, source]
                back = used_ref[1, source]
                used_ref[0, source] = jnp.where(here, used, used + 3 + 2 * side)
                used_ref[1, source] = jnp.where(here, back, back + 3 - 2 * side)
                task_ref[3 * side, number] = source
                task_ref[3 * side + 1, number] = jnp.where(here, block, jnp.minimum(used, SEND_ROWS - 5))
                task_ref[3 * side + 2, number] = back
                base = 4 * side
                field_ref[base + 3, pl.ds(number, 1), :] = request_ref[
                    owner, pl.ds(1 + 2 * turn + side, 1), :
                ].astype(F32)
                spot = near

                @pl.when(here)
                def _():
                    near_ref[0, spot] = block
                    near_ref[1, spot] = (side * size + number) * 8
                    for field in range(3):
                        field_ref[base + field, pl.ds(number, 1), :] = pos_ref[
                            field, pl.ds(block, 1), :
                        ]
                    if side == 1:
                        both = angles_ref[block]
                        field_ref[8, pl.ds(number, 1), :] = both[0:1]
                        field_ref[9, pl.ds(number, 1), :] = both[1:2]

                near = near + jnp.where(here, 1, 0)
            return (number + 1, near)

        number, near = carry
        count = jnp.minimum(list_ref[owner, 1], TASK_CAP)
        count = jnp.minimum(count, TASKS - number)
        return lax.fori_loop(0, count, task, (number, near))

    tasks, near = lax.fori_loop(0, devices, from_owner, (jnp.int32(0), jnp.int32(0)))
    task_ref[6, 0] = tasks
    near_ref[2, 0] = near


def pack_kernel(slots, rows_per, own_ref, map_ref, pos_ref, angles_ref, nodes_ref, out_ref, ids_ref):
    own = own_ref[0]
    devices = map_ref.shape[0] // rows_per
    owner = jnp.concatenate(
        [map_ref[pl.ds(own * rows_per + i, 1), :] for i in range(rows_per)], axis=1
    )
    blocks = owner.shape[1]
    mine = iota((devices, blocks), 0) == owner
    before = dot_nn(as_bf16(mine), strict_upper(blocks))
    rank = jnp.sum(jnp.where(mine, before, 0.0), axis=0, keepdims=True).astype(jnp.int32)
    place = owner * slots + rank
    move = as_bf16(iota((devices * slots, blocks), 0) == place)
    for field in range(5):
        values = pos_ref[field] if field < 3 else angles_ref[:, field - 3, :]
        moved = dot_nn(move, jnp.concatenate(split3(values), axis=1))
        moved = moved[:, :LANES] + moved[:, LANES : 2 * LANES] + moved[:, 2 * LANES :]
        out_ref[:, field * slots : (field + 1) * slots, :] = moved.reshape(devices, slots, LANES)
    nodes = nodes_ref[...]
    halves = jnp.concatenate(
        [(nodes >> 7).astype(F32).astype(BF16), (nodes & (LANES - 1)).astype(F32).astype(BF16)],
        axis=1,
    )
    moved = dot_nn(move, halves)
    ids_ref[...] = (moved[:, :LANES] * LANES + moved[:, LANES:]).astype(jnp.int32)


def sine_cosine(angle):
    half = 0.5 * angle
    sq = half * half
    sine = sq * (-1.0 / 39916800.0) + 1.0 / 362880.0
    for coef in (-1.0 / 5040.0, 1.0 / 120.0, -1.0 / 6.0, 1.0):
        sine = sine * sq + coef
    sine = sine * half
    cosine = sq * (1.0 / 479001600.0) - 1.0 / 3628800.0
    for coef in (1.0 / 40320.0, -1.0 / 720.0, 1.0 / 24.0, -0.5, 1.0):
        cosine = cosine * sq + coef
    return 2.0 * sine * cosine, 1.0 - 2.0 * sine * sine


def pair_kernel(
    slots, index_ref, count_ref, in_ref, masks_ref, out_ref, slave_ref, master_ref, sin_ref, cos_ref
):
    pairs = masks_ref.shape[1]
    count = jnp.minimum(count_ref[0], pairs)
    out_ref[...] = jnp.zeros_like(out_ref)

    def stage(pair, carry):
        source = index_ref[0, pair]
        slot = index_ref[1, pair]
        for field in range(3):
            slave_ref[pl.ds(pair * 8 + field, 1), :] = in_ref[source, pl.ds(field * slots + slot, 1), :]
        slave_ref[pl.ds(pair * 8 + 3, 1), :] = masks_ref[0, pl.ds(pair, 1), :].astype(F32)
        source = index_ref[2, pair]
        slot = index_ref[3, pair]
        for field in range(5):
            master_ref[pl.ds(pair * 8 + field, 1), :] = in_ref[source, pl.ds(field * slots + slot, 1), :]
        master_ref[pl.ds(pair * 8 + 5, 1), :] = masks_ref[1, pl.ds(pair, 1), :].astype(F32)
        return carry

    lax.fori_loop(0, count, stage, 0)
    sines, cosines = sine_cosine(master_ref[...])
    sin_ref[...] = sines
    cos_ref[...] = cosines

    def tile(pair, carry):
        base = pl.multiple_of(pair * 8, 8)
        slave = slave_ref[pl.ds(base, 8), :]
        columns = jnp.transpose(slave)
        master = master_ref[pl.ds(base, 8), :]
        sin_az = sin_ref[pl.ds(base + 3, 1), :]
        sin_pol = sin_ref[pl.ds(base + 4, 1), :]
        cos_az = cos_ref[pl.ds(base + 3, 1), :]
        cos_pol = cos_ref[pl.ds(base + 4, 1), :]
        normal = [cos_az * cos_pol, sin_az * cos_pol, sin_pol]
        shape = (LANES, LANES)
        dist = [
            jnp.broadcast_to(columns[:, k : k + 1], shape) - jnp.broadcast_to(master[k : k + 1], shape)
            for k in range(3)
        ]
        gap = dist[0] * normal[0] + dist[1] * normal[1] + dist[2] * normal[2]
        tang = dist[0] * dist[0] + dist[1] * dist[1] + dist[2] * dist[2] - gap * gap
        bend = gap * (-1.0 / PEN_DEPTH)
        soft = jnp.maximum(bend, 0.0) + jnp.log(1.0 + jnp.exp(-jnp.abs(bend)))
        press = soft * jnp.exp(-0.5 * tang)
        press = press * jnp.broadcast_to(columns[:, 3:4], shape)
        total = jnp.sum(press, axis=0, keepdims=True)
        scale = PEN_STIFF * PEN_DEPTH * master[5:6]
        push = [n * scale for n in normal]
        rows = jnp.concatenate(push + [jnp.zeros((5, LANES), F32)], axis=0)
        push_high, push_rest = split2(rows)
        both = jnp.concatenate([push_high, push_rest], axis=0)
        high, rest = split2(press)
        got = dot_nt(both, high) + dot_nt(both, rest)
        on_slave = got[0:8] + got[8:16]
        source = index_ref[0, pair]
        slot = index_ref[1, pair]
        for k in range(3):
            at = pl.ds(k * slots + slot, 1)
            out_ref[source, at, :] = out_ref[source, at, :] + on_slave[k : k + 1]
        source = index_ref[2, pair]
        slot = index_ref[3, pair]
        for k in range(3):
            at = pl.ds(k * slots + slot, 1)
            out_ref[source, at, :] = out_ref[source, at, :] - push[k] * total
        return carry

    lax.fori_loop(0, count, tile, 0)


def work_kernel(
    own_ref,
    task_ref,
    in_ref,
    start_ref,
    back_ref,
    force_ref,
    over_ref,
    field_ref,
    left_ref,
    gap_ref,
    far_ref,
    push_ref,
):
    own = own_ref[0]
    count = task_ref[6, 0]
    field_ref[...] = start_ref[...]
    over = jnp.max(in_ref[:, SEND_ROWS - 1, :])
    over_ref[0] = over.astype(jnp.int32)
    marks = force_ref.shape[0] - 8
    force_ref[marks:, :] = jnp.full((8, LANES), over, F32)

    def stage(task, carry):
        for side in range(2):
            source = task_ref[3 * side, task]
            first = task_ref[3 * side + 1, task]

            @pl.when(source != own)
            def _():
                for field in range(3):
                    field_ref[4 * side + field, pl.ds(task, 1), :] = in_ref[
                        source, pl.ds(first + field, 1), :
                    ]
                if side == 1:
                    for field in range(2):
                        field_ref[8 + field, pl.ds(task, 1), :] = in_ref[
                            source, pl.ds(first + 3 + field, 1), :
                        ]

        return carry

    lax.fori_loop(0, count, stage, 0)
    size = field_ref.shape[1]
    slave = [field_ref[k] for k in range(3)]
    master = [field_ref[4 + k] for k in range(3)]
    sin_az, cos_az = sine_cosine(field_ref[8])
    sin_pol, cos_pol = sine_cosine(field_ref[9])
    normal = [cos_az * cos_pol, sin_az * cos_pol, sin_pol]

    def inner(a, b):
        return a[0] * b[0] + a[1] * b[1] + a[2] * b[2]

    zero = jnp.zeros_like(sin_pol)
    one = zero + 1.0
    slope = -1.0 / PEN_DEPTH
    hidden = 30000.0
    slave_bias = -0.5 * inner(slave, slave) - hidden * (1.0 - field_ref[3])
    master_bias = -0.5 * inner(master, master) - hidden * (1.0 - field_ref[7])
    stacks = (
        (left_ref, slave + [one, slave_bias]),
        (gap_ref, [slope * n for n in normal] + [-slope * inner(normal, master), zero]),
        (far_ref, master + [master_bias, one]),
        (push_ref, [PEN_STIFF * PEN_DEPTH * n for n in normal] + [zero, zero]),
    )
    for ref, rows in stacks:
        for row, value in enumerate(rows + [zero] * 3):
            parts = split3(value)
            for part in range(ref.shape[0]):
                ref[part, pl.ds(row, size, stride=8), :] = parts[part].astype(F32)

    def tile(step, carry):
        tasks = [TASK_STEP * step + k for k in range(TASK_STEP)]
        bases = [pl.multiple_of(task * 8, 8) for task in tasks]
        fields = []
        for base in bases:
            high, mid, low = [left_ref[p, pl.ds(base, 8), :] for p in range(3)]
            left = jnp.concatenate([high, high, mid, mid, high, low], axis=0).astype(BF16)
            sides = []
            for ref in (gap_ref, far_ref):
                high, mid, low = [ref[p, pl.ds(base, 8), :] for p in range(3)]
                sides.append(jnp.concatenate([high, mid, high, mid, low, high], axis=0))
            fields.append(dot_tn(left, jnp.concatenate(sides, axis=1).astype(BF16)))
        presses = []
        for field in fields:
            bend = field[:, :LANES]
            power = field[:, LANES:] + bend * bend * (0.5 * PEN_DEPTH * PEN_DEPTH)
            soft = jnp.maximum(bend, 0.0) + jnp.log(1.0 + jnp.exp(-jnp.abs(bend)))
            presses.append(soft * jnp.exp(power))
        results = []
        for base, press in zip(bases, presses):
            push = jnp.concatenate([push_ref[p, pl.ds(base, 8), :] for p in range(2)], axis=0)
            push = push.astype(BF16)
            got = dot_nt(
                jnp.concatenate([push, push], axis=1), jnp.concatenate(split2(press), axis=1)
            )
            total = jnp.sum(press, axis=0, keepdims=True)
            results.append((got[0:8] + got[8:16], total * (PEN_STIFF * PEN_DEPTH)))
        for task, base, (on_slave, total) in zip(tasks, bases, results):
            normals = gap_ref[0, pl.ds(base, 8), :] + gap_ref[1, pl.ds(base, 8), :]
            normals = normals + gap_ref[2, pl.ds(base, 8), :]
            force_ref[pl.ds(base, 8), :] = on_slave
            force_ref[pl.ds(base + size * 8, 8), :] = normals * (total * (-1.0 / slope))
            live = task < count
            slave_from = task_ref[0, task]
            master_from = task_ref[3, task]

            @pl.when(live & (slave_from != own))
            def _():
                for k in range(3):
                    back_ref[slave_from, pl.ds(task_ref[2, task] + k, 1), :] = on_slave[k : k + 1]

            @pl.when(live & (master_from != own))
            def _():
                back_ref[master_from, pl.ds(task_ref[5, task], 1), :] = total

        return carry

    lax.fori_loop(0, (count + TASK_STEP - 1) // TASK_STEP, tile, 0)


def near_kernel(near_ref, nodes_ref, force_ref, inner_ref, whole_ref, out_ref):
    count = near_ref[2, 0]

    def step(turn, acc):
        ids = []
        forces = []
        for k in range(BLOCK_STEP):
            valid = BLOCK_STEP * turn + k < count
            number = jnp.where(valid, BLOCK_STEP * turn + k, 0)
            ids.append(nodes_ref[pl.ds(near_ref[0, number], 1), :])
            rows = force_ref[pl.ds(pl.multiple_of(near_ref[1, number], 8), 8), :]
            rows = jnp.where(valid, rows, 0.0)
            forces.append([rows[f : f + 1] for f in range(3)])
        return acc + scatter_terms(ids, forces)

    steps = (count + BLOCK_STEP - 1) // BLOCK_STEP
    acc = lax.fori_loop(0, steps, step, jnp.zeros((6 * GROUP, LANES), F32))
    marks = force_ref[force_ref.shape[0] - 8 :, :]
    total = inner_ref[...] + fold_terms(acc)
    rows = total.shape[0]
    out_ref[:rows, :] = jnp.where(marks[0:1] > 0.0, whole_ref[...], total)
    out_ref[rows:, :] = marks


def far_kernel(
    chunks,
    grid,
    own_ref,
    entry_ref,
    back_ref,
    nodes_ref,
    normal_ref,
    near_ref,
    faces_ref,
    out_ref,
    send_ref,
    value_ref,
):
    rows = out_ref.shape[0]
    count = jnp.where(jnp.max(near_ref[rows:, :]) > 0.0, 0, entry_ref[4, 0])

    def step(turn, acc):
        ids = []
        forces = []
        for k in range(BLOCK_STEP):
            valid = BLOCK_STEP * turn + k < count
            number = jnp.where(valid, BLOCK_STEP * turn + k, 0)
            block = entry_ref[0, number]
            role = entry_ref[1, number]
            worker = entry_ref[2, number]
            first = entry_ref[3, number]
            ids.append(nodes_ref[pl.ds(block, 1), :])
            total = back_ref[worker, pl.ds(first, 1), :]
            rows = []
            for field in range(3):
                row = back_ref[worker, pl.ds(jnp.minimum(first + field, BACK_ROWS - 1), 1), :]
                row = jnp.where(role == 1, -normal_ref[field, pl.ds(block, 1), :] * total, row)
                rows.append(jnp.where(valid, row, 0.0))
            forces.append(rows)
        return acc + scatter_terms(ids, forces)

    steps = (count + BLOCK_STEP - 1) // BLOCK_STEP
    acc = lax.fori_loop(0, steps, step, jnp.zeros((6 * GROUP, LANES), F32))
    out_ref[...] = near_ref[:rows, :] + fold_terms(acc)
    send_faces(own_ref[0], grid, out_ref, chunks, faces_ref, send_ref, value_ref)


def element_kernel(conn_ref, coords_ref, disp_ref, modulus_ref, out_ref, order_ref):
    chunks = coords_ref.shape[1] // LANES
    groups = conn_ref.shape[1] // LANES
    for group in range(groups):
        order_ref[pl.ds(group * 8, 8), :] = conn_ref[:, group * LANES : (group + 1) * LANES]
    pos = []
    disp = []
    for corner in range(8):
        ids = order_ref[pl.ds(corner, groups, stride=8), :]
        found = gather_chunks(
            lambda field, chunk: (coords_ref if field < 3 else disp_ref)[
                field % 3 : field % 3 + 1, chunk * LANES : (chunk + 1) * LANES
            ],
            6,
            chunks,
            ids,
        )
        pos.append(found[:3])
        disp.append(found[3:])
    first = list(pos[0])
    pos = [[pos[corner][j] - first[j] for j in range(3)] for corner in range(8)]

    def signed(values, signs):
        total = None
        for value, sign in zip(values, signs):
            if total is None:
                total = value if sign > 0 else -value
            else:
                total = total + value if sign > 0 else total - value
        return total

    corner_signs = [[XI_SIGNS[corner][k] for corner in range(8)] for k in range(3)]
    jac = [
        [signed([pos[c][j] for c in range(8)], corner_signs[k]) * 0.125 for k in range(3)]
        for j in range(3)
    ]
    cof = [
        [
            jac[(j + 1) % 3][(k + 1) % 3] * jac[(j + 2) % 3][(k + 2) % 3]
            - jac[(j + 1) % 3][(k + 2) % 3] * jac[(j + 2) % 3][(k + 1) % 3]
            for k in range(3)
        ]
        for j in range(3)
    ]
    det = jac[0][0] * cof[0][0] + jac[0][1] * cof[0][1] + jac[0][2] * cof[0][2]
    volume = 8.0 * det
    inverse = 1.0 / volume
    scaled = [[cof[j][k] * inverse for k in range(3)] for j in range(3)]
    grad = [[signed(scaled[j], XI_SIGNS[c]) for j in range(3)] for c in range(8)]

    def summed(terms):
        total = terms[0]
        for term in terms[1:]:
            total = total + term
        return total

    ugrad = [
        [summed([disp[c][i] * grad[c][j] for c in range(8)]) for j in range(3)] for i in range(3)
    ]
    modulus = modulus_ref[...]
    dilation = ugrad[0][0] + ugrad[1][1] + ugrad[2][2]
    stress = [[modulus * (ugrad[i][j] + ugrad[j][i]) for j in range(3)] for i in range(3)]
    for i in range(3):
        stress[i][i] = stress[i][i] + modulus * dilation
    squares = summed([grad[c][j] * grad[c][j] for c in range(8) for j in range(3)])
    hour_coef = HG_COEF * modulus * volume * squares
    shapes = []
    modes = []
    for a in range(4):
        hour_pos = [signed([pos[c][j] for c in range(8)], HOUR_VEC[a]) for j in range(3)]
        gam = [
            float(HOUR_VEC[a][c]) - summed([hour_pos[j] * grad[c][j] for j in range(3)])
            for c in range(8)
        ]
        shapes.append(gam)
        modes.append(
            [hour_coef * summed([disp[c][i] * gam[c] for c in range(8)]) for i in range(3)]
        )
    flux = [[volume * stress[i][j] for j in range(3)] for i in range(3)]
    acc = jnp.zeros((6 * GROUP, LANES), F32)
    for corner in range(8):
        ids = order_ref[pl.ds(corner, groups, stride=8), :]
        force = []
        for i in range(3):
            value = summed([flux[i][j] * grad[corner][j] for j in range(3)])
            value = value + summed([modes[a][i] * shapes[a][corner] for a in range(4)])
            force.append(-value)
        for group in range(0, groups, 2):
            picks = range(group, min(group + 2, groups))
            acc = acc + scatter_terms(
                [ids[g : g + 1] for g in picks], [[f[g : g + 1] for f in force] for g in picks]
            )
    out_ref[...] = fold_terms(acc)


def around(grid):
    return [(dx, dy) for dx in (-1, 0, 1) for dy in (-1, 0, 1) if (dx, dy) != (0, 0)]


def face_toward(dx, dy):
    if dx:
        return 1 if dx > 0 else 0
    return 3 if dy > 0 else 2


def neighbour(own, grid, dx, dy):
    ix = own // grid[1] + dx
    iy = own % grid[1] + dy
    there = (ix >= 0) & (ix < grid[0]) & (iy >= 0) & (iy < grid[1])
    return there, jnp.where(there, ix * grid[1] + iy, 0)


def send_faces(own, grid, total_ref, chunks, faces_ref, send_ref, value_ref):
    value_ref[...] = jnp.zeros_like(value_ref)
    parts = faces_ref.shape[1] // LANES
    for part in range(parts):
        ids = faces_ref[:, part * LANES : (part + 1) * LANES]
        found = gather_chunks(
            lambda field, chunk: total_ref[field * GROUP + chunk : field * GROUP + chunk + 1, :],
            3,
            chunks,
            ids,
        )
        for field in range(3):
            at = field * parts + part
            for face in range(4):
                value_ref[face, at : at + 1, :] = found[field][face : face + 1]
    for dx, dy in around(grid):
        there, target = neighbour(own, grid, dx, dy)

        @pl.when(there)
        def _():
            send_ref[target] = value_ref[face_toward(dx, dy)]


def face_map_kernel(chunks, faces_ref, low_ref, high_ref, table_ref):
    parts = faces_ref.shape[1] // LANES
    acc = None
    for row in range(2):
        ids = [faces_ref[row : row + 1, p * LANES : (p + 1) * LANES] for p in range(parts)]
        zero = jnp.zeros((1, LANES), F32)
        places = [(iota((1, LANES), 1) + (p * LANES + 1)).astype(F32) for p in range(parts)]
        fields = [[place if f == row else zero for f in range(3)] for place in places]
        terms = scatter_terms(ids, fields)
        acc = terms if acc is None else acc + terms
    table_ref[...] = fold_terms(acc)
    low_ref[...] = jnp.zeros_like(low_ref)
    high_ref[...] = jnp.zeros_like(high_ref)
    for part in range(parts):
        ids = faces_ref[:, part * LANES : (part + 1) * LANES]
        found = gather_chunks(
            lambda field, chunk: table_ref[field * GROUP + chunk : field * GROUP + chunk + 1, :],
            2,
            chunks,
            ids,
        )
        for field in range(2):
            at = field * parts + part
            low_ref[at : at + 1, :] = found[field][2:3]
            high_ref[at : at + 1, :] = found[field][3:4]


def moved_faces(values, places, parts):
    results = [None] * (3 * parts)
    for part in range(parts):
        place = places[part].astype(jnp.int32) - 1
        low = jnp.broadcast_to(place & (LANES - 1), values.shape)
        got = jnp.take_along_axis(values, low, axis=1, mode="promise_in_bounds")
        for field in range(3):
            total = jnp.zeros((1, LANES), F32)
            for source in range(parts):
                at = field * parts + source
                total = jnp.where(place >> 7 == source, got[at : at + 1], total)
            results[field * parts + part] = total
    return results


def assemble_kernel(slots, back_ref, ids_ref, inner_ref, out_ref):
    devices = back_ref.shape[0]

    def step(turn, acc):
        ids = ids_ref[pl.ds(turn * slots, slots), :]
        values = back_ref[turn]
        for slot in range(0, slots, 2):
            picks = range(slot, min(slot + 2, slots))
            acc = acc + scatter_terms(
                [ids[s : s + 1] for s in picks],
                [[values[f * slots + s : f * slots + s + 1] for f in range(3)] for s in picks],
            )
        return acc

    acc = lax.fori_loop(0, devices, step, jnp.zeros((6 * GROUP, LANES), F32))
    out_ref[...] = inner_ref[...] + fold_terms(acc)


def final_kernel(
    grid, own_ref, total_ref, got_ref, low_ref, high_ref, faces_ref, velocity_ref, mass_ref, out_ref, sum_ref
):
    own = own_ref[0]
    parts = faces_ref.shape[1] // LANES

    def block(dx, dy):
        there, source = neighbour(own, grid, dx, dy)
        return jnp.where(there, got_ref[source], 0.0)

    def rows_of(values):
        return [values[at : at + 1] for at in range(3 * parts)]

    def side(dy, map_ref):
        rows = rows_of(block(0, dy))
        for field, dx in enumerate((-1, 1)):
            places = [map_ref[field * parts + p : field * parts + p + 1, :] for p in range(parts)]
            rows = [a + b for a, b in zip(rows, moved_faces(block(dx, dy), places, parts))]
        return rows

    added = [rows_of(block(-1, 0)), rows_of(block(1, 0)), side(-1, low_ref), side(1, high_ref)]
    acc = jnp.zeros((6 * GROUP, LANES), F32)
    for face, rows in enumerate(added):
        ids = [faces_ref[face : face + 1, p * LANES : (p + 1) * LANES] for p in range(parts)]
        acc = acc + scatter_terms(
            ids, [[rows[f * parts + p] for f in range(3)] for p in range(parts)]
        )
    sum_ref[...] = total_ref[...] + fold_terms(acc)
    for chunk in range(out_ref.shape[1] // LANES):
        span = slice(chunk * LANES, (chunk + 1) * LANES)
        scale = TIME_STEP / mass_ref[chunk : chunk + 1, :]
        for field in range(3):
            row = field * GROUP + chunk
            out_ref[field : field + 1, span] = (
                velocity_ref[field : field + 1, span] + scale * sum_ref[row : row + 1, :]
            )


def call(kernel, outs, in_smem, args, scratch=(), out_smem=()):
    def spec(smem):
        return pl.BlockSpec(memory_space=pltpu.SMEM if smem else pltpu.VMEM)

    return pl.pallas_call(
        kernel,
        out_shape=[jax.ShapeDtypeStruct(shape, dtype) for shape, dtype in outs],
        in_specs=[spec(i in in_smem) for i in range(len(args))],
        out_specs=[spec(i in out_smem) for i in range(len(outs))],
        scratch_shapes=list(scratch),
        compiler_params=pltpu.CompilerParams(vmem_limit_bytes=VMEM_LIMIT),
    )(*args)


def exchange(low, high, axis):
    count = lax.axis_size(axis)
    forward = [(i, i + 1) for i in range(count - 1)]
    backward = [(target, source) for source, target in forward]
    return lax.ppermute(high, axis, forward), lax.ppermute(low, axis, backward)


def local(
    connectivity,
    face_nodes,
    coords,
    displacement,
    velocity,
    node_mass,
    modulus,
    surf_nodes,
    surf_ref,
    surf_angles,
    owner_map,
    pair_blocks,
    pair_masks,
    pair_count,
):
    axes = ("gx", "gy")
    devices = lax.axis_size("gx") * lax.axis_size("gy")
    per_dev = surf_nodes.shape[0]
    rows_per = per_dev // LANES
    node_count = coords.shape[1]
    chunks = node_count // LANES
    slots = 2 * per_dev // devices
    pairs = pair_blocks.shape[1]
    own = lax.axis_index(axes).reshape(1).astype(jnp.int32)
    owners = owner_map.reshape(devices * rows_per, LANES)
    face_pad = -face_nodes.shape[1] % LANES
    faces = jnp.pad(face_nodes, ((0, 4), (0, face_pad)), constant_values=-1)
    parts = faces.shape[1] // LANES
    face_rows = -(-3 * parts // 8) * 8
    total_shape = ((3 * GROUP, LANES), F32)
    face_shape = ((face_rows, LANES), F32)
    send_shape = ((devices, face_rows, LANES), F32)
    grid = (lax.axis_size("gx"), lax.axis_size("gy"))

    def to_all(values):
        return lax.all_to_all(values, axes, split_axis=0, concat_axis=0, tiled=True)

    [request] = call(
        functools.partial(request_kernel, rows_per),
        [((devices, REQUEST_ROWS, LANES), jnp.int32)],
        (0, 1),
        (own, pair_count, owners, pair_blocks, pair_masks),
    )
    asked = to_all(request)
    own_owners = lax.dynamic_slice_in_dim(owner_map, own[0] * per_dev, per_dev)
    pos, normals, block_of = call(
        functools.partial(segment_kernel, slots),
        [
            ((3, per_dev, LANES), F32),
            ((3, per_dev, LANES), F32),
            ((devices * slots,), jnp.int32),
        ],
        (0,),
        (own_owners, displacement, surf_nodes, surf_ref, surf_angles),
        [pltpu.SMEM((devices,), jnp.int32)],
        (2,),
    )
    [internal] = call(
        element_kernel,
        [total_shape],
        (),
        (connectivity, coords, displacement, modulus.reshape(-1, LANES)),
        [pltpu.VMEM((connectivity.shape[1] // LANES * 8, LANES), jnp.int32)],
    )
    map_low, map_high = call(
        functools.partial(face_map_kernel, chunks),
        [face_shape, face_shape],
        (),
        (faces,),
        [pltpu.VMEM((3 * GROUP, LANES), F32)],
    )
    map_low, map_high = exchange(map_low, map_high, "gy")
    lists = asked[:, 0, :]
    outbound, entries = call(
        functools.partial(plan_kernel, slots),
        [((devices, SEND_ROWS, LANES), F32), ((8, ENTRIES), jnp.int32)],
        (0, 1),
        (lists, block_of, pos, surf_angles),
        [pltpu.SMEM((2, devices), jnp.int32)],
        (1,),
    )
    tasks, near_list, fields = call(
        functools.partial(table_kernel, slots),
        [((8, TASKS), jnp.int32), ((8, 2 * TASKS), jnp.int32), ((10, TASKS, LANES), F32)],
        (0, 1, 2),
        (own, lists, block_of, asked, pos, surf_angles),
        [pltpu.SMEM((2, devices), jnp.int32)],
        (0, 1),
    )
    inbound = to_all(outbound)
    inbound, map_low, map_high = lax.optimization_barrier((inbound, map_low, map_high))
    back, forces, over = call(
        work_kernel,
        [
            ((devices, BACK_ROWS, LANES), F32),
            ((2 * TASKS * 8 + 8, LANES), F32),
            ((1,), jnp.int32),
        ],
        (0, 1),
        (own, tasks, inbound, fields),
        [
            pltpu.VMEM((10, TASKS, LANES), F32),
            pltpu.VMEM((3, TASKS * 8, LANES), F32),
            pltpu.VMEM((3, TASKS * 8, LANES), F32),
            pltpu.VMEM((3, TASKS * 8, LANES), F32),
            pltpu.VMEM((2, TASKS * 8, LANES), F32),
        ],
        (2,),
    )
    returned = to_all(back)

    def by_owners():
        [index] = call(
            functools.partial(routing_kernel, rows_per),
            [((4, pairs), jnp.int32)],
            (0, 1),
            (own, pair_count, owners, pair_blocks),
        )
        outbound, ids = call(
            functools.partial(pack_kernel, slots, rows_per),
            [((devices, 5 * slots, LANES), F32), ((devices * slots, LANES), jnp.int32)],
            (0,),
            (own, owners, pos, surf_angles, surf_nodes),
        )
        [forces] = call(
            functools.partial(pair_kernel, slots),
            [((devices, 3 * slots, LANES), F32)],
            (0, 1),
            (index, pair_count, to_all(outbound), pair_masks),
            [pltpu.VMEM((pairs * 8, LANES), F32)] * 4,
        )
        return call(
            functools.partial(assemble_kernel, slots),
            [total_shape],
            (),
            (to_all(forces), ids, internal),
        )[0]

    whole = lax.cond(over[0] > 0, by_owners, lambda: internal)
    [near] = call(
        near_kernel,
        [((3 * GROUP + 8, LANES), F32)],
        (0,),
        (near_list, surf_nodes, forces, internal, whole),
    )
    total, send = call(
        functools.partial(far_kernel, chunks, grid),
        [total_shape, send_shape],
        (0, 1),
        (own, entries, returned, surf_nodes, normals, near, faces),
        [pltpu.VMEM((4,) + face_shape[0], F32)],
    )
    [result] = call(
        functools.partial(final_kernel, grid),
        [((3, node_count), F32)],
        (0,),
        (
            own,
            total,
            to_all(send),
            map_low,
            map_high,
            faces,
            velocity,
            node_mass.reshape(chunks, LANES),
        ),
        [pltpu.VMEM((3 * GROUP, LANES), F32)],
    )
    return result


def solution(mesh):
    in_specs = (
        P(None, ("gx", "gy")),
        P(None, ("gx", "gy")),
        P(None, ("gx", "gy")),
        P(None, ("gx", "gy")),
        P(None, ("gx", "gy")),
        P(("gx", "gy")),
        P(("gx", "gy")),
        P(("gx", "gy"), None),
        P(("gx", "gy"), None, None),
        P(("gx", "gy"), None, None),
        P(),
        P(None, ("gx", "gy")),
        P(None, ("gx", "gy"), None),
        P(("gx", "gy")),
    )
    out_specs = P(None, ("gx", "gy"))
    return jax.shard_map(local, mesh=mesh, in_specs=in_specs, out_specs=out_specs, check_vma=False)
```

```python
import functools

import jax
import jax.numpy as jnp
from jax import lax
from jax.experimental import pallas as pl
from jax.experimental.pallas import tpu as pltpu
from jax.sharding import PartitionSpec as P

XI_SIGNS = [
    [-1, -1, -1],
    [1, -1, -1],
    [1, 1, -1],
    [-1, 1, -1],
    [-1, -1, 1],
    [1, -1, 1],
    [1, 1, 1],
    [-1, 1, 1],
]
HOUR_VEC = [
    [1, 1, -1, -1, -1, -1, 1, 1],
    [1, -1, -1, 1, -1, 1, 1, -1],
    [1, -1, 1, -1, 1, -1, 1, -1],
    [-1, 1, -1, 1, 1, -1, 1, -1],
]
HG_COEF = 0.05
PEN_STIFF = 0.05
PEN_DEPTH = 0.5
TIME_STEP = 0.2
LANES = 128
GROUP = 16
F32 = jnp.float32
BF16 = jnp.bfloat16
VMEM_LIMIT = 48 * 1024 * 1024
REQUEST_ROWS = 8
TASK_CAP = 3
OWN_CAP = 12
TASK_LANE = 64
TASK_FIELDS = 5
ENTRY_LANE = 4
ENTRY_CAP = 20
SEND_ROWS = 32
BACK_ROWS = 10
ENTRIES = 160
TASKS = 48
TASK_STEP = 8
BLOCK_STEP = 8


def iota(shape, dim):
    return lax.broadcasted_iota(jnp.int32, shape, dim)


def dot_nn(a, b):
    return lax.dot_general(a, b, (((1,), (0,)), ((), ())), preferred_element_type=F32)


def dot_nt(a, b):
    return lax.dot_general(a, b, (((1,), (1,)), ((), ())), preferred_element_type=F32)


def dot_tn(a, b):
    return lax.dot_general(a, b, (((0,), (0,)), ((), ())), preferred_element_type=F32)


def as_bf16(mask):
    return jnp.where(mask, 1.0, 0.0).astype(BF16)


def split2(x):
    high = x.astype(BF16)
    return high, (x - high.astype(F32)).astype(BF16)


def split3(x):
    high = x.astype(BF16)
    rest = x - high.astype(F32)
    mid = rest.astype(BF16)
    return high, mid, (rest - mid.astype(F32)).astype(BF16)


def span_of(row):
    return pl.ds(pl.multiple_of(row * LANES, LANES), LANES)


def strict_upper(size):
    return as_bf16(iota((size, size), 0) < iota((size, size), 1))


def take_lanes(row, index):
    table = jnp.broadcast_to(row, index.shape)
    return jnp.take_along_axis(table, index, axis=1, mode="promise_in_bounds")


def gather_chunks(rows_of, fields, chunks, ids):
    high = ids >> 7
    low = ids & (LANES - 1)
    found = [jnp.zeros(ids.shape, F32) for _ in range(fields)]
    for chunk in range(chunks):
        here = high == chunk
        for field in range(fields):
            found[field] = jnp.where(here, take_lanes(rows_of(field, chunk), low), found[field])
    return found


def scatter_terms(id_rows, force_rows):
    wide = []
    table = []
    for ids, forces in zip(id_rows, force_rows):
        here = jnp.broadcast_to(ids >> 7, (GROUP, LANES)) == iota((GROUP, LANES), 0)
        wide.append(
            jnp.concatenate(
                [jnp.where(here, jnp.broadcast_to(f, (GROUP, LANES)), 0.0) for f in forces], axis=0
            )
        )
        low = jnp.broadcast_to(ids & (LANES - 1), (LANES, LANES))
        table.append(as_bf16(low == iota((LANES, LANES), 0)))
    high, rest = split2(jnp.concatenate(wide, axis=1))
    both = jnp.concatenate([high, rest], axis=0)
    return dot_nt(both, jnp.concatenate(table, axis=1))


def fold_terms(acc):
    half = acc.shape[0] // 2
    return acc[:half] + acc[half:]


def routing_kernel(rows_per, own_ref, count_ref, map_ref, pairs_ref, index_ref):
    own = own_ref[0]
    rows = map_ref.shape[0]
    devices = rows // rows_per
    pairs = pairs_ref.shape[1]
    hit = as_bf16(map_ref[...] == own)
    source_of = iota((devices, rows), 1) // rows_per
    upto = as_bf16(source_of <= iota((devices, rows), 0))
    within = as_bf16(source_of == iota((devices, rows), 0))
    ends = jnp.sum(dot_nn(upto, hit), axis=1, keepdims=True)
    counts = jnp.sum(dot_nn(within, hit), axis=1, keepdims=True)
    ranks = pairs_ref[...].astype(F32)
    for side in range(2):
        rank = ranks[side : side + 1]
        below = jnp.broadcast_to(ends, (devices, pairs)) <= rank
        source = jnp.sum(jnp.where(below, 1.0, 0.0), axis=0, keepdims=True)
        source = jnp.minimum(source, devices - 1.0)
        start = jnp.sum(jnp.where(below, counts, 0.0), axis=0, keepdims=True)
        index_ref[2 * side : 2 * side + 1, :] = source.astype(jnp.int32)
        index_ref[2 * side + 1 : 2 * side + 2, :] = (rank - start).astype(jnp.int32)


def request_kernel(rows_per, own_ref, count_ref, map_ref, pairs_ref, masks_ref, out_ref):
    own = own_ref[0]
    rows = map_ref.shape[0]
    devices = rows // rows_per
    pairs = pairs_ref.shape[1]
    hit = as_bf16(map_ref[...] == own)
    source_of = iota((devices, rows), 1) // rows_per
    upto = as_bf16(source_of <= iota((devices, rows), 0))
    within = as_bf16(source_of == iota((devices, rows), 0))
    ends = jnp.sum(dot_nn(upto, hit), axis=1, keepdims=True)
    counts = jnp.sum(dot_nn(within, hit), axis=1, keepdims=True)
    ranks = pairs_ref[...].astype(F32)
    where_is = []
    for side in range(2):
        rank = ranks[side : side + 1]
        below = jnp.broadcast_to(ends, (devices, pairs)) <= rank
        source = jnp.sum(jnp.where(below, 1.0, 0.0), axis=0, keepdims=True)
        source = jnp.minimum(source, devices - 1.0)
        start = jnp.sum(jnp.where(below, counts, 0.0), axis=0, keepdims=True)
        where_is.append((source, rank - start))
    (slave, slave_rank), (master, master_rank) = where_is
    lane = iota((1, pairs), 1)
    live = lane < count_ref[0]
    me = own.astype(F32)
    device = iota((devices, pairs), 0).astype(F32)
    earlier = strict_upper(pairs)

    def pick(target, keep):
        return jnp.where((device == target) & keep, 1.0, 0.0)

    def turns(worker):
        tasks = pick(worker, live)
        ahead = dot_nn(tasks.astype(BF16), earlier)
        return tasks, jnp.sum(tasks * ahead, axis=0, keepdims=True)

    worker = jnp.where(lane == 0, me, slave)
    for other in (master, me):
        tasks, turn = turns(worker)
        worker = jnp.where((turn >= TASK_CAP) & (worker != me), other, worker)
    tasks, turn = turns(worker)
    room = turn < jnp.where(worker == me, float(OWN_CAP), float(TASK_CAP))
    send_slave = live & (slave != worker)
    send_master = live & (master != worker)
    from_slave = pick(slave, send_slave)
    from_master = pick(master, send_master)
    both = from_slave + from_master
    ahead = dot_nn(both.astype(BF16), earlier)
    slave_at = jnp.sum(from_slave * ahead, axis=0, keepdims=True)
    master_at = jnp.sum(from_master * ahead, axis=0, keepdims=True)
    master_at = master_at + jnp.where(send_slave & (slave == master), 1.0, 0.0)

    column = iota((LANES, pairs), 0).astype(F32)

    def placed(first, fields, fits):
        total = jnp.zeros((LANES, pairs), F32)
        for at, field in enumerate(fields):
            total = jnp.where((column == first + at) & fits, field, total)
        return total.astype(BF16)

    zero = jnp.zeros_like(slave)
    entry = placed(ENTRY_LANE + 3 * slave_at, (zero, slave_rank, worker), slave_at < ENTRY_CAP)
    line = dot_nt(from_slave.astype(BF16), entry)
    entry = placed(
        ENTRY_LANE + 3 * master_at, (zero + 1.0, master_rank, worker), master_at < ENTRY_CAP
    )
    line = line + dot_nt(from_master.astype(BF16), entry)
    entry = placed(
        TASK_LANE + TASK_FIELDS * turn,
        (slave, slave_rank, master, master_rank, lane.astype(F32)),
        room,
    )
    line = line + dot_nt(tasks.astype(BF16), entry)
    entry_count = jnp.sum(both, axis=1, keepdims=True)
    task_count = jnp.sum(tasks, axis=1, keepdims=True)
    limit = jnp.where(iota((devices, 1), 0) == own, float(OWN_CAP), float(TASK_CAP))
    over = jnp.where((entry_count > ENTRY_CAP) | (task_count > limit), 1.0, 0.0)
    over = jnp.max(over, axis=0, keepdims=True)
    spot = iota((devices, LANES), 1)
    line = jnp.where(spot == 0, entry_count, line)
    line = jnp.where(spot == 1, task_count, line)
    line = jnp.where(spot == 2, over, line)
    out_ref[:, 0, :] = line.astype(jnp.int32)
    chosen = [jnp.where(turn == t, tasks, 0.0) for t in range(TASK_CAP)]
    chosen = jnp.concatenate(chosen, axis=0).astype(BF16)
    masks = jnp.concatenate([masks_ref[0], masks_ref[1]], axis=1).astype(F32).astype(BF16)
    got = dot_nn(chosen, masks).astype(jnp.int32)
    for t in range(TASK_CAP):
        part = got[t * devices : (t + 1) * devices]
        out_ref[:, 1 + 2 * t, :] = part[:, :LANES]
        out_ref[:, 2 + 2 * t, :] = part[:, LANES:]
    for row in range(1 + 2 * TASK_CAP, REQUEST_ROWS):
        out_ref[:, row, :] = jnp.zeros((devices, LANES), jnp.int32)


def segment_kernel(
    cap,
    rows_per,
    own_ref,
    map_ref,
    disp_ref,
    nodes_ref,
    ref_ref,
    pos_ref,
    block_ref,
    group_ref,
    sem,
):
    chunks = disp_ref.shape[1] // LANES
    first = own_ref[0] * rows_per
    start = pl.multiple_of(first // 8 * 8, 8)
    move = pltpu.make_async_copy(map_ref.at[pl.ds(start, 8), :], group_ref, sem)
    move.start()

    def step(turn, carry):
        base = pl.multiple_of(turn * 8, 8)
        ids = nodes_ref[pl.ds(base, 8), :]
        found = gather_chunks(
            lambda field, chunk: disp_ref[field : field + 1, chunk * LANES : (chunk + 1) * LANES],
            3,
            chunks,
            ids,
        )
        for field in range(3):
            pos_ref[field, pl.ds(base, 8), :] = found[field] + ref_ref[field, pl.ds(base, 8), :]
        return carry

    lax.fori_loop(0, nodes_ref.shape[0] // 8, step, 0, unroll=2)
    move.wait()
    owner = jnp.concatenate(
        [group_ref[pl.ds(first - start + i, 1), :] for i in range(rows_per)], axis=1
    )
    blocks = owner.shape[1]
    total = block_ref.shape[0] * LANES
    mine = iota((total // cap, blocks), 0) == owner
    before = dot_nn(as_bf16(mine), strict_upper(blocks))
    rank = jnp.sum(jnp.where(mine, before, 0.0), axis=0, keepdims=True).astype(jnp.int32)
    hit = as_bf16(iota((total, blocks), 0) == owner * cap + rank)
    high, rest = split2(iota((8, blocks), 1).astype(F32))
    table = (dot_nt(high, hit) + dot_nt(rest, hit)).astype(jnp.int32)
    for row in range(total // LANES):
        block_ref[row : row + 1, :] = table[0:1, row * LANES : (row + 1) * LANES]


def block_at(block_ref, slot):
    return block_ref[slot >> 7, slot & (LANES - 1)]


def plan_kernel(cap, list_ref, block_ref, pos_ref, angles_ref, out_ref, entry_ref, used_ref):
    devices = list_ref.shape[0]

    def clear(device, carry):
        used_ref[0, device] = 0
        used_ref[1, device] = 0
        return carry

    lax.fori_loop(0, devices, clear, 0)

    def from_owner(owner, carry):
        def entry(turn, state):
            number, over = state
            at = ENTRY_LANE + 3 * turn
            role = list_ref[owner, at]
            block = block_at(block_ref, owner * cap + list_ref[owner, at + 1])
            worker = list_ref[owner, at + 2]
            first = used_ref[0, worker]
            back = used_ref[1, worker]
            after = first + 3 + 2 * role
            back_after = back + 3 - 2 * role
            used_ref[0, worker] = after
            used_ref[1, worker] = back_after
            fits = (after < SEND_ROWS) & (back_after <= BACK_ROWS) & (number < ENTRIES)

            @pl.when(fits)
            def _():
                for field in range(3):
                    out_ref[worker, pl.ds(first + field, 1), :] = pos_ref[field, pl.ds(block, 1), :]
                entry_ref[0, number] = block
                entry_ref[1, number] = role
                entry_ref[2, number] = worker
                entry_ref[3, number] = back

            @pl.when(fits & (role == 1))
            def _():
                out_ref[worker, pl.ds(first + 3, 2), :] = angles_ref[block]

            return (number + 1, jnp.where(fits, over, 1))

        entries, tasks, over = carry
        over = jnp.maximum(over, list_ref[owner, 2])
        entries, over = lax.fori_loop(
            0, jnp.minimum(list_ref[owner, 0], ENTRY_CAP), entry, (entries, over)
        )
        return (entries, tasks + list_ref[owner, 1], over)

    zero = jnp.int32(0)
    entries, tasks, over = lax.fori_loop(0, devices, from_owner, (zero, zero, zero))
    over = jnp.where(tasks > TASKS, 1, over)
    entry_ref[4, 0] = jnp.minimum(entries, ENTRIES)
    mark = jnp.full((devices, LANES), over.astype(F32), F32)
    out_ref[:, SEND_ROWS - 1, :] = mark


def table_kernel(
    cap,
    own_ref,
    list_ref,
    block_ref,
    request_ref,
    masks_ref,
    pos_ref,
    angles_ref,
    task_ref,
    near_ref,
    field_ref,
    used_ref,
):
    own = own_ref[0]
    devices = list_ref.shape[0]
    size = field_ref.shape[1]

    def clear(device, carry):
        used_ref[0, device] = 0
        used_ref[1, device] = 0
        return carry

    lax.fori_loop(0, devices, clear, 0)

    def from_owner(owner, carry):
        def task(turn, state):
            at = TASK_LANE + TASK_FIELDS * turn
            pair = list_ref[owner, at + 4]
            number, near = state
            for side in range(2):
                source = list_ref[owner, at + 2 * side]
                here = source == own
                block = block_at(block_ref, owner * cap + list_ref[owner, at + 2 * side + 1])
                used = used_ref[0, source]
                back = used_ref[1, source]
                used_ref[0, source] = jnp.where(here, used, used + 3 + 2 * side)
                used_ref[1, source] = jnp.where(here, back, back + 3 - 2 * side)
                task_ref[3 * side, number] = source
                task_ref[3 * side + 1, number] = jnp.where(here, block, jnp.minimum(used, SEND_ROWS - 5))
                task_ref[3 * side + 2, number] = back
                base = 4 * side

                @pl.when(owner == own)
                def _():
                    mask = masks_ref[side, pl.ds(pair, 1), :]
                    field_ref[base + 3, pl.ds(number, 1), :] = mask.astype(F32)

                @pl.when(owner != own)
                def _():
                    mask = request_ref[owner, pl.ds(1 + 2 * turn + side, 1), :]
                    field_ref[base + 3, pl.ds(number, 1), :] = mask.astype(F32)

                spot = near

                @pl.when(here)
                def _():
                    near_ref[0, spot] = block
                    near_ref[1, spot] = (side * size + number) * 8
                    for field in range(3):
                        field_ref[base + field, pl.ds(number, 1), :] = pos_ref[
                            field, pl.ds(block, 1), :
                        ]
                    if side == 1:
                        both = angles_ref[block]
                        field_ref[8, pl.ds(number, 1), :] = both[0:1]
                        field_ref[9, pl.ds(number, 1), :] = both[1:2]

                near = near + jnp.where(here, 1, 0)
            return (number + 1, near)

        number, near = carry
        count = jnp.minimum(list_ref[owner, 1], jnp.where(owner == own, OWN_CAP, TASK_CAP))
        count = jnp.minimum(count, TASKS - number)
        return lax.fori_loop(0, count, task, (number, near))

    tasks, near = lax.fori_loop(0, devices, from_owner, (jnp.int32(0), jnp.int32(0)))
    task_ref[6, 0] = tasks
    near_ref[2, 0] = near


def pack_kernel(slots, rows_per, own_ref, map_ref, pos_ref, angles_ref, nodes_ref, out_ref, ids_ref):
    own = own_ref[0]
    devices = map_ref.shape[0] // rows_per
    owner = jnp.concatenate(
        [map_ref[pl.ds(own * rows_per + i, 1), :] for i in range(rows_per)], axis=1
    )
    blocks = owner.shape[1]
    mine = iota((devices, blocks), 0) == owner
    before = dot_nn(as_bf16(mine), strict_upper(blocks))
    rank = jnp.sum(jnp.where(mine, before, 0.0), axis=0, keepdims=True).astype(jnp.int32)
    place = owner * slots + rank
    move = as_bf16(iota((devices * slots, blocks), 0) == place)
    for field in range(5):
        values = pos_ref[field] if field < 3 else angles_ref[:, field - 3, :]
        moved = dot_nn(move, jnp.concatenate(split3(values), axis=1))
        moved = moved[:, :LANES] + moved[:, LANES : 2 * LANES] + moved[:, 2 * LANES :]
        out_ref[:, field * slots : (field + 1) * slots, :] = moved.reshape(devices, slots, LANES)
    nodes = nodes_ref[...]
    halves = jnp.concatenate(
        [(nodes >> 7).astype(F32).astype(BF16), (nodes & (LANES - 1)).astype(F32).astype(BF16)],
        axis=1,
    )
    moved = dot_nn(move, halves)
    ids_ref[...] = (moved[:, :LANES] * LANES + moved[:, LANES:]).astype(jnp.int32)


def sine_cosine(angle):
    half = 0.5 * angle
    sq = half * half
    sine = sq * (-1.0 / 39916800.0) + 1.0 / 362880.0
    for coef in (-1.0 / 5040.0, 1.0 / 120.0, -1.0 / 6.0, 1.0):
        sine = sine * sq + coef
    sine = sine * half
    cosine = sq * (1.0 / 479001600.0) - 1.0 / 3628800.0
    for coef in (1.0 / 40320.0, -1.0 / 720.0, 1.0 / 24.0, -0.5, 1.0):
        cosine = cosine * sq + coef
    return 2.0 * sine * cosine, 1.0 - 2.0 * sine * sine


def pair_kernel(
    slots, index_ref, count_ref, in_ref, masks_ref, out_ref, slave_ref, master_ref, sin_ref, cos_ref
):
    pairs = masks_ref.shape[1]
    count = jnp.minimum(count_ref[0], pairs)
    out_ref[...] = jnp.zeros_like(out_ref)

    def stage(pair, carry):
        source = index_ref[0, pair]
        slot = index_ref[1, pair]
        for field in range(3):
            slave_ref[pl.ds(pair * 8 + field, 1), :] = in_ref[source, pl.ds(field * slots + slot, 1), :]
        slave_ref[pl.ds(pair * 8 + 3, 1), :] = masks_ref[0, pl.ds(pair, 1), :].astype(F32)
        source = index_ref[2, pair]
        slot = index_ref[3, pair]
        for field in range(5):
            master_ref[pl.ds(pair * 8 + field, 1), :] = in_ref[source, pl.ds(field * slots + slot, 1), :]
        master_ref[pl.ds(pair * 8 + 5, 1), :] = masks_ref[1, pl.ds(pair, 1), :].astype(F32)
        return carry

    lax.fori_loop(0, count, stage, 0)
    sines, cosines = sine_cosine(master_ref[...])
    sin_ref[...] = sines
    cos_ref[...] = cosines

    def tile(pair, carry):
        base = pl.multiple_of(pair * 8, 8)
        slave = slave_ref[pl.ds(base, 8), :]
        columns = jnp.transpose(slave)
        master = master_ref[pl.ds(base, 8), :]
        sin_az = sin_ref[pl.ds(base + 3, 1), :]
        sin_pol = sin_ref[pl.ds(base + 4, 1), :]
        cos_az = cos_ref[pl.ds(base + 3, 1), :]
        cos_pol = cos_ref[pl.ds(base + 4, 1), :]
        normal = [cos_az * cos_pol, sin_az * cos_pol, sin_pol]
        shape = (LANES, LANES)
        dist = [
            jnp.broadcast_to(columns[:, k : k + 1], shape) - jnp.broadcast_to(master[k : k + 1], shape)
            for k in range(3)
        ]
        gap = dist[0] * normal[0] + dist[1] * normal[1] + dist[2] * normal[2]
        tang = dist[0] * dist[0] + dist[1] * dist[1] + dist[2] * dist[2] - gap * gap
        bend = gap * (-1.0 / PEN_DEPTH)
        soft = jnp.maximum(bend, 0.0) + jnp.log(1.0 + jnp.exp(-jnp.abs(bend)))
        press = soft * jnp.exp(-0.5 * tang)
        press = press * jnp.broadcast_to(columns[:, 3:4], shape)
        total = jnp.sum(press, axis=0, keepdims=True)
        scale = PEN_STIFF * PEN_DEPTH * master[5:6]
        push = [n * scale for n in normal]
        rows = jnp.concatenate(push + [jnp.zeros((5, LANES), F32)], axis=0)
        push_high, push_rest = split2(rows)
        both = jnp.concatenate([push_high, push_rest], axis=0)
        high, rest = split2(press)
        got = dot_nt(both, high) + dot_nt(both, rest)
        on_slave = got[0:8] + got[8:16]
        source = index_ref[0, pair]
        slot = index_ref[1, pair]
        for k in range(3):
            at = pl.ds(k * slots + slot, 1)
            out_ref[source, at, :] = out_ref[source, at, :] + on_slave[k : k + 1]
        source = index_ref[2, pair]
        slot = index_ref[3, pair]
        for k in range(3):
            at = pl.ds(k * slots + slot, 1)
            out_ref[source, at, :] = out_ref[source, at, :] - push[k] * total
        return carry

    lax.fori_loop(0, count, tile, 0)


def work_kernel(
    own_ref,
    task_ref,
    in_ref,
    start_ref,
    back_ref,
    force_ref,
    over_ref,
    field_ref,
    left_ref,
    gap_ref,
    far_ref,
    push_ref,
):
    own = own_ref[0]
    count = task_ref[6, 0]
    field_ref[...] = start_ref[...]
    over = jnp.max(in_ref[:, SEND_ROWS - 1, :])
    over_ref[0] = over.astype(jnp.int32)
    marks = force_ref.shape[0] - 8
    force_ref[marks:, :] = jnp.full((8, LANES), over, F32)

    def stage(task, carry):
        for side in range(2):
            source = task_ref[3 * side, task]
            first = task_ref[3 * side + 1, task]

            @pl.when(source != own)
            def _():
                for field in range(3):
                    field_ref[4 * side + field, pl.ds(task, 1), :] = in_ref[
                        source, pl.ds(first + field, 1), :
                    ]
                if side == 1:
                    for field in range(2):
                        field_ref[8 + field, pl.ds(task, 1), :] = in_ref[
                            source, pl.ds(first + 3 + field, 1), :
                        ]

        return carry

    lax.fori_loop(0, count, stage, 0)
    size = field_ref.shape[1]
    slave = [field_ref[k] for k in range(3)]
    master = [field_ref[4 + k] for k in range(3)]
    sin_az, cos_az = sine_cosine(field_ref[8])
    sin_pol, cos_pol = sine_cosine(field_ref[9])
    normal = [cos_az * cos_pol, sin_az * cos_pol, sin_pol]

    def inner(a, b):
        return a[0] * b[0] + a[1] * b[1] + a[2] * b[2]

    zero = jnp.zeros_like(sin_pol)
    one = zero + 1.0
    slope = -1.0 / PEN_DEPTH
    hidden = 30000.0
    slave_bias = -0.5 * inner(slave, slave) - hidden * (1.0 - field_ref[3])
    master_bias = -0.5 * inner(master, master) - hidden * (1.0 - field_ref[7])
    stacks = (
        (left_ref, slave + [one, slave_bias]),
        (gap_ref, [slope * n for n in normal] + [-slope * inner(normal, master), zero]),
        (far_ref, master + [master_bias, one]),
        (push_ref, [PEN_STIFF * PEN_DEPTH * n for n in normal] + [zero, zero]),
    )
    for ref, rows in stacks:
        for row, value in enumerate(rows + [zero] * 3):
            parts = split3(value)
            for part in range(ref.shape[0]):
                ref[part, pl.ds(row, size, stride=8), :] = parts[part].astype(F32)

    def tile(step, carry):
        tasks = [TASK_STEP * step + k for k in range(TASK_STEP)]
        bases = [pl.multiple_of(task * 8, 8) for task in tasks]
        fields = []
        for base in bases:
            high, mid, low = [left_ref[p, pl.ds(base, 8), :] for p in range(3)]
            left = jnp.concatenate([high, high, mid, mid, high, low], axis=0).astype(BF16)
            sides = []
            for ref in (gap_ref, far_ref):
                high, mid, low = [ref[p, pl.ds(base, 8), :] for p in range(3)]
                sides.append(jnp.concatenate([high, mid, high, mid, low, high], axis=0))
            fields.append(dot_tn(left, jnp.concatenate(sides, axis=1).astype(BF16)))
        presses = []
        for field in fields:
            bend = field[:, :LANES]
            power = field[:, LANES:] + bend * bend * (0.5 * PEN_DEPTH * PEN_DEPTH)
            soft = jnp.maximum(bend, 0.0) + jnp.log(1.0 + jnp.exp(-jnp.abs(bend)))
            presses.append(soft * jnp.exp(power))
        results = []
        for base, press in zip(bases, presses):
            push = jnp.concatenate([push_ref[p, pl.ds(base, 8), :] for p in range(2)], axis=0)
            push = push.astype(BF16)
            got = dot_nt(
                jnp.concatenate([push, push], axis=1), jnp.concatenate(split2(press), axis=1)
            )
            total = jnp.sum(press, axis=0, keepdims=True)
            results.append((got[0:8] + got[8:16], total * (PEN_STIFF * PEN_DEPTH)))
        for task, base, (on_slave, total) in zip(tasks, bases, results):
            normals = gap_ref[0, pl.ds(base, 8), :] + gap_ref[1, pl.ds(base, 8), :]
            normals = normals + gap_ref[2, pl.ds(base, 8), :]
            force_ref[pl.ds(base, 8), :] = on_slave
            force_ref[pl.ds(base + size * 8, 8), :] = normals * (total * (-1.0 / slope))
            live = task < count
            slave_from = task_ref[0, task]
            master_from = task_ref[3, task]

            @pl.when(live & (slave_from != own))
            def _():
                for k in range(3):
                    back_ref[slave_from, :, span_of(task_ref[2, task] + k)] = on_slave[k : k + 1]

            @pl.when(live & (master_from != own))
            def _():
                back_ref[master_from, :, span_of(task_ref[5, task])] = total

        return carry

    lax.fori_loop(0, (count + TASK_STEP - 1) // TASK_STEP, tile, 0)


def near_kernel(
    near_ref, nodes_ref, force_ref, inner_ref, whole_ref, angles_ref, out_ref, normal_ref
):
    count = near_ref[2, 0]

    def step(turn, acc):
        ids = []
        forces = []
        for k in range(BLOCK_STEP):
            valid = BLOCK_STEP * turn + k < count
            number = jnp.where(valid, BLOCK_STEP * turn + k, 0)
            ids.append(nodes_ref[pl.ds(near_ref[0, number], 1), :])
            rows = force_ref[pl.ds(pl.multiple_of(near_ref[1, number], 8), 8), :]
            rows = jnp.where(valid, rows, 0.0)
            forces.append([rows[f : f + 1] for f in range(3)])
        return acc + scatter_terms(ids, forces)

    steps = (count + BLOCK_STEP - 1) // BLOCK_STEP
    acc = lax.fori_loop(0, steps, step, jnp.zeros((6 * GROUP, LANES), F32))
    marks = force_ref[force_ref.shape[0] - 8 :, :]
    total = inner_ref[...] + fold_terms(acc)
    rows = total.shape[0]
    out_ref[:rows, :] = jnp.where(marks[0:1] > 0.0, whole_ref[...], total)
    out_ref[rows:, :] = marks

    def turn_angles(turn, carry):
        at = pl.ds(pl.multiple_of(turn * 8, 8), 8)
        sin_az, cos_az = sine_cosine(angles_ref[at, 0, :])
        sin_pol, cos_pol = sine_cosine(angles_ref[at, 1, :])
        normal_ref[0, at, :] = cos_az * cos_pol
        normal_ref[1, at, :] = sin_az * cos_pol
        normal_ref[2, at, :] = sin_pol
        return carry

    lax.fori_loop(0, nodes_ref.shape[0] // 8, turn_angles, 0, unroll=4)


def far_kernel(
    chunks,
    grid,
    own_ref,
    entry_ref,
    back_ref,
    nodes_ref,
    normal_ref,
    near_ref,
    faces_ref,
    out_ref,
    send_ref,
    value_ref,
):
    rows = out_ref.shape[0]
    count = jnp.where(jnp.max(near_ref[rows:, :]) > 0.0, 0, entry_ref[4, 0])

    def step(turn, acc):
        ids = []
        forces = []
        for k in range(BLOCK_STEP):
            valid = BLOCK_STEP * turn + k < count
            number = jnp.where(valid, BLOCK_STEP * turn + k, 0)
            block = entry_ref[0, number]
            role = entry_ref[1, number]
            worker = entry_ref[2, number]
            first = entry_ref[3, number]
            ids.append(nodes_ref[pl.ds(block, 1), :])
            total = back_ref[worker, :, span_of(first)]
            rows = []
            for field in range(3):
                row = back_ref[worker, :, span_of(jnp.minimum(first + field, BACK_ROWS - 1))]
                row = jnp.where(role == 1, -normal_ref[field, pl.ds(block, 1), :] * total, row)
                rows.append(jnp.where(valid, row, 0.0))
            forces.append(rows)
        return acc + scatter_terms(ids, forces)

    steps = (count + BLOCK_STEP - 1) // BLOCK_STEP
    acc = lax.fori_loop(0, steps, step, jnp.zeros((6 * GROUP, LANES), F32))
    out_ref[...] = near_ref[:rows, :] + fold_terms(acc)
    send_faces(own_ref[0], grid, out_ref, chunks, faces_ref, send_ref, value_ref)


def element_kernel(conn_ref, coords_ref, disp_ref, modulus_ref, out_ref, order_ref):
    chunks = coords_ref.shape[1] // LANES
    groups = conn_ref.shape[1] // LANES
    for group in range(groups):
        order_ref[pl.ds(group * 8, 8), :] = conn_ref[:, group * LANES : (group + 1) * LANES]
    pos = []
    disp = []
    for corner in range(8):
        ids = order_ref[pl.ds(corner, groups, stride=8), :]
        found = gather_chunks(
            lambda field, chunk: (coords_ref if field < 3 else disp_ref)[
                field % 3 : field % 3 + 1, chunk * LANES : (chunk + 1) * LANES
            ],
            6,
            chunks,
            ids,
        )
        pos.append(found[:3])
        disp.append(found[3:])
    first = list(pos[0])
    pos = [[pos[corner][j] - first[j] for j in range(3)] for corner in range(8)]

    def signed(values, signs):
        total = None
        for value, sign in zip(values, signs):
            if total is None:
                total = value if sign > 0 else -value
            else:
                total = total + value if sign > 0 else total - value
        return total

    corner_signs = [[XI_SIGNS[corner][k] for corner in range(8)] for k in range(3)]
    jac = [
        [signed([pos[c][j] for c in range(8)], corner_signs[k]) * 0.125 for k in range(3)]
        for j in range(3)
    ]
    cof = [
        [
            jac[(j + 1) % 3][(k + 1) % 3] * jac[(j + 2) % 3][(k + 2) % 3]
            - jac[(j + 1) % 3][(k + 2) % 3] * jac[(j + 2) % 3][(k + 1) % 3]
            for k in range(3)
        ]
        for j in range(3)
    ]
    det = jac[0][0] * cof[0][0] + jac[0][1] * cof[0][1] + jac[0][2] * cof[0][2]
    volume = 8.0 * det
    inverse = 1.0 / volume
    scaled = [[cof[j][k] * inverse for k in range(3)] for j in range(3)]
    grad = [[signed(scaled[j], XI_SIGNS[c]) for j in range(3)] for c in range(8)]

    def summed(terms):
        total = terms[0]
        for term in terms[1:]:
            total = total + term
        return total

    ugrad = [
        [summed([disp[c][i] * grad[c][j] for c in range(8)]) for j in range(3)] for i in range(3)
    ]
    modulus = modulus_ref[...]
    dilation = ugrad[0][0] + ugrad[1][1] + ugrad[2][2]
    stress = [[modulus * (ugrad[i][j] + ugrad[j][i]) for j in range(3)] for i in range(3)]
    for i in range(3):
        stress[i][i] = stress[i][i] + modulus * dilation
    squares = summed([grad[c][j] * grad[c][j] for c in range(8) for j in range(3)])
    hour_coef = HG_COEF * modulus * volume * squares
    shapes = []
    modes = []
    for a in range(4):
        hour_pos = [signed([pos[c][j] for c in range(8)], HOUR_VEC[a]) for j in range(3)]
        gam = [
            float(HOUR_VEC[a][c]) - summed([hour_pos[j] * grad[c][j] for j in range(3)])
            for c in range(8)
        ]
        shapes.append(gam)
        modes.append(
            [hour_coef * summed([disp[c][i] * gam[c] for c in range(8)]) for i in range(3)]
        )
    flux = [[volume * stress[i][j] for j in range(3)] for i in range(3)]
    acc = jnp.zeros((6 * GROUP, LANES), F32)
    for corner in range(8):
        ids = order_ref[pl.ds(corner, groups, stride=8), :]
        force = []
        for i in range(3):
            value = summed([flux[i][j] * grad[corner][j] for j in range(3)])
            value = value + summed([modes[a][i] * shapes[a][corner] for a in range(4)])
            force.append(-value)
        for group in range(0, groups, 2):
            picks = range(group, min(group + 2, groups))
            acc = acc + scatter_terms(
                [ids[g : g + 1] for g in picks], [[f[g : g + 1] for f in force] for g in picks]
            )
    out_ref[...] = fold_terms(acc)


def around(grid):
    return [(dx, dy) for dx in (-1, 0, 1) for dy in (-1, 0, 1) if (dx, dy) != (0, 0)]


def face_toward(dx, dy):
    if dx:
        return 1 if dx > 0 else 0
    return 3 if dy > 0 else 2


def neighbour(own, grid, dx, dy):
    ix = own // grid[1] + dx
    iy = own % grid[1] + dy
    there = (ix >= 0) & (ix < grid[0]) & (iy >= 0) & (iy < grid[1])
    return there, jnp.where(there, ix * grid[1] + iy, 0)


def send_faces(own, grid, total_ref, chunks, faces_ref, send_ref, value_ref):
    value_ref[...] = jnp.zeros_like(value_ref)
    parts = faces_ref.shape[1] // LANES
    for part in range(parts):
        ids = faces_ref[:, part * LANES : (part + 1) * LANES]
        found = gather_chunks(
            lambda field, chunk: total_ref[field * GROUP + chunk : field * GROUP + chunk + 1, :],
            3,
            chunks,
            ids,
        )
        for field in range(3):
            at = field * parts + part
            for face in range(4):
                value_ref[face, at : at + 1, :] = found[field][face : face + 1]
    for dx, dy in around(grid):
        there, target = neighbour(own, grid, dx, dy)

        @pl.when(there)
        def _():
            for row in range(3 * parts):
                span = slice(row * LANES, (row + 1) * LANES)
                send_ref[target, :, span] = value_ref[face_toward(dx, dy), row : row + 1, :]


def face_map_kernel(chunks, faces_ref, low_ref, high_ref, table_ref):
    parts = faces_ref.shape[1] // LANES
    acc = None
    for row in range(2):
        ids = [faces_ref[row : row + 1, p * LANES : (p + 1) * LANES] for p in range(parts)]
        zero = jnp.zeros((1, LANES), F32)
        places = [(iota((1, LANES), 1) + (p * LANES + 1)).astype(F32) for p in range(parts)]
        fields = [[place if f == row else zero for f in range(3)] for place in places]
        terms = scatter_terms(ids, fields)
        acc = terms if acc is None else acc + terms
    table_ref[...] = fold_terms(acc)
    low_ref[...] = jnp.zeros_like(low_ref)
    high_ref[...] = jnp.zeros_like(high_ref)
    for part in range(parts):
        ids = faces_ref[:, part * LANES : (part + 1) * LANES]
        found = gather_chunks(
            lambda field, chunk: table_ref[field * GROUP + chunk : field * GROUP + chunk + 1, :],
            2,
            chunks,
            ids,
        )
        for field in range(2):
            at = field * parts + part
            low_ref[at : at + 1, :] = found[field][2:3]
            high_ref[at : at + 1, :] = found[field][3:4]


def moved_faces(values, places, parts):
    results = [None] * (3 * parts)
    for part in range(parts):
        place = places[part].astype(jnp.int32) - 1
        low = jnp.broadcast_to(place & (LANES - 1), values.shape)
        got = jnp.take_along_axis(values, low, axis=1, mode="promise_in_bounds")
        for field in range(3):
            total = jnp.zeros((1, LANES), F32)
            for source in range(parts):
                at = field * parts + source
                total = jnp.where(place >> 7 == source, got[at : at + 1], total)
            results[field * parts + part] = total
    return results


def assemble_kernel(slots, back_ref, ids_ref, inner_ref, out_ref):
    devices = back_ref.shape[0]

    def step(turn, acc):
        ids = ids_ref[pl.ds(turn * slots, slots), :]
        values = back_ref[turn]
        for slot in range(0, slots, 2):
            picks = range(slot, min(slot + 2, slots))
            acc = acc + scatter_terms(
                [ids[s : s + 1] for s in picks],
                [[values[f * slots + s : f * slots + s + 1] for f in range(3)] for s in picks],
            )
        return acc

    acc = lax.fori_loop(0, devices, step, jnp.zeros((6 * GROUP, LANES), F32))
    out_ref[...] = inner_ref[...] + fold_terms(acc)


def final_kernel(
    grid, own_ref, total_ref, got_ref, low_ref, high_ref, faces_ref, velocity_ref, mass_ref, out_ref, sum_ref
):
    own = own_ref[0]
    parts = faces_ref.shape[1] // LANES

    def block(dx, dy):
        there, source = neighbour(own, grid, dx, dy)
        spans = [slice(row * LANES, (row + 1) * LANES) for row in range(3 * parts)]
        return [jnp.where(there, got_ref[source, :, span], 0.0) for span in spans]

    def side(dy, map_ref):
        rows = block(0, dy)
        for field, dx in enumerate((-1, 1)):
            places = [map_ref[field * parts + p : field * parts + p + 1, :] for p in range(parts)]
            corner = block(dx, dy)
            corner = corner + [jnp.zeros((1, LANES), F32)] * (-len(corner) % 8)
            moved = moved_faces(jnp.concatenate(corner, axis=0), places, parts)
            rows = [a + b for a, b in zip(rows, moved)]
        return rows

    added = [block(-1, 0), block(1, 0), side(-1, low_ref), side(1, high_ref)]
    acc = jnp.zeros((6 * GROUP, LANES), F32)
    for face, rows in enumerate(added):
        ids = [faces_ref[face : face + 1, p * LANES : (p + 1) * LANES] for p in range(parts)]
        acc = acc + scatter_terms(
            ids, [[rows[f * parts + p] for f in range(3)] for p in range(parts)]
        )
    sum_ref[...] = total_ref[...] + fold_terms(acc)
    for chunk in range(out_ref.shape[1] // LANES):
        span = slice(chunk * LANES, (chunk + 1) * LANES)
        scale = TIME_STEP / mass_ref[chunk : chunk + 1, :]
        for field in range(3):
            row = field * GROUP + chunk
            out_ref[field : field + 1, span] = (
                velocity_ref[field : field + 1, span] + scale * sum_ref[row : row + 1, :]
            )


def call(kernel, outs, in_smem, args, scratch=(), out_smem=(), in_any=()):
    def spec(smem, anywhere=False):
        if anywhere:
            return pl.BlockSpec(memory_space=pl.ANY)
        return pl.BlockSpec(memory_space=pltpu.SMEM if smem else pltpu.VMEM)

    return pl.pallas_call(
        kernel,
        out_shape=[jax.ShapeDtypeStruct(shape, dtype) for shape, dtype in outs],
        in_specs=[spec(i in in_smem, i in in_any) for i in range(len(args))],
        out_specs=[spec(i in out_smem) for i in range(len(outs))],
        scratch_shapes=list(scratch),
        compiler_params=pltpu.CompilerParams(vmem_limit_bytes=VMEM_LIMIT),
    )(*args)


def exchange(low, high, axis):
    count = lax.axis_size(axis)
    forward = [(i, i + 1) for i in range(count - 1)]
    backward = [(target, source) for source, target in forward]
    return lax.ppermute(high, axis, forward), lax.ppermute(low, axis, backward)


def local(
    connectivity,
    face_nodes,
    coords,
    displacement,
    velocity,
    node_mass,
    modulus,
    surf_nodes,
    surf_ref,
    surf_angles,
    owner_map,
    pair_blocks,
    pair_masks,
    pair_count,
):
    axes = ("gx", "gy")
    devices = lax.axis_size("gx") * lax.axis_size("gy")
    per_dev = surf_nodes.shape[0]
    rows_per = per_dev // LANES
    node_count = coords.shape[1]
    chunks = node_count // LANES
    slots = 2 * per_dev // devices
    pairs = pair_blocks.shape[1]
    own = lax.axis_index(axes).reshape(1).astype(jnp.int32)
    owners = owner_map.reshape(devices * rows_per, LANES)
    face_pad = -face_nodes.shape[1] % LANES
    faces = jnp.pad(face_nodes, ((0, 4), (0, face_pad)), constant_values=-1)
    parts = faces.shape[1] // LANES
    face_rows = -(-3 * parts // 8) * 8
    total_shape = ((3 * GROUP, LANES), F32)
    face_shape = ((face_rows, LANES), F32)
    send_shape = ((devices, 1, 3 * parts * LANES), F32)
    grid = (lax.axis_size("gx"), lax.axis_size("gy"))

    def to_all(values):
        return lax.all_to_all(values, axes, split_axis=0, concat_axis=0, tiled=True)

    [request] = call(
        functools.partial(request_kernel, rows_per),
        [((devices, REQUEST_ROWS, LANES), jnp.int32)],
        (0, 1),
        (own, pair_count, owners, pair_blocks, pair_masks),
    )
    asked = to_all(request)
    pos, block_of = call(
        functools.partial(segment_kernel, slots, rows_per),
        [((3, per_dev, LANES), F32), ((devices * slots // LANES, LANES), jnp.int32)],
        (0,),
        (own, owners, displacement, surf_nodes, jnp.transpose(surf_ref, (1, 0, 2))),
        [pltpu.VMEM((8, LANES), jnp.int32), pltpu.SemaphoreType.DMA],
        (),
        (1,),
    )
    [internal] = call(
        element_kernel,
        [total_shape],
        (),
        (connectivity, coords, displacement, modulus.reshape(-1, LANES)),
        [pltpu.VMEM((connectivity.shape[1] // LANES * 8, LANES), jnp.int32)],
    )
    map_low, map_high = call(
        functools.partial(face_map_kernel, chunks),
        [face_shape, face_shape],
        (),
        (faces,),
        [pltpu.VMEM((3 * GROUP, LANES), F32)],
    )
    map_low, map_high = exchange(map_low, map_high, "gy")
    lists = asked[:, 0, :]
    outbound, entries = call(
        functools.partial(plan_kernel, slots),
        [((devices, SEND_ROWS, LANES), F32), ((8, ENTRIES), jnp.int32)],
        (0, 1),
        (lists, block_of, pos, surf_angles),
        [pltpu.SMEM((2, devices), jnp.int32)],
        (1,),
    )
    tasks, near_list, fields = call(
        functools.partial(table_kernel, slots),
        [((8, TASKS), jnp.int32), ((8, 2 * TASKS), jnp.int32), ((10, TASKS, LANES), F32)],
        (0, 1, 2),
        (own, lists, block_of, asked, pair_masks, pos, surf_angles),
        [pltpu.SMEM((2, devices), jnp.int32)],
        (0, 1),
    )
    inbound = to_all(outbound)
    inbound, map_low, map_high = lax.optimization_barrier((inbound, map_low, map_high))
    back, forces, over = call(
        work_kernel,
        [
            ((devices, 1, BACK_ROWS * LANES), F32),
            ((2 * TASKS * 8 + 8, LANES), F32),
            ((1,), jnp.int32),
        ],
        (0, 1),
        (own, tasks, inbound, fields),
        [
            pltpu.VMEM((10, TASKS, LANES), F32),
            pltpu.VMEM((3, TASKS * 8, LANES), F32),
            pltpu.VMEM((3, TASKS * 8, LANES), F32),
            pltpu.VMEM((3, TASKS * 8, LANES), F32),
            pltpu.VMEM((2, TASKS * 8, LANES), F32),
        ],
        (2,),
    )
    returned = to_all(back)

    def by_owners():
        [index] = call(
            functools.partial(routing_kernel, rows_per),
            [((4, pairs), jnp.int32)],
            (0, 1),
            (own, pair_count, owners, pair_blocks),
        )
        outbound, ids = call(
            functools.partial(pack_kernel, slots, rows_per),
            [((devices, 5 * slots, LANES), F32), ((devices * slots, LANES), jnp.int32)],
            (0,),
            (own, owners, pos, surf_angles, surf_nodes),
        )
        [forces] = call(
            functools.partial(pair_kernel, slots),
            [((devices, 3 * slots, LANES), F32)],
            (0, 1),
            (index, pair_count, to_all(outbound), pair_masks),
            [pltpu.VMEM((pairs * 8, LANES), F32)] * 4,
        )
        return call(
            functools.partial(assemble_kernel, slots),
            [total_shape],
            (),
            (to_all(forces), ids, internal),
        )[0]

    whole = lax.cond(over[0] > 0, by_owners, lambda: internal)
    near, normals = call(
        near_kernel,
        [((3 * GROUP + 8, LANES), F32), ((3, per_dev, LANES), F32)],
        (0,),
        (near_list, surf_nodes, forces, internal, whole, surf_angles),
    )
    total, send = call(
        functools.partial(far_kernel, chunks, grid),
        [total_shape, send_shape],
        (0, 1),
        (own, entries, returned, surf_nodes, normals, near, faces),
        [pltpu.VMEM((4,) + face_shape[0], F32)],
    )
    [result] = call(
        functools.partial(final_kernel, grid),
        [((3, node_count), F32)],
        (0,),
        (
            own,
            total,
            to_all(send),
            map_low,
            map_high,
            faces,
            velocity,
            node_mass.reshape(chunks, LANES),
        ),
        [pltpu.VMEM((3 * GROUP, LANES), F32)],
    )
    return result


def solution(mesh):
    in_specs = (
        P(None, ("gx", "gy")),
        P(None, ("gx", "gy")),
        P(None, ("gx", "gy")),
        P(None, ("gx", "gy")),
        P(None, ("gx", "gy")),
        P(("gx", "gy")),
        P(("gx", "gy")),
        P(("gx", "gy"), None),
        P(("gx", "gy"), None, None),
        P(("gx", "gy"), None, None),
        P(),
        P(None, ("gx", "gy")),
        P(None, ("gx", "gy"), None),
        P(("gx", "gy")),
    )
    out_specs = P(None, ("gx", "gy"))
    return jax.shard_map(local, mesh=mesh, in_specs=in_specs, out_specs=out_specs, check_vma=False)
```

```python
import functools

import jax
import jax.numpy as jnp
from jax import lax
from jax.experimental import pallas as pl
from jax.experimental.pallas import tpu as pltpu
from jax.sharding import PartitionSpec as P

XI_SIGNS = [
    [-1, -1, -1],
    [1, -1, -1],
    [1, 1, -1],
    [-1, 1, -1],
    [-1, -1, 1],
    [1, -1, 1],
    [1, 1, 1],
    [-1, 1, 1],
]
HOUR_VEC = [
    [1, 1, -1, -1, -1, -1, 1, 1],
    [1, -1, -1, 1, -1, 1, 1, -1],
    [1, -1, 1, -1, 1, -1, 1, -1],
    [-1, 1, -1, 1, 1, -1, 1, -1],
]
HG_COEF = 0.05
PEN_STIFF = 0.05
PEN_DEPTH = 0.5
TIME_STEP = 0.2
LANES = 128
GROUP = 16
F32 = jnp.float32
BF16 = jnp.bfloat16
VMEM_LIMIT = 48 * 1024 * 1024
REQUEST_ROWS = 8
TASK_CAP = 3
OWN_CAP = 12
TASK_LANE = 64
TASK_FIELDS = 5
ENTRY_LANE = 4
ENTRY_CAP = 20
SEND_ROWS = 32
BACK_ROWS = 10
ENTRIES = 160
TASKS = 48
TASK_STEP = 8
BLOCK_STEP = 8


def iota(shape, dim):
    return lax.broadcasted_iota(jnp.int32, shape, dim)


def dot_nn(a, b):
    return lax.dot_general(a, b, (((1,), (0,)), ((), ())), preferred_element_type=F32)


def dot_nt(a, b):
    return lax.dot_general(a, b, (((1,), (1,)), ((), ())), preferred_element_type=F32)


def dot_tn(a, b):
    return lax.dot_general(a, b, (((0,), (0,)), ((), ())), preferred_element_type=F32)


def as_bf16(mask):
    return jnp.where(mask, 1.0, 0.0).astype(BF16)


def split2(x):
    high = x.astype(BF16)
    return high, (x - high.astype(F32)).astype(BF16)


def split3(x):
    high = x.astype(BF16)
    rest = x - high.astype(F32)
    mid = rest.astype(BF16)
    return high, mid, (rest - mid.astype(F32)).astype(BF16)


def span_of(row):
    return pl.ds(pl.multiple_of(row * LANES, LANES), LANES)


def strict_upper(size):
    return as_bf16(iota((size, size), 0) < iota((size, size), 1))


def take_lanes(row, index):
    table = jnp.broadcast_to(row, index.shape)
    return jnp.take_along_axis(table, index, axis=1, mode="promise_in_bounds")


def gather_chunks(rows_of, fields, chunks, ids):
    high = ids >> 7
    low = ids & (LANES - 1)
    found = [jnp.zeros(ids.shape, F32) for _ in range(fields)]
    for chunk in range(chunks):
        here = high == chunk
        for field in range(fields):
            found[field] = jnp.where(here, take_lanes(rows_of(field, chunk), low), found[field])
    return found


def scatter_terms(id_rows, force_rows):
    wide = []
    table = []
    for ids, forces in zip(id_rows, force_rows):
        here = jnp.broadcast_to(ids >> 7, (GROUP, LANES)) == iota((GROUP, LANES), 0)
        wide.append(
            jnp.concatenate(
                [jnp.where(here, jnp.broadcast_to(f, (GROUP, LANES)), 0.0) for f in forces], axis=0
            )
        )
        low = jnp.broadcast_to(ids & (LANES - 1), (LANES, LANES))
        table.append(as_bf16(low == iota((LANES, LANES), 0)))
    high, rest = split2(jnp.concatenate(wide, axis=1))
    both = jnp.concatenate([high, rest], axis=0)
    return dot_nt(both, jnp.concatenate(table, axis=1))


def fold_terms(acc):
    half = acc.shape[0] // 2
    return acc[:half] + acc[half:]


def routing_kernel(rows_per, own_ref, count_ref, map_ref, pairs_ref, index_ref):
    own = own_ref[0]
    rows = map_ref.shape[0]
    devices = rows // rows_per
    pairs = pairs_ref.shape[1]
    hit = as_bf16(map_ref[...] == own)
    source_of = iota((devices, rows), 1) // rows_per
    upto = as_bf16(source_of <= iota((devices, rows), 0))
    within = as_bf16(source_of == iota((devices, rows), 0))
    ends = jnp.sum(dot_nn(upto, hit), axis=1, keepdims=True)
    counts = jnp.sum(dot_nn(within, hit), axis=1, keepdims=True)
    ranks = pairs_ref[...].astype(F32)
    for side in range(2):
        rank = ranks[side : side + 1]
        below = jnp.broadcast_to(ends, (devices, pairs)) <= rank
        source = jnp.sum(jnp.where(below, 1.0, 0.0), axis=0, keepdims=True)
        source = jnp.minimum(source, devices - 1.0)
        start = jnp.sum(jnp.where(below, counts, 0.0), axis=0, keepdims=True)
        index_ref[2 * side : 2 * side + 1, :] = source.astype(jnp.int32)
        index_ref[2 * side + 1 : 2 * side + 2, :] = (rank - start).astype(jnp.int32)


def request_kernel(rows_per, own_ref, count_ref, map_ref, pairs_ref, masks_ref, out_ref):
    own = own_ref[0]
    rows = map_ref.shape[0]
    devices = rows // rows_per
    pairs = pairs_ref.shape[1]
    hit = as_bf16(map_ref[...] == own)
    source_of = iota((devices, rows), 1) // rows_per
    upto = as_bf16(source_of <= iota((devices, rows), 0))
    within = as_bf16(source_of == iota((devices, rows), 0))
    ends = jnp.sum(dot_nn(upto, hit), axis=1, keepdims=True)
    counts = jnp.sum(dot_nn(within, hit), axis=1, keepdims=True)
    ranks = pairs_ref[...].astype(F32)
    where_is = []
    for side in range(2):
        rank = ranks[side : side + 1]
        below = jnp.broadcast_to(ends, (devices, pairs)) <= rank
        source = jnp.sum(jnp.where(below, 1.0, 0.0), axis=0, keepdims=True)
        source = jnp.minimum(source, devices - 1.0)
        start = jnp.sum(jnp.where(below, counts, 0.0), axis=0, keepdims=True)
        where_is.append((source, rank - start))
    (slave, slave_rank), (master, master_rank) = where_is
    lane = iota((1, pairs), 1)
    live = lane < count_ref[0]
    me = own.astype(F32)
    device = iota((devices, pairs), 0).astype(F32)
    earlier = strict_upper(pairs)

    def pick(target, keep):
        return jnp.where((device == target) & keep, 1.0, 0.0)

    def turns(worker):
        tasks = pick(worker, live)
        ahead = dot_nn(tasks.astype(BF16), earlier)
        return tasks, jnp.sum(tasks * ahead, axis=0, keepdims=True)

    worker = jnp.where(lane == 0, me, slave)
    for other in (master, me):
        tasks, turn = turns(worker)
        worker = jnp.where((turn >= TASK_CAP) & (worker != me), other, worker)
    tasks, turn = turns(worker)
    room = turn < jnp.where(worker == me, float(OWN_CAP), float(TASK_CAP))
    send_slave = live & (slave != worker)
    send_master = live & (master != worker)
    from_slave = pick(slave, send_slave)
    from_master = pick(master, send_master)
    both = from_slave + from_master
    ahead = dot_nn(both.astype(BF16), earlier)
    slave_at = jnp.sum(from_slave * ahead, axis=0, keepdims=True)
    master_at = jnp.sum(from_master * ahead, axis=0, keepdims=True)
    master_at = master_at + jnp.where(send_slave & (slave == master), 1.0, 0.0)

    column = iota((LANES, pairs), 0).astype(F32)

    def placed(first, fields, fits):
        total = jnp.zeros((LANES, pairs), F32)
        for at, field in enumerate(fields):
            total = jnp.where((column == first + at) & fits, field, total)
        return total.astype(BF16)

    zero = jnp.zeros_like(slave)
    entry = placed(ENTRY_LANE + 3 * slave_at, (zero, slave_rank, worker), slave_at < ENTRY_CAP)
    line = dot_nt(from_slave.astype(BF16), entry)
    entry = placed(
        ENTRY_LANE + 3 * master_at, (zero + 1.0, master_rank, worker), master_at < ENTRY_CAP
    )
    line = line + dot_nt(from_master.astype(BF16), entry)
    entry = placed(
        TASK_LANE + TASK_FIELDS * turn,
        (slave, slave_rank, master, master_rank, lane.astype(F32)),
        room,
    )
    line = line + dot_nt(tasks.astype(BF16), entry)
    entry_count = jnp.sum(both, axis=1, keepdims=True)
    task_count = jnp.sum(tasks, axis=1, keepdims=True)
    limit = jnp.where(iota((devices, 1), 0) == own, float(OWN_CAP), float(TASK_CAP))
    over = jnp.where((entry_count > ENTRY_CAP) | (task_count > limit), 1.0, 0.0)
    over = jnp.max(over, axis=0, keepdims=True)
    spot = iota((devices, LANES), 1)
    line = jnp.where(spot == 0, entry_count, line)
    line = jnp.where(spot == 1, task_count, line)
    line = jnp.where(spot == 2, over, line)
    out_ref[:, 0, :] = line.astype(jnp.int32)
    chosen = [jnp.where(turn == t, tasks, 0.0) for t in range(TASK_CAP)]
    chosen = jnp.concatenate(chosen, axis=0).astype(BF16)
    masks = jnp.concatenate([masks_ref[0], masks_ref[1]], axis=1).astype(F32).astype(BF16)
    got = dot_nn(chosen, masks).astype(jnp.int32)
    for t in range(TASK_CAP):
        part = got[t * devices : (t + 1) * devices]
        out_ref[:, 1 + 2 * t, :] = part[:, :LANES]
        out_ref[:, 2 + 2 * t, :] = part[:, LANES:]
    for row in range(1 + 2 * TASK_CAP, REQUEST_ROWS):
        out_ref[:, row, :] = jnp.zeros((devices, LANES), jnp.int32)


def segment_kernel(
    cap,
    rows_per,
    own_ref,
    map_ref,
    disp_ref,
    nodes_ref,
    moved_ref,
    block_ref,
    group_ref,
    sem,
):
    chunks = disp_ref.shape[1] // LANES
    first = own_ref[0] * rows_per
    start = pl.multiple_of(first // 8 * 8, 8)
    move = pltpu.make_async_copy(map_ref.at[pl.ds(start, 8), :], group_ref, sem)
    move.start()

    def step(turn, carry):
        base = pl.multiple_of(turn * 8, 8)
        ids = nodes_ref[pl.ds(base, 8), :]
        found = gather_chunks(
            lambda field, chunk: disp_ref[field : field + 1, chunk * LANES : (chunk + 1) * LANES],
            3,
            chunks,
            ids,
        )
        for field in range(3):
            moved_ref[field, pl.ds(base, 8), :] = found[field]
        return carry

    lax.fori_loop(0, nodes_ref.shape[0] // 8, step, 0, unroll=2)
    move.wait()
    owner = jnp.concatenate(
        [group_ref[pl.ds(first - start + i, 1), :] for i in range(rows_per)], axis=1
    )
    blocks = owner.shape[1]
    total = block_ref.shape[0] * LANES
    mine = iota((total // cap, blocks), 0) == owner
    before = dot_nn(as_bf16(mine), strict_upper(blocks))
    rank = jnp.sum(jnp.where(mine, before, 0.0), axis=0, keepdims=True).astype(jnp.int32)
    hit = as_bf16(iota((total, blocks), 0) == owner * cap + rank)
    high, rest = split2(iota((8, blocks), 1).astype(F32))
    table = (dot_nt(high, hit) + dot_nt(rest, hit)).astype(jnp.int32)
    for row in range(total // LANES):
        block_ref[row : row + 1, :] = table[0:1, row * LANES : (row + 1) * LANES]


def block_at(block_ref, slot):
    return block_ref[slot >> 7, slot & (LANES - 1)]


def plan_kernel(
    cap, list_ref, block_ref, moved_ref, rest_ref, angles_ref, out_ref, entry_ref, used_ref
):
    devices = list_ref.shape[0]

    def clear(device, carry):
        used_ref[0, device] = 0
        used_ref[1, device] = 0
        return carry

    lax.fori_loop(0, devices, clear, 0)

    def from_owner(owner, carry):
        def entry(turn, state):
            number, over = state
            at = ENTRY_LANE + 3 * turn
            role = list_ref[owner, at]
            block = block_at(block_ref, owner * cap + list_ref[owner, at + 1])
            worker = list_ref[owner, at + 2]
            first = used_ref[0, worker]
            back = used_ref[1, worker]
            after = first + 3 + 2 * role
            back_after = back + 3 - 2 * role
            used_ref[0, worker] = after
            used_ref[1, worker] = back_after
            fits = (after < SEND_ROWS) & (first <= SEND_ROWS - 5)
            fits = fits & (back_after <= BACK_ROWS) & (number < ENTRIES)

            @pl.when(fits)
            def _():
                for field in range(3):
                    out_ref[worker, pl.ds(first + field, 1), :] = (
                        moved_ref[field, pl.ds(block, 1), :] + rest_ref[field, pl.ds(block, 1), :]
                    )
                entry_ref[0, number] = block
                entry_ref[1, number] = role
                entry_ref[2, number] = worker
                entry_ref[3, number] = back
                out_ref[worker, pl.ds(first + 3, 2), :] = angles_ref[block]

            return (number + 1, jnp.where(fits, over, 1))

        entries, tasks, over = carry
        over = jnp.maximum(over, list_ref[owner, 2])
        entries, over = lax.fori_loop(
            0, jnp.minimum(list_ref[owner, 0], ENTRY_CAP), entry, (entries, over)
        )
        return (entries, tasks + list_ref[owner, 1], over)

    zero = jnp.int32(0)
    entries, tasks, over = lax.fori_loop(0, devices, from_owner, (zero, zero, zero))
    over = jnp.where(tasks > TASKS, 1, over)
    entry_ref[4, 0] = jnp.minimum(entries, ENTRIES)
    mark = jnp.full((devices, LANES), over.astype(F32), F32)
    out_ref[:, SEND_ROWS - 1, :] = mark


def table_kernel(
    cap,
    own_ref,
    list_ref,
    block_ref,
    request_ref,
    masks_ref,
    moved_ref,
    rest_ref,
    angles_ref,
    task_ref,
    near_ref,
    field_ref,
    used_ref,
):
    own = own_ref[0]
    devices = list_ref.shape[0]
    size = field_ref.shape[1]

    def clear(device, carry):
        used_ref[0, device] = 0
        used_ref[1, device] = 0
        return carry

    lax.fori_loop(0, devices, clear, 0)

    def from_owner(owner, carry):
        def task(turn, state):
            at = TASK_LANE + TASK_FIELDS * turn
            pair = list_ref[owner, at + 4]
            number, near = state
            for side in range(2):
                source = list_ref[owner, at + 2 * side]
                here = source == own
                block = block_at(block_ref, owner * cap + list_ref[owner, at + 2 * side + 1])
                used = used_ref[0, source]
                back = used_ref[1, source]
                used_ref[0, source] = jnp.where(here, used, used + 3 + 2 * side)
                used_ref[1, source] = jnp.where(here, back, back + 3 - 2 * side)
                task_ref[3 * side, number] = source
                task_ref[3 * side + 1, number] = jnp.where(
                    here, block, jnp.minimum(used, SEND_ROWS - 4 - 2 * side)
                )
                task_ref[3 * side + 2, number] = jnp.minimum(back, BACK_ROWS - 3 + 2 * side)
                base = 4 * side

                @pl.when(owner == own)
                def _():
                    mask = masks_ref[side, pl.ds(pair, 1), :]
                    field_ref[base + 3, pl.ds(number, 1), :] = mask.astype(F32)

                @pl.when(owner != own)
                def _():
                    mask = request_ref[owner, pl.ds(1 + 2 * turn + side, 1), :]
                    field_ref[base + 3, pl.ds(number, 1), :] = mask.astype(F32)

                spot = near

                @pl.when(here)
                def _():
                    near_ref[0, spot] = block
                    near_ref[1, spot] = (side * size + number) * 8
                    for field in range(3):
                        field_ref[base + field, pl.ds(number, 1), :] = (
                            moved_ref[field, pl.ds(block, 1), :]
                            + rest_ref[field, pl.ds(block, 1), :]
                        )
                    if side == 1:
                        both = angles_ref[block]
                        field_ref[8, pl.ds(number, 1), :] = both[0:1]
                        field_ref[9, pl.ds(number, 1), :] = both[1:2]

                near = near + jnp.where(here, 1, 0)
            return (number + 1, near)

        number, near = carry
        count = jnp.minimum(list_ref[owner, 1], jnp.where(owner == own, OWN_CAP, TASK_CAP))
        count = jnp.minimum(count, TASKS - number)
        return lax.fori_loop(0, count, task, (number, near))

    tasks, near = lax.fori_loop(0, devices, from_owner, (jnp.int32(0), jnp.int32(0)))
    task_ref[6, 0] = tasks
    near_ref[2, 0] = near


def pack_kernel(
    slots,
    rows_per,
    own_ref,
    map_ref,
    moved_ref,
    rest_ref,
    angles_ref,
    nodes_ref,
    out_ref,
    ids_ref,
):
    own = own_ref[0]
    devices = map_ref.shape[0] // rows_per
    owner = jnp.concatenate(
        [map_ref[pl.ds(own * rows_per + i, 1), :] for i in range(rows_per)], axis=1
    )
    blocks = owner.shape[1]
    mine = iota((devices, blocks), 0) == owner
    before = dot_nn(as_bf16(mine), strict_upper(blocks))
    rank = jnp.sum(jnp.where(mine, before, 0.0), axis=0, keepdims=True).astype(jnp.int32)
    place = owner * slots + rank
    move = as_bf16(iota((devices * slots, blocks), 0) == place)
    for field in range(5):
        if field < 3:
            values = moved_ref[field] + rest_ref[field]
        else:
            values = angles_ref[:, field - 3, :]
        moved = dot_nn(move, jnp.concatenate(split3(values), axis=1))
        moved = moved[:, :LANES] + moved[:, LANES : 2 * LANES] + moved[:, 2 * LANES :]
        out_ref[:, field * slots : (field + 1) * slots, :] = moved.reshape(devices, slots, LANES)
    nodes = nodes_ref[...]
    halves = jnp.concatenate(
        [(nodes >> 7).astype(F32).astype(BF16), (nodes & (LANES - 1)).astype(F32).astype(BF16)],
        axis=1,
    )
    moved = dot_nn(move, halves)
    ids_ref[...] = (moved[:, :LANES] * LANES + moved[:, LANES:]).astype(jnp.int32)


def sine_cosine(angle):
    half = 0.5 * angle
    sq = half * half
    sine = sq * (-1.0 / 39916800.0) + 1.0 / 362880.0
    for coef in (-1.0 / 5040.0, 1.0 / 120.0, -1.0 / 6.0, 1.0):
        sine = sine * sq + coef
    sine = sine * half
    cosine = sq * (1.0 / 479001600.0) - 1.0 / 3628800.0
    for coef in (1.0 / 40320.0, -1.0 / 720.0, 1.0 / 24.0, -0.5, 1.0):
        cosine = cosine * sq + coef
    return 2.0 * sine * cosine, 1.0 - 2.0 * sine * sine


def pair_kernel(
    slots, index_ref, count_ref, in_ref, masks_ref, out_ref, slave_ref, master_ref, sin_ref, cos_ref
):
    pairs = masks_ref.shape[1]
    count = jnp.minimum(count_ref[0], pairs)
    out_ref[...] = jnp.zeros_like(out_ref)

    def stage(pair, carry):
        source = index_ref[0, pair]
        slot = index_ref[1, pair]
        for field in range(3):
            slave_ref[pl.ds(pair * 8 + field, 1), :] = in_ref[source, pl.ds(field * slots + slot, 1), :]
        slave_ref[pl.ds(pair * 8 + 3, 1), :] = masks_ref[0, pl.ds(pair, 1), :].astype(F32)
        source = index_ref[2, pair]
        slot = index_ref[3, pair]
        for field in range(5):
            master_ref[pl.ds(pair * 8 + field, 1), :] = in_ref[source, pl.ds(field * slots + slot, 1), :]
        master_ref[pl.ds(pair * 8 + 5, 1), :] = masks_ref[1, pl.ds(pair, 1), :].astype(F32)
        return carry

    lax.fori_loop(0, count, stage, 0)
    sines, cosines = sine_cosine(master_ref[...])
    sin_ref[...] = sines
    cos_ref[...] = cosines

    def tile(pair, carry):
        base = pl.multiple_of(pair * 8, 8)
        slave = slave_ref[pl.ds(base, 8), :]
        columns = jnp.transpose(slave)
        master = master_ref[pl.ds(base, 8), :]
        sin_az = sin_ref[pl.ds(base + 3, 1), :]
        sin_pol = sin_ref[pl.ds(base + 4, 1), :]
        cos_az = cos_ref[pl.ds(base + 3, 1), :]
        cos_pol = cos_ref[pl.ds(base + 4, 1), :]
        normal = [cos_az * cos_pol, sin_az * cos_pol, sin_pol]
        shape = (LANES, LANES)
        dist = [
            jnp.broadcast_to(columns[:, k : k + 1], shape) - jnp.broadcast_to(master[k : k + 1], shape)
            for k in range(3)
        ]
        gap = dist[0] * normal[0] + dist[1] * normal[1] + dist[2] * normal[2]
        tang = dist[0] * dist[0] + dist[1] * dist[1] + dist[2] * dist[2] - gap * gap
        bend = gap * (-1.0 / PEN_DEPTH)
        soft = jnp.maximum(bend, 0.0) + jnp.log(1.0 + jnp.exp(-jnp.abs(bend)))
        press = soft * jnp.exp(-0.5 * tang)
        press = press * jnp.broadcast_to(columns[:, 3:4], shape)
        total = jnp.sum(press, axis=0, keepdims=True)
        scale = PEN_STIFF * PEN_DEPTH * master[5:6]
        push = [n * scale for n in normal]
        rows = jnp.concatenate(push + [jnp.zeros((5, LANES), F32)], axis=0)
        push_high, push_rest = split2(rows)
        both = jnp.concatenate([push_high, push_rest], axis=0)
        high, rest = split2(press)
        got = dot_nt(both, high) + dot_nt(both, rest)
        on_slave = got[0:8] + got[8:16]
        source = index_ref[0, pair]
        slot = index_ref[1, pair]
        for k in range(3):
            at = pl.ds(k * slots + slot, 1)
            out_ref[source, at, :] = out_ref[source, at, :] + on_slave[k : k + 1]
        source = index_ref[2, pair]
        slot = index_ref[3, pair]
        for k in range(3):
            at = pl.ds(k * slots + slot, 1)
            out_ref[source, at, :] = out_ref[source, at, :] - push[k] * total
        return carry

    lax.fori_loop(0, count, tile, 0)


def work_kernel(
    own_ref,
    task_ref,
    in_ref,
    start_ref,
    back_ref,
    force_ref,
    over_ref,
    field_ref,
    left_ref,
    gap_ref,
    far_ref,
    push_ref,
):
    own = own_ref[0]
    count = task_ref[6, 0]
    field_ref[...] = start_ref[...]
    over = jnp.max(in_ref[:, SEND_ROWS - 1, :])
    over_ref[0] = over.astype(jnp.int32)
    marks = force_ref.shape[0] - 8
    force_ref[marks:, :] = jnp.full((8, LANES), over, F32)

    def stage(task, carry):
        for side in range(2):
            source = task_ref[3 * side, task]
            first = task_ref[3 * side + 1, task]

            @pl.when(source != own)
            def _():
                for field in range(3):
                    field_ref[4 * side + field, pl.ds(task, 1), :] = in_ref[
                        source, pl.ds(first + field, 1), :
                    ]
                if side == 1:
                    for field in range(2):
                        field_ref[8 + field, pl.ds(task, 1), :] = in_ref[
                            source, pl.ds(first + 3 + field, 1), :
                        ]

        return carry

    lax.fori_loop(0, count, stage, 0)
    size = field_ref.shape[1]
    slave = [field_ref[k] for k in range(3)]
    master = [field_ref[4 + k] for k in range(3)]
    sin_az, cos_az = sine_cosine(field_ref[8])
    sin_pol, cos_pol = sine_cosine(field_ref[9])
    normal = [cos_az * cos_pol, sin_az * cos_pol, sin_pol]

    def inner(a, b):
        return a[0] * b[0] + a[1] * b[1] + a[2] * b[2]

    zero = jnp.zeros_like(sin_pol)
    one = zero + 1.0
    slope = -1.0 / PEN_DEPTH
    hidden = 30000.0
    slave_bias = -0.5 * inner(slave, slave) - hidden * (1.0 - field_ref[3])
    master_bias = -0.5 * inner(master, master) - hidden * (1.0 - field_ref[7])
    stacks = (
        (left_ref, slave + [one, slave_bias]),
        (gap_ref, [slope * n for n in normal] + [-slope * inner(normal, master), zero]),
        (far_ref, master + [master_bias, one]),
        (push_ref, [PEN_STIFF * PEN_DEPTH * n for n in normal] + [zero, zero]),
    )
    for ref, rows in stacks:
        for row, value in enumerate(rows + [zero] * 3):
            parts = split3(value)
            for part in range(ref.shape[0]):
                ref[part, pl.ds(row, size, stride=8), :] = parts[part].astype(F32)

    def tile(step, carry):
        tasks = [TASK_STEP * step + k for k in range(TASK_STEP)]
        bases = [pl.multiple_of(task * 8, 8) for task in tasks]
        fields = []
        for base in bases:
            high, mid, low = [left_ref[p, pl.ds(base, 8), :] for p in range(3)]
            left = jnp.concatenate([high, high, mid, mid, high, low], axis=0).astype(BF16)
            sides = []
            for ref in (gap_ref, far_ref):
                high, mid, low = [ref[p, pl.ds(base, 8), :] for p in range(3)]
                sides.append(jnp.concatenate([high, mid, high, mid, low, high], axis=0))
            fields.append(dot_tn(left, jnp.concatenate(sides, axis=1).astype(BF16)))
        presses = []
        for field in fields:
            bend = field[:, :LANES]
            power = field[:, LANES:] + bend * bend * (0.5 * PEN_DEPTH * PEN_DEPTH)
            soft = jnp.maximum(bend, 0.0) + jnp.log(1.0 + jnp.exp(-jnp.abs(bend)))
            presses.append(soft * jnp.exp(power))
        results = []
        for base, press in zip(bases, presses):
            push = jnp.concatenate([push_ref[p, pl.ds(base, 8), :] for p in range(2)], axis=0)
            push = push.astype(BF16)
            got = dot_nt(
                jnp.concatenate([push, push], axis=1), jnp.concatenate(split2(press), axis=1)
            )
            total = jnp.sum(press, axis=0, keepdims=True)
            results.append((got[0:8] + got[8:16], total * (PEN_STIFF * PEN_DEPTH)))
        for task, base, (on_slave, total) in zip(tasks, bases, results):
            normals = gap_ref[0, pl.ds(base, 8), :] + gap_ref[1, pl.ds(base, 8), :]
            normals = normals + gap_ref[2, pl.ds(base, 8), :]
            force_ref[pl.ds(base, 8), :] = on_slave
            force_ref[pl.ds(base + size * 8, 8), :] = normals * (total * (-1.0 / slope))
            live = task < count
            slave_from = task_ref[0, task]
            master_from = task_ref[3, task]

            @pl.when(live & (slave_from != own))
            def _():
                for k in range(3):
                    back_ref[slave_from, :, span_of(task_ref[2, task] + k)] = on_slave[k : k + 1]

            @pl.when(live & (master_from != own))
            def _():
                back_ref[master_from, :, span_of(task_ref[5, task])] = total

        return carry

    lax.fori_loop(0, (count + TASK_STEP - 1) // TASK_STEP, tile, 0)


def near_kernel(
    near_ref,
    entry_ref,
    nodes_ref,
    force_ref,
    inner_ref,
    whole_ref,
    angles_ref,
    out_ref,
    normal_ref,
):
    count = near_ref[2, 0]

    def step(turn, acc):
        ids = []
        forces = []
        for k in range(BLOCK_STEP):
            valid = BLOCK_STEP * turn + k < count
            number = jnp.where(valid, BLOCK_STEP * turn + k, 0)
            ids.append(nodes_ref[pl.ds(near_ref[0, number], 1), :])
            rows = force_ref[pl.ds(pl.multiple_of(near_ref[1, number], 8), 8), :]
            rows = jnp.where(valid, rows, 0.0)
            forces.append([rows[f : f + 1] for f in range(3)])
        return acc + scatter_terms(ids, forces)

    steps = (count + BLOCK_STEP - 1) // BLOCK_STEP
    acc = lax.fori_loop(0, steps, step, jnp.zeros((6 * GROUP, LANES), F32))
    marks = force_ref[force_ref.shape[0] - 8 :, :]
    total = fold_terms(acc)
    rows = total.shape[0]
    total = jnp.where(marks[0:1] > 0.0, whole_ref[:rows, :], total)
    out_ref[:rows, :] = inner_ref[...] + total
    out_ref[rows:, :] = marks
    entries = jnp.where(jnp.max(marks) > 0.0, 0, entry_ref[4, 0])

    def turn_angles(turn, carry):
        both = []
        for k in range(8):
            block = entry_ref[0, jnp.minimum(8 * turn + k, entries - 1)]
            both.append(angles_ref[block])
        azimuth = jnp.concatenate([pair[0:1] for pair in both], axis=0)
        polar = jnp.concatenate([pair[1:2] for pair in both], axis=0)
        sin_az, cos_az = sine_cosine(azimuth)
        sin_pol, cos_pol = sine_cosine(polar)
        at = pl.ds(pl.multiple_of(turn * 8, 8), 8)
        normal_ref[0, at, :] = cos_az * cos_pol
        normal_ref[1, at, :] = sin_az * cos_pol
        normal_ref[2, at, :] = sin_pol
        return carry

    lax.fori_loop(0, (entries + 7) // 8, turn_angles, 0)


def far_kernel(
    chunks,
    grid,
    own_ref,
    entry_ref,
    back_ref,
    nodes_ref,
    normal_ref,
    near_ref,
    faces_ref,
    out_ref,
    send_ref,
    value_ref,
):
    rows = out_ref.shape[0]
    count = jnp.where(jnp.max(near_ref[rows:, :]) > 0.0, 0, entry_ref[4, 0])

    def step(turn, acc):
        ids = []
        forces = []
        for k in range(BLOCK_STEP):
            valid = BLOCK_STEP * turn + k < count
            number = jnp.where(valid, BLOCK_STEP * turn + k, 0)
            block = entry_ref[0, number]
            role = entry_ref[1, number]
            worker = entry_ref[2, number]
            first = entry_ref[3, number]
            ids.append(nodes_ref[pl.ds(block, 1), :])
            total = back_ref[worker, :, span_of(first)]
            rows = []
            for field in range(3):
                row = back_ref[worker, :, span_of(jnp.minimum(first + field, BACK_ROWS - 1))]
                row = jnp.where(role == 1, -normal_ref[field, pl.ds(number, 1), :] * total, row)
                rows.append(jnp.where(valid, row, 0.0))
            forces.append(rows)
        return acc + scatter_terms(ids, forces)

    steps = (count + BLOCK_STEP - 1) // BLOCK_STEP
    acc = lax.fori_loop(0, steps, step, jnp.zeros((6 * GROUP, LANES), F32))
    out_ref[...] = near_ref[:rows, :] + fold_terms(acc)
    send_faces(own_ref[0], grid, out_ref, chunks, faces_ref, send_ref, value_ref)


def element_kernel(conn_ref, coords_ref, disp_ref, modulus_ref, out_ref, order_ref):
    chunks = coords_ref.shape[1] // LANES
    groups = conn_ref.shape[1] // LANES
    for group in range(groups):
        order_ref[pl.ds(group * 8, 8), :] = conn_ref[:, group * LANES : (group + 1) * LANES]
    pos = []
    disp = []
    for corner in range(8):
        ids = order_ref[pl.ds(corner, groups, stride=8), :]
        found = gather_chunks(
            lambda field, chunk: (coords_ref if field < 3 else disp_ref)[
                field % 3 : field % 3 + 1, chunk * LANES : (chunk + 1) * LANES
            ],
            6,
            chunks,
            ids,
        )
        pos.append(found[:3])
        disp.append(found[3:])
    first = list(pos[0])
    pos = [[pos[corner][j] - first[j] for j in range(3)] for corner in range(8)]

    def signed(values, signs):
        total = None
        for value, sign in zip(values, signs):
            if total is None:
                total = value if sign > 0 else -value
            else:
                total = total + value if sign > 0 else total - value
        return total

    corner_signs = [[XI_SIGNS[corner][k] for corner in range(8)] for k in range(3)]
    jac = [
        [signed([pos[c][j] for c in range(8)], corner_signs[k]) * 0.125 for k in range(3)]
        for j in range(3)
    ]
    cof = [
        [
            jac[(j + 1) % 3][(k + 1) % 3] * jac[(j + 2) % 3][(k + 2) % 3]
            - jac[(j + 1) % 3][(k + 2) % 3] * jac[(j + 2) % 3][(k + 1) % 3]
            for k in range(3)
        ]
        for j in range(3)
    ]
    det = jac[0][0] * cof[0][0] + jac[0][1] * cof[0][1] + jac[0][2] * cof[0][2]
    volume = 8.0 * det
    inverse = 1.0 / volume
    scaled = [[cof[j][k] * inverse for k in range(3)] for j in range(3)]
    grad = [[signed(scaled[j], XI_SIGNS[c]) for j in range(3)] for c in range(8)]

    def summed(terms):
        total = terms[0]
        for term in terms[1:]:
            total = total + term
        return total

    ugrad = [
        [summed([disp[c][i] * grad[c][j] for c in range(8)]) for j in range(3)] for i in range(3)
    ]
    modulus = modulus_ref[...]
    dilation = ugrad[0][0] + ugrad[1][1] + ugrad[2][2]
    stress = [[modulus * (ugrad[i][j] + ugrad[j][i]) for j in range(3)] for i in range(3)]
    for i in range(3):
        stress[i][i] = stress[i][i] + modulus * dilation
    squares = summed([grad[c][j] * grad[c][j] for c in range(8) for j in range(3)])
    hour_coef = HG_COEF * modulus * volume * squares
    shapes = []
    modes = []
    for a in range(4):
        hour_pos = [signed([pos[c][j] for c in range(8)], HOUR_VEC[a]) for j in range(3)]
        gam = [
            float(HOUR_VEC[a][c]) - summed([hour_pos[j] * grad[c][j] for j in range(3)])
            for c in range(8)
        ]
        shapes.append(gam)
        modes.append(
            [hour_coef * summed([disp[c][i] * gam[c] for c in range(8)]) for i in range(3)]
        )
    flux = [[volume * stress[i][j] for j in range(3)] for i in range(3)]
    acc = jnp.zeros((6 * GROUP, LANES), F32)
    for corner in range(8):
        ids = order_ref[pl.ds(corner, groups, stride=8), :]
        force = []
        for i in range(3):
            value = summed([flux[i][j] * grad[corner][j] for j in range(3)])
            value = value + summed([modes[a][i] * shapes[a][corner] for a in range(4)])
            force.append(-value)
        for group in range(0, groups, 2):
            picks = range(group, min(group + 2, groups))
            acc = acc + scatter_terms(
                [ids[g : g + 1] for g in picks], [[f[g : g + 1] for f in force] for g in picks]
            )
    out_ref[...] = fold_terms(acc)


def around(grid):
    return [(dx, dy) for dx in (-1, 0, 1) for dy in (-1, 0, 1) if (dx, dy) != (0, 0)]


def face_toward(dx, dy):
    if dx:
        return 1 if dx > 0 else 0
    return 3 if dy > 0 else 2


def neighbour(own, grid, dx, dy):
    ix = own // grid[1] + dx
    iy = own % grid[1] + dy
    there = (ix >= 0) & (ix < grid[0]) & (iy >= 0) & (iy < grid[1])
    return there, jnp.where(there, ix * grid[1] + iy, 0)


def send_faces(own, grid, total_ref, chunks, faces_ref, send_ref, value_ref):
    value_ref[...] = jnp.zeros_like(value_ref)
    parts = faces_ref.shape[1] // LANES
    for part in range(parts):
        ids = faces_ref[:, part * LANES : (part + 1) * LANES]
        found = gather_chunks(
            lambda field, chunk: total_ref[field * GROUP + chunk : field * GROUP + chunk + 1, :],
            3,
            chunks,
            ids,
        )
        for field in range(3):
            at = field * parts + part
            for face in range(4):
                value_ref[face, at : at + 1, :] = found[field][face : face + 1]
    for dx, dy in around(grid):
        there, target = neighbour(own, grid, dx, dy)

        @pl.when(there)
        def _():
            for row in range(3 * parts):
                span = slice(row * LANES, (row + 1) * LANES)
                send_ref[target, :, span] = value_ref[face_toward(dx, dy), row : row + 1, :]


def face_map_kernel(chunks, faces_ref, low_ref, high_ref, table_ref):
    parts = faces_ref.shape[1] // LANES
    acc = None
    for row in range(2):
        ids = [faces_ref[row : row + 1, p * LANES : (p + 1) * LANES] for p in range(parts)]
        zero = jnp.zeros((1, LANES), F32)
        places = [(iota((1, LANES), 1) + (p * LANES + 1)).astype(F32) for p in range(parts)]
        fields = [[place if f == row else zero for f in range(3)] for place in places]
        terms = scatter_terms(ids, fields)
        acc = terms if acc is None else acc + terms
    table_ref[...] = fold_terms(acc)
    low_ref[...] = jnp.zeros_like(low_ref)
    high_ref[...] = jnp.zeros_like(high_ref)
    for part in range(parts):
        ids = faces_ref[:, part * LANES : (part + 1) * LANES]
        found = gather_chunks(
            lambda field, chunk: table_ref[field * GROUP + chunk : field * GROUP + chunk + 1, :],
            2,
            chunks,
            ids,
        )
        for field in range(2):
            at = field * parts + part
            low_ref[at : at + 1, :] = found[field][2:3]
            high_ref[at : at + 1, :] = found[field][3:4]


def moved_faces(values, places, parts):
    results = [None] * (3 * parts)
    for part in range(parts):
        place = places[part].astype(jnp.int32) - 1
        low = jnp.broadcast_to(place & (LANES - 1), values.shape)
        got = jnp.take_along_axis(values, low, axis=1, mode="promise_in_bounds")
        for field in range(3):
            total = jnp.zeros((1, LANES), F32)
            for source in range(parts):
                at = field * parts + source
                total = jnp.where(place >> 7 == source, got[at : at + 1], total)
            results[field * parts + part] = total
    return results


def assemble_kernel(slots, back_ref, ids_ref, out_ref):
    devices = back_ref.shape[0]

    def step(turn, acc):
        ids = ids_ref[pl.ds(turn * slots, slots), :]
        values = back_ref[turn]
        for slot in range(0, slots, 2):
            picks = range(slot, min(slot + 2, slots))
            acc = acc + scatter_terms(
                [ids[s : s + 1] for s in picks],
                [[values[f * slots + s : f * slots + s + 1] for f in range(3)] for s in picks],
            )
        return acc

    acc = lax.fori_loop(0, devices, step, jnp.zeros((6 * GROUP, LANES), F32))
    out_ref[...] = fold_terms(acc)


def final_kernel(
    grid, own_ref, total_ref, got_ref, low_ref, high_ref, faces_ref, velocity_ref, mass_ref, out_ref, sum_ref
):
    own = own_ref[0]
    parts = faces_ref.shape[1] // LANES

    def block(dx, dy):
        there, source = neighbour(own, grid, dx, dy)
        spans = [slice(row * LANES, (row + 1) * LANES) for row in range(3 * parts)]
        return [jnp.where(there, got_ref[source, :, span], 0.0) for span in spans]

    def side(dy, map_ref):
        rows = block(0, dy)
        for field, dx in enumerate((-1, 1)):
            places = [map_ref[field * parts + p : field * parts + p + 1, :] for p in range(parts)]
            corner = block(dx, dy)
            corner = corner + [jnp.zeros((1, LANES), F32)] * (-len(corner) % 8)
            moved = moved_faces(jnp.concatenate(corner, axis=0), places, parts)
            rows = [a + b for a, b in zip(rows, moved)]
        return rows

    added = [block(-1, 0), block(1, 0), side(-1, low_ref), side(1, high_ref)]
    acc = jnp.zeros((6 * GROUP, LANES), F32)
    for face, rows in enumerate(added):
        ids = [faces_ref[face : face + 1, p * LANES : (p + 1) * LANES] for p in range(parts)]
        acc = acc + scatter_terms(
            ids, [[rows[f * parts + p] for f in range(3)] for p in range(parts)]
        )
    sum_ref[...] = total_ref[...] + fold_terms(acc)
    for chunk in range(out_ref.shape[1] // LANES):
        span = slice(chunk * LANES, (chunk + 1) * LANES)
        scale = TIME_STEP / mass_ref[chunk : chunk + 1, :]
        for field in range(3):
            row = field * GROUP + chunk
            out_ref[field : field + 1, span] = (
                velocity_ref[field : field + 1, span] + scale * sum_ref[row : row + 1, :]
            )


def call(kernel, outs, in_smem, args, scratch=(), out_smem=(), in_any=()):
    def spec(smem, anywhere=False):
        if anywhere:
            return pl.BlockSpec(memory_space=pl.ANY)
        return pl.BlockSpec(memory_space=pltpu.SMEM if smem else pltpu.VMEM)

    return pl.pallas_call(
        kernel,
        out_shape=[jax.ShapeDtypeStruct(shape, dtype) for shape, dtype in outs],
        in_specs=[spec(i in in_smem, i in in_any) for i in range(len(args))],
        out_specs=[spec(i in out_smem) for i in range(len(outs))],
        scratch_shapes=list(scratch),
        compiler_params=pltpu.CompilerParams(vmem_limit_bytes=VMEM_LIMIT),
    )(*args)


def exchange(low, high, axis):
    count = lax.axis_size(axis)
    forward = [(i, i + 1) for i in range(count - 1)]
    backward = [(target, source) for source, target in forward]
    return lax.ppermute(high, axis, forward), lax.ppermute(low, axis, backward)


def local(
    connectivity,
    face_nodes,
    coords,
    displacement,
    velocity,
    node_mass,
    modulus,
    surf_nodes,
    surf_ref,
    surf_angles,
    owner_map,
    pair_blocks,
    pair_masks,
    pair_count,
):
    axes = ("gx", "gy")
    devices = lax.axis_size("gx") * lax.axis_size("gy")
    per_dev = surf_nodes.shape[0]
    rows_per = per_dev // LANES
    node_count = coords.shape[1]
    chunks = node_count // LANES
    slots = 2 * per_dev // devices
    pairs = pair_blocks.shape[1]
    own = lax.axis_index(axes).reshape(1).astype(jnp.int32)
    owners = owner_map.reshape(devices * rows_per, LANES)
    face_pad = -face_nodes.shape[1] % LANES
    faces = jnp.pad(face_nodes, ((0, 4), (0, face_pad)), constant_values=-1)
    parts = faces.shape[1] // LANES
    face_rows = -(-3 * parts // 8) * 8
    total_shape = ((3 * GROUP, LANES), F32)
    face_shape = ((face_rows, LANES), F32)
    send_shape = ((devices, 1, 3 * parts * LANES), F32)
    grid = (lax.axis_size("gx"), lax.axis_size("gy"))

    def to_all(values):
        return lax.all_to_all(values, axes, split_axis=0, concat_axis=0, tiled=True)

    [request] = call(
        functools.partial(request_kernel, rows_per),
        [((devices, REQUEST_ROWS, LANES), jnp.int32)],
        (0, 1),
        (own, pair_count, owners, pair_blocks, pair_masks),
    )
    asked = to_all(request)
    rest = jnp.transpose(surf_ref, (1, 0, 2))
    moved, block_of = call(
        functools.partial(segment_kernel, slots, rows_per),
        [((3, per_dev, LANES), F32), ((devices * slots // LANES, LANES), jnp.int32)],
        (0,),
        (own, owners, displacement, surf_nodes),
        [pltpu.VMEM((8, LANES), jnp.int32), pltpu.SemaphoreType.DMA],
        (),
        (1,),
    )
    map_low, map_high = call(
        functools.partial(face_map_kernel, chunks),
        [face_shape, face_shape],
        (),
        (faces,),
        [pltpu.VMEM((3 * GROUP, LANES), F32)],
    )
    map_low, map_high = exchange(map_low, map_high, "gy")
    lists = asked[:, 0, :]
    outbound, entries = call(
        functools.partial(plan_kernel, slots),
        [((devices, SEND_ROWS, LANES), F32), ((8, ENTRIES), jnp.int32)],
        (0, 1),
        (lists, block_of, moved, rest, surf_angles),
        [pltpu.SMEM((2, devices), jnp.int32)],
        (1,),
    )
    tasks, near_list, fields = call(
        functools.partial(table_kernel, slots),
        [((8, TASKS), jnp.int32), ((8, 2 * TASKS), jnp.int32), ((10, TASKS, LANES), F32)],
        (0, 1, 2),
        (own, lists, block_of, asked, pair_masks, moved, rest, surf_angles),
        [pltpu.SMEM((2, devices), jnp.int32)],
        (0, 1),
    )
    inbound = to_all(outbound)
    inbound, map_low, map_high = lax.optimization_barrier((inbound, map_low, map_high))
    back, forces, over = call(
        work_kernel,
        [
            ((devices, 1, BACK_ROWS * LANES), F32),
            ((2 * TASKS * 8 + 8, LANES), F32),
            ((1,), jnp.int32),
        ],
        (0, 1),
        (own, tasks, inbound, fields),
        [
            pltpu.VMEM((10, TASKS, LANES), F32),
            pltpu.VMEM((3, TASKS * 8, LANES), F32),
            pltpu.VMEM((3, TASKS * 8, LANES), F32),
            pltpu.VMEM((3, TASKS * 8, LANES), F32),
            pltpu.VMEM((2, TASKS * 8, LANES), F32),
        ],
        (2,),
    )
    returned = to_all(back)

    def by_owners():
        [index] = call(
            functools.partial(routing_kernel, rows_per),
            [((4, pairs), jnp.int32)],
            (0, 1),
            (own, pair_count, owners, pair_blocks),
        )
        outbound, ids = call(
            functools.partial(pack_kernel, slots, rows_per),
            [((devices, 5 * slots, LANES), F32), ((devices * slots, LANES), jnp.int32)],
            (0,),
            (own, owners, moved, rest, surf_angles, surf_nodes),
        )
        [owned] = call(
            functools.partial(pair_kernel, slots),
            [((devices, 3 * slots, LANES), F32)],
            (0, 1),
            (index, pair_count, to_all(outbound), pair_masks),
            [pltpu.VMEM((pairs * 8, LANES), F32)] * 4,
        )
        [whole] = call(
            functools.partial(assemble_kernel, slots), [total_shape], (), (to_all(owned), ids)
        )
        return jnp.pad(whole, ((0, forces.shape[0] - whole.shape[0]), (0, 0)))

    whole = lax.cond(over[0] > 0, by_owners, lambda: forces)
    late, unused = lax.optimization_barrier((coords, over))
    [internal] = call(
        element_kernel,
        [total_shape],
        (),
        (connectivity, late, displacement, modulus.reshape(-1, LANES)),
        [pltpu.VMEM((connectivity.shape[1] // LANES * 8, LANES), jnp.int32)],
    )
    near, normals = call(
        near_kernel,
        [((3 * GROUP + 8, LANES), F32), ((3, ENTRIES, LANES), F32)],
        (0, 1),
        (near_list, entries, surf_nodes, forces, internal, whole, surf_angles),
    )
    total, send = call(
        functools.partial(far_kernel, chunks, grid),
        [total_shape, send_shape],
        (0, 1),
        (own, entries, returned, surf_nodes, normals, near, faces),
        [pltpu.VMEM((4,) + face_shape[0], F32)],
    )
    [result] = call(
        functools.partial(final_kernel, grid),
        [((3, node_count), F32)],
        (0,),
        (
            own,
            total,
            to_all(send),
            map_low,
            map_high,
            faces,
            velocity,
            node_mass.reshape(chunks, LANES),
        ),
        [pltpu.VMEM((3 * GROUP, LANES), F32)],
    )
    return result


def solution(mesh):
    in_specs = (
        P(None, ("gx", "gy")),
        P(None, ("gx", "gy")),
        P(None, ("gx", "gy")),
        P(None, ("gx", "gy")),
        P(None, ("gx", "gy")),
        P(("gx", "gy")),
        P(("gx", "gy")),
        P(("gx", "gy"), None),
        P(("gx", "gy"), None, None),
        P(("gx", "gy"), None, None),
        P(),
        P(None, ("gx", "gy")),
        P(None, ("gx", "gy"), None),
        P(("gx", "gy")),
    )
    out_specs = P(None, ("gx", "gy"))
    return jax.shard_map(local, mesh=mesh, in_specs=in_specs, out_specs=out_specs, check_vma=False)
```

```python
import functools

import jax
import jax.numpy as jnp
from jax import lax
from jax.experimental import pallas as pl
from jax.experimental.pallas import tpu as pltpu
from jax.sharding import PartitionSpec as P

XI_SIGNS = [
    [-1, -1, -1],
    [1, -1, -1],
    [1, 1, -1],
    [-1, 1, -1],
    [-1, -1, 1],
    [1, -1, 1],
    [1, 1, 1],
    [-1, 1, 1],
]
HOUR_VEC = [
    [1, 1, -1, -1, -1, -1, 1, 1],
    [1, -1, -1, 1, -1, 1, 1, -1],
    [1, -1, 1, -1, 1, -1, 1, -1],
    [-1, 1, -1, 1, 1, -1, 1, -1],
]
HG_COEF = 0.05
PEN_STIFF = 0.05
PEN_DEPTH = 0.5
TIME_STEP = 0.2
LANES = 128
GROUP = 16
F32 = jnp.float32
BF16 = jnp.bfloat16
VMEM_LIMIT = 48 * 1024 * 1024
REQUEST_ROWS = 8
TASK_CAP = 3
OWN_CAP = 12
TASK_LANE = 64
TASK_FIELDS = 5
ENTRY_LANE = 4
ENTRY_CAP = 20
SEND_ROWS = 32
BACK_ROWS = 10
ENTRIES = 160
TASKS = 48
TASK_STEP = 8
BLOCK_STEP = 16
COPY_STEP = 4


def iota(shape, dim):
    return lax.broadcasted_iota(jnp.int32, shape, dim)


def dot_nn(a, b):
    return lax.dot_general(a, b, (((1,), (0,)), ((), ())), preferred_element_type=F32)


def dot_nt(a, b):
    return lax.dot_general(a, b, (((1,), (1,)), ((), ())), preferred_element_type=F32)


def dot_tn(a, b):
    return lax.dot_general(a, b, (((0,), (0,)), ((), ())), preferred_element_type=F32)


def as_bf16(mask):
    return jnp.where(mask, 1.0, 0.0).astype(BF16)


def split2(x):
    high = x.astype(BF16)
    return high, (x - high.astype(F32)).astype(BF16)


def split3(x):
    high = x.astype(BF16)
    rest = x - high.astype(F32)
    mid = rest.astype(BF16)
    return high, mid, (rest - mid.astype(F32)).astype(BF16)


def span_of(row):
    return pl.ds(pl.multiple_of(row * LANES, LANES), LANES)


def strict_upper(size):
    return as_bf16(iota((size, size), 0) < iota((size, size), 1))


def take_lanes(row, index):
    table = jnp.broadcast_to(row, index.shape)
    return jnp.take_along_axis(table, index, axis=1, mode="promise_in_bounds")


def gather_chunks(rows_of, fields, chunks, ids):
    high = ids >> 7
    low = ids & (LANES - 1)
    found = [jnp.zeros(ids.shape, F32) for _ in range(fields)]
    for chunk in range(chunks):
        here = high == chunk
        for field in range(fields):
            found[field] = jnp.where(here, take_lanes(rows_of(field, chunk), low), found[field])
    return found


def scatter_terms(id_rows, force_rows):
    wide = []
    table = []
    for ids, forces in zip(id_rows, force_rows):
        here = jnp.broadcast_to(ids >> 7, (GROUP, LANES)) == iota((GROUP, LANES), 0)
        wide.append(
            jnp.concatenate(
                [jnp.where(here, jnp.broadcast_to(f, (GROUP, LANES)), 0.0) for f in forces], axis=0
            )
        )
        low = jnp.broadcast_to(ids & (LANES - 1), (LANES, LANES))
        table.append(as_bf16(low == iota((LANES, LANES), 0)))
    high, rest = split2(jnp.concatenate(wide, axis=1))
    both = jnp.concatenate([high, rest], axis=0)
    return dot_nt(both, jnp.concatenate(table, axis=1))


def fold_terms(acc):
    half = acc.shape[0] // 2
    return acc[:half] + acc[half:]


def routing_kernel(rows_per, own_ref, count_ref, map_ref, pairs_ref, index_ref):
    own = own_ref[0]
    rows = map_ref.shape[0]
    devices = rows // rows_per
    pairs = pairs_ref.shape[1]
    hit = as_bf16(map_ref[...] == own)
    source_of = iota((devices, rows), 1) // rows_per
    upto = as_bf16(source_of <= iota((devices, rows), 0))
    within = as_bf16(source_of == iota((devices, rows), 0))
    ends = jnp.sum(dot_nn(upto, hit), axis=1, keepdims=True)
    counts = jnp.sum(dot_nn(within, hit), axis=1, keepdims=True)
    ranks = pairs_ref[...].astype(F32)
    for side in range(2):
        rank = ranks[side : side + 1]
        below = jnp.broadcast_to(ends, (devices, pairs)) <= rank
        source = jnp.sum(jnp.where(below, 1.0, 0.0), axis=0, keepdims=True)
        source = jnp.minimum(source, devices - 1.0)
        start = jnp.sum(jnp.where(below, counts, 0.0), axis=0, keepdims=True)
        index_ref[2 * side : 2 * side + 1, :] = source.astype(jnp.int32)
        index_ref[2 * side + 1 : 2 * side + 2, :] = (rank - start).astype(jnp.int32)


def request_kernel(rows_per, count_ref, map_ref, pairs_ref, masks_ref, out_ref):
    own = lax.axis_index("gx") * lax.axis_size("gy") + lax.axis_index("gy")
    rows = map_ref.shape[0]
    devices = rows // rows_per
    pairs = pairs_ref.shape[1]
    hit = as_bf16(map_ref[...] == own)
    source_of = iota((devices, rows), 1) // rows_per
    upto = as_bf16(source_of <= iota((devices, rows), 0))
    within = as_bf16(source_of == iota((devices, rows), 0))
    ends = jnp.sum(dot_nn(upto, hit), axis=1, keepdims=True)
    counts = jnp.sum(dot_nn(within, hit), axis=1, keepdims=True)
    ranks = pairs_ref[...].astype(F32)
    where_is = []
    for side in range(2):
        rank = ranks[side : side + 1]
        below = jnp.broadcast_to(ends, (devices, pairs)) <= rank
        source = jnp.sum(jnp.where(below, 1.0, 0.0), axis=0, keepdims=True)
        source = jnp.minimum(source, devices - 1.0)
        start = jnp.sum(jnp.where(below, counts, 0.0), axis=0, keepdims=True)
        where_is.append((source, rank - start))
    (slave, slave_rank), (master, master_rank) = where_is
    lane = iota((1, pairs), 1)
    live = lane < jnp.broadcast_to(count_ref[...], (1, pairs))
    me = own.astype(F32)
    device = iota((devices, pairs), 0).astype(F32)
    earlier = strict_upper(pairs)

    def pick(target, keep):
        return jnp.where((device == target) & keep, 1.0, 0.0)

    def turns(worker):
        tasks = pick(worker, live)
        ahead = dot_nn(tasks.astype(BF16), earlier)
        return tasks, jnp.sum(tasks * ahead, axis=0, keepdims=True)

    worker = jnp.where(lane == 0, me, slave)
    for other in (master, me):
        tasks, turn = turns(worker)
        worker = jnp.where((turn >= TASK_CAP) & (worker != me), other, worker)
    tasks, turn = turns(worker)
    room = turn < jnp.where(worker == me, float(OWN_CAP), float(TASK_CAP))
    send_slave = live & (slave != worker)
    send_master = live & (master != worker)
    from_slave = pick(slave, send_slave)
    from_master = pick(master, send_master)
    both = from_slave + from_master
    ahead = dot_nn(both.astype(BF16), earlier)
    slave_at = jnp.sum(from_slave * ahead, axis=0, keepdims=True)
    master_at = jnp.sum(from_master * ahead, axis=0, keepdims=True)
    master_at = master_at + jnp.where(send_slave & (slave == master), 1.0, 0.0)

    column = iota((LANES, pairs), 0).astype(F32)

    def placed(first, fields, fits):
        total = jnp.zeros((LANES, pairs), F32)
        for at, field in enumerate(fields):
            total = jnp.where((column == first + at) & fits, field, total)
        return total.astype(BF16)

    zero = jnp.zeros_like(slave)
    entry = placed(ENTRY_LANE + 3 * slave_at, (zero, slave_rank, worker), slave_at < ENTRY_CAP)
    line = dot_nt(from_slave.astype(BF16), entry)
    entry = placed(
        ENTRY_LANE + 3 * master_at, (zero + 1.0, master_rank, worker), master_at < ENTRY_CAP
    )
    line = line + dot_nt(from_master.astype(BF16), entry)
    entry = placed(
        TASK_LANE + TASK_FIELDS * turn,
        (slave, slave_rank, master, master_rank, lane.astype(F32)),
        room,
    )
    line = line + dot_nt(tasks.astype(BF16), entry)
    entry_count = jnp.sum(both, axis=1, keepdims=True)
    task_count = jnp.sum(tasks, axis=1, keepdims=True)
    limit = jnp.where(iota((devices, 1), 0) == own, float(OWN_CAP), float(TASK_CAP))
    over = jnp.where((entry_count > ENTRY_CAP) | (task_count > limit), 1.0, 0.0)
    over = jnp.max(over, axis=0, keepdims=True)
    spot = iota((devices, LANES), 1)
    line = jnp.where(spot == 0, entry_count, line)
    line = jnp.where(spot == 1, task_count, line)
    line = jnp.where(spot == 2, over, line)
    out_ref[:, 0, :] = line.astype(jnp.int32)
    chosen = [jnp.where(turn == t, tasks, 0.0) for t in range(TASK_CAP)]
    chosen = jnp.concatenate(chosen, axis=0).astype(BF16)
    masks = jnp.concatenate([masks_ref[0], masks_ref[1]], axis=1).astype(F32).astype(BF16)
    got = dot_nn(chosen, masks).astype(jnp.int32)
    for t in range(TASK_CAP):
        part = got[t * devices : (t + 1) * devices]
        out_ref[:, 1 + 2 * t, :] = part[:, :LANES]
        out_ref[:, 2 + 2 * t, :] = part[:, LANES:]
    for row in range(1 + 2 * TASK_CAP, REQUEST_ROWS):
        out_ref[:, row, :] = jnp.zeros((devices, LANES), jnp.int32)


def segment_kernel(
    cap,
    rows_per,
    own_ref,
    map_ref,
    disp_ref,
    nodes_ref,
    moved_ref,
    block_ref,
    group_ref,
    sem,
):
    chunks = disp_ref.shape[1] // LANES
    first = own_ref[0] * rows_per
    start = pl.multiple_of(first // 8 * 8, 8)
    move = pltpu.make_async_copy(map_ref.at[pl.ds(start, 8), :], group_ref, sem)
    move.start()

    def step(turn, carry):
        base = pl.multiple_of(turn * 8, 8)
        ids = nodes_ref[pl.ds(base, 8), :]
        found = gather_chunks(
            lambda field, chunk: disp_ref[field : field + 1, chunk * LANES : (chunk + 1) * LANES],
            3,
            chunks,
            ids,
        )
        for field in range(3):
            moved_ref[field, pl.ds(base, 8), :] = found[field]
        return carry

    lax.fori_loop(0, nodes_ref.shape[0] // 8, step, 0, unroll=2)
    move.wait()
    owner = jnp.concatenate(
        [group_ref[pl.ds(first - start + i, 1), :] for i in range(rows_per)], axis=1
    )
    blocks = owner.shape[1]
    total = block_ref.shape[0] * LANES
    mine = iota((total // cap, blocks), 0) == owner
    before = dot_nn(as_bf16(mine), strict_upper(blocks))
    rank = jnp.sum(jnp.where(mine, before, 0.0), axis=0, keepdims=True).astype(jnp.int32)
    hit = as_bf16(iota((total, blocks), 0) == owner * cap + rank)
    high, rest = split2(iota((8, blocks), 1).astype(F32))
    table = (dot_nt(high, hit) + dot_nt(rest, hit)).astype(jnp.int32)
    for row in range(total // LANES):
        block_ref[row : row + 1, :] = table[0:1, row * LANES : (row + 1) * LANES]


def block_at(block_ref, slot):
    return block_ref[slot >> 7, slot & (LANES - 1)]


def plan_kernel(
    cap, list_ref, block_ref, moved_ref, rest_ref, angles_ref, out_ref, entry_ref, used_ref
):
    devices = list_ref.shape[0]

    def clear(device, carry):
        used_ref[0, device] = 0
        used_ref[1, device] = 0
        return carry

    lax.fori_loop(0, devices, clear, 0)

    def from_owner(owner, carry):
        def entry(turn, state):
            number, over = state
            at = ENTRY_LANE + 3 * turn
            role = list_ref[owner, at]
            block = block_at(block_ref, owner * cap + list_ref[owner, at + 1])
            worker = list_ref[owner, at + 2]
            first = used_ref[0, worker]
            back = used_ref[1, worker]
            after = first + 3 + 2 * role
            back_after = back + 3 - 2 * role
            used_ref[0, worker] = after
            used_ref[1, worker] = back_after
            fits = (after < SEND_ROWS) & (first <= SEND_ROWS - 5)
            fits = fits & (back_after <= BACK_ROWS) & (number < ENTRIES)

            @pl.when(fits)
            def _():
                for field in range(3):
                    out_ref[worker, pl.ds(first + field, 1), :] = (
                        moved_ref[field, pl.ds(block, 1), :] + rest_ref[field, pl.ds(block, 1), :]
                    )
                entry_ref[0, number] = block
                entry_ref[1, number] = role
                entry_ref[2, number] = worker
                entry_ref[3, number] = back
                out_ref[worker, pl.ds(first + 3, 2), :] = angles_ref[block]

            return (number + 1, jnp.where(fits, over, 1))

        entries, tasks, over = carry
        over = jnp.maximum(over, list_ref[owner, 2])
        entries, over = lax.fori_loop(
            0, jnp.minimum(list_ref[owner, 0], ENTRY_CAP), entry, (entries, over)
        )
        return (entries, tasks + list_ref[owner, 1], over)

    zero = jnp.int32(0)
    entries, tasks, over = lax.fori_loop(0, devices, from_owner, (zero, zero, zero))
    over = jnp.where(tasks > TASKS, 1, over)
    entry_ref[4, 0] = jnp.minimum(entries, ENTRIES)
    mark = jnp.full((devices, LANES), over.astype(F32), F32)
    out_ref[:, SEND_ROWS - 1, :] = mark


def table_kernel(
    cap,
    own_ref,
    list_ref,
    block_ref,
    request_ref,
    masks_ref,
    moved_ref,
    rest_ref,
    angles_ref,
    task_ref,
    near_ref,
    field_ref,
    used_ref,
):
    own = own_ref[0]
    devices = list_ref.shape[0]
    size = field_ref.shape[1]

    def clear(device, carry):
        used_ref[0, device] = 0
        used_ref[1, device] = 0
        return carry

    lax.fori_loop(0, devices, clear, 0)

    def from_owner(owner, carry):
        def task(turn, state):
            at = TASK_LANE + TASK_FIELDS * turn
            pair = list_ref[owner, at + 4]
            number, near = state
            for side in range(2):
                source = list_ref[owner, at + 2 * side]
                here = source == own
                block = block_at(block_ref, owner * cap + list_ref[owner, at + 2 * side + 1])
                used = used_ref[0, source]
                back = used_ref[1, source]
                used_ref[0, source] = jnp.where(here, used, used + 3 + 2 * side)
                used_ref[1, source] = jnp.where(here, back, back + 3 - 2 * side)
                task_ref[3 * side, number] = source
                task_ref[3 * side + 1, number] = jnp.where(
                    here, block, jnp.minimum(used, SEND_ROWS - 4 - 2 * side)
                )
                task_ref[3 * side + 2, number] = jnp.minimum(back, BACK_ROWS - 3 + 2 * side)
                base = 4 * side

                @pl.when(owner == own)
                def _():
                    mask = masks_ref[side, pl.ds(pair, 1), :]
                    field_ref[base + 3, pl.ds(number, 1), :] = mask.astype(F32)

                @pl.when(owner != own)
                def _():
                    mask = request_ref[owner, pl.ds(1 + 2 * turn + side, 1), :]
                    field_ref[base + 3, pl.ds(number, 1), :] = mask.astype(F32)

                spot = near

                @pl.when(here)
                def _():
                    near_ref[0, spot] = block
                    near_ref[1, spot] = (side * size + number) * 8
                    for field in range(3):
                        field_ref[base + field, pl.ds(number, 1), :] = (
                            moved_ref[field, pl.ds(block, 1), :]
                            + rest_ref[field, pl.ds(block, 1), :]
                        )
                    if side == 1:
                        both = angles_ref[block]
                        field_ref[8, pl.ds(number, 1), :] = both[0:1]
                        field_ref[9, pl.ds(number, 1), :] = both[1:2]

                near = near + jnp.where(here, 1, 0)
            return (number + 1, near)

        number, near = carry
        count = jnp.minimum(list_ref[owner, 1], jnp.where(owner == own, OWN_CAP, TASK_CAP))
        count = jnp.minimum(count, TASKS - number)
        return lax.fori_loop(0, count, task, (number, near))

    tasks, near = lax.fori_loop(0, devices, from_owner, (jnp.int32(0), jnp.int32(0)))
    task_ref[6, 0] = tasks
    near_ref[2, 0] = near


def pack_kernel(
    slots,
    rows_per,
    own_ref,
    map_ref,
    moved_ref,
    rest_ref,
    angles_ref,
    nodes_ref,
    out_ref,
    ids_ref,
):
    own = own_ref[0]
    devices = map_ref.shape[0] // rows_per
    owner = jnp.concatenate(
        [map_ref[pl.ds(own * rows_per + i, 1), :] for i in range(rows_per)], axis=1
    )
    blocks = owner.shape[1]
    mine = iota((devices, blocks), 0) == owner
    before = dot_nn(as_bf16(mine), strict_upper(blocks))
    rank = jnp.sum(jnp.where(mine, before, 0.0), axis=0, keepdims=True).astype(jnp.int32)
    place = owner * slots + rank
    move = as_bf16(iota((devices * slots, blocks), 0) == place)
    for field in range(5):
        if field < 3:
            values = moved_ref[field] + rest_ref[field]
        else:
            values = angles_ref[:, field - 3, :]
        moved = dot_nn(move, jnp.concatenate(split3(values), axis=1))
        moved = moved[:, :LANES] + moved[:, LANES : 2 * LANES] + moved[:, 2 * LANES :]
        out_ref[:, field * slots : (field + 1) * slots, :] = moved.reshape(devices, slots, LANES)
    nodes = nodes_ref[...]
    halves = jnp.concatenate(
        [(nodes >> 7).astype(F32).astype(BF16), (nodes & (LANES - 1)).astype(F32).astype(BF16)],
        axis=1,
    )
    moved = dot_nn(move, halves)
    ids_ref[...] = (moved[:, :LANES] * LANES + moved[:, LANES:]).astype(jnp.int32)


def sine_cosine(angle):
    half = 0.5 * angle
    sq = half * half
    sine = sq * (-1.0 / 39916800.0) + 1.0 / 362880.0
    for coef in (-1.0 / 5040.0, 1.0 / 120.0, -1.0 / 6.0, 1.0):
        sine = sine * sq + coef
    sine = sine * half
    cosine = sq * (1.0 / 479001600.0) - 1.0 / 3628800.0
    for coef in (1.0 / 40320.0, -1.0 / 720.0, 1.0 / 24.0, -0.5, 1.0):
        cosine = cosine * sq + coef
    return 2.0 * sine * cosine, 1.0 - 2.0 * sine * sine


def pair_kernel(
    slots, index_ref, count_ref, in_ref, masks_ref, out_ref, slave_ref, master_ref, sin_ref, cos_ref
):
    pairs = masks_ref.shape[1]
    count = jnp.minimum(count_ref[0], pairs)
    out_ref[...] = jnp.zeros_like(out_ref)

    def stage(pair, carry):
        source = index_ref[0, pair]
        slot = index_ref[1, pair]
        for field in range(3):
            slave_ref[pl.ds(pair * 8 + field, 1), :] = in_ref[source, pl.ds(field * slots + slot, 1), :]
        slave_ref[pl.ds(pair * 8 + 3, 1), :] = masks_ref[0, pl.ds(pair, 1), :].astype(F32)
        source = index_ref[2, pair]
        slot = index_ref[3, pair]
        for field in range(5):
            master_ref[pl.ds(pair * 8 + field, 1), :] = in_ref[source, pl.ds(field * slots + slot, 1), :]
        master_ref[pl.ds(pair * 8 + 5, 1), :] = masks_ref[1, pl.ds(pair, 1), :].astype(F32)
        return carry

    lax.fori_loop(0, count, stage, 0)
    sines, cosines = sine_cosine(master_ref[...])
    sin_ref[...] = sines
    cos_ref[...] = cosines

    def tile(pair, carry):
        base = pl.multiple_of(pair * 8, 8)
        slave = slave_ref[pl.ds(base, 8), :]
        columns = jnp.transpose(slave)
        master = master_ref[pl.ds(base, 8), :]
        sin_az = sin_ref[pl.ds(base + 3, 1), :]
        sin_pol = sin_ref[pl.ds(base + 4, 1), :]
        cos_az = cos_ref[pl.ds(base + 3, 1), :]
        cos_pol = cos_ref[pl.ds(base + 4, 1), :]
        normal = [cos_az * cos_pol, sin_az * cos_pol, sin_pol]
        shape = (LANES, LANES)
        dist = [
            jnp.broadcast_to(columns[:, k : k + 1], shape) - jnp.broadcast_to(master[k : k + 1], shape)
            for k in range(3)
        ]
        gap = dist[0] * normal[0] + dist[1] * normal[1] + dist[2] * normal[2]
        tang = dist[0] * dist[0] + dist[1] * dist[1] + dist[2] * dist[2] - gap * gap
        bend = gap * (-1.0 / PEN_DEPTH)
        soft = jnp.maximum(bend, 0.0) + jnp.log(1.0 + jnp.exp(-jnp.abs(bend)))
        press = soft * jnp.exp(-0.5 * tang)
        press = press * jnp.broadcast_to(columns[:, 3:4], shape)
        total = jnp.sum(press, axis=0, keepdims=True)
        scale = PEN_STIFF * PEN_DEPTH * master[5:6]
        push = [n * scale for n in normal]
        rows = jnp.concatenate(push + [jnp.zeros((5, LANES), F32)], axis=0)
        push_high, push_rest = split2(rows)
        both = jnp.concatenate([push_high, push_rest], axis=0)
        high, rest = split2(press)
        got = dot_nt(both, high) + dot_nt(both, rest)
        on_slave = got[0:8] + got[8:16]
        source = index_ref[0, pair]
        slot = index_ref[1, pair]
        for k in range(3):
            at = pl.ds(k * slots + slot, 1)
            out_ref[source, at, :] = out_ref[source, at, :] + on_slave[k : k + 1]
        source = index_ref[2, pair]
        slot = index_ref[3, pair]
        for k in range(3):
            at = pl.ds(k * slots + slot, 1)
            out_ref[source, at, :] = out_ref[source, at, :] - push[k] * total
        return carry

    lax.fori_loop(0, count, tile, 0)


def work_kernel(
    own_ref,
    task_ref,
    in_ref,
    start_ref,
    back_ref,
    force_ref,
    over_ref,
    field_ref,
    left_ref,
    gap_ref,
    far_ref,
    push_ref,
):
    own = own_ref[0]
    count = task_ref[6, 0]
    field_ref[...] = start_ref[...]
    over = jnp.max(in_ref[:, SEND_ROWS - 1, :])
    over_ref[0] = over.astype(jnp.int32)
    marks = force_ref.shape[0] - 8
    force_ref[marks:, :] = jnp.full((8, LANES), over, F32)

    def stage(step, carry):
        rows = []
        for k in range(COPY_STEP):
            task = jnp.minimum(COPY_STEP * step + k, count - 1)
            for side in range(2):
                source = task_ref[3 * side, task]
                first = jnp.minimum(task_ref[3 * side + 1, task], SEND_ROWS - 4 - 2 * side)
                places = range(3) if side == 0 else (4, 5, 6, 8, 9)
                for row, place in enumerate(places):
                    got = in_ref[source, pl.ds(first + row, 1), :]
                    here = start_ref[place, pl.ds(task, 1), :]
                    rows.append((place, task, jnp.where(source != own, got, here)))
        for place, task, row in rows:
            field_ref[place, pl.ds(task, 1), :] = row
        return carry

    lax.fori_loop(0, (count + COPY_STEP - 1) // COPY_STEP, stage, 0)
    size = field_ref.shape[1]
    slave = [field_ref[k] for k in range(3)]
    master = [field_ref[4 + k] for k in range(3)]
    sin_az, cos_az = sine_cosine(field_ref[8])
    sin_pol, cos_pol = sine_cosine(field_ref[9])
    normal = [cos_az * cos_pol, sin_az * cos_pol, sin_pol]

    def inner(a, b):
        return a[0] * b[0] + a[1] * b[1] + a[2] * b[2]

    zero = jnp.zeros_like(sin_pol)
    one = zero + 1.0
    slope = -1.0 / PEN_DEPTH
    hidden = 30000.0
    slave_bias = -0.5 * inner(slave, slave) - hidden * (1.0 - field_ref[3])
    master_bias = -0.5 * inner(master, master) - hidden * (1.0 - field_ref[7])
    stacks = (
        (left_ref, slave + [one, slave_bias]),
        (gap_ref, [slope * n for n in normal] + [-slope * inner(normal, master), zero]),
        (far_ref, master + [master_bias, one]),
        (push_ref, [PEN_STIFF * PEN_DEPTH * n for n in normal] + [zero, zero]),
    )
    for ref, rows in stacks:
        for row, value in enumerate(rows + [zero] * 3):
            parts = split3(value)
            for part in range(ref.shape[0]):
                ref[part, pl.ds(row, size, stride=8), :] = parts[part].astype(F32)

    def tile(step, carry):
        tasks = [TASK_STEP * step + k for k in range(TASK_STEP)]
        bases = [pl.multiple_of(task * 8, 8) for task in tasks]
        fields = []
        for base in bases:
            high, mid, low = [left_ref[p, pl.ds(base, 8), :] for p in range(3)]
            left = jnp.concatenate([high, high, mid, mid, high, low], axis=0).astype(BF16)
            sides = []
            for ref in (gap_ref, far_ref):
                high, mid, low = [ref[p, pl.ds(base, 8), :] for p in range(3)]
                sides.append(jnp.concatenate([high, mid, high, mid, low, high], axis=0))
            fields.append(dot_tn(left, jnp.concatenate(sides, axis=1).astype(BF16)))
        presses = []
        for field in fields:
            bend = field[:, :LANES]
            power = field[:, LANES:] + bend * bend * (0.5 * PEN_DEPTH * PEN_DEPTH)
            soft = jnp.maximum(bend, 0.0) + jnp.log(1.0 + jnp.exp(-jnp.abs(bend)))
            presses.append(soft * jnp.exp(power))
        results = []
        for base, press in zip(bases, presses):
            push = jnp.concatenate([push_ref[p, pl.ds(base, 8), :] for p in range(2)], axis=0)
            push = push.astype(BF16)
            got = dot_nt(
                jnp.concatenate([push, push], axis=1), jnp.concatenate(split2(press), axis=1)
            )
            total = jnp.sum(press, axis=0, keepdims=True)
            results.append((got[0:8] + got[8:16], total * (PEN_STIFF * PEN_DEPTH)))
        for task, base, (on_slave, total) in zip(tasks, bases, results):
            normals = gap_ref[0, pl.ds(base, 8), :] + gap_ref[1, pl.ds(base, 8), :]
            normals = normals + gap_ref[2, pl.ds(base, 8), :]
            force_ref[pl.ds(base, 8), :] = on_slave
            force_ref[pl.ds(base + size * 8, 8), :] = normals * (total * (-1.0 / slope))
            live = task < count
            slave_from = task_ref[0, task]
            master_from = task_ref[3, task]

            @pl.when(live & (slave_from != own))
            def _():
                for k in range(3):
                    back_ref[slave_from, :, span_of(task_ref[2, task] + k)] = on_slave[k : k + 1]

            @pl.when(live & (master_from != own))
            def _():
                back_ref[master_from, :, span_of(task_ref[5, task])] = total

        return carry

    lax.fori_loop(0, (count + TASK_STEP - 1) // TASK_STEP, tile, 0)


def near_kernel(
    near_ref,
    entry_ref,
    nodes_ref,
    force_ref,
    inner_ref,
    whole_ref,
    angles_ref,
    out_ref,
    normal_ref,
):
    count = near_ref[2, 0]

    def step(turn, acc):
        ids = []
        forces = []
        for k in range(BLOCK_STEP):
            valid = BLOCK_STEP * turn + k < count
            number = jnp.where(valid, BLOCK_STEP * turn + k, 0)
            ids.append(nodes_ref[pl.ds(near_ref[0, number], 1), :])
            rows = force_ref[pl.ds(pl.multiple_of(near_ref[1, number], 8), 8), :]
            rows = jnp.where(valid, rows, 0.0)
            forces.append([rows[f : f + 1] for f in range(3)])
        return acc + scatter_terms(ids, forces)

    steps = (count + BLOCK_STEP - 1) // BLOCK_STEP
    acc = lax.fori_loop(0, steps, step, jnp.zeros((6 * GROUP, LANES), F32))
    marks = force_ref[force_ref.shape[0] - 8 :, :]
    total = fold_terms(acc)
    rows = total.shape[0]
    total = jnp.where(marks[0:1] > 0.0, whole_ref[:rows, :], total)
    out_ref[:rows, :] = inner_ref[...] + total
    out_ref[rows:, :] = marks
    entries = jnp.where(jnp.max(marks) > 0.0, 0, entry_ref[4, 0])

    def turn_angles(turn, carry):
        both = []
        for k in range(8):
            block = entry_ref[0, jnp.minimum(8 * turn + k, entries - 1)]
            both.append(angles_ref[block])
        azimuth = jnp.concatenate([pair[0:1] for pair in both], axis=0)
        polar = jnp.concatenate([pair[1:2] for pair in both], axis=0)
        sin_az, cos_az = sine_cosine(azimuth)
        sin_pol, cos_pol = sine_cosine(polar)
        at = pl.ds(pl.multiple_of(turn * 8, 8), 8)
        normal_ref[0, at, :] = cos_az * cos_pol
        normal_ref[1, at, :] = sin_az * cos_pol
        normal_ref[2, at, :] = sin_pol
        return carry

    lax.fori_loop(0, (entries + 7) // 8, turn_angles, 0)


def far_kernel(
    chunks,
    grid,
    own_ref,
    entry_ref,
    back_ref,
    nodes_ref,
    normal_ref,
    near_ref,
    faces_ref,
    out_ref,
    send_ref,
    value_ref,
):
    rows = out_ref.shape[0]
    count = jnp.where(jnp.max(near_ref[rows:, :]) > 0.0, 0, entry_ref[4, 0])

    def step(turn, acc):
        ids = []
        forces = []
        for k in range(BLOCK_STEP):
            valid = BLOCK_STEP * turn + k < count
            number = jnp.where(valid, BLOCK_STEP * turn + k, 0)
            block = entry_ref[0, number]
            role = entry_ref[1, number]
            worker = entry_ref[2, number]
            first = entry_ref[3, number]
            ids.append(nodes_ref[pl.ds(block, 1), :])
            total = back_ref[worker, :, span_of(first)]
            rows = []
            for field in range(3):
                row = back_ref[worker, :, span_of(jnp.minimum(first + field, BACK_ROWS - 1))]
                row = jnp.where(role == 1, -normal_ref[field, pl.ds(number, 1), :] * total, row)
                rows.append(jnp.where(valid, row, 0.0))
            forces.append(rows)
        return acc + scatter_terms(ids, forces)

    steps = (count + BLOCK_STEP - 1) // BLOCK_STEP
    acc = lax.fori_loop(0, steps, step, jnp.zeros((6 * GROUP, LANES), F32))
    out_ref[...] = near_ref[:rows, :] + fold_terms(acc)
    send_faces(own_ref[0], grid, out_ref, chunks, faces_ref, send_ref, value_ref)


def element_kernel(conn_ref, coords_ref, disp_ref, modulus_ref, out_ref, order_ref):
    chunks = coords_ref.shape[1] // LANES
    groups = conn_ref.shape[1] // LANES
    for group in range(groups):
        order_ref[pl.ds(group * 8, 8), :] = conn_ref[:, group * LANES : (group + 1) * LANES]
    pos = []
    disp = []
    for corner in range(8):
        ids = order_ref[pl.ds(corner, groups, stride=8), :]
        found = gather_chunks(
            lambda field, chunk: (coords_ref if field < 3 else disp_ref)[
                field % 3 : field % 3 + 1, chunk * LANES : (chunk + 1) * LANES
            ],
            6,
            chunks,
            ids,
        )
        pos.append(found[:3])
        disp.append(found[3:])
    first = list(pos[0])
    pos = [[pos[corner][j] - first[j] for j in range(3)] for corner in range(8)]

    def signed(values, signs):
        total = None
        for value, sign in zip(values, signs):
            if total is None:
                total = value if sign > 0 else -value
            else:
                total = total + value if sign > 0 else total - value
        return total

    corner_signs = [[XI_SIGNS[corner][k] for corner in range(8)] for k in range(3)]
    jac = [
        [signed([pos[c][j] for c in range(8)], corner_signs[k]) * 0.125 for k in range(3)]
        for j in range(3)
    ]
    cof = [
        [
            jac[(j + 1) % 3][(k + 1) % 3] * jac[(j + 2) % 3][(k + 2) % 3]
            - jac[(j + 1) % 3][(k + 2) % 3] * jac[(j + 2) % 3][(k + 1) % 3]
            for k in range(3)
        ]
        for j in range(3)
    ]
    det = jac[0][0] * cof[0][0] + jac[0][1] * cof[0][1] + jac[0][2] * cof[0][2]
    volume = 8.0 * det
    inverse = 1.0 / volume
    scaled = [[cof[j][k] * inverse for k in range(3)] for j in range(3)]
    grad = [[signed(scaled[j], XI_SIGNS[c]) for j in range(3)] for c in range(8)]

    def summed(terms):
        total = terms[0]
        for term in terms[1:]:
            total = total + term
        return total

    ugrad = [
        [summed([disp[c][i] * grad[c][j] for c in range(8)]) for j in range(3)] for i in range(3)
    ]
    modulus = modulus_ref[...]
    dilation = ugrad[0][0] + ugrad[1][1] + ugrad[2][2]
    stress = [[modulus * (ugrad[i][j] + ugrad[j][i]) for j in range(3)] for i in range(3)]
    for i in range(3):
        stress[i][i] = stress[i][i] + modulus * dilation
    squares = summed([grad[c][j] * grad[c][j] for c in range(8) for j in range(3)])
    hour_coef = HG_COEF * modulus * volume * squares
    shapes = []
    modes = []
    for a in range(4):
        hour_pos = [signed([pos[c][j] for c in range(8)], HOUR_VEC[a]) for j in range(3)]
        gam = [
            float(HOUR_VEC[a][c]) - summed([hour_pos[j] * grad[c][j] for j in range(3)])
            for c in range(8)
        ]
        shapes.append(gam)
        modes.append(
            [hour_coef * summed([disp[c][i] * gam[c] for c in range(8)]) for i in range(3)]
        )
    flux = [[volume * stress[i][j] for j in range(3)] for i in range(3)]
    acc = jnp.zeros((6 * GROUP, LANES), F32)
    for corner in range(8):
        ids = order_ref[pl.ds(corner, groups, stride=8), :]
        force = []
        for i in range(3):
            value = summed([flux[i][j] * grad[corner][j] for j in range(3)])
            value = value + summed([modes[a][i] * shapes[a][corner] for a in range(4)])
            force.append(-value)
        for group in range(0, groups, 2):
            picks = range(group, min(group + 2, groups))
            acc = acc + scatter_terms(
                [ids[g : g + 1] for g in picks], [[f[g : g + 1] for f in force] for g in picks]
            )
    out_ref[...] = fold_terms(acc)


def around(grid):
    return [(dx, dy) for dx in (-1, 0, 1) for dy in (-1, 0, 1) if (dx, dy) != (0, 0)]


def face_toward(dx, dy):
    if dx:
        return 1 if dx > 0 else 0
    return 3 if dy > 0 else 2


def neighbour(own, grid, dx, dy):
    ix = own // grid[1] + dx
    iy = own % grid[1] + dy
    there = (ix >= 0) & (ix < grid[0]) & (iy >= 0) & (iy < grid[1])
    return there, jnp.where(there, ix * grid[1] + iy, 0)


def send_faces(own, grid, total_ref, chunks, faces_ref, send_ref, value_ref):
    value_ref[...] = jnp.zeros_like(value_ref)
    parts = faces_ref.shape[1] // LANES
    for part in range(parts):
        ids = faces_ref[:, part * LANES : (part + 1) * LANES]
        found = gather_chunks(
            lambda field, chunk: total_ref[field * GROUP + chunk : field * GROUP + chunk + 1, :],
            3,
            chunks,
            ids,
        )
        for field in range(3):
            at = field * parts + part
            for face in range(4):
                value_ref[face, at : at + 1, :] = found[field][face : face + 1]
    for dx, dy in around(grid):
        there, target = neighbour(own, grid, dx, dy)

        @pl.when(there)
        def _():
            for row in range(3 * parts):
                span = slice(row * LANES, (row + 1) * LANES)
                send_ref[target, :, span] = value_ref[face_toward(dx, dy), row : row + 1, :]


def face_map_kernel(chunks, faces_ref, low_ref, high_ref, table_ref):
    parts = faces_ref.shape[1] // LANES
    acc = None
    for row in range(2):
        ids = [faces_ref[row : row + 1, p * LANES : (p + 1) * LANES] for p in range(parts)]
        zero = jnp.zeros((1, LANES), F32)
        places = [(iota((1, LANES), 1) + (p * LANES + 1)).astype(F32) for p in range(parts)]
        fields = [[place if f == row else zero for f in range(3)] for place in places]
        terms = scatter_terms(ids, fields)
        acc = terms if acc is None else acc + terms
    table_ref[...] = fold_terms(acc)
    low_ref[...] = jnp.zeros_like(low_ref)
    high_ref[...] = jnp.zeros_like(high_ref)
    for part in range(parts):
        ids = faces_ref[:, part * LANES : (part + 1) * LANES]
        found = gather_chunks(
            lambda field, chunk: table_ref[field * GROUP + chunk : field * GROUP + chunk + 1, :],
            2,
            chunks,
            ids,
        )
        for field in range(2):
            at = field * parts + part
            low_ref[at : at + 1, :] = found[field][2:3]
            high_ref[at : at + 1, :] = found[field][3:4]


def moved_faces(values, places, parts):
    results = [None] * (3 * parts)
    for part in range(parts):
        place = places[part].astype(jnp.int32) - 1
        low = jnp.broadcast_to(place & (LANES - 1), values.shape)
        got = jnp.take_along_axis(values, low, axis=1, mode="promise_in_bounds")
        for field in range(3):
            total = jnp.zeros((1, LANES), F32)
            for source in range(parts):
                at = field * parts + source
                total = jnp.where(place >> 7 == source, got[at : at + 1], total)
            results[field * parts + part] = total
    return results


def assemble_kernel(slots, back_ref, ids_ref, out_ref):
    devices = back_ref.shape[0]

    def step(turn, acc):
        ids = ids_ref[pl.ds(turn * slots, slots), :]
        values = back_ref[turn]
        for slot in range(0, slots, 2):
            picks = range(slot, min(slot + 2, slots))
            acc = acc + scatter_terms(
                [ids[s : s + 1] for s in picks],
                [[values[f * slots + s : f * slots + s + 1] for f in range(3)] for s in picks],
            )
        return acc

    acc = lax.fori_loop(0, devices, step, jnp.zeros((6 * GROUP, LANES), F32))
    out_ref[...] = fold_terms(acc)


def final_kernel(
    grid, own_ref, total_ref, got_ref, low_ref, high_ref, faces_ref, velocity_ref, mass_ref, out_ref, sum_ref
):
    own = own_ref[0]
    parts = faces_ref.shape[1] // LANES

    def block(dx, dy):
        there, source = neighbour(own, grid, dx, dy)
        spans = [slice(row * LANES, (row + 1) * LANES) for row in range(3 * parts)]
        return [jnp.where(there, got_ref[source, :, span], 0.0) for span in spans]

    def side(dy, map_ref):
        rows = block(0, dy)
        for field, dx in enumerate((-1, 1)):
            places = [map_ref[field * parts + p : field * parts + p + 1, :] for p in range(parts)]
            corner = block(dx, dy)
            corner = corner + [jnp.zeros((1, LANES), F32)] * (-len(corner) % 8)
            moved = moved_faces(jnp.concatenate(corner, axis=0), places, parts)
            rows = [a + b for a, b in zip(rows, moved)]
        return rows

    added = [block(-1, 0), block(1, 0), side(-1, low_ref), side(1, high_ref)]
    acc = jnp.zeros((6 * GROUP, LANES), F32)
    for face, rows in enumerate(added):
        ids = [faces_ref[face : face + 1, p * LANES : (p + 1) * LANES] for p in range(parts)]
        acc = acc + scatter_terms(
            ids, [[rows[f * parts + p] for f in range(3)] for p in range(parts)]
        )
    sum_ref[...] = total_ref[...] + fold_terms(acc)
    for chunk in range(out_ref.shape[1] // LANES):
        span = slice(chunk * LANES, (chunk + 1) * LANES)
        scale = TIME_STEP / mass_ref[chunk : chunk + 1, :]
        for field in range(3):
            row = field * GROUP + chunk
            out_ref[field : field + 1, span] = (
                velocity_ref[field : field + 1, span] + scale * sum_ref[row : row + 1, :]
            )


def call(kernel, outs, in_smem, args, scratch=(), out_smem=(), in_any=()):
    def spec(smem, anywhere=False):
        if anywhere:
            return pl.BlockSpec(memory_space=pl.ANY)
        return pl.BlockSpec(memory_space=pltpu.SMEM if smem else pltpu.VMEM)

    return pl.pallas_call(
        kernel,
        out_shape=[jax.ShapeDtypeStruct(shape, dtype) for shape, dtype in outs],
        in_specs=[spec(i in in_smem, i in in_any) for i in range(len(args))],
        out_specs=[spec(i in out_smem) for i in range(len(outs))],
        scratch_shapes=list(scratch),
        compiler_params=pltpu.CompilerParams(vmem_limit_bytes=VMEM_LIMIT),
    )(*args)


def exchange(low, high, axis):
    count = lax.axis_size(axis)
    forward = [(i, i + 1) for i in range(count - 1)]
    backward = [(target, source) for source, target in forward]
    return lax.ppermute(high, axis, forward), lax.ppermute(low, axis, backward)


def local(
    connectivity,
    face_nodes,
    coords,
    displacement,
    velocity,
    node_mass,
    modulus,
    surf_nodes,
    surf_ref,
    surf_angles,
    owner_map,
    pair_blocks,
    pair_masks,
    pair_count,
):
    axes = ("gx", "gy")
    devices = lax.axis_size("gx") * lax.axis_size("gy")
    per_dev = surf_nodes.shape[0]
    rows_per = per_dev // LANES
    node_count = coords.shape[1]
    chunks = node_count // LANES
    slots = 2 * per_dev // devices
    pairs = pair_blocks.shape[1]
    own = lax.axis_index(axes).reshape(1).astype(jnp.int32)
    owners = owner_map.reshape(devices * rows_per, LANES)
    face_pad = -face_nodes.shape[1] % LANES
    faces = jnp.pad(face_nodes, ((0, 4), (0, face_pad)), constant_values=-1)
    parts = faces.shape[1] // LANES
    face_rows = -(-3 * parts // 8) * 8
    total_shape = ((3 * GROUP, LANES), F32)
    face_shape = ((face_rows, LANES), F32)
    send_shape = ((devices, 1, 3 * parts * LANES), F32)
    grid = (lax.axis_size("gx"), lax.axis_size("gy"))

    def to_all(values):
        return lax.all_to_all(values, axes, split_axis=0, concat_axis=0, tiled=True)

    [request] = call(
        functools.partial(request_kernel, rows_per),
        [((devices, REQUEST_ROWS, LANES), jnp.int32)],
        (),
        (pair_count.reshape(1, 1), owners, pair_blocks, pair_masks),
    )
    asked = to_all(request)
    rest = jnp.transpose(surf_ref, (1, 0, 2))
    moved, block_of = call(
        functools.partial(segment_kernel, slots, rows_per),
        [((3, per_dev, LANES), F32), ((devices * slots // LANES, LANES), jnp.int32)],
        (0,),
        (own, owners, displacement, surf_nodes),
        [pltpu.VMEM((8, LANES), jnp.int32), pltpu.SemaphoreType.DMA],
        (),
        (1,),
    )
    map_low, map_high = call(
        functools.partial(face_map_kernel, chunks),
        [face_shape, face_shape],
        (),
        (faces,),
        [pltpu.VMEM((3 * GROUP, LANES), F32)],
    )
    map_low, map_high = exchange(map_low, map_high, "gy")
    lists = asked[:, 0, :]
    outbound, entries = call(
        functools.partial(plan_kernel, slots),
        [((devices, SEND_ROWS, LANES), F32), ((8, ENTRIES), jnp.int32)],
        (0, 1),
        (lists, block_of, moved, rest, surf_angles),
        [pltpu.SMEM((2, devices), jnp.int32)],
        (1,),
    )
    tasks, near_list, fields = call(
        functools.partial(table_kernel, slots),
        [((8, TASKS), jnp.int32), ((8, 2 * TASKS), jnp.int32), ((10, TASKS, LANES), F32)],
        (0, 1, 2),
        (own, lists, block_of, asked, pair_masks, moved, rest, surf_angles),
        [pltpu.SMEM((2, devices), jnp.int32)],
        (0, 1),
    )
    inbound = to_all(outbound)
    inbound, map_low, map_high = lax.optimization_barrier((inbound, map_low, map_high))
    back, forces, over = call(
        work_kernel,
        [
            ((devices, 1, BACK_ROWS * LANES), F32),
            ((2 * TASKS * 8 + 8, LANES), F32),
            ((1,), jnp.int32),
        ],
        (0, 1),
        (own, tasks, inbound, fields),
        [
            pltpu.VMEM((10, TASKS, LANES), F32),
            pltpu.VMEM((3, TASKS * 8, LANES), F32),
            pltpu.VMEM((3, TASKS * 8, LANES), F32),
            pltpu.VMEM((3, TASKS * 8, LANES), F32),
            pltpu.VMEM((2, TASKS * 8, LANES), F32),
        ],
        (2,),
    )
    returned = to_all(back)

    def by_owners():
        [index] = call(
            functools.partial(routing_kernel, rows_per),
            [((4, pairs), jnp.int32)],
            (0, 1),
            (own, pair_count, owners, pair_blocks),
        )
        outbound, ids = call(
            functools.partial(pack_kernel, slots, rows_per),
            [((devices, 5 * slots, LANES), F32), ((devices * slots, LANES), jnp.int32)],
            (0,),
            (own, owners, moved, rest, surf_angles, surf_nodes),
        )
        [owned] = call(
            functools.partial(pair_kernel, slots),
            [((devices, 3 * slots, LANES), F32)],
            (0, 1),
            (index, pair_count, to_all(outbound), pair_masks),
            [pltpu.VMEM((pairs * 8, LANES), F32)] * 4,
        )
        [whole] = call(
            functools.partial(assemble_kernel, slots), [total_shape], (), (to_all(owned), ids)
        )
        return jnp.pad(whole, ((0, forces.shape[0] - whole.shape[0]), (0, 0)))

    whole = lax.cond(over[0] > 0, by_owners, lambda: forces)
    late, unused = lax.optimization_barrier((coords, over))
    [internal] = call(
        element_kernel,
        [total_shape],
        (),
        (connectivity, late, displacement, modulus.reshape(-1, LANES)),
        [pltpu.VMEM((connectivity.shape[1] // LANES * 8, LANES), jnp.int32)],
    )
    near, normals = call(
        near_kernel,
        [((3 * GROUP + 8, LANES), F32), ((3, ENTRIES, LANES), F32)],
        (0, 1),
        (near_list, entries, surf_nodes, forces, internal, whole, surf_angles),
    )
    total, send = call(
        functools.partial(far_kernel, chunks, grid),
        [total_shape, send_shape],
        (0, 1),
        (own, entries, returned, surf_nodes, normals, near, faces),
        [pltpu.VMEM((4,) + face_shape[0], F32)],
    )
    [result] = call(
        functools.partial(final_kernel, grid),
        [((3, node_count), F32)],
        (0,),
        (
            own,
            total,
            to_all(send),
            map_low,
            map_high,
            faces,
            velocity,
            node_mass.reshape(chunks, LANES),
        ),
        [pltpu.VMEM((3 * GROUP, LANES), F32)],
    )
    return result


def solution(mesh):
    in_specs = (
        P(None, ("gx", "gy")),
        P(None, ("gx", "gy")),
        P(None, ("gx", "gy")),
        P(None, ("gx", "gy")),
        P(None, ("gx", "gy")),
        P(("gx", "gy")),
        P(("gx", "gy")),
        P(("gx", "gy"), None),
        P(("gx", "gy"), None, None),
        P(("gx", "gy"), None, None),
        P(),
        P(None, ("gx", "gy")),
        P(None, ("gx", "gy"), None),
        P(("gx", "gy")),
    )
    out_specs = P(None, ("gx", "gy"))
    return jax.shard_map(local, mesh=mesh, in_specs=in_specs, out_specs=out_specs, check_vma=False)
```

```python
import functools

import jax
import jax.numpy as jnp
from jax import lax
from jax.experimental import pallas as pl
from jax.experimental.pallas import tpu as pltpu
from jax.sharding import PartitionSpec as P

XI_SIGNS = [
    [-1, -1, -1],
    [1, -1, -1],
    [1, 1, -1],
    [-1, 1, -1],
    [-1, -1, 1],
    [1, -1, 1],
    [1, 1, 1],
    [-1, 1, 1],
]
HOUR_VEC = [
    [1, 1, -1, -1, -1, -1, 1, 1],
    [1, -1, -1, 1, -1, 1, 1, -1],
    [1, -1, 1, -1, 1, -1, 1, -1],
    [-1, 1, -1, 1, 1, -1, 1, -1],
]
HG_COEF = 0.05
PEN_STIFF = 0.05
PEN_DEPTH = 0.5
TIME_STEP = 0.2
LANES = 128
GROUP = 16
F32 = jnp.float32
BF16 = jnp.bfloat16
VMEM_LIMIT = 48 * 1024 * 1024
REQUEST_ROWS = 8
TASK_CAP = 3
OWN_CAP = 12
TASK_LANE = 64
TASK_FIELDS = 5
ENTRY_LANE = 4
ENTRY_CAP = 20
SEND_ROWS = 32
BACK_ROWS = 12
ENTRIES = 160
TASKS = 48
TASK_STEP = 8
BLOCK_STEP = 16
COPY_STEP = 4


def iota(shape, dim):
    return lax.broadcasted_iota(jnp.int32, shape, dim)


def dot_nn(a, b):
    return lax.dot_general(a, b, (((1,), (0,)), ((), ())), preferred_element_type=F32)


def dot_nt(a, b):
    return lax.dot_general(a, b, (((1,), (1,)), ((), ())), preferred_element_type=F32)


def dot_tn(a, b):
    return lax.dot_general(a, b, (((0,), (0,)), ((), ())), preferred_element_type=F32)


def as_bf16(mask):
    return jnp.where(mask, 1.0, 0.0).astype(BF16)


def split2(x):
    high = x.astype(BF16)
    return high, (x - high.astype(F32)).astype(BF16)


def split3(x):
    high = x.astype(BF16)
    rest = x - high.astype(F32)
    mid = rest.astype(BF16)
    return high, mid, (rest - mid.astype(F32)).astype(BF16)


def span_of(row):
    return pl.ds(pl.multiple_of(row * LANES, LANES), LANES)


def strict_upper(size):
    return as_bf16(iota((size, size), 0) < iota((size, size), 1))


def take_lanes(row, index):
    table = jnp.broadcast_to(row, index.shape)
    return jnp.take_along_axis(table, index, axis=1, mode="promise_in_bounds")


def gather_chunks(rows_of, fields, chunks, ids):
    high = ids >> 7
    low = ids & (LANES - 1)
    found = [jnp.zeros(ids.shape, F32) for _ in range(fields)]
    for chunk in range(chunks):
        here = high == chunk
        for field in range(fields):
            found[field] = jnp.where(here, take_lanes(rows_of(field, chunk), low), found[field])
    return found


def scatter_terms(id_rows, force_rows):
    wide = []
    table = []
    for ids, forces in zip(id_rows, force_rows):
        here = jnp.broadcast_to(ids >> 7, (GROUP, LANES)) == iota((GROUP, LANES), 0)
        wide.append(
            jnp.concatenate(
                [jnp.where(here, jnp.broadcast_to(f, (GROUP, LANES)), 0.0) for f in forces], axis=0
            )
        )
        low = jnp.broadcast_to(ids & (LANES - 1), (LANES, LANES))
        table.append(as_bf16(low == iota((LANES, LANES), 0)))
    high, rest = split2(jnp.concatenate(wide, axis=1))
    both = jnp.concatenate([high, rest], axis=0)
    return dot_nt(both, jnp.concatenate(table, axis=1))


def fold_terms(acc):
    half = acc.shape[0] // 2
    return acc[:half] + acc[half:]


def routing_kernel(rows_per, own_ref, count_ref, map_ref, pairs_ref, index_ref):
    own = own_ref[0]
    rows = map_ref.shape[0]
    devices = rows // rows_per
    pairs = pairs_ref.shape[1]
    hit = as_bf16(map_ref[...] == own)
    source_of = iota((devices, rows), 1) // rows_per
    upto = as_bf16(source_of <= iota((devices, rows), 0))
    within = as_bf16(source_of == iota((devices, rows), 0))
    ends = jnp.sum(dot_nn(upto, hit), axis=1, keepdims=True)
    counts = jnp.sum(dot_nn(within, hit), axis=1, keepdims=True)
    ranks = pairs_ref[...].astype(F32)
    for side in range(2):
        rank = ranks[side : side + 1]
        below = jnp.broadcast_to(ends, (devices, pairs)) <= rank
        source = jnp.sum(jnp.where(below, 1.0, 0.0), axis=0, keepdims=True)
        source = jnp.minimum(source, devices - 1.0)
        start = jnp.sum(jnp.where(below, counts, 0.0), axis=0, keepdims=True)
        index_ref[2 * side : 2 * side + 1, :] = source.astype(jnp.int32)
        index_ref[2 * side + 1 : 2 * side + 2, :] = (rank - start).astype(jnp.int32)


def request_kernel(rows_per, count_ref, map_ref, pairs_ref, masks_ref, out_ref):
    own = lax.axis_index("gx") * lax.axis_size("gy") + lax.axis_index("gy")
    rows = map_ref.shape[0]
    devices = rows // rows_per
    pairs = pairs_ref.shape[1]
    hit = as_bf16(map_ref[...] == own)
    source_of = iota((devices, rows), 1) // rows_per
    upto = as_bf16(source_of <= iota((devices, rows), 0))
    within = as_bf16(source_of == iota((devices, rows), 0))
    ends = jnp.sum(dot_nn(upto, hit), axis=1, keepdims=True)
    counts = jnp.sum(dot_nn(within, hit), axis=1, keepdims=True)
    ranks = pairs_ref[...].astype(F32)
    where_is = []
    for side in range(2):
        rank = ranks[side : side + 1]
        below = jnp.broadcast_to(ends, (devices, pairs)) <= rank
        source = jnp.sum(jnp.where(below, 1.0, 0.0), axis=0, keepdims=True)
        source = jnp.minimum(source, devices - 1.0)
        start = jnp.sum(jnp.where(below, counts, 0.0), axis=0, keepdims=True)
        where_is.append((source, rank - start))
    (slave, slave_rank), (master, master_rank) = where_is
    lane = iota((1, pairs), 1)
    live = lane < jnp.broadcast_to(count_ref[...], (1, pairs))
    me = own.astype(F32)
    device = iota((devices, pairs), 0).astype(F32)
    earlier = strict_upper(pairs)

    def pick(target, keep):
        return jnp.where((device == target) & keep, 1.0, 0.0)

    def turns(worker):
        tasks = pick(worker, live)
        ahead = dot_nn(tasks.astype(BF16), earlier)
        return tasks, jnp.sum(tasks * ahead, axis=0, keepdims=True)

    worker = jnp.where(lane == 0, me, slave)
    for other in (master, me):
        tasks, turn = turns(worker)
        worker = jnp.where((turn >= TASK_CAP) & (worker != me), other, worker)
    tasks, turn = turns(worker)
    room = turn < jnp.where(worker == me, float(OWN_CAP), float(TASK_CAP))
    send_slave = live & (slave != worker)
    send_master = live & (master != worker)
    from_slave = pick(slave, send_slave)
    from_master = pick(master, send_master)
    both = from_slave + from_master
    ahead = dot_nn(both.astype(BF16), earlier)
    slave_at = jnp.sum(from_slave * ahead, axis=0, keepdims=True)
    master_at = jnp.sum(from_master * ahead, axis=0, keepdims=True)
    master_at = master_at + jnp.where(send_slave & (slave == master), 1.0, 0.0)

    column = iota((LANES, pairs), 0).astype(F32)

    def placed(first, fields, fits):
        total = jnp.zeros((LANES, pairs), F32)
        for at, field in enumerate(fields):
            total = jnp.where((column == first + at) & fits, field, total)
        return total.astype(BF16)

    zero = jnp.zeros_like(slave)
    entry = placed(ENTRY_LANE + 3 * slave_at, (zero, slave_rank, worker), slave_at < ENTRY_CAP)
    line = dot_nt(from_slave.astype(BF16), entry)
    entry = placed(
        ENTRY_LANE + 3 * master_at, (zero + 1.0, master_rank, worker), master_at < ENTRY_CAP
    )
    line = line + dot_nt(from_master.astype(BF16), entry)
    entry = placed(
        TASK_LANE + TASK_FIELDS * turn,
        (slave, slave_rank, master, master_rank, lane.astype(F32)),
        room,
    )
    line = line + dot_nt(tasks.astype(BF16), entry)
    entry_count = jnp.sum(both, axis=1, keepdims=True)
    task_count = jnp.sum(tasks, axis=1, keepdims=True)
    limit = jnp.where(iota((devices, 1), 0) == own, float(OWN_CAP), float(TASK_CAP))
    over = jnp.where((entry_count > ENTRY_CAP) | (task_count > limit), 1.0, 0.0)
    over = jnp.max(over, axis=0, keepdims=True)
    spot = iota((devices, LANES), 1)
    line = jnp.where(spot == 0, entry_count, line)
    line = jnp.where(spot == 1, task_count, line)
    line = jnp.where(spot == 2, over, line)
    out_ref[:, 0, :] = line.astype(jnp.int32)
    chosen = [jnp.where(turn == t, tasks, 0.0) for t in range(TASK_CAP)]
    chosen = jnp.concatenate(chosen, axis=0).astype(BF16)
    masks = jnp.concatenate([masks_ref[0], masks_ref[1]], axis=1).astype(F32).astype(BF16)
    got = dot_nn(chosen, masks).astype(jnp.int32)
    for t in range(TASK_CAP):
        part = got[t * devices : (t + 1) * devices]
        out_ref[:, 1 + 2 * t, :] = part[:, :LANES]
        out_ref[:, 2 + 2 * t, :] = part[:, LANES:]
    for row in range(1 + 2 * TASK_CAP, REQUEST_ROWS):
        out_ref[:, row, :] = jnp.zeros((devices, LANES), jnp.int32)


def segment_kernel(
    cap,
    rows_per,
    own_ref,
    map_ref,
    disp_ref,
    nodes_ref,
    moved_ref,
    block_ref,
    group_ref,
    sem,
):
    chunks = disp_ref.shape[1] // LANES
    first = own_ref[0] * rows_per
    start = pl.multiple_of(first // 8 * 8, 8)
    move = pltpu.make_async_copy(map_ref.at[pl.ds(start, 8), :], group_ref, sem)
    move.start()

    def step(turn, carry):
        base = pl.multiple_of(turn * 8, 8)
        ids = nodes_ref[pl.ds(base, 8), :]
        found = gather_chunks(
            lambda field, chunk: disp_ref[field : field + 1, chunk * LANES : (chunk + 1) * LANES],
            3,
            chunks,
            ids,
        )
        for field in range(3):
            moved_ref[field, pl.ds(base, 8), :] = found[field]
        return carry

    lax.fori_loop(0, nodes_ref.shape[0] // 8, step, 0, unroll=2)
    move.wait()
    owner = jnp.concatenate(
        [group_ref[pl.ds(first - start + i, 1), :] for i in range(rows_per)], axis=1
    )
    blocks = owner.shape[1]
    total = block_ref.shape[0] * LANES
    mine = iota((total // cap, blocks), 0) == owner
    before = dot_nn(as_bf16(mine), strict_upper(blocks))
    rank = jnp.sum(jnp.where(mine, before, 0.0), axis=0, keepdims=True).astype(jnp.int32)
    hit = as_bf16(iota((total, blocks), 0) == owner * cap + rank)
    high, rest = split2(iota((8, blocks), 1).astype(F32))
    table = (dot_nt(high, hit) + dot_nt(rest, hit)).astype(jnp.int32)
    for row in range(total // LANES):
        block_ref[row : row + 1, :] = table[0:1, row * LANES : (row + 1) * LANES]


def block_at(block_ref, slot):
    return block_ref[slot >> 7, slot & (LANES - 1)]


def plan_kernel(
    cap, list_ref, block_ref, moved_ref, rest_ref, angles_ref, out_ref, entry_ref, used_ref
):
    devices = list_ref.shape[0]

    def clear(device, carry):
        used_ref[0, device] = 0
        used_ref[1, device] = 0
        return carry

    lax.fori_loop(0, devices, clear, 0)

    def from_owner(owner, carry):
        def entry(turn, state):
            number, over = state
            at = ENTRY_LANE + 3 * turn
            role = list_ref[owner, at]
            block = block_at(block_ref, owner * cap + list_ref[owner, at + 1])
            worker = list_ref[owner, at + 2]
            first = used_ref[0, worker]
            back = used_ref[1, worker]
            after = first + 3 + 2 * role
            back_after = back + 3 - 2 * role
            used_ref[0, worker] = after
            used_ref[1, worker] = back_after
            fits = (after < SEND_ROWS) & (first <= SEND_ROWS - 5)
            fits = fits & (back_after <= BACK_ROWS) & (number < ENTRIES)

            @pl.when(fits)
            def _():
                for field in range(3):
                    out_ref[worker, pl.ds(first + field, 1), :] = (
                        moved_ref[field, pl.ds(block, 1), :] + rest_ref[field, pl.ds(block, 1), :]
                    )
                entry_ref[0, number] = block
                entry_ref[1, number] = role
                entry_ref[2, number] = worker
                entry_ref[3, number] = back
                out_ref[worker, pl.ds(first + 3, 2), :] = angles_ref[block]

            return (number + 1, jnp.where(fits, over, 1))

        entries, tasks, over = carry
        over = jnp.maximum(over, list_ref[owner, 2])
        entries, over = lax.fori_loop(
            0, jnp.minimum(list_ref[owner, 0], ENTRY_CAP), entry, (entries, over)
        )
        return (entries, tasks + list_ref[owner, 1], over)

    zero = jnp.int32(0)
    entries, tasks, over = lax.fori_loop(0, devices, from_owner, (zero, zero, zero))
    over = jnp.where(tasks > TASKS, 1, over)
    entry_ref[4, 0] = jnp.minimum(entries, ENTRIES)
    mark = jnp.full((devices, LANES), over.astype(F32), F32)
    out_ref[:, SEND_ROWS - 1, :] = mark


def table_kernel(
    cap,
    own_ref,
    list_ref,
    block_ref,
    request_ref,
    masks_ref,
    moved_ref,
    rest_ref,
    angles_ref,
    task_ref,
    near_ref,
    field_ref,
    used_ref,
):
    own = own_ref[0]
    devices = list_ref.shape[0]
    size = field_ref.shape[1]

    def clear(device, carry):
        used_ref[0, device] = 0
        used_ref[1, device] = 0
        return carry

    lax.fori_loop(0, devices, clear, 0)

    def from_owner(owner, carry):
        def task(turn, state):
            at = TASK_LANE + TASK_FIELDS * turn
            pair = list_ref[owner, at + 4]
            number, near = state
            for side in range(2):
                source = list_ref[owner, at + 2 * side]
                here = source == own
                block = block_at(block_ref, owner * cap + list_ref[owner, at + 2 * side + 1])
                used = used_ref[0, source]
                back = used_ref[1, source]
                used_ref[0, source] = jnp.where(here, used, used + 3 + 2 * side)
                used_ref[1, source] = jnp.where(here, back, back + 3 - 2 * side)
                task_ref[3 * side, number] = source
                task_ref[3 * side + 1, number] = jnp.where(
                    here, block, jnp.minimum(used, SEND_ROWS - 4 - 2 * side)
                )
                task_ref[3 * side + 2, number] = jnp.minimum(back, BACK_ROWS - 3 + 2 * side)
                base = 4 * side

                @pl.when(owner == own)
                def _():
                    mask = masks_ref[side, pl.ds(pair, 1), :]
                    field_ref[base + 3, pl.ds(number, 1), :] = mask.astype(F32)

                @pl.when(owner != own)
                def _():
                    mask = request_ref[owner, pl.ds(1 + 2 * turn + side, 1), :]
                    field_ref[base + 3, pl.ds(number, 1), :] = mask.astype(F32)

                spot = near

                @pl.when(here)
                def _():
                    near_ref[0, spot] = block
                    near_ref[1, spot] = (side * size + number) * 8
                    for field in range(3):
                        field_ref[base + field, pl.ds(number, 1), :] = (
                            moved_ref[field, pl.ds(block, 1), :]
                            + rest_ref[field, pl.ds(block, 1), :]
                        )
                    if side == 1:
                        both = angles_ref[block]
                        field_ref[8, pl.ds(number, 1), :] = both[0:1]
                        field_ref[9, pl.ds(number, 1), :] = both[1:2]

                near = near + jnp.where(here, 1, 0)
            return (number + 1, near)

        number, near = carry
        count = jnp.minimum(list_ref[owner, 1], jnp.where(owner == own, OWN_CAP, TASK_CAP))
        count = jnp.minimum(count, TASKS - number)
        return lax.fori_loop(0, count, task, (number, near))

    tasks, near = lax.fori_loop(0, devices, from_owner, (jnp.int32(0), jnp.int32(0)))
    task_ref[6, 0] = tasks
    near_ref[2, 0] = near


def pack_kernel(
    slots,
    rows_per,
    own_ref,
    map_ref,
    moved_ref,
    rest_ref,
    angles_ref,
    nodes_ref,
    out_ref,
    ids_ref,
):
    own = own_ref[0]
    devices = map_ref.shape[0] // rows_per
    owner = jnp.concatenate(
        [map_ref[pl.ds(own * rows_per + i, 1), :] for i in range(rows_per)], axis=1
    )
    blocks = owner.shape[1]
    mine = iota((devices, blocks), 0) == owner
    before = dot_nn(as_bf16(mine), strict_upper(blocks))
    rank = jnp.sum(jnp.where(mine, before, 0.0), axis=0, keepdims=True).astype(jnp.int32)
    place = owner * slots + rank
    move = as_bf16(iota((devices * slots, blocks), 0) == place)
    for field in range(5):
        if field < 3:
            values = moved_ref[field] + rest_ref[field]
        else:
            values = angles_ref[:, field - 3, :]
        moved = dot_nn(move, jnp.concatenate(split3(values), axis=1))
        moved = moved[:, :LANES] + moved[:, LANES : 2 * LANES] + moved[:, 2 * LANES :]
        out_ref[:, field * slots : (field + 1) * slots, :] = moved.reshape(devices, slots, LANES)
    nodes = nodes_ref[...]
    halves = jnp.concatenate(
        [(nodes >> 7).astype(F32).astype(BF16), (nodes & (LANES - 1)).astype(F32).astype(BF16)],
        axis=1,
    )
    moved = dot_nn(move, halves)
    ids_ref[...] = (moved[:, :LANES] * LANES + moved[:, LANES:]).astype(jnp.int32)


def sine_cosine(angle):
    half = 0.5 * angle
    sq = half * half
    sine = sq * (-1.0 / 39916800.0) + 1.0 / 362880.0
    for coef in (-1.0 / 5040.0, 1.0 / 120.0, -1.0 / 6.0, 1.0):
        sine = sine * sq + coef
    sine = sine * half
    cosine = sq * (1.0 / 479001600.0) - 1.0 / 3628800.0
    for coef in (1.0 / 40320.0, -1.0 / 720.0, 1.0 / 24.0, -0.5, 1.0):
        cosine = cosine * sq + coef
    return 2.0 * sine * cosine, 1.0 - 2.0 * sine * sine


def pair_kernel(
    slots, index_ref, count_ref, in_ref, masks_ref, out_ref, slave_ref, master_ref, sin_ref, cos_ref
):
    pairs = masks_ref.shape[1]
    count = jnp.minimum(count_ref[0], pairs)
    out_ref[...] = jnp.zeros_like(out_ref)

    def stage(pair, carry):
        source = index_ref[0, pair]
        slot = index_ref[1, pair]
        for field in range(3):
            slave_ref[pl.ds(pair * 8 + field, 1), :] = in_ref[source, pl.ds(field * slots + slot, 1), :]
        slave_ref[pl.ds(pair * 8 + 3, 1), :] = masks_ref[0, pl.ds(pair, 1), :].astype(F32)
        source = index_ref[2, pair]
        slot = index_ref[3, pair]
        for field in range(5):
            master_ref[pl.ds(pair * 8 + field, 1), :] = in_ref[source, pl.ds(field * slots + slot, 1), :]
        master_ref[pl.ds(pair * 8 + 5, 1), :] = masks_ref[1, pl.ds(pair, 1), :].astype(F32)
        return carry

    lax.fori_loop(0, count, stage, 0)
    sines, cosines = sine_cosine(master_ref[...])
    sin_ref[...] = sines
    cos_ref[...] = cosines

    def tile(pair, carry):
        base = pl.multiple_of(pair * 8, 8)
        slave = slave_ref[pl.ds(base, 8), :]
        columns = jnp.transpose(slave)
        master = master_ref[pl.ds(base, 8), :]
        sin_az = sin_ref[pl.ds(base + 3, 1), :]
        sin_pol = sin_ref[pl.ds(base + 4, 1), :]
        cos_az = cos_ref[pl.ds(base + 3, 1), :]
        cos_pol = cos_ref[pl.ds(base + 4, 1), :]
        normal = [cos_az * cos_pol, sin_az * cos_pol, sin_pol]
        shape = (LANES, LANES)
        dist = [
            jnp.broadcast_to(columns[:, k : k + 1], shape) - jnp.broadcast_to(master[k : k + 1], shape)
            for k in range(3)
        ]
        gap = dist[0] * normal[0] + dist[1] * normal[1] + dist[2] * normal[2]
        tang = dist[0] * dist[0] + dist[1] * dist[1] + dist[2] * dist[2] - gap * gap
        bend = gap * (-1.0 / PEN_DEPTH)
        soft = jnp.maximum(bend, 0.0) + jnp.log(1.0 + jnp.exp(-jnp.abs(bend)))
        press = soft * jnp.exp(-0.5 * tang)
        press = press * jnp.broadcast_to(columns[:, 3:4], shape)
        total = jnp.sum(press, axis=0, keepdims=True)
        scale = PEN_STIFF * PEN_DEPTH * master[5:6]
        push = [n * scale for n in normal]
        rows = jnp.concatenate(push + [jnp.zeros((5, LANES), F32)], axis=0)
        push_high, push_rest = split2(rows)
        both = jnp.concatenate([push_high, push_rest], axis=0)
        high, rest = split2(press)
        got = dot_nt(both, high) + dot_nt(both, rest)
        on_slave = got[0:8] + got[8:16]
        source = index_ref[0, pair]
        slot = index_ref[1, pair]
        for k in range(3):
            at = pl.ds(k * slots + slot, 1)
            out_ref[source, at, :] = out_ref[source, at, :] + on_slave[k : k + 1]
        source = index_ref[2, pair]
        slot = index_ref[3, pair]
        for k in range(3):
            at = pl.ds(k * slots + slot, 1)
            out_ref[source, at, :] = out_ref[source, at, :] - push[k] * total
        return carry

    lax.fori_loop(0, count, tile, 0)


def work_kernel(
    own_ref,
    task_ref,
    in_ref,
    start_ref,
    back_ref,
    force_ref,
    over_ref,
    field_ref,
    left_ref,
    gap_ref,
    far_ref,
    push_ref,
):
    own = own_ref[0]
    count = task_ref[6, 0]
    field_ref[...] = start_ref[...]
    over = jnp.max(in_ref[:, SEND_ROWS - 1, :])
    over_ref[0] = over.astype(jnp.int32)
    marks = force_ref.shape[0] - 8
    force_ref[marks:, :] = jnp.full((8, LANES), over, F32)

    def stage(step, carry):
        rows = []
        for k in range(COPY_STEP):
            task = jnp.minimum(COPY_STEP * step + k, count - 1)
            for side in range(2):
                source = task_ref[3 * side, task]
                first = jnp.minimum(task_ref[3 * side + 1, task], SEND_ROWS - 4 - 2 * side)
                places = range(3) if side == 0 else (4, 5, 6, 8, 9)
                for row, place in enumerate(places):
                    got = in_ref[source, pl.ds(first + row, 1), :]
                    here = start_ref[place, pl.ds(task, 1), :]
                    rows.append((place, task, jnp.where(source != own, got, here)))
        for place, task, row in rows:
            field_ref[place, pl.ds(task, 1), :] = row
        return carry

    lax.fori_loop(0, (count + COPY_STEP - 1) // COPY_STEP, stage, 0)
    size = field_ref.shape[1]
    slave = [field_ref[k] for k in range(3)]
    master = [field_ref[4 + k] for k in range(3)]
    sin_az, cos_az = sine_cosine(field_ref[8])
    sin_pol, cos_pol = sine_cosine(field_ref[9])
    normal = [cos_az * cos_pol, sin_az * cos_pol, sin_pol]

    def inner(a, b):
        return a[0] * b[0] + a[1] * b[1] + a[2] * b[2]

    zero = jnp.zeros_like(sin_pol)
    one = zero + 1.0
    slope = -1.0 / PEN_DEPTH
    hidden = 30000.0
    slave_bias = -0.5 * inner(slave, slave) - hidden * (1.0 - field_ref[3])
    master_bias = -0.5 * inner(master, master) - hidden * (1.0 - field_ref[7])
    stacks = (
        (left_ref, slave + [one, slave_bias]),
        (gap_ref, [slope * n for n in normal] + [-slope * inner(normal, master), zero]),
        (far_ref, master + [master_bias, one]),
        (push_ref, [PEN_STIFF * PEN_DEPTH * n for n in normal] + [zero, zero]),
    )
    for ref, rows in stacks:
        for row, value in enumerate(rows + [zero] * 3):
            parts = split3(value)
            for part in range(ref.shape[0]):
                ref[part, pl.ds(row, size, stride=8), :] = parts[part].astype(F32)

    def tile(step, carry):
        tasks = [TASK_STEP * step + k for k in range(TASK_STEP)]
        bases = [pl.multiple_of(task * 8, 8) for task in tasks]
        fields = []
        for base in bases:
            high, mid, low = [left_ref[p, pl.ds(base, 8), :] for p in range(3)]
            left = jnp.concatenate([high, high, mid, mid, high, low], axis=0).astype(BF16)
            sides = []
            for ref in (gap_ref, far_ref):
                high, mid, low = [ref[p, pl.ds(base, 8), :] for p in range(3)]
                sides.append(jnp.concatenate([high, mid, high, mid, low, high], axis=0))
            fields.append(dot_tn(left, jnp.concatenate(sides, axis=1).astype(BF16)))
        presses = []
        for field in fields:
            bend = field[:, :LANES]
            power = field[:, LANES:] + bend * bend * (0.5 * PEN_DEPTH * PEN_DEPTH)
            soft = jnp.maximum(bend, 0.0) + jnp.log(1.0 + jnp.exp(-jnp.abs(bend)))
            presses.append(soft * jnp.exp(power))
        results = []
        for base, press in zip(bases, presses):
            push = jnp.concatenate([push_ref[p, pl.ds(base, 8), :] for p in range(2)], axis=0)
            push = push.astype(BF16)
            got = dot_nt(
                jnp.concatenate([push, push], axis=1), jnp.concatenate(split2(press), axis=1)
            )
            total = jnp.sum(press, axis=0, keepdims=True)
            results.append((got[0:8] + got[8:16], total * (PEN_STIFF * PEN_DEPTH)))
        for task, base, (on_slave, total) in zip(tasks, bases, results):
            normals = gap_ref[0, pl.ds(base, 8), :] + gap_ref[1, pl.ds(base, 8), :]
            normals = normals + gap_ref[2, pl.ds(base, 8), :]
            force_ref[pl.ds(base, 8), :] = on_slave
            force_ref[pl.ds(base + size * 8, 8), :] = normals * (total * (-1.0 / slope))
            live = task < count
            slave_from = task_ref[0, task]
            master_from = task_ref[3, task]

            @pl.when(live & (slave_from != own))
            def _():
                for k in range(3):
                    back_ref[slave_from, :, span_of(task_ref[2, task] + k)] = on_slave[k : k + 1]

            @pl.when(live & (master_from != own))
            def _():
                back_ref[master_from, :, span_of(task_ref[5, task])] = total

        return carry

    lax.fori_loop(0, (count + TASK_STEP - 1) // TASK_STEP, tile, 0)


def near_kernel(
    near_ref,
    entry_ref,
    nodes_ref,
    force_ref,
    inner_ref,
    whole_ref,
    angles_ref,
    out_ref,
    normal_ref,
):
    count = near_ref[2, 0]

    def step(turn, acc):
        ids = []
        forces = []
        for k in range(BLOCK_STEP):
            valid = BLOCK_STEP * turn + k < count
            number = jnp.where(valid, BLOCK_STEP * turn + k, 0)
            ids.append(nodes_ref[pl.ds(near_ref[0, number], 1), :])
            rows = force_ref[pl.ds(pl.multiple_of(near_ref[1, number], 8), 8), :]
            rows = jnp.where(valid, rows, 0.0)
            forces.append([rows[f : f + 1] for f in range(3)])
        return acc + scatter_terms(ids, forces)

    steps = (count + BLOCK_STEP - 1) // BLOCK_STEP
    acc = lax.fori_loop(0, steps, step, jnp.zeros((6 * GROUP, LANES), F32))
    marks = force_ref[force_ref.shape[0] - 8 :, :]
    total = fold_terms(acc)
    rows = total.shape[0]
    total = jnp.where(marks[0:1] > 0.0, whole_ref[:rows, :], total)
    out_ref[:rows, :] = inner_ref[...] + total
    out_ref[rows:, :] = marks
    entries = jnp.where(jnp.max(marks) > 0.0, 0, entry_ref[4, 0])

    def turn_angles(turn, carry):
        both = []
        for k in range(8):
            block = entry_ref[0, jnp.minimum(8 * turn + k, entries - 1)]
            both.append(angles_ref[block])
        azimuth = jnp.concatenate([pair[0:1] for pair in both], axis=0)
        polar = jnp.concatenate([pair[1:2] for pair in both], axis=0)
        sin_az, cos_az = sine_cosine(azimuth)
        sin_pol, cos_pol = sine_cosine(polar)
        at = pl.ds(pl.multiple_of(turn * 8, 8), 8)
        normal_ref[0, at, :] = cos_az * cos_pol
        normal_ref[1, at, :] = sin_az * cos_pol
        normal_ref[2, at, :] = sin_pol
        return carry

    lax.fori_loop(0, (entries + 7) // 8, turn_angles, 0)


def far_kernel(
    chunks,
    grid,
    own_ref,
    entry_ref,
    back_ref,
    nodes_ref,
    normal_ref,
    near_ref,
    faces_ref,
    out_ref,
    send_ref,
    value_ref,
):
    rows = out_ref.shape[0]
    count = jnp.where(jnp.max(near_ref[rows:, :]) > 0.0, 0, entry_ref[4, 0])

    def step(turn, acc):
        ids = []
        forces = []
        for k in range(BLOCK_STEP):
            valid = BLOCK_STEP * turn + k < count
            number = jnp.where(valid, BLOCK_STEP * turn + k, 0)
            block = entry_ref[0, number]
            role = entry_ref[1, number]
            worker = entry_ref[2, number]
            first = entry_ref[3, number]
            ids.append(nodes_ref[pl.ds(block, 1), :])
            total = back_ref[worker, :, span_of(first)]
            rows = []
            for field in range(3):
                row = back_ref[worker, :, span_of(jnp.minimum(first + field, BACK_ROWS - 1))]
                row = jnp.where(role == 1, -normal_ref[field, pl.ds(number, 1), :] * total, row)
                rows.append(jnp.where(valid, row, 0.0))
            forces.append(rows)
        return acc + scatter_terms(ids, forces)

    steps = (count + BLOCK_STEP - 1) // BLOCK_STEP
    acc = lax.fori_loop(0, steps, step, jnp.zeros((6 * GROUP, LANES), F32))
    out_ref[...] = near_ref[:rows, :] + fold_terms(acc)
    send_faces(own_ref[0], grid, out_ref, chunks, faces_ref, send_ref, value_ref)


def element_kernel(conn_ref, coords_ref, disp_ref, modulus_ref, out_ref, order_ref):
    chunks = coords_ref.shape[1] // LANES
    groups = conn_ref.shape[1] // LANES
    for group in range(groups):
        order_ref[pl.ds(group * 8, 8), :] = conn_ref[:, group * LANES : (group + 1) * LANES]
    pos = []
    disp = []
    for corner in range(8):
        ids = order_ref[pl.ds(corner, groups, stride=8), :]
        found = gather_chunks(
            lambda field, chunk: (coords_ref if field < 3 else disp_ref)[
                field % 3 : field % 3 + 1, chunk * LANES : (chunk + 1) * LANES
            ],
            6,
            chunks,
            ids,
        )
        pos.append(found[:3])
        disp.append(found[3:])
    first = list(pos[0])
    pos = [[pos[corner][j] - first[j] for j in range(3)] for corner in range(8)]

    def signed(values, signs):
        total = None
        for value, sign in zip(values, signs):
            if total is None:
                total = value if sign > 0 else -value
            else:
                total = total + value if sign > 0 else total - value
        return total

    corner_signs = [[XI_SIGNS[corner][k] for corner in range(8)] for k in range(3)]
    jac = [
        [signed([pos[c][j] for c in range(8)], corner_signs[k]) * 0.125 for k in range(3)]
        for j in range(3)
    ]
    cof = [
        [
            jac[(j + 1) % 3][(k + 1) % 3] * jac[(j + 2) % 3][(k + 2) % 3]
            - jac[(j + 1) % 3][(k + 2) % 3] * jac[(j + 2) % 3][(k + 1) % 3]
            for k in range(3)
        ]
        for j in range(3)
    ]
    det = jac[0][0] * cof[0][0] + jac[0][1] * cof[0][1] + jac[0][2] * cof[0][2]
    volume = 8.0 * det
    inverse = 1.0 / volume
    scaled = [[cof[j][k] * inverse for k in range(3)] for j in range(3)]
    grad = [[signed(scaled[j], XI_SIGNS[c]) for j in range(3)] for c in range(8)]

    def summed(terms):
        total = terms[0]
        for term in terms[1:]:
            total = total + term
        return total

    ugrad = [
        [summed([disp[c][i] * grad[c][j] for c in range(8)]) for j in range(3)] for i in range(3)
    ]
    modulus = modulus_ref[...]
    dilation = ugrad[0][0] + ugrad[1][1] + ugrad[2][2]
    stress = [[modulus * (ugrad[i][j] + ugrad[j][i]) for j in range(3)] for i in range(3)]
    for i in range(3):
        stress[i][i] = stress[i][i] + modulus * dilation
    squares = summed([grad[c][j] * grad[c][j] for c in range(8) for j in range(3)])
    hour_coef = HG_COEF * modulus * volume * squares
    shapes = []
    modes = []
    for a in range(4):
        hour_pos = [signed([pos[c][j] for c in range(8)], HOUR_VEC[a]) for j in range(3)]
        gam = [
            float(HOUR_VEC[a][c]) - summed([hour_pos[j] * grad[c][j] for j in range(3)])
            for c in range(8)
        ]
        shapes.append(gam)
        modes.append(
            [hour_coef * summed([disp[c][i] * gam[c] for c in range(8)]) for i in range(3)]
        )
    flux = [[volume * stress[i][j] for j in range(3)] for i in range(3)]
    acc = jnp.zeros((6 * GROUP, LANES), F32)
    for corner in range(8):
        ids = order_ref[pl.ds(corner, groups, stride=8), :]
        force = []
        for i in range(3):
            value = summed([flux[i][j] * grad[corner][j] for j in range(3)])
            value = value + summed([modes[a][i] * shapes[a][corner] for a in range(4)])
            force.append(-value)
        for group in range(0, groups, 2):
            picks = range(group, min(group + 2, groups))
            acc = acc + scatter_terms(
                [ids[g : g + 1] for g in picks], [[f[g : g + 1] for f in force] for g in picks]
            )
    out_ref[...] = fold_terms(acc)


def around(grid):
    return [(dx, dy) for dx in (-1, 0, 1) for dy in (-1, 0, 1) if (dx, dy) != (0, 0)]


def face_toward(dx, dy):
    if dx:
        return 1 if dx > 0 else 0
    return 3 if dy > 0 else 2


def neighbour(own, grid, dx, dy):
    ix = own // grid[1] + dx
    iy = own % grid[1] + dy
    there = (ix >= 0) & (ix < grid[0]) & (iy >= 0) & (iy < grid[1])
    return there, jnp.where(there, ix * grid[1] + iy, 0)


def send_faces(own, grid, total_ref, chunks, faces_ref, send_ref, value_ref):
    value_ref[...] = jnp.zeros_like(value_ref)
    parts = faces_ref.shape[1] // LANES
    for part in range(parts):
        ids = faces_ref[:, part * LANES : (part + 1) * LANES]
        found = gather_chunks(
            lambda field, chunk: total_ref[field * GROUP + chunk : field * GROUP + chunk + 1, :],
            3,
            chunks,
            ids,
        )
        for field in range(3):
            at = field * parts + part
            for face in range(4):
                value_ref[face, at : at + 1, :] = found[field][face : face + 1]
    for dx, dy in around(grid):
        there, target = neighbour(own, grid, dx, dy)

        @pl.when(there)
        def _():
            for row in range(3 * parts):
                span = slice(row * LANES, (row + 1) * LANES)
                send_ref[target, :, span] = value_ref[face_toward(dx, dy), row : row + 1, :]


def face_map_kernel(chunks, faces_ref, low_ref, high_ref, table_ref):
    parts = faces_ref.shape[1] // LANES
    acc = None
    for row in range(2):
        ids = [faces_ref[row : row + 1, p * LANES : (p + 1) * LANES] for p in range(parts)]
        zero = jnp.zeros((1, LANES), F32)
        places = [(iota((1, LANES), 1) + (p * LANES + 1)).astype(F32) for p in range(parts)]
        fields = [[place if f == row else zero for f in range(3)] for place in places]
        terms = scatter_terms(ids, fields)
        acc = terms if acc is None else acc + terms
    table_ref[...] = fold_terms(acc)
    low_ref[...] = jnp.zeros_like(low_ref)
    high_ref[...] = jnp.zeros_like(high_ref)
    for part in range(parts):
        ids = faces_ref[:, part * LANES : (part + 1) * LANES]
        found = gather_chunks(
            lambda field, chunk: table_ref[field * GROUP + chunk : field * GROUP + chunk + 1, :],
            2,
            chunks,
            ids,
        )
        for field in range(2):
            at = field * parts + part
            low_ref[at : at + 1, :] = found[field][2:3]
            high_ref[at : at + 1, :] = found[field][3:4]


def moved_faces(values, places, parts):
    results = [None] * (3 * parts)
    for part in range(parts):
        place = places[part].astype(jnp.int32) - 1
        low = jnp.broadcast_to(place & (LANES - 1), values.shape)
        got = jnp.take_along_axis(values, low, axis=1, mode="promise_in_bounds")
        for field in range(3):
            total = jnp.zeros((1, LANES), F32)
            for source in range(parts):
                at = field * parts + source
                total = jnp.where(place >> 7 == source, got[at : at + 1], total)
            results[field * parts + part] = total
    return results


def assemble_kernel(slots, back_ref, ids_ref, out_ref):
    devices = back_ref.shape[0]

    def step(turn, acc):
        ids = ids_ref[pl.ds(turn * slots, slots), :]
        values = back_ref[turn]
        for slot in range(0, slots, 2):
            picks = range(slot, min(slot + 2, slots))
            acc = acc + scatter_terms(
                [ids[s : s + 1] for s in picks],
                [[values[f * slots + s : f * slots + s + 1] for f in range(3)] for s in picks],
            )
        return acc

    acc = lax.fori_loop(0, devices, step, jnp.zeros((6 * GROUP, LANES), F32))
    out_ref[...] = fold_terms(acc)


def final_kernel(
    grid, own_ref, total_ref, got_ref, low_ref, high_ref, faces_ref, velocity_ref, mass_ref, out_ref, sum_ref
):
    own = own_ref[0]
    parts = faces_ref.shape[1] // LANES

    def block(dx, dy):
        there, source = neighbour(own, grid, dx, dy)
        spans = [slice(row * LANES, (row + 1) * LANES) for row in range(3 * parts)]
        return [jnp.where(there, got_ref[source, :, span], 0.0) for span in spans]

    def side(dy, map_ref):
        rows = block(0, dy)
        for field, dx in enumerate((-1, 1)):
            places = [map_ref[field * parts + p : field * parts + p + 1, :] for p in range(parts)]
            corner = block(dx, dy)
            corner = corner + [jnp.zeros((1, LANES), F32)] * (-len(corner) % 8)
            moved = moved_faces(jnp.concatenate(corner, axis=0), places, parts)
            rows = [a + b for a, b in zip(rows, moved)]
        return rows

    added = [block(-1, 0), block(1, 0), side(-1, low_ref), side(1, high_ref)]
    acc = jnp.zeros((6 * GROUP, LANES), F32)
    for face, rows in enumerate(added):
        ids = [faces_ref[face : face + 1, p * LANES : (p + 1) * LANES] for p in range(parts)]
        acc = acc + scatter_terms(
            ids, [[rows[f * parts + p] for f in range(3)] for p in range(parts)]
        )
    sum_ref[...] = total_ref[...] + fold_terms(acc)
    for chunk in range(out_ref.shape[1] // LANES):
        span = slice(chunk * LANES, (chunk + 1) * LANES)
        scale = TIME_STEP / mass_ref[chunk : chunk + 1, :]
        for field in range(3):
            row = field * GROUP + chunk
            out_ref[field : field + 1, span] = (
                velocity_ref[field : field + 1, span] + scale * sum_ref[row : row + 1, :]
            )


def call(kernel, outs, in_smem, args, scratch=(), out_smem=(), in_any=()):
    def spec(smem, anywhere=False):
        if anywhere:
            return pl.BlockSpec(memory_space=pl.ANY)
        return pl.BlockSpec(memory_space=pltpu.SMEM if smem else pltpu.VMEM)

    return pl.pallas_call(
        kernel,
        out_shape=[jax.ShapeDtypeStruct(shape, dtype) for shape, dtype in outs],
        in_specs=[spec(i in in_smem, i in in_any) for i in range(len(args))],
        out_specs=[spec(i in out_smem) for i in range(len(outs))],
        scratch_shapes=list(scratch),
        compiler_params=pltpu.CompilerParams(vmem_limit_bytes=VMEM_LIMIT),
    )(*args)


def exchange(low, high, axis):
    count = lax.axis_size(axis)
    forward = [(i, i + 1) for i in range(count - 1)]
    backward = [(target, source) for source, target in forward]
    return lax.ppermute(high, axis, forward), lax.ppermute(low, axis, backward)


def local(
    connectivity,
    face_nodes,
    coords,
    displacement,
    velocity,
    node_mass,
    modulus,
    surf_nodes,
    surf_ref,
    surf_angles,
    owner_map,
    pair_blocks,
    pair_masks,
    pair_count,
):
    axes = ("gx", "gy")
    devices = lax.axis_size("gx") * lax.axis_size("gy")
    per_dev = surf_nodes.shape[0]
    rows_per = per_dev // LANES
    node_count = coords.shape[1]
    chunks = node_count // LANES
    slots = 2 * per_dev // devices
    pairs = pair_blocks.shape[1]
    own = lax.axis_index(axes).reshape(1).astype(jnp.int32)
    owners = owner_map.reshape(devices * rows_per, LANES)
    face_pad = -face_nodes.shape[1] % LANES
    faces = jnp.pad(face_nodes, ((0, 4), (0, face_pad)), constant_values=-1)
    parts = faces.shape[1] // LANES
    face_rows = -(-3 * parts // 8) * 8
    total_shape = ((3 * GROUP, LANES), F32)
    face_shape = ((face_rows, LANES), F32)
    send_shape = ((devices, 1, 3 * parts * LANES), F32)
    grid = (lax.axis_size("gx"), lax.axis_size("gy"))

    def to_all(values):
        return lax.all_to_all(values, axes, split_axis=0, concat_axis=0, tiled=True)

    [request] = call(
        functools.partial(request_kernel, rows_per),
        [((devices, REQUEST_ROWS, LANES), jnp.int32)],
        (),
        (pair_count.reshape(1, 1), owners, pair_blocks, pair_masks),
    )
    asked = to_all(request)
    rest = jnp.transpose(surf_ref, (1, 0, 2))
    moved, block_of = call(
        functools.partial(segment_kernel, slots, rows_per),
        [((3, per_dev, LANES), F32), ((devices * slots // LANES, LANES), jnp.int32)],
        (0,),
        (own, owners, displacement, surf_nodes),
        [pltpu.VMEM((8, LANES), jnp.int32), pltpu.SemaphoreType.DMA],
        (),
        (1,),
    )
    map_low, map_high = call(
        functools.partial(face_map_kernel, chunks),
        [face_shape, face_shape],
        (),
        (faces,),
        [pltpu.VMEM((3 * GROUP, LANES), F32)],
    )
    map_low, map_high = exchange(map_low, map_high, "gy")
    lists = asked[:, 0, :]
    outbound, entries = call(
        functools.partial(plan_kernel, slots),
        [((devices, SEND_ROWS, LANES), F32), ((8, ENTRIES), jnp.int32)],
        (0, 1),
        (lists, block_of, moved, rest, surf_angles),
        [pltpu.SMEM((2, devices), jnp.int32)],
        (1,),
    )
    tasks, near_list, fields = call(
        functools.partial(table_kernel, slots),
        [((8, TASKS), jnp.int32), ((8, 2 * TASKS), jnp.int32), ((10, TASKS, LANES), F32)],
        (0, 1, 2),
        (own, lists, block_of, asked, pair_masks, moved, rest, surf_angles),
        [pltpu.SMEM((2, devices), jnp.int32)],
        (0, 1),
    )
    inbound = to_all(outbound)
    inbound, map_low, map_high = lax.optimization_barrier((inbound, map_low, map_high))
    back, forces, over = call(
        work_kernel,
        [
            ((devices, 1, BACK_ROWS * LANES), F32),
            ((2 * TASKS * 8 + 8, LANES), F32),
            ((1,), jnp.int32),
        ],
        (0, 1),
        (own, tasks, inbound, fields),
        [
            pltpu.VMEM((10, TASKS, LANES), F32),
            pltpu.VMEM((3, TASKS * 8, LANES), F32),
            pltpu.VMEM((3, TASKS * 8, LANES), F32),
            pltpu.VMEM((3, TASKS * 8, LANES), F32),
            pltpu.VMEM((2, TASKS * 8, LANES), F32),
        ],
        (2,),
    )
    returned = to_all(back)

    def by_owners():
        [index] = call(
            functools.partial(routing_kernel, rows_per),
            [((4, pairs), jnp.int32)],
            (0, 1),
            (own, pair_count, owners, pair_blocks),
        )
        outbound, ids = call(
            functools.partial(pack_kernel, slots, rows_per),
            [((devices, 5 * slots, LANES), F32), ((devices * slots, LANES), jnp.int32)],
            (0,),
            (own, owners, moved, rest, surf_angles, surf_nodes),
        )
        [owned] = call(
            functools.partial(pair_kernel, slots),
            [((devices, 3 * slots, LANES), F32)],
            (0, 1),
            (index, pair_count, to_all(outbound), pair_masks),
            [pltpu.VMEM((pairs * 8, LANES), F32)] * 4,
        )
        [whole] = call(
            functools.partial(assemble_kernel, slots), [total_shape], (), (to_all(owned), ids)
        )
        return jnp.pad(whole, ((0, forces.shape[0] - whole.shape[0]), (0, 0)))

    whole = lax.cond(over[0] > 0, by_owners, lambda: forces)
    late, unused = lax.optimization_barrier((coords, over))
    [internal] = call(
        element_kernel,
        [total_shape],
        (),
        (connectivity, late, displacement, modulus.reshape(-1, LANES)),
        [pltpu.VMEM((connectivity.shape[1] // LANES * 8, LANES), jnp.int32)],
    )
    near, normals = call(
        near_kernel,
        [((3 * GROUP + 8, LANES), F32), ((3, ENTRIES, LANES), F32)],
        (0, 1),
        (near_list, entries, surf_nodes, forces, internal, whole, surf_angles),
    )
    total, send = call(
        functools.partial(far_kernel, chunks, grid),
        [total_shape, send_shape],
        (0, 1),
        (own, entries, returned, surf_nodes, normals, near, faces),
        [pltpu.VMEM((4,) + face_shape[0], F32)],
    )
    [result] = call(
        functools.partial(final_kernel, grid),
        [((3, node_count), F32)],
        (0,),
        (
            own,
            total,
            to_all(send),
            map_low,
            map_high,
            faces,
            velocity,
            node_mass.reshape(chunks, LANES),
        ),
        [pltpu.VMEM((3 * GROUP, LANES), F32)],
    )
    return result


def solution(mesh):
    in_specs = (
        P(None, ("gx", "gy")),
        P(None, ("gx", "gy")),
        P(None, ("gx", "gy")),
        P(None, ("gx", "gy")),
        P(None, ("gx", "gy")),
        P(("gx", "gy")),
        P(("gx", "gy")),
        P(("gx", "gy"), None),
        P(("gx", "gy"), None, None),
        P(("gx", "gy"), None, None),
        P(),
        P(None, ("gx", "gy")),
        P(None, ("gx", "gy"), None),
        P(("gx", "gy")),
    )
    out_specs = P(None, ("gx", "gy"))
    return jax.shard_map(local, mesh=mesh, in_specs=in_specs, out_specs=out_specs, check_vma=False)
```
